32 devices in a mesh: dp: 8 (over z, y), sub: 4 (over x, core).
Axes of the slice: x: 2, y: 2, z: 4, core: 2. Of those that a mesh axis runs over, the one named last changes fastest.
Arguments:
- latents: float32 [64, 128, 768], P(('dp', 'sub')), may hold values from -6 to 6
- inputs: bfloat16 [64, 1024, 768], P(('dp', 'sub')), may hold values from -6 to 6
- counts: int32 [64], P(('dp', 'sub')), may hold values from 512 to 1024, as said below
- flags: int32 [2], replicated, may hold values from 0 to 1, as said below
- cross_attn: bfloat16 [768, 3072], P('dp', 'sub'), may hold values from -2.8 to 2.8
- cross_up: bfloat16 [768, 3072], P('dp', 'sub'), may hold values from -0.21875 to 0.21875
- cross_down: bfloat16 [3072, 768], P('dp', 'sub'), may hold values from -0.109375 to 0.109375
- self_attn: bfloat16 [768, 3072], P('dp', 'sub'), may hold values from -1 to 1
- self_up: bfloat16 [768, 3072], P('dp', 'sub'), may hold values from -0.21875 to 0.21875
- self_down: bfloat16 [3072, 768], P('dp', 'sub'), may hold values from -0.109375 to 0.109375
- gains: bfloat16 [5, 768], P(None, 'dp'), may hold values from 0.5 to 1.5
- cotangent: float32 [64, 128, 768], P(('dp', 'sub')), may hold values from -6 to 6
Outputs:
- latents_out: float32 [64, 128, 768], P(('dp', 'sub'))
- latents_grad: float32 [64, 128, 768], P(('dp', 'sub'))
- inputs_grad: float32 [64, 1024, 768], P(('dp', 'sub'))
- cross_attn_grad: float32 [768, 3072], P('dp', 'sub')
- cross_up_grad: float32 [768, 3072], P('dp', 'sub')
- cross_down_grad: float32 [3072, 768], P('dp', 'sub')
- self_attn_grad: float32 [768, 3072], P('dp', 'sub')
- self_up_grad: float32 [768, 3072], P('dp', 'sub')
- self_down_grad: float32 [3072, 768], P('dp', 'sub')
- gains_grad: float32 [5, 768], P(None, 'dp')
The draws below stay inside these ranges and needn't reach their ends.
Inputs may be any that keep to these rules, and one draw needn't show every extreme that they name: `counts`: within each aligned group of 2 items one item has all 1024 slots live. `flags`: at least one step has flag 1 and at least one has flag 0.
All inputs are finite; a program needn't handle non-finite values.
Results may differ from the reference program's by a relative error of at most 0.019.
Values may be sent and summed in bfloat16 or wider, within the bound.
A program may use at most 256 MiB of HBM per device.

```python
import jax
import jax.numpy as jnp
from jax import lax

D = 768
HEADS = 12
HEAD = 64
FF = 3072
LAT = 128
ITEM_TOK = 1024
ITEMS_DEV = 2
STEPS = 2
ITEMS = 64


def draw_counts(key, part):
    lengths = jax.random.randint(jax.random.fold_in(key, 1), (ITEMS,), ITEM_TOK // 2, ITEM_TOK + 1)
    chosen = jax.random.randint(jax.random.fold_in(key, 2), (ITEMS // ITEMS_DEV,), 0, ITEMS_DEV)
    full_item = jnp.arange(ITEMS) % ITEMS_DEV == jnp.repeat(chosen, ITEMS_DEV)
    return jnp.where(full_item, ITEM_TOK, lengths).astype(jnp.int32)


def draw_flags(key, part):
    bits = jax.random.randint(jax.random.fold_in(key, 3), (STEPS,), 0, 2)
    set_one = jax.random.randint(jax.random.fold_in(key, 6), (), 0, STEPS)
    offset = jax.random.randint(jax.random.fold_in(key, 7), (), 1, STEPS)
    set_zero = (set_one + offset) % STEPS
    position = jnp.arange(STEPS)
    bits = jnp.where(position == set_one, 1, bits)
    bits = jnp.where(position == set_zero, 0, bits)
    return bits.astype(jnp.int32)


def attention_weight(key, out_scale):
    base = jax.random.truncated_normal(key, -4.0, 4.0, (D, 4 * D), jnp.float32)
    column = jnp.arange(4 * D)[None, :]
    return base * jnp.where(column < 3 * D, D ** (-0.5), out_scale)


def draw_cross_attn(key, part):
    return attention_weight(jax.random.fold_in(key, 4), 0.7).astype(jnp.bfloat16)


def draw_self_attn(key, part):
    return attention_weight(jax.random.fold_in(key, 5), 0.25).astype(jnp.bfloat16)


def steps_of(rng, dims, cuts, low, high):
    level = 1.0
    for axis_at, shards_of in cuts:
        steps = jax.random.uniform(jax.random.fold_in(jax.random.fold_in(rng, 6), axis_at), (shards_of,), jnp.float32, low / len(cuts), high / len(cuts))
        level = level * jnp.repeat(jnp.exp(steps), dims[axis_at] // shards_of).reshape((-1,) + (1,) * (len(dims) - 1 - axis_at))
    return level


def scatter_about(key, dims, deviation, most, split=(), kind=jnp.bfloat16):
    values = jax.random.normal(key, dims, jnp.float32) * deviation
    if len(split) > 0:
        values = steps_of(key, dims, split, -0.22, 0.18) * values
    return jnp.clip(values, min=-most, max=most).astype(kind)


def setup_inputs(seed: int = 0) -> dict:
    key_list = jax.random.split(jax.random.key(seed), 13)
    return {
        "latents": scatter_about(key_list[0], (ITEMS, LAT, D), 1.0, 6.0, ((0, 32),), jnp.float32),
        "inputs": scatter_about(key_list[1], (ITEMS, ITEM_TOK, D), 1.0, 6.0, ((0, 32),)),
        "counts": draw_counts(jax.random.fold_in(key_list[12], 71), 0),
        "flags": draw_flags(jax.random.fold_in(key_list[12], 71), 0),
        "cross_attn": draw_cross_attn(jax.random.fold_in(key_list[12], 71), 0),
        "cross_up": scatter_about(key_list[5], (D, FF), D ** -0.5, 0.21875, ((0, 8), (1, 4))),
        "cross_down": scatter_about(key_list[6], (FF, D), FF ** -0.5, 0.109375, ((0, 8), (1, 4))),
        "self_attn": draw_self_attn(jax.random.fold_in(key_list[12], 71), 0),
        "self_up": scatter_about(key_list[8], (D, FF), D ** -0.5, 0.21875, ((0, 8), (1, 4))),
        "self_down": scatter_about(key_list[9], (FF, D), FF ** -0.5, 0.109375, ((0, 8), (1, 4))),
        "gains": jnp.clip(1.0 + 0.1 * jax.random.normal(key_list[10], (5, D), jnp.float32), 0.5, 1.5).astype(jnp.bfloat16),
        "cotangent": scatter_about(key_list[11], (ITEMS, LAT, D), 1.0, 6.0, ((0, 32),), jnp.float32),
    }


EPSILON = 1e-05
MASKED = -1e+30

@jax.custom_vjp
def low(v):
    return lax.optimization_barrier(v.astype(jnp.bfloat16)).astype(jnp.float32)

@jax.custom_vjp
def low_back(v):
    return v

def low_keep(v):
    return (low(v), None)

def low_pass(kept, grad):
    return (grad,)

def back_keep(v):
    return (v, None)

def back_low(kept, grad):
    return (low(grad),)
low.defvjp(low_keep, low_pass)
low_back.defvjp(back_keep, back_low)

def layer_norm(values, gain_row):
    centred = values - lax.optimization_barrier(jnp.mean(values, axis=-1, keepdims=True))
    inverse = lax.rsqrt(lax.optimization_barrier(jnp.mean(centred * centred, axis=-1, keepdims=True)) + EPSILON)
    return centred * inverse * gain_row

def product(left_side, right_side):
    return jnp.dot(left_side, right_side, precision=lax.Precision.HIGHEST, preferred_element_type=jnp.float32)

def attend(queries, keys, values, valid_keys):
    query_heads = queries.reshape(queries.shape[0], HEADS, HEAD)
    key_heads = keys.reshape(keys.shape[0], HEADS, HEAD)
    value_heads = values.reshape(values.shape[0], HEADS, HEAD)
    raw_scores = jnp.einsum('qhd,khd->hqk', query_heads, key_heads, precision=lax.Precision.HIGHEST) * HEAD ** (-0.5)
    scores = jnp.where(valid_keys[None, None, :], low_back(raw_scores), MASKED)
    weights = low(jax.nn.softmax(scores, axis=-1))
    mixed = jnp.einsum('hqk,khd->qhd', weights, value_heads, precision=lax.Precision.HIGHEST)
    return mixed.reshape(queries.shape[0], D)

def feed_forward(residual, gain_row, up_weight, down_weight):
    normed = low(layer_norm(residual, gain_row))
    pre_act = low_back(product(normed, up_weight))
    hidden = low(jax.nn.gelu(pre_act, approximate=True))
    return low_back(product(hidden, down_weight))

def item_layer(weight_all, latent, tokens, count, keep_one):
    cross_w, cross_upw, cross_downw, self_w, self_upw, self_downw, gain_all = weight_all
    latent_norm = low(layer_norm(latent, gain_all[0]))
    token_norm = low(layer_norm(tokens, gain_all[1]))
    queries = low(low_back(product(latent_norm, cross_w[:, :D])))
    key_value = low(low_back(product(token_norm, cross_w[:, D:3 * D])))
    valid_keys = jnp.arange(ITEM_TOK) < count
    attended = low(low_back(attend(queries, key_value[:, :D], key_value[:, D:], valid_keys)))
    middle = latent + keep_one * low_back(product(attended, cross_w[:, 3 * D:]))
    after_cross = middle + keep_one * feed_forward(middle, gain_all[2], cross_upw, cross_downw)
    self_norm = low(layer_norm(after_cross, gain_all[3]))
    self_qkv = low(low_back(product(self_norm, self_w[:, :3 * D])))
    every_key = jnp.ones((LAT,), dtype=bool)
    self_out = low(low_back(attend(self_qkv[:, :D], self_qkv[:, D:2 * D], self_qkv[:, 2 * D:], every_key)))
    after_attn = after_cross + low_back(product(self_out, self_w[:, 3 * D:]))
    return after_attn + feed_forward(after_attn, gain_all[4], self_upw, self_downw)

def reference(latents, inputs, counts, flags, cross_attn, cross_up, cross_down, self_attn, self_up, self_down, gains, cotangent):
    weight_list = (cross_attn, cross_up, cross_down, self_attn, self_up, self_down, gains)
    weights = tuple((matrix.astype(jnp.float32) for matrix in weight_list))
    tokens_all = inputs.astype(jnp.float32)
    step_index = jnp.arange(ITEMS) % ITEMS_DEV * STEPS // ITEMS_DEV
    keep_all = (1 - flags[step_index]).astype(jnp.float32)

    def forward(latent_all, token_all, weight_all):

        def one_item(packed):
            return item_layer(weight_all, packed[0], packed[1], packed[2], packed[3])
        return lax.map(jax.checkpoint(one_item), (latent_all, token_all, counts, keep_all))
    result, pull_back = jax.vjp(forward, latents, tokens_all, weights)
    grad_latent, grad_tokens, grad_weights = pull_back(cotangent)
    return (result, grad_latent, grad_tokens, grad_weights[0], grad_weights[1], grad_weights[2], grad_weights[3], grad_weights[4], grad_weights[5], grad_weights[6])
```

```python
import functools

import jax
import jax.numpy as jnp
from jax import lax
from jax.experimental import pallas as pl
from jax.experimental.pallas import tpu as pltpu
from jax.sharding import PartitionSpec as P

HEADS = 12
EPSILON = 1e-05
MASKED = -1e30
MESH_ID = pl.DeviceIdType.MESH
F32 = jnp.float32
BF16 = jnp.bfloat16
ANY = pl.BlockSpec(memory_space=pl.ANY)
VMEM = pl.BlockSpec(memory_space=pltpu.VMEM)


class Place:
    def __init__(self):
        dp, sub = lax.axis_index("dp"), lax.axis_index("sub")
        self.z, self.y, self.x, self.c = dp // 2, dp % 2, sub // 2, sub % 2

    def dev(self, z=None, y=None, x=None, c=None):
        z = self.z if z is None else z
        y = self.y if y is None else y
        x = self.x if x is None else x
        c = self.c if c is None else c
        return (z * 2 + y, x * 2 + c)

    def zk(self, k):
        return (self.z + k) % 4


class Sems:
    def __init__(self, send, recv):
        self.send, self.recv, self.count, self.sent = send, recv, 0, []

    def copy(self, src, dst, device):
        made = pltpu.make_async_remote_copy(
            src_ref=src,
            dst_ref=dst,
            send_sem=self.send.at[self.count],
            recv_sem=self.recv.at[self.count],
            device_id=device,
            device_id_type=MESH_ID,
        )
        self.count += 1
        made.start()
        self.sent.append(made)
        return made

    def drain(self):
        for made in self.sent:
            made.wait_send()


def greet(place, devices):
    barrier = pltpu.get_barrier_semaphore()
    for device in devices:
        pl.semaphore_signal(barrier, inc=1, device_id=device, device_id_type=MESH_ID)
    pl.semaphore_wait(barrier, len(devices))


def partners(place):
    found = [
        place.dev(c=1 - place.c),
        place.dev(x=1 - place.x),
        place.dev(y=1 - place.y),
    ]
    for k in (1, 2, 3):
        found.append(place.dev(z=place.zk(k)))
    for k in (1, 2, 3):
        found.append(place.dev(z=place.zk(k), y=1 - place.y))
    return found


def wait_all(copies):
    for made in copies:
        made.wait_recv()


def gather_kernel(count, *refs):
    own, gain = refs[:count], refs[count]
    full, gain_all = refs[count + 1 : 2 * count + 1], refs[2 * count + 1]
    send, recv, local = refs[2 * count + 2 :]
    place = Place()
    x, y, z, c = place.x, place.y, place.z, place.c
    sems = Sems(send, recv)
    greet(place, partners(place))
    px, py, pc = place.dev(x=1 - x), place.dev(y=1 - y), place.dev(c=1 - c)

    me_dp = z * 2 + y
    gain_copies = []
    for k in range(1, 8):
        other = (me_dp + k) % 8
        gain_copies.append(
            sems.copy(gain, gain_all.at[me_dp], place.dev(z=other // 2, y=other % 2))
        )
    gain_own = pltpu.make_async_copy(gain, gain_all.at[me_dp], local.at[count])
    gain_own.start()

    def step_one(m):
        w, g = own[m], full[m]
        r = w.shape[0]
        made = pltpu.make_async_copy(w, g.at[x, c, z, y], local.at[m])
        made.start()
        middle = pl.ds(r // 6, 2 * r // 3)
        top, low = pl.ds(0, r // 6), pl.ds(5 * r // 6, r // 6)
        got = []
        for k in (1, 2, 3):
            got.append(
                sems.copy(w.at[middle], g.at[x, c, z, y, middle], place.dev(z=place.zk(k)))
            )
        got.append(sems.copy(w.at[top], g.at[x, c, z, y, top], px))
        got.append(sems.copy(w.at[low], g.at[x, c, z, y, low], py))
        return made, got

    def step_two(m):
        g = full[m]
        r = own[m].shape[0]
        pa, pb = pl.ds(r // 6, r // 3), pl.ds(r // 2, r // 3)
        top, low = pl.ds(0, r // 6), pl.ds(5 * r // 6, r // 6)
        got = [
            sems.copy(g.at[x, c, :, y, pa], g.at[x, c, :, y, pa], px),
            sems.copy(g.at[x, c, :, y, pb], g.at[x, c, :, y, pb], py),
        ]
        for k in (1, 2, 3):
            there = place.dev(z=place.zk(k))
            got.append(sems.copy(g.at[:, c, z, y, top], g.at[:, c, z, y, top], there))
            got.append(sems.copy(g.at[x, c, z, :, low], g.at[x, c, z, :, low], there))
        return got

    def step_three(m):
        g = full[m]
        r = own[m].shape[0]
        ca, bd = pl.ds(0, r // 2), pl.ds(r // 2, r // 2)
        got = [
            sems.copy(g.at[:, c, :, y, ca], g.at[:, c, :, y, ca], py),
            sems.copy(g.at[x, c, :, :, bd], g.at[x, c, :, :, bd], px),
        ]
        across = [
            sems.copy(g.at[:, c, :, y, ca], g.at[:, c, :, y, ca], pc),
            sems.copy(g.at[x, c, :, :, bd], g.at[x, c, :, :, bd], pc),
        ]
        return got, across

    def step_four(m):
        g = full[m]
        r = own[m].shape[0]
        ca, bd = pl.ds(0, r // 2), pl.ds(r // 2, r // 2)
        return [
            sems.copy(g.at[:, c, :, 1 - y, ca], g.at[:, c, :, 1 - y, ca], pc),
            sems.copy(g.at[1 - x, c, :, :, bd], g.at[1 - x, c, :, :, bd], pc),
        ]

    ones, twos, threes, last = {}, {}, {}, []
    ones[0] = step_one(0)
    for t in range(count + 2):
        if t + 1 < count:
            ones[t + 1] = step_one(t + 1)
        if t < count:
            made, got = ones.pop(t)
            made.wait()
            wait_all(got)
            twos[t] = step_two(t)
        if 0 <= t - 1 < count:
            wait_all(twos.pop(t - 1))
            threes[t - 1], across = step_three(t - 1)
            last += across
        if 0 <= t - 2 < count:
            wait_all(threes.pop(t - 2))
            last += step_four(t - 2)
    wait_all(last)
    wait_all(gain_copies)
    gain_own.wait()
    sems.drain()


def gather_all(own, gain):
    count = len(own)
    copies = 7 + count * (5 + 8 + 4 + 2)
    shapes = [jax.ShapeDtypeStruct((2, 2, 4, 2) + w.shape, BF16) for w in own]
    shapes.append(jax.ShapeDtypeStruct((8,) + gain.shape, BF16))
    return pl.pallas_call(
        functools.partial(gather_kernel, count),
        out_shape=shapes,
        in_specs=[ANY] * (count + 1),
        out_specs=[ANY] * (count + 1),
        scratch_shapes=[
            pltpu.SemaphoreType.DMA((copies,)),
            pltpu.SemaphoreType.DMA((copies,)),
            pltpu.SemaphoreType.DMA((count + 1,)),
        ],
        compiler_params=pltpu.CompilerParams(
            collective_id=0, has_side_effects=True, vmem_limit_bytes=4 << 20
        ),
        name="gather_weights",
    )(*own, gain)


def add_blocks(total, where, part, there):
    total[where] = (total[where].astype(F32) + part[there].astype(F32)).astype(BF16)


def scatter_kernel(count, *refs):
    grads, gain = refs[:count], refs[count]
    outs, gain_out = refs[count + 1 : 2 * count + 1], refs[2 * count + 1]
    refs = refs[2 * count + 2 :]
    total, from_core, from_y, from_x, from_a, from_b, from_c, from_d, from_z, end_c, end_d = (
        refs[i * count : (i + 1) * count] for i in range(11)
    )
    gain_sub, gain_sum, gain_dp, send, recv, local = refs[11 * count :]
    place = Place()
    x, y, z, c = place.x, place.y, place.z, place.c
    sems = Sems(send, recv)
    me_dp, me_sub = z * 2 + y, x * 2 + c
    sub_peers = [(me_dp, (me_sub + k) % 4) for k in (1, 2, 3)]
    dp_peers = [((me_dp + k) % 8, me_sub) for k in range(1, 8)]
    greet(place, sub_peers + dp_peers)
    px, py, pc = place.dev(x=1 - x), place.dev(y=1 - y), place.dev(c=1 - c)

    def step_zero(m):
        p = grads[m]
        made = pltpu.make_async_copy(p.at[:, c], total[m], local.at[m])
        made.start()
        return made, [sems.copy(p.at[:, 1 - c], from_core[m], pc)]

    def step_one(m):
        a, r0 = total[m], from_core[m]
        r = a.shape[3]

        @pl.loop(0, 16)
        def _(i):
            at = (i // 8, (i // 2) % 4, i % 2)
            add_blocks(a, at, r0, at)

        ca, bd = pl.ds(0, r // 2), pl.ds(r // 2, r // 2)
        return [
            sems.copy(a.at[:, :, 1 - y, ca], from_y[m], py),
            sems.copy(a.at[1 - x, :, :, bd], from_x[m], px),
        ]

    def step_two(m):
        a = total[m]
        r = a.shape[3]
        ca, bd = pl.ds(0, r // 2), pl.ds(r // 2, r // 2)

        @pl.loop(0, 8)
        def _(i):
            add_blocks(a, (i // 4, i % 4, y, ca), from_y[m], (i // 4, i % 4))
            add_blocks(a, (x, i // 2, i % 2, bd), from_x[m], (i // 2, i % 2))

        pa, pb = pl.ds(r // 6, r // 3), pl.ds(r // 2, r // 3)
        top, low = pl.ds(0, r // 6), pl.ds(5 * r // 6, r // 6)
        got = [
            sems.copy(a.at[1 - x, :, y, pa], from_a[m], px),
            sems.copy(a.at[x, :, 1 - y, pb], from_b[m], py),
        ]
        for k in (1, 2, 3):
            zk = place.zk(k)
            there = place.dev(z=zk)
            got.append(sems.copy(a.at[:, zk, y, top], from_c[m].at[k - 1], there))
            got.append(sems.copy(a.at[x, zk, :, low], from_d[m].at[k - 1], there))
        return got

    def step_three(m):
        a = total[m]
        r = a.shape[3]
        pa, pb = pl.ds(r // 6, r // 3), pl.ds(r // 2, r // 3)
        top, low = pl.ds(0, r // 6), pl.ds(5 * r // 6, r // 6)

        @pl.loop(0, 4)
        def _(i):
            add_blocks(a, (x, i, y, pa), from_a[m], i)
            add_blocks(a, (x, i, y, pb), from_b[m], i)

        for i in range(2):
            fc, fd = from_c[m], from_d[m]
            a[i, z, y, top] = (
                a[i, z, y, top].astype(F32)
                + fc[0, i].astype(F32)
                + fc[1, i].astype(F32)
                + fc[2, i].astype(F32)
            ).astype(BF16)
            a[x, z, i, low] = (
                a[x, z, i, low].astype(F32)
                + fd[0, i].astype(F32)
                + fd[1, i].astype(F32)
                + fd[2, i].astype(F32)
            ).astype(BF16)
        middle = pl.ds(r // 6, 2 * r // 3)
        got = []
        for k in (1, 2, 3):
            zk = place.zk(k)
            got.append(sems.copy(a.at[x, zk, y, middle], from_z[m].at[k - 1], place.dev(z=zk)))
        got.append(sems.copy(a.at[1 - x, z, y, top], end_c[m], px))
        got.append(sems.copy(a.at[x, z, 1 - y, low], end_d[m], py))
        return got

    def step_four(m):
        a, o, fz = total[m], outs[m], from_z[m]
        r = a.shape[3]
        middle = pl.ds(r // 6, 2 * r // 3)
        top, low = pl.ds(0, r // 6), pl.ds(5 * r // 6, r // 6)
        o[middle] = (
            a[x, z, y, middle].astype(F32)
            + fz[0].astype(F32)
            + fz[1].astype(F32)
            + fz[2].astype(F32)
        )
        o[top] = a[x, z, y, top].astype(F32) + end_c[m][...].astype(F32)
        o[low] = a[x, z, y, low].astype(F32) + end_d[m][...].astype(F32)

    zeros = [step_zero(m) for m in range(count)]
    gain_one = [sems.copy(gain, gain_sub.at[k], sub_peers[k]) for k in range(3)]
    ones, twos, threes = {}, {}, {}

    def begin(m):
        made, got = zeros[m]
        made.wait()
        wait_all(got)
        ones[m] = step_one(m)

    begin(0)
    gain_two = None
    for t in range(count + 2):
        if t + 1 < count:
            begin(t + 1)
        if t < count:
            wait_all(ones.pop(t))
            twos[t] = step_two(t)
        if t == 0:
            wait_all(gain_one)
            gain_sum[...] = gain[...] + gain_sub[0] + gain_sub[1] + gain_sub[2]
            gain_two = [
                sems.copy(gain_sum.at[(me_dp + k) % 8], gain_dp.at[k - 1], dp_peers[k - 1])
                for k in range(1, 8)
            ]
        if 0 <= t - 1 < count:
            wait_all(twos.pop(t - 1))
            threes[t - 1] = step_three(t - 1)
        if 0 <= t - 2 < count:
            wait_all(threes.pop(t - 2))
            step_four(t - 2)
    wait_all(gain_two)
    gain_out[...] = gain_sum[me_dp] + jnp.sum(gain_dp[...], axis=0)
    sems.drain()


def scatter_all(grads, gain):
    count = len(grads)
    copies = 10 + count * (1 + 2 + 8 + 5)
    dims = [p.shape[4:] for p in grads]
    scratch = []
    for lead, part in (
        ((2, 4, 2), 1),
        ((2, 4, 2), 1),
        ((2, 4), 2),
        ((4, 2), 2),
        ((4,), 3),
        ((4,), 3),
        ((3, 2), 6),
        ((3, 2), 6),
        ((3,), 1.5),
        ((), 6),
        ((), 6),
    ):
        for rows, columns in dims:
            scratch.append(pltpu.VMEM(lead + (int(rows / part), columns), BF16))
    scratch += [
        pltpu.VMEM((3,) + gain.shape, F32),
        pltpu.VMEM(gain.shape, F32),
        pltpu.VMEM((7,) + gain.shape[1:], F32),
        pltpu.SemaphoreType.DMA((copies,)),
        pltpu.SemaphoreType.DMA((copies,)),
        pltpu.SemaphoreType.DMA((count,)),
    ]
    shapes = [jax.ShapeDtypeStruct(d, F32) for d in dims]
    shapes.append(jax.ShapeDtypeStruct(gain.shape[1:], F32))
    return pl.pallas_call(
        functools.partial(scatter_kernel, count),
        out_shape=shapes,
        in_specs=[ANY] * count + [VMEM],
        out_specs=[VMEM] * (count + 1),
        scratch_shapes=scratch,
        compiler_params=pltpu.CompilerParams(
            collective_id=1, has_side_effects=True, vmem_limit_bytes=60 << 20
        ),
        name="scatter_gradients",
    )(*grads, gain)


def layer_norm(values, gain_row):
    centred = values - jnp.mean(values, axis=-1, keepdims=True)
    inverse = lax.rsqrt(jnp.mean(centred * centred, axis=-1, keepdims=True) + EPSILON)
    return centred * inverse * gain_row


def norm_backward(values, gain_row, gradient):
    unused, pull_back = jax.vjp(layer_norm, values, gain_row)
    return pull_back(gradient)


def gelu_tanh(values):
    return jax.nn.gelu(values, approximate=True)


def mm(left_side, weight):
    return jnp.dot(left_side, weight, preferred_element_type=F32)


def mm_nt(left_side, weight):
    return lax.dot_general(left_side, weight, (((1,), (1,)), ((), ())), preferred_element_type=F32)


def mm_tn(left_side, gradient):
    return lax.dot_general(
        left_side, gradient, (((0,), (0,)), ((), ())), preferred_element_type=F32
    )


def low(values):
    return values.astype(BF16)


def heads_of(values):
    return values.reshape(values.shape[:-1] + (HEADS, values.shape[-1] // HEADS))


def mlp_forward(residual, gain_row, up, down_t):
    normed = low(layer_norm(residual, gain_row))
    pre_act = mm(normed, up)
    hidden = low(gelu_tanh(pre_act))
    return normed, pre_act, hidden, mm_nt(hidden, down_t)


def mlp_backward(residual, gain_row, normed, pre_act, hidden, up, down_t, grad_out):
    grad_low = low(grad_out)
    grad_down_t = mm_tn(grad_low, hidden)
    grad_hidden = mm(grad_low, down_t)
    unused, gelu_back = jax.vjp(gelu_tanh, pre_act)
    grad_pre = low(gelu_back(grad_hidden)[0])
    grad_up = mm_tn(normed, grad_pre)
    grad_resid, grad_gain = norm_backward(residual, gain_row, mm_nt(grad_pre, up))
    return grad_resid, grad_gain, grad_up, grad_down_t


def live_layer(live_lat, dead_lat, tokens, count, live_cot, dead_cot, weights, norm_gain):
    c_attn, c_up, c_down_t, s_attn, s_up, s_down_t = weights
    rows, width = live_lat.shape
    scale = (width // HEADS) ** (-0.5)
    lat_low = low(layer_norm(live_lat, norm_gain[0]))
    queries = low(mm(lat_low, c_attn[:, :width]))
    token_values = tokens.astype(F32)
    tok_low = low(layer_norm(token_values, norm_gain[1]))
    kv_weight = c_attn[:, width : 3 * width]
    key_value = low(mm(tok_low, kv_weight))
    keys, values = heads_of(key_value[:, :width]), heads_of(key_value[:, width:])
    scores = (
        jnp.einsum("qhd,khd->hqk", heads_of(queries), keys, preferred_element_type=F32) * scale
    )
    valid = (jnp.arange(tokens.shape[0]) < count)[None, None, :]
    probs = jax.nn.softmax(jnp.where(valid, scores, MASKED), axis=-1)
    probs_low = low(probs)
    attended = jnp.einsum("hqk,khd->qhd", probs_low, values, preferred_element_type=F32)
    attended = attended.reshape(rows, width)
    cross_low = low(attended)
    middle = live_lat + mm(cross_low, c_attn[:, 3 * width :])
    c_norm, c_pre, c_hidden, c_mlp = mlp_forward(middle, norm_gain[2], c_up, c_down_t)
    after_cross = jnp.concatenate([middle + c_mlp, dead_lat], axis=0)

    self_low = low(layer_norm(after_cross, norm_gain[3]))
    qkv = low(mm(self_low, s_attn[:, : 3 * width])).reshape(2, rows, 3 * width)
    s_q = heads_of(qkv[..., :width])
    s_k = heads_of(qkv[..., width : 2 * width])
    s_v = heads_of(qkv[..., 2 * width :])
    s_scores = jnp.einsum("iqhd,ikhd->ihqk", s_q, s_k, preferred_element_type=F32) * scale
    s_probs = jax.nn.softmax(s_scores, axis=-1)
    s_probs_low = low(s_probs)
    s_out = jnp.einsum("ihqk,ikhd->iqhd", s_probs_low, s_v, preferred_element_type=F32)
    s_out_low = low(s_out.reshape(2 * rows, width))
    after_attn = after_cross + mm(s_out_low, s_attn[:, 3 * width :])
    m_norm, m_pre, m_hidden, m_mlp = mlp_forward(after_attn, norm_gain[4], s_up, s_down_t)
    result = after_attn + m_mlp

    cotangent = jnp.concatenate([live_cot, dead_cot], axis=0)
    grad_in, gain_four, d_s_up, d_s_down_t = mlp_backward(
        after_attn, norm_gain[4], m_norm, m_pre, m_hidden, s_up, s_down_t, cotangent
    )
    grad_attn = cotangent + grad_in
    grad_y = low(grad_attn)
    d_s_o = mm_tn(s_out_low, grad_y)
    grad_out = heads_of(low(mm_nt(grad_y, s_attn[:, 3 * width :])).reshape(2, rows, width))
    grad_probs = jnp.einsum("iqhd,ikhd->ihqk", grad_out, s_v, preferred_element_type=F32)
    delta = jnp.sum(grad_probs * s_probs, axis=-1, keepdims=True)
    grad_scores = low(s_probs * (grad_probs - delta))
    g_q = jnp.einsum("ihqk,ikhd->iqhd", grad_scores, s_k, preferred_element_type=F32) * scale
    g_k = jnp.einsum("ihqk,iqhd->ikhd", grad_scores, s_q, preferred_element_type=F32) * scale
    g_v = jnp.einsum("ihqk,iqhd->ikhd", s_probs_low, grad_out, preferred_element_type=F32)
    grad_qkv = low(
        jnp.concatenate([g.reshape(2 * rows, width) for g in (g_q, g_k, g_v)], axis=-1)
    )
    d_s_qkv = mm_tn(self_low, grad_qkv)
    grad_in, gain_three = norm_backward(
        after_cross, norm_gain[3], mm_nt(grad_qkv, s_attn[:, : 3 * width])
    )
    grad_cross = grad_attn + grad_in
    live_grad, dead_grad = grad_cross[:rows], grad_cross[rows:]
    grad_in, gain_two, d_c_up, d_c_down_t = mlp_backward(
        middle, norm_gain[2], c_norm, c_pre, c_hidden, c_up, c_down_t, live_grad
    )
    grad_middle = live_grad + grad_in
    grad_cross_y = low(grad_middle)
    d_c_o = mm_tn(cross_low, grad_cross_y)
    grad_cross_out = low(mm_nt(grad_cross_y, c_attn[:, 3 * width :]))
    out_heads = heads_of(grad_cross_out)
    grad_weights = jnp.einsum("qhd,khd->hqk", out_heads, values, preferred_element_type=F32)
    row_delta = jnp.transpose(jnp.sum(heads_of(grad_cross_out.astype(F32) * attended), axis=-1))
    grad_scores = low(probs * (grad_weights - row_delta[..., None]))
    grad_query = low(
        (
            jnp.einsum("hqk,khd->qhd", grad_scores, keys, preferred_element_type=F32) * scale
        ).reshape(rows, width)
    )
    grad_keys = (
        jnp.einsum("hqk,qhd->khd", grad_scores, heads_of(queries), preferred_element_type=F32)
        * scale
    )
    grad_values = jnp.einsum("hqk,qhd->khd", probs_low, out_heads, preferred_element_type=F32)
    grad_kv = low(
        jnp.concatenate(
            [grad_keys.reshape(-1, width), grad_values.reshape(-1, width)], axis=-1
        )
    )
    d_c_kv = mm_tn(tok_low, grad_kv)
    grad_tokens, gain_one = norm_backward(token_values, norm_gain[1], mm_nt(grad_kv, kv_weight))
    d_c_q = mm_tn(lat_low, grad_query)
    grad_in, gain_zero = norm_backward(
        live_lat, norm_gain[0], mm_nt(grad_query, c_attn[:, :width])
    )
    live_lat_grad = grad_middle + grad_in
    d_c_attn = low(jnp.concatenate([d_c_q, d_c_kv, d_c_o], axis=1))
    d_s_attn = low(jnp.concatenate([d_s_qkv, d_s_o], axis=1))
    gain_grad = jnp.stack([gain_zero, gain_one, gain_two, gain_three, gain_four])
    grads = (d_c_attn, low(d_c_up), low(d_c_down_t), d_s_attn, low(d_s_up), low(d_s_down_t))
    return result, live_lat_grad, dead_grad, grad_tokens, grads, gain_grad


def column_blocks(blocks):
    sub, dp, rows, columns = blocks.shape
    return blocks.transpose(1, 2, 0, 3).reshape(dp * rows, sub * columns)


def row_blocks(blocks):
    sub, dp, rows, columns = blocks.shape
    return blocks.transpose(0, 2, 1, 3).reshape(sub * rows, dp * columns)


def shards(*arrays, dp_size, sub_size):
    latents, inputs, counts, flags = arrays[:4]
    cross_attn, cross_up, cross_down, self_attn, self_up, self_down, gains, cotangent = arrays[4:]
    width = latents.shape[-1]
    own = (
        cross_attn,
        cross_up,
        jnp.transpose(cross_down),
        self_attn,
        self_up,
        jnp.transpose(self_down),
    )
    kernels = dp_size == 8 and sub_size == 4
    if kernels:
        padded = jnp.pad(gains, ((0, 16 - gains.shape[0]), (0, 128 - gains.shape[1])))
        *blocks, gain_blocks = gather_all(own, padded)
        blocks = [b.reshape((sub_size, dp_size) + w.shape) for b, w in zip(blocks, own)]
        norm_gain = gain_blocks[:, : gains.shape[0], : gains.shape[1]]
        norm_gain = norm_gain.transpose(1, 0, 2).reshape(gains.shape[0], width)
    else:
        blocks = [lax.all_gather(lax.all_gather(w, "dp", axis=0), "sub", axis=0) for w in own]
        norm_gain = lax.all_gather(gains, "dp", axis=1, tiled=True)
    transposed = (False, False, True, False, False, True)
    weights = [
        row_blocks(b) if flip else column_blocks(b) for b, flip in zip(blocks, transposed)
    ]
    live = jnp.where(flags[0] == 0, 0, 1)

    def item(array, index):
        return lax.dynamic_index_in_dim(array, index, 0, keepdims=False)

    result, live_grad, dead_grad, grad_tokens, grads, gain_grad = live_layer(
        item(latents, live),
        item(latents, 1 - live),
        item(inputs, live),
        item(counts, live),
        item(cotangent, live),
        item(cotangent, 1 - live),
        weights,
        norm_gain.astype(F32),
    )

    def both(live_part, dead_part):
        first = jnp.where(live == 0, live_part, dead_part)
        second = jnp.where(live == 0, dead_part, live_part)
        return jnp.stack([first, second])

    rows = latents.shape[1]
    result = both(result[:rows], result[rows:])
    grad_latents = both(live_grad, dead_grad)
    here = jnp.arange(inputs.shape[0]) == live
    grad_inputs = jnp.where(here[:, None, None], grad_tokens[None], 0.0)

    def blocks_of(grad, shape, flip):
        r, c = shape
        if flip:
            return grad.reshape(sub_size, r, dp_size, c).transpose(0, 2, 1, 3)
        return grad.reshape(dp_size, r, sub_size, c).transpose(2, 0, 1, 3)

    grads = [blocks_of(g, w.shape, flip) for g, w, flip in zip(grads, own, transposed)]
    if kernels:
        gain_parts = gain_grad.reshape(gains.shape[0], dp_size, -1).transpose(1, 0, 2)
        gain_parts = jnp.pad(
            gain_parts, ((0, 0), (0, 8 - gains.shape[0]), (0, 128 - gains.shape[1]))
        )
        *owned, gain_owned = scatter_all(
            [g.reshape((2, 2, 4, 2) + g.shape[2:]) for g in grads], gain_parts
        )
        gain_owned = gain_owned[: gains.shape[0], : gains.shape[1]]
    else:
        owned = [lax.psum_scatter(g, "sub", scatter_dimension=0) for g in grads]
        owned = [lax.psum_scatter(g.astype(F32), "dp", scatter_dimension=0) for g in owned]
        gain_owned = lax.psum(gain_grad, "sub")
        gain_owned = lax.psum_scatter(gain_owned, "dp", scatter_dimension=1, tiled=True)
    owned = [jnp.transpose(g) if flip else g for g, flip in zip(owned, transposed)]
    return (result, grad_latents, grad_inputs, *owned, gain_owned)


def solution(mesh):
    item = P(("dp", "sub"), None, None)
    weight = P("dp", "sub")
    gain = P(None, "dp")
    placed = (item, item, P(("dp", "sub")), P()) + (weight,) * 6 + (gain, item)
    return jax.shard_map(
        functools.partial(shards, dp_size=mesh.shape["dp"], sub_size=mesh.shape["sub"]),
        mesh=mesh,
        in_specs=placed,
        out_specs=(item, item, item) + (weight,) * 6 + (gain,),
        check_vma=False,
    )
```

```python
import functools

import jax
import jax.numpy as jnp
from jax import lax
from jax.experimental import pallas as pl
from jax.experimental.pallas import tpu as pltpu
from jax.sharding import PartitionSpec as P

HEADS = 12
EPSILON = 1e-05
MASKED = -1e30
MESH_ID = pl.DeviceIdType.MESH
F32 = jnp.float32
BF16 = jnp.bfloat16
ANY = pl.BlockSpec(memory_space=pl.ANY)
VMEM = pl.BlockSpec(memory_space=pltpu.VMEM)
SMEM = pl.BlockSpec(memory_space=pltpu.SMEM)


class Place:
    def __init__(self):
        dp, sub = lax.axis_index("dp"), lax.axis_index("sub")
        self.z, self.y, self.x, self.c = dp // 2, dp % 2, sub // 2, sub % 2

    def dev(self, z=None, y=None, x=None, c=None):
        z = self.z if z is None else z
        y = self.y if y is None else y
        x = self.x if x is None else x
        c = self.c if c is None else c
        return (z * 2 + y, x * 2 + c)

    def zk(self, k):
        return (self.z + k) % 4


def now(ref):
    return ref() if callable(ref) else ref


class Flight:
    def __init__(self, place, dst, send_sem, recv_sem):
        self.place, self.dst, self.send_sem, self.recv_sem = place, dst, send_sem, recv_sem

    def made(self):
        return pltpu.make_async_remote_copy(
            src_ref=now(self.dst),
            dst_ref=now(self.dst),
            send_sem=self.send_sem[0].at[self.send_sem[1]],
            recv_sem=self.recv_sem[0].at[self.recv_sem[1]],
            device_id=self.place.dev(c=1 - self.place.c),
            device_id_type=MESH_ID,
        )

    def wait_send(self):
        self.made().wait_send()

    def wait_recv(self):
        self.made().wait_recv()


class Sems:
    def __init__(self, place, send, recv):
        self.place, self.send, self.recv, self.count, self.sent = place, send, recv, 0, []

    def copy(self, src, dst, device, later=True):
        pltpu.make_async_remote_copy(
            src_ref=src,
            dst_ref=now(dst),
            send_sem=self.send.at[self.count],
            recv_sem=self.recv.at[self.count],
            device_id=device,
            device_id_type=MESH_ID,
        ).start()
        flight = Flight(self.place, dst, (self.send, self.count), (self.recv, self.count))
        self.count += 1
        if later:
            self.sent.append(flight)
        return flight

    def drain(self):
        for flight in self.sent:
            flight.wait_send()


def greet(place, devices):
    barrier = pltpu.get_barrier_semaphore()
    for device in devices:
        pl.semaphore_signal(barrier, inc=1, device_id=device, device_id_type=MESH_ID)
    pl.semaphore_wait(barrier, len(devices))


def partners(place):
    found = [
        place.dev(c=1 - place.c),
        place.dev(x=1 - place.x),
        place.dev(y=1 - place.y),
    ]
    for k in (1, 2, 3):
        found.append(place.dev(z=place.zk(k)))
    for k in (1, 2, 3):
        found.append(place.dev(z=place.zk(k), y=1 - place.y))
    return found


def wait_all(copies):
    for made in copies:
        made.wait_recv()


def add_blocks(total, where, part, there):
    total[where] = (total[where].astype(F32) + part[there].astype(F32)).astype(BF16)


def dot(a, b):
    return jnp.dot(a, b, preferred_element_type=F32)


def dot_nt(a, b):
    return lax.dot_general(a, b, (((1,), (1,)), ((), ())), preferred_element_type=F32)


def low(values):
    return values.astype(BF16)


def normed(values):
    centred = values - jnp.mean(values, axis=-1, keepdims=True)
    inverse = lax.rsqrt(jnp.mean(centred * centred, axis=-1, keepdims=True) + EPSILON)
    return centred * inverse, inverse


def gelu_both(u):
    k, a = 0.7978845608028654, 0.044715
    square = u * u
    t = jnp.tanh(k * u * (1.0 + a * square))
    half = 0.5 * (1.0 + t)
    slope = half + (0.5 * k) * u * (1.0 - t * t) * (1.0 + (3.0 * a) * square)
    return u * half, slope


def square_block(ref, x, c):
    block = ref[x, c]
    return block.reshape(block.shape[0] * block.shape[1] * block.shape[2], block.shape[3])


def hidden_block(ref, z):
    parts = []
    for y in range(2):
        block = ref[:, :, z, y]
        parts.append(block.reshape(4 * block.shape[2], block.shape[3]))
    return jnp.concatenate(parts, axis=1)


def left_half(shape):
    return lax.broadcasted_iota(jnp.int32, shape, 1) < 64


def stack_heads(values):
    left = left_half(values.shape)
    zero = jnp.zeros_like(values)
    return jnp.concatenate([jnp.where(left, values, zero), jnp.where(left, zero, values)], axis=0)


def join_heads(values):
    rows = values.shape[0] // 2
    top, bottom = values[:rows], values[rows:]
    return jnp.where(left_half(top.shape), top, bottom)


def lanes(index, size):
    return pl.ds(pl.multiple_of(index * size, size), size)


def kept_shapes(rows, tokens, width, hidden):
    two = 2 * rows
    return {
        "cq": ((rows, width), BF16),
        "kv": ((2, tokens, width), BF16),
        "cp": ((width // 128, two, tokens), BF16),
        "co": ((rows, width), F32),
        "mid": ((rows, width), F32),
        "gpc": ((rows, hidden), BF16),
        "ac": ((two, width), F32),
        "sqkv": ((3, two, width), BF16),
        "sp": ((2 * (width // 128), two, rows), BF16),
        "aa": ((two, width), F32),
        "gps": ((two, hidden), BF16),
        "xl": ((tokens, width), BF16),
    }


def paired_shapes(rows, tokens, width, hidden):
    two = 2 * rows
    return {
        "gyt": ((2, width // 4, 2 * two), BF16),
        "mh": ((2 * two, hidden), BF16),
        "mnt": ((width, 2 * two), BF16),
        "sbt": ((width, 2 * two), BF16),
        "l1t": ((width, 2 * two), BF16),
        "ch": ((two, hidden), BF16),
        "cnt": ((width, two), BF16),
        "lst": ((width, two), BF16),
        "xbt": ((width, 2 * tokens), BF16),
    }


def forward_kernel(names, dims, *refs):
    rows, tokens, width, hidden = dims
    two = 2 * rows
    count = 6
    refs = list(refs)

    def take(n):
        out = refs[:n]
        del refs[:n]
        return out

    own = take(count)
    gain, lat, tok, cot, live_counts, flags = take(6)
    full = take(count)
    gain_out, result = take(2)
    kept = dict(zip(names, take(len(names))))
    gain_all, lat_v, cot_v, tok_v, z2, xb, xbt, gyt, lst, wr0, wr1, wt = take(12)
    cq, kv, cp, co, mid, ch, gpc, ac, sqkv, sp, so, aa, mh, gps, xl, lt, cnt, mnt = take(18)
    send, recv, local = take(3)
    wr = (wr0, wr1)
    place = Place()
    x, y, z, c = place.x, place.y, place.z, place.c
    sems = Sems(place, send, recv)
    local_count = [0]
    local_open = []

    def local_copy(src, dst):
        made = pltpu.make_async_copy(src, dst, local.at[local_count[0]])
        local_count[0] += 1
        made.start()
        return made

    in_lat, in_tok, in_cot = local_copy(lat, lat_v), local_copy(tok, tok_v), local_copy(cot, cot_v)
    greet(place, partners(place))
    px, py, pc = place.dev(x=1 - x), place.dev(y=1 - y), place.dev(c=1 - c)

    me_dp = z * 2 + y
    gain_copies = []
    for k in range(1, 8):
        other = (me_dp + k) % 8
        gain_copies.append(
            sems.copy(gain, gain_all.at[me_dp], place.dev(z=other // 2, y=other % 2))
        )
    gain_own = local_copy(gain, gain_all.at[me_dp])

    ones, twos, threes, across = {}, {}, {}, {m: [] for m in range(count)}

    def step_one(m):
        w, g = own[m], full[m]
        r = w.shape[0]
        made = local_copy(w, g.at[x, c, z, y])
        middle = pl.ds(r // 6, 2 * r // 3)
        top, low_rows = pl.ds(0, r // 6), pl.ds(5 * r // 6, r // 6)
        got = []
        for k in (1, 2, 3):
            got.append(
                sems.copy(w.at[middle], g.at[x, c, z, y, middle], place.dev(z=place.zk(k)))
            )
        got.append(sems.copy(w.at[top], g.at[x, c, z, y, top], px))
        got.append(sems.copy(w.at[low_rows], g.at[x, c, z, y, low_rows], py))
        ones[m] = made, got

    def step_two(m):
        made, got = ones.pop(m)
        made.wait()
        wait_all(got)
        g = full[m]
        r = own[m].shape[0]
        pa, pb = pl.ds(r // 6, r // 3), pl.ds(r // 2, r // 3)
        top, low_rows = pl.ds(0, r // 6), pl.ds(5 * r // 6, r // 6)
        got = [
            sems.copy(g.at[x, c, :, y, pa], g.at[x, c, :, y, pa], px),
            sems.copy(g.at[x, c, :, y, pb], g.at[x, c, :, y, pb], py),
        ]
        for k in (1, 2, 3):
            there = place.dev(z=place.zk(k))
            got.append(sems.copy(g.at[:, c, z, y, top], g.at[:, c, z, y, top], there))
            got.append(sems.copy(g.at[x, c, z, :, low_rows], g.at[x, c, z, :, low_rows], there))
        twos[m] = got

    def step_three(m):
        wait_all(twos.pop(m))
        g = full[m]
        r = own[m].shape[0]
        ca, bd = pl.ds(0, r // 2), pl.ds(r // 2, r // 2)
        threes[m] = [
            sems.copy(g.at[:, c, :, y, ca], g.at[:, c, :, y, ca], py),
            sems.copy(g.at[x, c, :, :, bd], g.at[x, c, :, :, bd], px),
        ]
        across[m] += [
            sems.copy(g.at[:, c, :, y, ca], g.at[:, c, :, y, ca], pc),
            sems.copy(g.at[x, c, :, :, bd], g.at[x, c, :, :, bd], pc),
        ]

    def step_four(m):
        wait_all(threes.pop(m))
        g = full[m]
        r = own[m].shape[0]
        ca, bd = pl.ds(0, r // 2), pl.ds(r // 2, r // 2)
        across[m] += [
            sems.copy(g.at[:, c, :, 1 - y, ca], g.at[:, c, :, 1 - y, ca], pc),
            sems.copy(g.at[1 - x, c, :, :, bd], g.at[1 - x, c, :, :, bd], pc),
        ]

    def load(m, dst):
        wait_all(across.pop(m))
        local_copy(full[m], dst).wait()

    def keep(name, src):
        local_open.append(local_copy(src, kept[name]))

    def pair(name, mine, theirs, axis_size, axis):
        here, there = pl.ds(0, axis_size), pl.ds(axis_size, axis_size)
        dst = kept[name]

        def part(where):
            return dst.at[where] if axis == 0 else dst.at[:, where] if axis == 1 else dst.at[:, :, where]

        local_open.append(local_copy(mine, part(here)))
        across_pairs.append(sems.copy(theirs, part(there), pc))

    across_pairs = []
    gains = {}

    def pick(flag_first, first, second):
        return jnp.where(flag_first, first, second)

    first_live = flags[0] == 0
    live_count = jnp.where(first_live, live_counts[0], live_counts[1])

    def start():
        wait_all(gain_copies)
        gain_own.wait()
        row = lax.broadcasted_iota(jnp.int32, (128, width), 0)
        column = lax.broadcasted_iota(jnp.int32, (128, width), 1)
        total = jnp.zeros((16, width), F32)
        share = width // 8
        for i in range(8):
            spread = low(jnp.where((column == row + share * i) & (row < share), 1.0, 0.0))
            total += dot(gain_all[i], spread)
        gain_out[...] = total
        in_lat.wait()
        in_cot.wait()
        z2[:rows] = pick(first_live, lat_v[0], lat_v[1])
        z2[rows:] = pick(first_live, lat_v[1], lat_v[0])
        zb = low(normed(z2[:rows])[0] * gain_out[0:1])
        lst[0] = zb.T
        gy_first = low(pick(first_live, cot_v[0], cot_v[1]))
        gy_last = low(pick(first_live, cot_v[1], cot_v[0]))
        gyt[:, :, :, :rows] = gy_first.T.reshape(2, 2, width // 4, rows)
        gyt[:, :, :, rows:] = gy_last.T.reshape(2, 2, width // 4, rows)
        pair("gyt", gyt.at[:, c], gyt.at[:, 1 - c], two, 2)

    def tokens_part():
        in_tok.wait()

        @pl.loop(0, tokens // 128)
        def _(i):
            at = lanes(i, 128)
            here = pick(first_live, tok_v[0, at], tok_v[1, at])
            xl[at] = here
            value = low(normed(here.astype(F32))[0] * gain_out[1:2])
            xb[at] = value
            xbt[:, at] = value.T

        keep("xl", xl)
        pair("xbt", xbt, xbt, tokens, 1)

    def queries_keys():
        w = wr[0]
        zb = lst[0].T
        cq[...] = low(dot(zb, square_block(w, 0, 0)))
        keep("cq", cq)

        @pl.loop(0, tokens // 256)
        def _(i):
            at = lanes(i, 256)
            here = xb[at]
            kv[0, at] = low(dot(here, square_block(w, 0, 1)))
            kv[1, at] = low(dot(here, square_block(w, 1, 0)))

        keep("kv", kv)

    def cross_attention():
        @pl.loop(0, width // 128)
        def _(p):
            at = lanes(p, 128)
            q = stack_heads(cq[:, at] * jnp.asarray(0.125, BF16))
            s = dot_nt(q, kv[0, :, at])
            s = jnp.where(lax.broadcasted_iota(jnp.int32, s.shape, 1) < live_count, s, MASKED)
            e = jnp.exp(s - jnp.max(s, axis=-1, keepdims=True))
            prob = low(e * (1.0 / jnp.sum(e, axis=-1, keepdims=True)))
            cp[p] = prob
            co[:, at] = join_heads(dot(prob, kv[1, :, at]))

        keep("cp", cp)
        keep("co", co)

    def cross_out():
        cob = low(co[...])
        lst[1] = cob.T
        pair("lst", lst.at[c], lst.at[1 - c], rows, 1)
        mid[...] = z2[:rows] + dot(cob, square_block(wr[0], 1, 1))
        keep("mid", mid)
        cnb = low(normed(mid[...])[0] * gain_out[2:3])
        cnt[...] = cnb.T
        pair("cnt", cnt, cnt, rows, 1)

    def up(w, left, out, slope):
        @pl.loop(0, 4)
        def _(s):
            at = lanes(s, hidden // 4)
            value, grad = gelu_both(dot(left(), square_block(w, s // 2, s % 2)))
            out[:, at] = low(value)
            slope[:, at] = low(grad)

    def down(w, act):
        total = jnp.zeros((act.shape[0], width), F32)
        for s in range(4):
            at = pl.ds(s * (hidden // 4), hidden // 4)
            total += dot_nt(act[:, at], hidden_block(w, s))
        return total

    def cross_up():
        up(wr[1], lambda: cnt[...].T, ch, gpc)
        pair("ch", ch, ch, rows, 0)
        keep("gpc", gpc)

    def cross_down():
        ac[:rows] = mid[...] + down(wt, ch)
        ac[rows:] = z2[rows:]
        keep("ac", ac)
        sb = low(normed(ac[...])[0] * gain_out[3:4])
        lt[0] = sb.T
        pair("sbt", lt.at[0], lt.at[0], two, 1)

    def self_project():
        sb = lt[0].T
        for i, (a, b) in enumerate(((0, 0), (0, 1), (1, 0))):
            sqkv[i] = low(dot(sb, square_block(wr[0], a, b)))
        keep("sqkv", sqkv)

    def self_attention():
        pairs = width // 128

        @pl.loop(0, 2 * pairs)
        def _(i):
            at, row_at = lanes(i % pairs, 128), lanes(i // pairs, rows)
            q = stack_heads(sqkv[0, row_at, at] * jnp.asarray(0.125, BF16))
            s = dot_nt(q, sqkv[1, row_at, at])
            e = jnp.exp(s - jnp.max(s, axis=-1, keepdims=True))
            prob = low(e * (1.0 / jnp.sum(e, axis=-1, keepdims=True)))
            sp[i] = prob
            so[row_at, at] = low(join_heads(dot(prob, sqkv[2, row_at, at])))

        keep("sp", sp)

    def self_out():
        lt[1] = so[...].T
        pair("l1t", lt.at[c], lt.at[1 - c], two, 1)
        aa[...] = ac[...] + dot(so[...], square_block(wr[0], 1, 1))
        keep("aa", aa)
        mnb = low(normed(aa[...])[0] * gain_out[4:5])
        mnt[...] = mnb.T
        pair("mnt", mnt, mnt, two, 1)

    def self_up():
        up(wr[1], lambda: mnt[...].T, mh, gps)
        pair("mh", mh, mh, two, 0)
        keep("gps", gps)

    def self_down():
        total = aa[...] + down(wt, mh)
        result[0] = pick(first_live, total[:rows], total[rows:])
        result[1] = pick(first_live, total[rows:], total[:rows])

    step_one(0)
    for t in range(count + 3):
        if t + 1 < count:
            step_one(t + 1)
        if t == 0:
            start()
        if t < count:
            step_two(t)
        if t == 0:
            tokens_part()
        if t == 3:
            load(0, wr[0])
            queries_keys()
        if t == 4:
            load(1, wr[1])
            cross_up()
        if t == 5:
            load(2, wt)
            cross_down()
        if t == 6:
            load(3, wr[0])
            self_project()
        if t == 7:
            load(4, wr[1])
            self_up()
        if t == 8:
            load(5, wt)
            self_down()
        if 0 <= t - 1 < count:
            step_three(t - 1)
        if t == 3:
            cross_attention()
        if t == 6:
            self_attention()
        if 0 <= t - 2 < count:
            step_four(t - 2)
        if t == 3:
            cross_out()
        if t == 6:
            self_out()
    wait_all(across_pairs)
    for made in local_open:
        made.wait()
    sems.drain()


def forward_all(own, gain, latents, inputs, cotangent, counts, flags):
    count = len(own)
    rows, width = latents.shape[1:]
    tokens = inputs.shape[1]
    hidden = own[1].shape[1] * 4
    dims = (rows, tokens, width, hidden)
    two = 2 * rows
    kept = {**kept_shapes(*dims), **paired_shapes(*dims)}
    names = tuple(kept)
    copies = 7 + count * (5 + 8 + 4 + 2) + len(paired_shapes(*dims))
    shapes = [jax.ShapeDtypeStruct((2, 2, 4, 2) + w.shape, BF16) for w in own]
    shapes += [
        jax.ShapeDtypeStruct((16, width), F32),
        jax.ShapeDtypeStruct(latents.shape, F32),
    ]
    shapes += [jax.ShapeDtypeStruct(s, t) for s, t in kept.values()]
    row_type, turned = (2, 2, 4, 2) + own[0].shape, (2, 2, 4, 2) + own[2].shape
    pairs = width // 128
    scratch = [
        ((8,) + gain.shape, BF16),
        (latents.shape, F32),
        (latents.shape, F32),
        (inputs.shape, BF16),
        ((two, width), F32),
        ((tokens, width), BF16),
        ((width, tokens), BF16),
        ((2, 2, width // 4, two), BF16),
        ((2, width, rows), BF16),
        (row_type, BF16),
        (row_type, BF16),
        (turned, BF16),
        ((rows, width), BF16),
        ((2, tokens, width), BF16),
        ((pairs, two, tokens), BF16),
        ((rows, width), F32),
        ((rows, width), F32),
        ((rows, hidden), BF16),
        ((rows, hidden), BF16),
        ((two, width), F32),
        ((3, two, width), BF16),
        ((2 * pairs, two, rows), BF16),
        ((two, width), BF16),
        ((two, width), F32),
        ((two, hidden), BF16),
        ((two, hidden), BF16),
        ((tokens, width), BF16),
        ((2, width, two), BF16),
        ((width, rows), BF16),
        ((width, two), BF16),
    ]
    outs = pl.pallas_call(
        functools.partial(forward_kernel, names, dims),
        out_shape=shapes,
        in_specs=[ANY] * (count + 4) + [SMEM, SMEM],
        out_specs=[ANY] * count + [VMEM, VMEM] + [ANY] * len(names),
        scratch_shapes=[pltpu.VMEM(s, t) for s, t in scratch]
        + [
            pltpu.SemaphoreType.DMA((copies,)),
            pltpu.SemaphoreType.DMA((copies,)),
            pltpu.SemaphoreType.DMA((4 + 2 * count + len(names),)),
        ],
        compiler_params=pltpu.CompilerParams(
            collective_id=0, has_side_effects=True, vmem_limit_bytes=60 << 20
        ),
        name="gather_and_forward",
    )(*own, gain, latents, inputs, cotangent, counts, flags)
    full, (norm_gain, result) = outs[:count], outs[count : count + 2]
    return full, norm_gain, result, dict(zip(names, outs[count + 2 :]))


def norm_back(values, gain_row, gradient):
    unit, inverse = normed(values)
    scaled = gradient * gain_row
    grad = inverse * (
        scaled
        - jnp.mean(scaled, axis=-1, keepdims=True)
        - unit * jnp.mean(scaled * unit, axis=-1, keepdims=True)
    )
    return grad, jnp.sum(gradient * unit, axis=0, keepdims=True)


def dot_tn(a, b):
    return lax.dot_general(a, b, (((0,), (0,)), ((), ())), preferred_element_type=F32)


def attention_back(q, k, v, out_grad, prob, delta):
    prob_grad = dot_nt(out_grad, v)
    weight = prob.astype(F32)
    if delta is None:
        delta = jnp.sum(weight * prob_grad, axis=-1, keepdims=True)
    score_grad = low(weight * (prob_grad - delta))
    q_grad = join_heads(dot(score_grad, k)) * 0.125
    k_grad = dot_tn(score_grad, q) * 0.125
    v_grad = dot_tn(prob, out_grad)
    return low(q_grad), low(k_grad), low(v_grad)


def spot(ref, index):
    return lambda: ref.at[index]


def backward_kernel(names, dims, *refs):
    rows, tokens, width, hidden = dims
    two, quarter, pairs = 2 * rows, hidden // 4, width // 128
    count = 6
    order = (5, 4, 3, 2, 1, 0)
    refs = list(refs)

    def take(n):
        out = refs[:n]
        del refs[:n]
        return out

    full = take(count)
    gain, lat, cot, flags = take(4)
    kept = dict(zip(names, take(len(names))))
    outs = take(count)
    gain_out, lat_grad, dx = take(3)
    total = take(count)
    from_y, from_x = take(3), take(3)
    from_a, from_b, from_c, from_d, from_z, end_c, end_d = (take(count) for _ in range(7))
    wr, wt, grad_ac, du_sib, r_sib, ge_sib, dcu_sib, rs_sib, dkv_sib = take(9)
    gain_acc, gain_sub, gain_dp, send, recv, local, free = take(7)
    place = Place()
    x, y, z, c = place.x, place.y, place.z, place.c
    sems = Sems(place, send, recv)
    local_count = [0]

    def local_copy(src, dst):
        made = pltpu.make_async_copy(src, dst, local.at[local_count[0]])
        local_count[0] += 1
        made.start()
        return made

    me_dp, me_sub = z * 2 + y, x * 2 + c
    sub_peers = [(me_dp, (me_sub + k) % 4) for k in (1, 2, 3)]
    dp_peers = [((me_dp + k) % 8, me_sub) for k in range(1, 8)]
    px, py, pc = place.dev(x=1 - x), place.dev(y=1 - y), place.dev(c=1 - c)
    first_live = flags[0] == 0
    gain_acc[...] = jnp.zeros_like(gain_acc)

    ones, twos, threes = {}, {}, {}

    def step_one(i):
        m = order[i]
        a = total[m]
        r = a.shape[3]
        if i >= 3:
            pl.semaphore_wait(free.at[i - 3], 2)
        ca, bd = pl.ds(0, r // 2), pl.ds(r // 2, r // 2)
        ones[i] = [
            sems.copy(a.at[:, :, 1 - y, ca], from_y[i % 3], py),
            sems.copy(a.at[1 - x, :, :, bd], from_x[i % 3], px),
        ]

    def step_two(i):
        m = order[i]
        wait_all(ones.pop(i))
        a = total[m]
        r = a.shape[3]
        ca, bd = pl.ds(0, r // 2), pl.ds(r // 2, r // 2)
        fy, fx = from_y[i % 3], from_x[i % 3]

        @pl.loop(0, 8)
        def _(j):
            add_blocks(a, (j // 4, j % 4, y, ca), fy, (j // 4, j % 4))
            add_blocks(a, (x, j // 2, j % 2, bd), fx, (j // 2, j % 2))

        if i < 3:
            for device in (px, py):
                pl.semaphore_signal(free.at[i], inc=1, device_id=device, device_id_type=MESH_ID)
        pa, pb = pl.ds(r // 6, r // 3), pl.ds(r // 2, r // 3)
        top, last = pl.ds(0, r // 6), pl.ds(5 * r // 6, r // 6)
        got = [
            sems.copy(a.at[1 - x, :, y, pa], from_a[m], px),
            sems.copy(a.at[x, :, 1 - y, pb], from_b[m], py),
        ]
        for k in (1, 2, 3):
            zk = place.zk(k)
            there = place.dev(z=zk)
            got.append(sems.copy(a.at[:, zk, y, top], spot(from_c[m], k - 1), there))
            got.append(sems.copy(a.at[x, zk, :, last], spot(from_d[m], k - 1), there))
        twos[i] = got

    def step_three(i):
        m = order[i]
        wait_all(twos.pop(i))
        a = total[m]
        r = a.shape[3]
        pa, pb = pl.ds(r // 6, r // 3), pl.ds(r // 2, r // 3)
        top, last = pl.ds(0, r // 6), pl.ds(5 * r // 6, r // 6)

        @pl.loop(0, 4)
        def _(j):
            add_blocks(a, (x, j, y, pa), from_a[m], j)
            add_blocks(a, (x, j, y, pb), from_b[m], j)

        for j in range(2):
            fc, fd = from_c[m], from_d[m]
            a[j, z, y, top] = low(
                a[j, z, y, top].astype(F32)
                + fc[0, j].astype(F32)
                + fc[1, j].astype(F32)
                + fc[2, j].astype(F32)
            )
            a[x, z, j, last] = low(
                a[x, z, j, last].astype(F32)
                + fd[0, j].astype(F32)
                + fd[1, j].astype(F32)
                + fd[2, j].astype(F32)
            )
        middle = pl.ds(r // 6, 2 * r // 3)
        got = []
        for k in (1, 2, 3):
            zk = place.zk(k)
            got.append(sems.copy(a.at[x, zk, y, middle], spot(from_z[m], k - 1), place.dev(z=zk)))
        got.append(sems.copy(a.at[1 - x, z, y, top], end_c[m], px))
        got.append(sems.copy(a.at[x, z, 1 - y, last], end_d[m], py))
        threes[i] = got

    def step_four(i):
        m = order[i]
        wait_all(threes.pop(i))
        a, o, fz = total[m], outs[m], from_z[m]
        r = a.shape[3]
        middle = pl.ds(r // 6, 2 * r // 3)
        top, last = pl.ds(0, r // 6), pl.ds(5 * r // 6, r // 6)
        o[middle] = (
            a[x, z, y, middle].astype(F32)
            + fz[0].astype(F32)
            + fz[1].astype(F32)
            + fz[2].astype(F32)
        )
        o[top] = a[x, z, y, top].astype(F32) + end_c[m][...].astype(F32)
        o[last] = a[x, z, y, last].astype(F32) + end_d[m][...].astype(F32)

    def slot(t):
        if 0 <= t < count:
            step_two(t)
        if 0 <= t - 1 < count:
            step_three(t - 1)
        if 0 <= t - 2 < count:
            step_four(t - 2)

    def put_square(m, at, value):
        shape = total[m].shape
        total[m][at] = low(value).reshape(shape[1:])

    def put_hidden(m, zz, value):
        shape = total[m].shape
        for yy in range(2):
            part = value[:, yy * shape[4] : (yy + 1) * shape[4]]
            total[m][:, zz, yy] = low(part).reshape(2, shape[3], shape[4])

    def hidden_grad(m, left, right):
        for zz in range(4):
            put_hidden(m, zz, dot(left, right[:, zz * quarter : (zz + 1) * quarter]))

    def both(own, other):
        return jnp.concatenate([own, other], axis=0)

    def send_off(src, dst):
        return sems.copy(src, dst, pc, later=False)

    def pick(first, second):
        return jnp.where(first_live, first, second)

    def back_through(act, blocks):
        out = None
        for i, (a, b) in enumerate(blocks):
            term = dot_nt(act[a, b], square_block(wr, a, b))
            out = term if out is None else out + term
        return out

    every = ((0, 0), (0, 1), (1, 0), (1, 1))

    def self_part(mh, gps, gyt, mnt, sbt, l1t, du, r, cot_v, aa, ac, sqkv, sp, grad_aa, out_grad):
        loads = {
            name: local_copy(src, dst)
            for name, src, dst in (
                ("gyt", kept["gyt"], gyt),
                ("mh", kept["mh"], mh),
                ("wt", full[5], wt),
                ("cot", cot, cot_v),
                ("gps", kept["gps"], gps),
                ("wr", full[4], wr),
                ("aa", kept["aa"], aa),
                ("mnt", kept["mnt"], mnt),
                ("sqkv", kept["sqkv"], sqkv),
                ("sp", kept["sp"], sp),
                ("ac", kept["ac"], ac),
                ("sbt", kept["sbt"], sbt),
                ("l1t", kept["l1t"], l1t),
            )
        }
        greet(place, sub_peers + dp_peers)
        loads["gyt"].wait()
        loads["mh"].wait()
        hidden_grad(5, gyt[...].reshape(width // 2, 2 * two), mh)
        step_one(0)

        for name in ("wt", "cot", "gps"):
            loads[name].wait()
        for at, value in (
            (pl.ds(0, rows), pick(cot_v[0], cot_v[1])),
            (pl.ds(rows, rows), pick(cot_v[1], cot_v[0])),
        ):
            grad_aa[at] = value
        gy = low(grad_aa[...])
        for s in range(4):
            at = pl.ds(s * quarter, quarter)
            du[s // 2, s % 2] = low(dot(gy, hidden_block(wt, s)) * gps[:, at].astype(F32))
        sent = send_off(du.at[:, 1 - c], du_sib)
        for name in ("wr", "aa", "mnt"):
            loads[name].wait()
        grad, gain_row = norm_back(aa[...], gain[4:5], back_through(du, every))
        grad_aa[...] += grad
        gain_acc[0, 4:5] = gain_row
        next_wr = local_copy(full[3], wr)
        next_wt = local_copy(full[2], wt)
        sent.wait_recv()
        for a in range(2):
            put_square(4, a, dot(mnt[...], both(du[a, c], du_sib[a])))
        step_one(1)
        slot(0)

        r[1, 1] = low(grad_aa[...])
        for made in (next_wr, loads["sqkv"], loads["sp"], loads["ac"], loads["sbt"], loads["l1t"]):
            made.wait()
        out_grad[...] = low(dot_nt(r[1, 1], square_block(wr, 1, 1)))

        @pl.loop(0, 2 * pairs)
        def _(i):
            at, row_at = lanes(i % pairs, 128), lanes(i // pairs, rows)
            r[0, 0, row_at, at], r[0, 1, row_at, at], r[1, 0, row_at, at] = attention_back(
                stack_heads(sqkv[0, row_at, at]),
                sqkv[1, row_at, at],
                sqkv[2, row_at, at],
                stack_heads(out_grad[row_at, at]),
                sp[i],
                None,
            )

        sent_r = send_off(r.at[:, 1 - c], r_sib)
        grad, gain_row = norm_back(ac[...], gain[3:4], back_through(r, every[:3]))
        grad_ac[...] = grad_aa[...] + grad
        gain_acc[0, 3:4] = gain_row
        sent_r.wait_recv()
        put_square(3, 0, dot(sbt[...], both(r[0, c], r_sib[0])))
        put_square(3, 1, dot(l1t[...], both(r[1, c], r_sib[1])))
        step_one(2)
        slot(1)
        sent.wait_send()
        sent_r.wait_send()
        next_wt.wait()

    def cross_part(
        ch, gpc, ge, cnt, du, mid, lst, rs, xbt, kv, cp, cq, co, dco, xl, dxs, lat_v, grad_mid
    ):
        loads = {
            name: local_copy(src, dst)
            for name, src, dst in (
                ("ch", kept["ch"], ch),
                ("gpc", kept["gpc"], gpc),
                ("wr", full[1], wr),
                ("mid", kept["mid"], mid),
                ("cnt", kept["cnt"], cnt),
                ("cq", kept["cq"], cq),
                ("co", kept["co"], co),
                ("kv", kept["kv"], kv),
                ("cp", kept["cp"], cp),
                ("lst", kept["lst"], lst),
                ("xbt", kept["xbt"], xbt),
                ("lat", lat, lat_v),
            )
        }
        for i in range(2):
            lat_grad_dead = grad_ac[rows:]
            lat_grad[i] = lat_grad_dead
        low_grad = low(grad_ac[:rows])
        ge[...] = low_grad.T.reshape(2, 2, width // 4, rows)
        sent = [send_off(ge.at[:, 1 - c], ge_sib)]
        loads["gpc"].wait()
        for s in range(4):
            at = pl.ds(s * quarter, quarter)
            du[s // 2, s % 2] = low(dot(low_grad, hidden_block(wt, s)) * gpc[:, at].astype(F32))
        sent.append(send_off(du.at[:, 1 - c], dcu_sib))
        loads["ch"].wait()
        sent[0].wait_recv()
        left = jnp.concatenate(
            [ge[:, c].reshape(width // 2, rows), ge_sib[...].reshape(width // 2, rows)], axis=1
        )
        hidden_grad(2, left, ch)
        step_one(3)
        slot(2)

        for name in ("wr", "mid", "cnt"):
            loads[name].wait()
        grad, gain_row = norm_back(mid[...], gain[2:3], back_through(du, every))
        grad_mid[...] = grad_ac[:rows] + grad
        gain_acc[0, 2:3] = gain_row
        next_wr = local_copy(full[0], wr)
        sent[1].wait_recv()
        for a in range(2):
            put_square(1, a, dot(cnt[...], both(du[a, c], dcu_sib[a])))
        step_one(4)
        slot(3)

        rs[1] = low(grad_mid[...])
        next_wr.wait()
        dco[...] = low(dot_nt(rs[1], square_block(wr, 1, 1)))
        for name in ("cq", "co", "kv", "cp"):
            loads[name].wait()

        @pl.loop(0, pairs)
        def _(p):
            at = lanes(p, 128)
            out_grad = stack_heads(dco[:, at])
            attended = co[:, at]
            delta = jnp.sum(
                out_grad.astype(F32) * both(attended, attended), axis=-1, keepdims=True
            )
            rs[0, :, at], kv[0, :, at], kv[1, :, at] = attention_back(
                stack_heads(cq[:, at]), kv[0, :, at], kv[1, :, at], out_grad, cp[p], delta
            )

        sent.append(send_off(rs.at[1 - c], rs_sib))
        sent.append(send_off(kv.at[c], dkv_sib))
        for name in ("lst", "xbt", "lat"):
            loads[name].wait()
        sent[2].wait_recv()
        sent[3].wait_recv()
        put_square(0, c, dot(lst[...], both(rs[c], rs_sib[...])))
        put_square(
            0, 1 - c, dot(xbt[:, :tokens], kv[1 - c]) + dot(xbt[:, tokens:], dkv_sib[...])
        )
        step_one(5)

        grad, gain_row = norm_back(
            pick(lat_v[0], lat_v[1]), gain[0:1], dot_nt(rs[0], square_block(wr, 0, 0))
        )
        gain_acc[0, 0:1] = gain_row
        live_grad = grad_mid[...] + grad
        lat_grad[0] = pick(live_grad, lat_grad[0])
        lat_grad[1] = pick(lat_grad[1], live_grad)
        slot(4)
        out = []
        parts = tokens // 128

        def fetch(i):
            return local_copy(kept["xl"].at[pl.ds(i * 128, 128)], xl.at[i % 2])

        fetched = fetch(0)
        for i in range(parts):
            at = pl.ds(i * 128, 128)
            fetched.wait()
            if i + 1 < parts:
                fetched = fetch(i + 1)
            if i >= 2:
                out[i - 2].wait()
            term = dot_nt(kv[0, at], square_block(wr, 0, 1))
            term += dot_nt(kv[1, at], square_block(wr, 1, 0))
            grad, gain_row = norm_back(xl[i % 2].astype(F32), gain[1:2], term)
            dxs[i % 2] = grad
            gain_acc[0, 1:2] += gain_row
            out.append(local_copy(dxs.at[i % 2], dx.at[at]))
        for made in out[-2:]:
            made.wait()
        gain_one = [sems.copy(gain_acc.at[0], spot(gain_sub, k), sub_peers[k]) for k in range(3)]
        slot(5)
        wait_all(gain_one)
        gain_acc[1] = gain_acc[0] + gain_sub[0] + gain_sub[1] + gain_sub[2]
        gain_two = [sems.copy(gain_acc.at[1], spot(gain_dp, k), dp_peers[k]) for k in range(7)]
        for made in sent:
            made.wait_send()
        return gain_two

    def vmem(*shape, dtype=BF16):
        return pltpu.VMEM(shape, dtype)

    holder = {}

    pl.run_scoped(
        self_part,
        vmem(2 * two, hidden),
        vmem(two, hidden),
        vmem(2, width // 4, 2 * two),
        vmem(width, 2 * two),
        vmem(width, 2 * two),
        vmem(width, 2 * two),
        vmem(2, 2, two, quarter),
        vmem(2, 2, two, width),
        vmem(2, rows, width, dtype=F32),
        vmem(two, width, dtype=F32),
        vmem(two, width, dtype=F32),
        vmem(3, two, width),
        vmem(2 * pairs, two, rows),
        vmem(two, width, dtype=F32),
        vmem(two, width),
    )

    def run_cross(*bufs):
        holder["gain"] = cross_part(*bufs)

    pl.run_scoped(
        run_cross,
        vmem(two, hidden),
        vmem(rows, hidden),
        vmem(2, 2, width // 4, rows),
        vmem(width, two),
        vmem(2, 2, rows, quarter),
        vmem(rows, width, dtype=F32),
        vmem(width, two),
        vmem(2, rows, width),
        vmem(width, 2 * tokens),
        vmem(2, tokens, width),
        vmem(pairs, two, tokens),
        vmem(rows, width),
        vmem(rows, width, dtype=F32),
        vmem(rows, width),
        vmem(2, 128, width),
        vmem(2, 128, width, dtype=F32),
        vmem(2, rows, width, dtype=F32),
        vmem(rows, width, dtype=F32),
    )
    slot(6)
    slot(7)
    wait_all(holder["gain"])
    gain_out[...] = gain_acc[1] + jnp.sum(gain_dp[...], axis=0)
    sems.drain()


def backward_all(full, norm_gain, latents, cotangent, flags, kept):
    count = len(full)
    rows, width = latents.shape[1:]
    tokens, hidden = kept["xl"].shape[0], kept["mh"].shape[1]
    dims = (rows, tokens, width, hidden)
    two = 2 * rows
    copies = 10 + 6 + count * (2 + 8 + 5)
    shard = [p.shape[4:] for p in full]
    order = (5, 4, 3, 2, 1, 0)

    def room(lead, part, which):
        return [pltpu.VMEM(lead + (int(r / part), n), BF16) for r, n in which]

    ring = [shard[order[i]] for i in range(3)]
    scratch = room((2, 4, 2), 1, shard)
    scratch += room((2, 4), 2, ring) + room((4, 2), 2, ring)
    for lead, part in (
        ((4,), 3),
        ((4,), 3),
        ((3, 2), 6),
        ((3, 2), 6),
        ((3,), 1.5),
        ((), 6),
        ((), 6),
    ):
        scratch += room(lead, part, shard)
    scratch += [
        pltpu.VMEM(full[0].shape, BF16),
        pltpu.VMEM(full[2].shape, BF16),
        pltpu.VMEM((two, width), F32),
        pltpu.VMEM((2, two, hidden // 4), BF16),
        pltpu.VMEM((2, two, width), BF16),
        pltpu.VMEM((2, width // 4, rows), BF16),
        pltpu.VMEM((2, rows, hidden // 4), BF16),
        pltpu.VMEM((rows, width), BF16),
        pltpu.VMEM((tokens, width), BF16),
        pltpu.VMEM((2, 8, width), F32),
        pltpu.VMEM((3, 8, width), F32),
        pltpu.VMEM((7, 8, width), F32),
        pltpu.SemaphoreType.DMA((copies,)),
        pltpu.SemaphoreType.DMA((copies,)),
        pltpu.SemaphoreType.DMA((48,)),
        pltpu.SemaphoreType.REGULAR((3,)),
    ]
    shapes = [jax.ShapeDtypeStruct(d, F32) for d in shard]
    shapes += [
        jax.ShapeDtypeStruct((8, width), F32),
        jax.ShapeDtypeStruct(latents.shape, F32),
        jax.ShapeDtypeStruct((tokens, width), F32),
    ]
    outs = pl.pallas_call(
        functools.partial(backward_kernel, tuple(kept), dims),
        out_shape=shapes,
        in_specs=[ANY] * count + [VMEM, ANY, ANY, SMEM] + [ANY] * len(kept),
        out_specs=[VMEM] * (count + 2) + [ANY],
        scratch_shapes=scratch,
        compiler_params=pltpu.CompilerParams(
            collective_id=1, has_side_effects=True, vmem_limit_bytes=60 << 20
        ),
        name="backward_and_scatter",
    )(*full, norm_gain, latents, cotangent, flags, *kept.values())
    return outs[:count], *outs[count:]


def layer_norm(values, gain_row):
    centred = values - jnp.mean(values, axis=-1, keepdims=True)
    inverse = lax.rsqrt(jnp.mean(centred * centred, axis=-1, keepdims=True) + EPSILON)
    return centred * inverse * gain_row


def norm_backward(values, gain_row, gradient):
    unused, pull_back = jax.vjp(layer_norm, values, gain_row)
    return pull_back(gradient)


def gelu_tanh(values):
    return jax.nn.gelu(values, approximate=True)


def mm(left_side, weight):
    return jnp.dot(left_side, weight, preferred_element_type=F32)


def mm_nt(left_side, weight):
    return lax.dot_general(left_side, weight, (((1,), (1,)), ((), ())), preferred_element_type=F32)


def mm_tn(left_side, gradient):
    return lax.dot_general(
        left_side, gradient, (((0,), (0,)), ((), ())), preferred_element_type=F32
    )


def low(values):
    return values.astype(BF16)


def heads_of(values):
    return values.reshape(values.shape[:-1] + (HEADS, values.shape[-1] // HEADS))


def mlp_forward(residual, gain_row, up, down_t):
    normed = low(layer_norm(residual, gain_row))
    pre_act = mm(normed, up)
    hidden = low(gelu_tanh(pre_act))
    return normed, pre_act, hidden, mm_nt(hidden, down_t)


def mlp_backward(residual, gain_row, normed, pre_act, hidden, up, down_t, grad_out):
    grad_low = low(grad_out)
    grad_down_t = mm_tn(grad_low, hidden)
    grad_hidden = mm(grad_low, down_t)
    unused, gelu_back = jax.vjp(gelu_tanh, pre_act)
    grad_pre = low(gelu_back(grad_hidden)[0])
    grad_up = mm_tn(normed, grad_pre)
    grad_resid, grad_gain = norm_backward(residual, gain_row, mm_nt(grad_pre, up))
    return grad_resid, grad_gain, grad_up, grad_down_t


def live_layer(live_lat, dead_lat, tokens, count, live_cot, dead_cot, weights, norm_gain):
    c_attn, c_up, c_down_t, s_attn, s_up, s_down_t = weights
    rows, width = live_lat.shape
    scale = (width // HEADS) ** (-0.5)
    lat_low = low(layer_norm(live_lat, norm_gain[0]))
    queries = low(mm(lat_low, c_attn[:, :width]))
    token_values = tokens.astype(F32)
    tok_low = low(layer_norm(token_values, norm_gain[1]))
    kv_weight = c_attn[:, width : 3 * width]
    key_value = low(mm(tok_low, kv_weight))
    keys, values = heads_of(key_value[:, :width]), heads_of(key_value[:, width:])
    scores = (
        jnp.einsum("qhd,khd->hqk", heads_of(queries), keys, preferred_element_type=F32) * scale
    )
    valid = (jnp.arange(tokens.shape[0]) < count)[None, None, :]
    probs = jax.nn.softmax(jnp.where(valid, scores, MASKED), axis=-1)
    probs_low = low(probs)
    attended = jnp.einsum("hqk,khd->qhd", probs_low, values, preferred_element_type=F32)
    attended = attended.reshape(rows, width)
    cross_low = low(attended)
    middle = live_lat + mm(cross_low, c_attn[:, 3 * width :])
    c_norm, c_pre, c_hidden, c_mlp = mlp_forward(middle, norm_gain[2], c_up, c_down_t)
    after_cross = jnp.concatenate([middle + c_mlp, dead_lat], axis=0)

    self_low = low(layer_norm(after_cross, norm_gain[3]))
    qkv = low(mm(self_low, s_attn[:, : 3 * width])).reshape(2, rows, 3 * width)
    s_q = heads_of(qkv[..., :width])
    s_k = heads_of(qkv[..., width : 2 * width])
    s_v = heads_of(qkv[..., 2 * width :])
    s_scores = jnp.einsum("iqhd,ikhd->ihqk", s_q, s_k, preferred_element_type=F32) * scale
    s_probs = jax.nn.softmax(s_scores, axis=-1)
    s_probs_low = low(s_probs)
    s_out = jnp.einsum("ihqk,ikhd->iqhd", s_probs_low, s_v, preferred_element_type=F32)
    s_out_low = low(s_out.reshape(2 * rows, width))
    after_attn = after_cross + mm(s_out_low, s_attn[:, 3 * width :])
    m_norm, m_pre, m_hidden, m_mlp = mlp_forward(after_attn, norm_gain[4], s_up, s_down_t)
    result = after_attn + m_mlp

    cotangent = jnp.concatenate([live_cot, dead_cot], axis=0)
    grad_in, gain_four, d_s_up, d_s_down_t = mlp_backward(
        after_attn, norm_gain[4], m_norm, m_pre, m_hidden, s_up, s_down_t, cotangent
    )
    grad_attn = cotangent + grad_in
    grad_y = low(grad_attn)
    d_s_o = mm_tn(s_out_low, grad_y)
    grad_out = heads_of(low(mm_nt(grad_y, s_attn[:, 3 * width :])).reshape(2, rows, width))
    grad_probs = jnp.einsum("iqhd,ikhd->ihqk", grad_out, s_v, preferred_element_type=F32)
    delta = jnp.sum(grad_probs * s_probs, axis=-1, keepdims=True)
    grad_scores = low(s_probs * (grad_probs - delta))
    g_q = jnp.einsum("ihqk,ikhd->iqhd", grad_scores, s_k, preferred_element_type=F32) * scale
    g_k = jnp.einsum("ihqk,iqhd->ikhd", grad_scores, s_q, preferred_element_type=F32) * scale
    g_v = jnp.einsum("ihqk,iqhd->ikhd", s_probs_low, grad_out, preferred_element_type=F32)
    grad_qkv = low(
        jnp.concatenate([g.reshape(2 * rows, width) for g in (g_q, g_k, g_v)], axis=-1)
    )
    d_s_qkv = mm_tn(self_low, grad_qkv)
    grad_in, gain_three = norm_backward(
        after_cross, norm_gain[3], mm_nt(grad_qkv, s_attn[:, : 3 * width])
    )
    grad_cross = grad_attn + grad_in
    live_grad, dead_grad = grad_cross[:rows], grad_cross[rows:]
    grad_in, gain_two, d_c_up, d_c_down_t = mlp_backward(
        middle, norm_gain[2], c_norm, c_pre, c_hidden, c_up, c_down_t, live_grad
    )
    grad_middle = live_grad + grad_in
    grad_cross_y = low(grad_middle)
    d_c_o = mm_tn(cross_low, grad_cross_y)
    grad_cross_out = low(mm_nt(grad_cross_y, c_attn[:, 3 * width :]))
    out_heads = heads_of(grad_cross_out)
    grad_weights = jnp.einsum("qhd,khd->hqk", out_heads, values, preferred_element_type=F32)
    row_delta = jnp.transpose(jnp.sum(heads_of(grad_cross_out.astype(F32) * attended), axis=-1))
    grad_scores = low(probs * (grad_weights - row_delta[..., None]))
    grad_query = low(
        (
            jnp.einsum("hqk,khd->qhd", grad_scores, keys, preferred_element_type=F32) * scale
        ).reshape(rows, width)
    )
    grad_keys = (
        jnp.einsum("hqk,qhd->khd", grad_scores, heads_of(queries), preferred_element_type=F32)
        * scale
    )
    grad_values = jnp.einsum("hqk,qhd->khd", probs_low, out_heads, preferred_element_type=F32)
    grad_kv = low(
        jnp.concatenate(
            [grad_keys.reshape(-1, width), grad_values.reshape(-1, width)], axis=-1
        )
    )
    d_c_kv = mm_tn(tok_low, grad_kv)
    grad_tokens, gain_one = norm_backward(token_values, norm_gain[1], mm_nt(grad_kv, kv_weight))
    d_c_q = mm_tn(lat_low, grad_query)
    grad_in, gain_zero = norm_backward(
        live_lat, norm_gain[0], mm_nt(grad_query, c_attn[:, :width])
    )
    live_lat_grad = grad_middle + grad_in
    d_c_attn = low(jnp.concatenate([d_c_q, d_c_kv, d_c_o], axis=1))
    d_s_attn = low(jnp.concatenate([d_s_qkv, d_s_o], axis=1))
    gain_grad = jnp.stack([gain_zero, gain_one, gain_two, gain_three, gain_four])
    grads = (d_c_attn, low(d_c_up), low(d_c_down_t), d_s_attn, low(d_s_up), low(d_s_down_t))
    return result, live_lat_grad, dead_grad, grad_tokens, grads, gain_grad


def column_blocks(blocks):
    sub, dp, rows, columns = blocks.shape
    return blocks.transpose(1, 2, 0, 3).reshape(dp * rows, sub * columns)


def row_blocks(blocks):
    sub, dp, rows, columns = blocks.shape
    return blocks.transpose(0, 2, 1, 3).reshape(sub * rows, dp * columns)


def shards(*arrays, dp_size, sub_size):
    latents, inputs, counts, flags = arrays[:4]
    cross_attn, cross_up, cross_down, self_attn, self_up, self_down, gains, cotangent = arrays[4:]
    width = latents.shape[-1]
    own = (
        cross_attn,
        cross_up,
        jnp.transpose(cross_down),
        self_attn,
        self_up,
        jnp.transpose(self_down),
    )
    live = jnp.where(flags[0] == 0, 0, 1)
    here = (jnp.arange(inputs.shape[0]) == live)[:, None, None]
    if dp_size == 8 and sub_size == 4:
        padded = jnp.pad(gains, ((0, 16 - gains.shape[0]), (0, 128 - gains.shape[1])))
        full, norm_gain, result, kept = forward_all(
            own, padded, latents, inputs, cotangent, counts, flags
        )
        owned, gain_total, grad_latents, grad_tokens = backward_all(
            full, norm_gain, latents, cotangent, flags, kept
        )
        grad_inputs = jnp.where(here, grad_tokens[None], 0.0)
        gain_owned = lax.dynamic_slice_in_dim(
            gain_total[: gains.shape[0]],
            lax.axis_index("dp") * gains.shape[1],
            gains.shape[1],
            1,
        )
        owned = [jnp.transpose(g) if i in (2, 5) else g for i, g in enumerate(owned)]
        return (result, grad_latents, grad_inputs, *owned, gain_owned)

    blocks = [lax.all_gather(lax.all_gather(w, "dp", axis=0), "sub", axis=0) for w in own]
    norm_gain = lax.all_gather(gains, "dp", axis=1, tiled=True)
    transposed = (False, False, True, False, False, True)
    weights = [
        row_blocks(b) if flip else column_blocks(b) for b, flip in zip(blocks, transposed)
    ]

    def item(array, index):
        return lax.dynamic_index_in_dim(array, index, 0, keepdims=False)

    result, live_grad, dead_grad, grad_tokens, grads, gain_grad = live_layer(
        item(latents, live),
        item(latents, 1 - live),
        item(inputs, live),
        item(counts, live),
        item(cotangent, live),
        item(cotangent, 1 - live),
        weights,
        norm_gain.astype(F32),
    )

    def both(live_part, dead_part):
        first = jnp.where(live == 0, live_part, dead_part)
        second = jnp.where(live == 0, dead_part, live_part)
        return jnp.stack([first, second])

    rows = latents.shape[1]
    result = both(result[:rows], result[rows:])
    grad_latents = both(live_grad, dead_grad)
    grad_inputs = jnp.where(here, grad_tokens[None], 0.0)

    def blocks_of(grad, shape, flip):
        r, c = shape
        if flip:
            return grad.reshape(sub_size, r, dp_size, c).transpose(0, 2, 1, 3)
        return grad.reshape(dp_size, r, sub_size, c).transpose(2, 0, 1, 3)

    grads = [blocks_of(g, w.shape, flip) for g, w, flip in zip(grads, own, transposed)]
    owned = [lax.psum_scatter(g, "sub", scatter_dimension=0) for g in grads]
    owned = [lax.psum_scatter(g.astype(F32), "dp", scatter_dimension=0) for g in owned]
    gain_owned = lax.psum(gain_grad, "sub")
    gain_owned = lax.psum_scatter(gain_owned, "dp", scatter_dimension=1, tiled=True)
    owned = [jnp.transpose(g) if flip else g for g, flip in zip(owned, transposed)]
    return (result, grad_latents, grad_inputs, *owned, gain_owned)


def solution(mesh):
    item = P(("dp", "sub"), None, None)
    weight = P("dp", "sub")
    gain = P(None, "dp")
    placed = (item, item, P(("dp", "sub")), P()) + (weight,) * 6 + (gain, item)
    return jax.shard_map(
        functools.partial(shards, dp_size=mesh.shape["dp"], sub_size=mesh.shape["sub"]),
        mesh=mesh,
        in_specs=placed,
        out_specs=(item, item, item) + (weight,) * 6 + (gain,),
        check_vma=False,
    )
```

```python
import collections
import functools

import jax
import jax.numpy as jnp
from jax import lax
from jax.experimental import pallas as pl
from jax.experimental.pallas import tpu as pltpu
from jax.sharding import PartitionSpec as P

HEADS = 12
EPSILON = 1e-05
MASKED = -1e30
MESH_ID = pl.DeviceIdType.MESH
F32 = jnp.float32
BF16 = jnp.bfloat16
ANY = pl.BlockSpec(memory_space=pl.ANY)
VMEM = pl.BlockSpec(memory_space=pltpu.VMEM)
SMEM = pl.BlockSpec(memory_space=pltpu.SMEM)


PIECES = {
    "C": (0, 2),
    "A": (2, 1),
    "B": (3, 1),
    "D": (4, 2),
    "CA": (0, 3),
    "AB": (2, 2),
    "BD": (3, 3),
}


def piece(name, rows):
    first, size = PIECES[name]
    return pl.ds(first * (rows // 6), size * (rows // 6))


class Place:
    def __init__(self):
        dp, sub = lax.axis_index("dp"), lax.axis_index("sub")
        self.z, self.y, self.x, self.c = dp // 2, dp % 2, sub // 2, sub % 2

    def dev(self, z=None, y=None, x=None, c=None):
        z = self.z if z is None else z
        y = self.y if y is None else y
        x = self.x if x is None else x
        c = self.c if c is None else c
        return (z * 2 + y, x * 2 + c)

    def zk(self, k):
        return (self.z + k) % 4


def now(ref):
    return ref() if callable(ref) else ref


def spot(ref, index):
    return lambda: ref.at[index]


def only_if(condition, action):
    if condition is None:
        action()
    else:
        pl.when(condition())(action)


class Flight:
    def __init__(self, sems, ref, send_index, recv_index):
        self.sems, self.ref, self.send_index, self.recv_index = sems, ref, send_index, recv_index

    def made(self):
        place = self.sems.place
        return pltpu.make_async_remote_copy(
            src_ref=now(self.ref),
            dst_ref=now(self.ref),
            send_sem=self.sems.send.at[self.send_index],
            recv_sem=self.sems.recv.at[self.recv_index],
            device_id=place.dev(c=1 - place.c),
            device_id_type=MESH_ID,
        )

    def wait_send(self):
        self.made().wait_send()

    def wait_recv(self):
        self.made().wait_recv()


class Sems:
    def __init__(self, place, send, recv):
        self.place, self.send, self.recv, self.count, self.sent = place, send, recv, 0, []

    def reserve(self, n):
        self.count += n
        return self.count - n

    def start(self, src, dst, device, send_index, recv_index, condition=None, later=True):
        def action():
            pltpu.make_async_remote_copy(
                src_ref=now(src),
                dst_ref=now(dst),
                send_sem=self.send.at[send_index],
                recv_sem=self.recv.at[recv_index],
                device_id=device,
                device_id_type=MESH_ID,
            ).start()

        only_if(condition, action)
        flight = Flight(self, dst, send_index, recv_index)
        if later:
            self.sent.append((condition, flight))
        return flight

    def copy(self, src, dst, device, later=True):
        index = self.reserve(1)
        return self.start(src, dst, device, index, index, later=later)

    def drain(self):
        for condition, flight in self.sent:
            only_if(condition, flight.wait_send)


def greet(place, devices):
    barrier = pltpu.get_barrier_semaphore()
    for device in devices:
        pl.semaphore_signal(barrier, inc=1, device_id=device, device_id_type=MESH_ID)
    pl.semaphore_wait(barrier, len(devices))


def wait_all(copies):
    for made in copies:
        made.wait_recv()


class Spread:
    def __init__(self, sems, src, where):
        self.sems, self.where, place = sems, where, sems.place
        self.base = sems.reserve(4)
        z = place.z
        for k, condition in ((1, lambda: z != 3), (2, None), (3, lambda: z != 0)):
            at = self.base + k - 1
            sems.start(src, where(z), place.dev(z=place.zk(k)), at, at, condition)

    def arrived(self, k):
        origin = self.sems.place.zk(4 - k)
        Flight(self.sems, self.where(origin), self.base + 3, self.base + k - 1).wait_recv()

    def forward(self):
        self.arrived(2)
        place = self.sems.place
        block = self.where(place.zk(2))
        for z, target, k in ((2, 3, 3), (1, 0, 1)):
            self.sems.start(
                block,
                block,
                place.dev(z=target),
                self.base + 3,
                self.base + k - 1,
                functools.partial(lambda z: place.z == z, z),
            )

    def finish(self):
        self.arrived(1)
        self.arrived(3)


class Collect:
    def __init__(self, sems, part, into, through):
        self.sems, self.part, self.into, self.through = sems, part, into, through
        place = sems.place
        self.base = sems.reserve(4)
        z = place.z
        for k, condition in (
            (1, lambda: z != 3),
            (2, lambda: (z == 0) | (z == 3)),
            (3, lambda: z != 0),
        ):
            self.send(k, condition)
        for k, end, middle in ((1, 3, 2), (3, 0, 1)):
            at = self.base + 3
            sems.start(part(place.zk(k)), through, place.dev(z=middle), at, at, functools.partial(lambda end: z == end, end))

    def send(self, k, condition):
        place, at = self.sems.place, self.base + k - 1
        self.sems.start(
            self.part(place.zk(k)),
            spot(self.into, k - 1),
            place.dev(z=place.zk(k)),
            at,
            at,
            condition,
        )

    def forward(self, add):
        place = self.sems.place

        def middle():
            return (place.z == 1) | (place.z == 2)

        @pl.when(middle())
        def _():
            Flight(self.sems, self.through, self.base + 3, self.base + 3).wait_recv()
            add(place.zk(2))

        self.send(2, middle)

    def finish(self):
        z = self.sems.place.z
        for k, condition in ((1, lambda: z != 0), (2, None), (3, lambda: z != 3)):
            flight = Flight(self.sems, spot(self.into, k - 1), self.base + 3, self.base + k - 1)
            only_if(condition, flight.wait_recv)


def slots(count, places, order):
    steps = []
    for slot in range(min(places.values()), count + max(places.values())):
        for name in order:
            i = slot - places[name]
            if 0 <= i < count:
                steps.append((slot, name, i))
    return steps


def dot(a, b):
    return jnp.dot(a, b, preferred_element_type=F32)


def dot_nt(a, b):
    return lax.dot_general(a, b, (((1,), (1,)), ((), ())), preferred_element_type=F32)


def low(values):
    return values.astype(BF16)


def normed(values):
    centred = values - jnp.mean(values, axis=-1, keepdims=True)
    inverse = lax.rsqrt(jnp.mean(centred * centred, axis=-1, keepdims=True) + EPSILON)
    return centred * inverse, inverse


def gelu_both(u):
    k, a = 0.7978845608028654, 0.044715
    square = u * u
    t = jnp.tanh(k * u * (1.0 + a * square))
    half = 0.5 * (1.0 + t)
    slope = half + (0.5 * k) * u * (1.0 - t * t) * (1.0 + (3.0 * a) * square)
    return u * half, slope


def square_block(ref, x, c):
    halves = []
    for h in range(2):
        block = ref[h, x, c]
        halves.append(block.reshape(-1, block.shape[3]))
    return jnp.concatenate(halves, axis=1)


def hidden_block(ref, z):
    parts = []
    for y in range(2):
        rows = [ref[h, x, c, z, y] for x in range(2) for c in range(2) for h in range(2)]
        parts.append(jnp.concatenate(rows, axis=0))
    return jnp.concatenate(parts, axis=1)


def left_half(shape):
    return lax.broadcasted_iota(jnp.int32, shape, 1) < 64


def stack_heads(values):
    left = left_half(values.shape)
    zero = jnp.zeros_like(values)
    return jnp.concatenate([jnp.where(left, values, zero), jnp.where(left, zero, values)], axis=0)


def join_heads(values):
    rows = values.shape[0] // 2
    top, bottom = values[:rows], values[rows:]
    return jnp.where(left_half(top.shape), top, bottom)


def lanes(index, size):
    return pl.ds(pl.multiple_of(index * size, size), size)


def kept_shapes(rows, tokens, width, hidden):
    two = 2 * rows
    return {
        "cq": ((rows, width), BF16),
        "kv": ((2, tokens, width), BF16),
        "cp": ((width // 128, two, tokens), BF16),
        "co": ((rows, width), F32),
        "mid": ((rows, width), F32),
        "gpc": ((rows, hidden), BF16),
        "ac": ((two, width), F32),
        "sqkv": ((3, two, width), BF16),
        "sp": ((2 * (width // 128), two, rows), BF16),
        "aa": ((two, width), F32),
        "gps": ((two, hidden), BF16),
        "xl": ((tokens, width), BF16),
    }


def paired_shapes(rows, tokens, width, hidden):
    two = 2 * rows
    return {
        "gyt": ((2, width // 4, 2 * two), BF16),
        "mh": ((2 * two, hidden), BF16),
        "mnt": ((width, 2 * two), BF16),
        "sbt": ((width, 2 * two), BF16),
        "l1t": ((width, 2 * two), BF16),
        "ch": ((two, hidden), BF16),
        "cnt": ((width, two), BF16),
        "lst": ((width, two), BF16),
        "xbt": ((width, 2 * tokens), BF16),
    }


def forward_kernel(names, dims, *refs):
    rows, tokens, width, hidden = dims
    two = 2 * rows
    count = 6
    refs = list(refs)

    def take(n):
        out = refs[:n]
        del refs[:n]
        return out

    own = take(count)
    gain, lat, tok, cot, live_counts, flags = take(6)
    full = take(count)
    gain_out, result = take(2)
    kept = dict(zip(names, take(len(names))))
    gain_all, lat_v, cot_v, tok_v, z2, xb, xbt, gyt, lst, wr0, wr1, wt = take(12)
    cq, kv, cp, co, mid, ch, gpc, ac, sqkv, sp, so, aa, mh, gps, xl, lt, cnt, mnt = take(18)
    gain_own, gain_one, zb_v, nb = take(4)
    send, recv, local = take(3)
    wr = (wr0, wr1)
    place = Place()
    x, y, z, c = place.x, place.y, place.z, place.c
    sems = Sems(place, send, recv)
    local_count = [0]
    local_open = []

    def local_copy(src, dst):
        made = pltpu.make_async_copy(src, dst, local.at[local_count[0]])
        local_count[0] += 1
        made.start()
        return made

    in_gain = local_copy(gain, gain_own)
    in_lat, in_tok, in_cot = local_copy(lat, lat_v), local_copy(tok, tok_v), local_copy(cot, cot_v)
    px, py, pc = place.dev(x=1 - x), place.dev(y=1 - y), place.dev(c=1 - c)
    me_dp = z * 2 + y
    dp_peers = [((me_dp + k) % 8, x * 2 + c) for k in range(1, 8)]
    greet(place, dp_peers + [px, pc])

    halves = 2 * count
    blocks = [full[i // 2].at[i % 2] for i in range(halves)]
    ones, twos, threes, across, placed = {}, {}, {}, {i: [] for i in range(halves)}, {}
    block_rows = full[0].shape[5]

    def shard(i):
        w, h = own[i // 2], i % 2
        if w.shape[0] == block_rows:
            return w, slice(None), pl.ds(h * (w.shape[1] // 2), w.shape[1] // 2), 0
        return w, slice(None), pl.ds(0, w.shape[1]), h * block_rows

    def own_piece(i, name):
        w, unused, columns, first = shard(i)
        at = piece(name, block_rows)
        return w.at[pl.ds(first + at.start, at.size), columns]

    def step_one(i):
        g = blocks[i]
        w, unused, columns, first = shard(i)
        placed[i] = local_copy(w.at[pl.ds(first, block_rows), columns], g.at[x, c, z, y])
        ab, pc_, pd = (piece(n, block_rows) for n in ("AB", "C", "D"))
        spread = Spread(sems, own_piece(i, "AB"), lambda o: g.at[x, c, o, y, ab])
        ones[i] = (
            spread,
            [
                sems.copy(own_piece(i, "C"), g.at[x, c, z, y, pc_], px),
                sems.copy(own_piece(i, "D"), g.at[x, c, z, y, pd], py),
            ],
        )

    def step_one_forward(i):
        ones[i][0].forward()

    def step_two(i):
        g = blocks[i]
        spread, got = ones.pop(i)
        placed.pop(i).wait()
        wait_all(got)
        pa, pb, pc_, pd = (piece(n, block_rows) for n in ("A", "B", "C", "D"))
        spread_c = Spread(sems, g.at[:, c, z, y, pc_], lambda o: g.at[:, c, o, y, pc_])
        spread_d = Spread(sems, g.at[x, c, z, :, pd], lambda o: g.at[x, c, o, :, pd])
        spread.finish()
        got = [
            sems.copy(g.at[x, c, :, y, pa], g.at[x, c, :, y, pa], px),
            sems.copy(g.at[x, c, :, y, pb], g.at[x, c, :, y, pb], py),
        ]
        twos[i] = ((spread_c, spread_d), got)

    def step_two_forward(i):
        for spread in twos[i][0]:
            spread.forward()

    def step_three(i):
        g = blocks[i]
        spreads, got = twos.pop(i)
        for spread in spreads:
            spread.finish()
        wait_all(got)
        ca, bd = piece("CA", block_rows), piece("BD", block_rows)
        threes[i] = [
            sems.copy(g.at[:, c, :, y, ca], g.at[:, c, :, y, ca], py),
            sems.copy(g.at[x, c, :, :, bd], g.at[x, c, :, :, bd], px),
        ]
        across[i] += [
            sems.copy(g.at[:, c, :, y, ca], g.at[:, c, :, y, ca], pc),
            sems.copy(g.at[x, c, :, :, bd], g.at[x, c, :, :, bd], pc),
        ]

    def step_four(i):
        wait_all(threes.pop(i))
        g = blocks[i]
        ca, bd = piece("CA", block_rows), piece("BD", block_rows)
        across[i] += [
            sems.copy(g.at[:, c, :, 1 - y, ca], g.at[:, c, :, 1 - y, ca], pc),
            sems.copy(g.at[1 - x, c, :, :, bd], g.at[1 - x, c, :, :, bd], pc),
        ]

    loading = {}

    def load(m, dst):
        def begin():
            for h in range(2):
                wait_all(across.pop(2 * m + h))
            loading[m] = local_copy(full[m], dst)

        return begin

    def keep(name, src):
        local_open.append(local_copy(src, kept[name]))

    def pair(name, mine, theirs, axis_size, axis):
        here, there = pl.ds(0, axis_size), pl.ds(axis_size, axis_size)
        dst = kept[name]

        def part(where):
            return dst.at[where] if axis == 0 else dst.at[:, where] if axis == 1 else dst.at[:, :, where]

        local_open.append(local_copy(mine, part(here)))
        across_pairs.append(sems.copy(theirs, part(there), pc))

    across_pairs = []
    gain_copies = []

    def pick(flag_first, first, second):
        return jnp.where(flag_first, first, second)

    first_live = flags[0] == 0
    live_count = jnp.where(first_live, live_counts[0], live_counts[1])

    def send_gains():
        in_gain.wait()
        gain_one[...] = jnp.zeros_like(gain_one)
        gain_one[: gain.shape[0], : gain.shape[1]] = gain_own[...]
        gain_all[me_dp] = gain_one[...]
        for device in dp_peers:
            gain_copies.append(sems.copy(gain_one, gain_all.at[me_dp], device))

    def start():
        wait_all(gain_copies)
        row = lax.broadcasted_iota(jnp.int32, (128, width), 0)
        column = lax.broadcasted_iota(jnp.int32, (128, width), 1)
        total = jnp.zeros((16, width), F32)
        share = width // 8
        for i in range(8):
            spread = low(jnp.where((column == row + share * i) & (row < share), 1.0, 0.0))
            total += dot(gain_all[i], spread)
        gain_out[...] = total
        in_lat.wait()
        in_cot.wait()
        z2[:rows] = pick(first_live, lat_v[0], lat_v[1])
        z2[rows:] = pick(first_live, lat_v[1], lat_v[0])
        zb = low(normed(z2[:rows])[0] * gain_out[0:1])
        zb_v[...] = zb
        lst[0] = zb.T
        gy_first = low(pick(first_live, cot_v[0], cot_v[1]))
        gy_last = low(pick(first_live, cot_v[1], cot_v[0]))
        gyt[:, :, :, :rows] = gy_first.T.reshape(2, 2, width // 4, rows)
        gyt[:, :, :, rows:] = gy_last.T.reshape(2, 2, width // 4, rows)
        pair("gyt", gyt.at[:, c], gyt.at[:, 1 - c], two, 2)

    def tokens_part(first, last):
        def run():
            if first == 0:
                in_tok.wait()

            @pl.loop(first, last)
            def _(i):
                at = lanes(i, 128)
                here = pick(first_live, tok_v[0, at], tok_v[1, at])
                xl[at] = here
                value = low(normed(here.astype(F32))[0] * gain_out[1:2])
                xb[at] = value
                xbt[:, at] = value.T

            if last == tokens // 128:
                keep("xl", xl)
                pair("xbt", xbt, xbt, tokens, 1)

        return run

    def cross_queries():
        loading[0].wait()
        cq[...] = low(dot(zb_v[...], square_block(wr[0], 0, 0)))
        keep("cq", cq)

    def keys_values(first, last):
        def run():
            for i in range(first, last):
                at = pl.ds(i * 256, 256)
                here = xb[at]
                kv[0, at] = low(dot(here, square_block(wr[0], 0, 1)))
                kv[1, at] = low(dot(here, square_block(wr[0], 1, 0)))
            if last == tokens // 256:
                keep("kv", kv)

        return run

    def cross_attention(first, last):
        def run():
            @pl.loop(first, last)
            def _(p):
                at = lanes(p, 128)
                q = stack_heads(cq[:, at] * jnp.asarray(0.125, BF16))
                s = dot_nt(q, kv[0, :, at])
                s = jnp.where(lax.broadcasted_iota(jnp.int32, s.shape, 1) < live_count, s, MASKED)
                e = jnp.exp(s - jnp.max(s, axis=-1, keepdims=True))
                prob = low(e * (1.0 / jnp.sum(e, axis=-1, keepdims=True)))
                cp[p] = prob
                co[:, at] = join_heads(dot(prob, kv[1, :, at]))

            if last == width // 128:
                keep("cp", cp)
                keep("co", co)

        return run

    def cross_out():
        cob = low(co[...])
        lst[1] = cob.T
        pair("lst", lst.at[c], lst.at[1 - c], rows, 1)
        mid[...] = z2[:rows] + dot(cob, square_block(wr[0], 1, 1))
        keep("mid", mid)
        cnb = low(normed(mid[...])[0] * gain_out[2:3])
        nb[:rows] = cnb
        cnt[...] = cnb.T
        pair("cnt", cnt, cnt, rows, 1)

    def up(m, w, left, out, slope, first, last, after):
        def run():
            if first == 0:
                loading[m].wait()

            @pl.loop(first, last)
            def _(s):
                at = lanes(s, hidden // 4)
                value, grad = gelu_both(dot(nb[:left], square_block(w, s // 2, s % 2)))
                out[:, at] = low(value)
                slope[:, at] = low(grad)

            if last == 4:
                after()

        return run

    def down(m, act):
        loading[m].wait()
        total = jnp.zeros((act.shape[0], width), F32)
        for s in range(4):
            at = pl.ds(s * (hidden // 4), hidden // 4)
            total += dot_nt(act[:, at], hidden_block(wt, s))
        return total

    def cross_up_done():
        pair("ch", ch, ch, rows, 0)
        keep("gpc", gpc)

    def self_up_done():
        pair("mh", mh, mh, two, 0)
        keep("gps", gps)

    def cross_down():
        ac[:rows] = mid[...] + down(2, ch)
        ac[rows:] = z2[rows:]
        keep("ac", ac)
        sb = low(normed(ac[...])[0] * gain_out[3:4])
        nb[...] = sb
        lt[0] = sb.T
        pair("sbt", lt.at[0], lt.at[0], two, 1)

    def self_project():
        loading[3].wait()
        sb = nb[...]
        for i, (a, b) in enumerate(((0, 0), (0, 1), (1, 0))):
            sqkv[i] = low(dot(sb, square_block(wr[0], a, b)))
        keep("sqkv", sqkv)

    def self_attention(first, last):
        pairs = width // 128

        def run():
            @pl.loop(first, last)
            def _(i):
                at, row_at = lanes(i % pairs, 128), lanes(i // pairs, rows)
                q = stack_heads(sqkv[0, row_at, at] * jnp.asarray(0.125, BF16))
                s = dot_nt(q, sqkv[1, row_at, at])
                e = jnp.exp(s - jnp.max(s, axis=-1, keepdims=True))
                prob = low(e * (1.0 / jnp.sum(e, axis=-1, keepdims=True)))
                sp[i] = prob
                so[row_at, at] = low(join_heads(dot(prob, sqkv[2, row_at, at])))

            if last == 2 * pairs:
                keep("sp", sp)

        return run

    def self_out():
        lt[1] = so[...].T
        pair("l1t", lt.at[c], lt.at[1 - c], two, 1)
        aa[...] = ac[...] + dot(so[...], square_block(wr[0], 1, 1))
        keep("aa", aa)
        mnb = low(normed(aa[...])[0] * gain_out[4:5])
        nb[...] = mnb
        mnt[...] = mnb.T
        pair("mnt", mnt, mnt, two, 1)

    def self_down():
        total = aa[...] + down(5, mh)
        result[0] = pick(first_live, total[:rows], total[rows:])
        result[1] = pick(first_live, total[rows:], total[:rows])

    pairs = width // 128
    work = collections.deque([(-2, send_gains), (-1, start)])
    for n in range(4):
        work.append((-1, tokens_part(n * tokens // 512, (n + 1) * tokens // 512)))
    for slot, part in (
        (4, load(0, wr[0])),
        (4, cross_queries),
        (4, keys_values(0, 1)),
        (4, keys_values(1, 2)),
        (4, keys_values(2, 3)),
        (4, keys_values(3, tokens // 256)),
        (4, cross_attention(0, 2)),
        (4, cross_attention(2, 4)),
        (4, cross_attention(4, pairs)),
        (4, cross_out),
        (6, load(1, wr[1])),
        (6, up(1, wr[1], rows, ch, gpc, 0, 2, cross_up_done)),
        (6, up(1, wr[1], rows, ch, gpc, 2, 4, cross_up_done)),
        (8, load(2, wt)),
        (8, cross_down),
        (10, load(3, wr[0])),
        (10, self_project),
        (10, self_attention(0, pairs)),
        (10, self_attention(pairs, 2 * pairs)),
        (10, self_out),
        (12, load(4, wr[1])),
        (12, up(4, wr[1], two, mh, gps, 0, 2, self_up_done)),
        (12, up(4, wr[1], two, mh, gps, 2, 4, self_up_done)),
        (14, load(5, wt)),
        (14, self_down),
    ):
        work.append((slot, part))
    steps = {
        "1": step_one,
        "f": step_one_forward,
        "2": step_two,
        "g": step_two_forward,
        "3": step_three,
        "4": step_four,
    }
    places = {"1": -2, "f": -1, "2": 0, "g": 0, "3": 1, "4": 2}
    for slot, name, i in slots(halves, places, "231fg4"):
        steps[name](i)
        if work and work[0][0] <= slot:
            work.popleft()[1]()
    while work:
        work.popleft()[1]()
    wait_all(across_pairs)
    for made in local_open:
        made.wait()
    sems.drain()


def half_shape(shard):
    return shard.shape[0], shard.shape[1] // 2


def forward_all(own, gain, latents, inputs, cotangent, counts, flags):
    count = len(own)
    rows, width = latents.shape[1:]
    tokens = inputs.shape[1]
    hidden = own[1].shape[1] * 4
    dims = (rows, tokens, width, hidden)
    two = 2 * rows
    kept = {**kept_shapes(*dims), **paired_shapes(*dims)}
    names = tuple(kept)
    copies = 7 + 2 * count * (6 + 10 + 4 + 2) + len(paired_shapes(*dims))
    block = (2, 2, 2, 4, 2) + half_shape(own[0])
    shapes = [jax.ShapeDtypeStruct(block, BF16) for w in own]
    shapes += [
        jax.ShapeDtypeStruct((16, width), F32),
        jax.ShapeDtypeStruct(latents.shape, F32),
    ]
    shapes += [jax.ShapeDtypeStruct(s, t) for s, t in kept.values()]
    pairs = width // 128
    scratch = [
        ((8, 16, 128), BF16),
        (latents.shape, F32),
        (latents.shape, F32),
        (inputs.shape, BF16),
        ((two, width), F32),
        ((tokens, width), BF16),
        ((width, tokens), BF16),
        ((2, 2, width // 4, two), BF16),
        ((2, width, rows), BF16),
        (block, BF16),
        (block, BF16),
        (block, BF16),
        ((rows, width), BF16),
        ((2, tokens, width), BF16),
        ((pairs, two, tokens), BF16),
        ((rows, width), F32),
        ((rows, width), F32),
        ((rows, hidden), BF16),
        ((rows, hidden), BF16),
        ((two, width), F32),
        ((3, two, width), BF16),
        ((2 * pairs, two, rows), BF16),
        ((two, width), BF16),
        ((two, width), F32),
        ((two, hidden), BF16),
        ((two, hidden), BF16),
        ((tokens, width), BF16),
        ((2, width, two), BF16),
        ((width, rows), BF16),
        ((width, two), BF16),
        (gain.shape, BF16),
        ((16, 128), BF16),
        ((rows, width), BF16),
        ((two, width), BF16),
    ]
    outs = pl.pallas_call(
        functools.partial(forward_kernel, names, dims),
        out_shape=shapes,
        in_specs=[ANY] * (count + 4) + [SMEM, SMEM],
        out_specs=[ANY] * count + [VMEM, VMEM] + [ANY] * len(names),
        scratch_shapes=[pltpu.VMEM(s, t) for s, t in scratch]
        + [
            pltpu.SemaphoreType.DMA((copies,)),
            pltpu.SemaphoreType.DMA((copies,)),
            pltpu.SemaphoreType.DMA((5 + 3 * count + len(names),)),
        ],
        compiler_params=pltpu.CompilerParams(
            collective_id=0, has_side_effects=True, vmem_limit_bytes=60 << 20
        ),
        name="gather_and_forward",
    )(*own, gain, latents, inputs, cotangent, counts, flags)
    full, (norm_gain, result) = outs[:count], outs[count : count + 2]
    return full, norm_gain, result, dict(zip(names, outs[count + 2 :]))


def norm_back(values, gain_row, gradient):
    unit, inverse = normed(values)
    scaled = gradient * gain_row
    grad = inverse * (
        scaled
        - jnp.mean(scaled, axis=-1, keepdims=True)
        - unit * jnp.mean(scaled * unit, axis=-1, keepdims=True)
    )
    return grad, jnp.sum(gradient * unit, axis=0, keepdims=True)


def dot_tn(a, b):
    return lax.dot_general(a, b, (((0,), (0,)), ((), ())), preferred_element_type=F32)


def attention_back(q, k, v, out_grad, prob, delta):
    prob_grad = dot_nt(out_grad, v)
    weight = prob.astype(F32)
    if delta is None:
        delta = jnp.sum(weight * prob_grad, axis=-1, keepdims=True)
    score_grad = low(weight * (prob_grad - delta))
    q_grad = join_heads(dot(score_grad, k)) * 0.125
    k_grad = dot_tn(score_grad, q) * 0.125
    v_grad = dot_tn(prob, out_grad)
    return low(q_grad), low(k_grad), low(v_grad)


def add_blocks(total, where, part, there):
    total[where] = (total[where].astype(F32) + part[there].astype(F32)).astype(BF16)


def backward_kernel(names, dims, *refs):
    rows, tokens, width, hidden = dims
    two, quarter, pairs = 2 * rows, hidden // 4, width // 128
    count = 6
    halves, ring = 2 * count, 3
    order = (5, 4, 3, 2, 1, 0)
    refs = list(refs)

    def take(n):
        out = refs[:n]
        del refs[:n]
        return out

    full = take(count)
    gain, lat, cot, flags = take(4)
    kept = dict(zip(names, take(len(names))))
    outs = take(count)
    gain_out, lat_grad, dx = take(3)
    total = take(count)
    from_y, from_x = take(ring), take(ring)
    from_a, from_b, from_c, from_d, from_z, end_c, end_d = (take(halves) for _ in range(7))
    by_c, by_d, by_z = (take(halves) for _ in range(3))
    wr, wt, grad_ac, du_sib, r_sib, ge_sib, dcu_sib, rs_sib, dkv_sib = take(9)
    gain_acc, gain_sub, gain_dp, send, recv, local, free = take(7)
    place = Place()
    x, y, z, c = place.x, place.y, place.z, place.c
    sems = Sems(place, send, recv)
    local_count = [0]

    def local_copy(src, dst):
        made = pltpu.make_async_copy(src, dst, local.at[local_count[0]])
        local_count[0] += 1
        made.start()
        return made

    me_dp, me_sub = z * 2 + y, x * 2 + c
    sub_peers = [(me_dp, (me_sub + k) % 4) for k in (1, 2, 3)]
    dp_peers = [((me_dp + k) % 8, me_sub) for k in range(1, 8)]
    px, py, pc = place.dev(x=1 - x), place.dev(y=1 - y), place.dev(c=1 - c)
    first_live = flags[0] == 0
    gain_acc[...] = jnp.zeros_like(gain_acc)

    ones, twos, threes = {}, {}, {}
    block_rows, block_columns = total[0].shape[4:]

    def where(i):
        return total[order[i // 2]], i % 2

    def clear():
        for into in (*from_c, *from_d, *from_z):

            @pl.when(z == 0)
            def _():
                into[0] = jnp.zeros(into.shape[1:], BF16)

            @pl.when(z == 3)
            def _():
                into[2] = jnp.zeros(into.shape[1:], BF16)

    def step_one(i):
        a, h = where(i)
        if i >= ring:
            pl.semaphore_wait(free.at[i - ring], 2)
        ones[i] = [
            sems.copy(a.at[h, :, :, 1 - y, piece("CA", block_rows)], from_y[i % ring], py),
            sems.copy(a.at[h, 1 - x, :, :, piece("BD", block_rows)], from_x[i % ring], px),
        ]

    def step_two(i):
        a, h = where(i)
        wait_all(ones.pop(i))
        ca, bd = piece("CA", block_rows), piece("BD", block_rows)
        pa, pb, pc_, pd = (piece(n, block_rows) for n in ("A", "B", "C", "D"))
        fy, fx = from_y[i % ring], from_x[i % ring]

        @pl.loop(0, 8)
        def _(j):
            add_blocks(a, (h, j // 4, j % 4, y, ca), fy, (j // 4, j % 4))
            add_blocks(a, (h, x, j // 2, j % 2, bd), fx, (j // 2, j % 2))

        if i + ring < halves:
            for device in (px, py):
                pl.semaphore_signal(free.at[i], inc=1, device_id=device, device_id_type=MESH_ID)
        collect_c = Collect(sems, lambda o: a.at[h, :, o, y, pc_], from_c[i], by_c[i])
        collect_d = Collect(sems, lambda o: a.at[h, x, o, :, pd], from_d[i], by_d[i])
        got = [
            sems.copy(a.at[h, 1 - x, :, y, pa], from_a[i], px),
            sems.copy(a.at[h, x, :, 1 - y, pb], from_b[i], py),
        ]
        twos[i] = (collect_c, collect_d, got)

    def step_two_forward(i):
        a, h = where(i)
        pc_, pd = piece("C", block_rows), piece("D", block_rows)

        def add_c(o):
            for j in range(2):
                add_blocks(a, (h, j, o, y, pc_), by_c[i], j)

        def add_d(o):
            for j in range(2):
                add_blocks(a, (h, x, o, j, pd), by_d[i], j)

        twos[i][0].part = lambda o: a.at[h, :, o, y, pc_]
        twos[i][1].part = lambda o: a.at[h, x, o, :, pd]
        twos[i][0].forward(add_c)
        twos[i][1].forward(add_d)

    def step_three(i):
        a, h = where(i)
        collect_c, collect_d, got = twos.pop(i)
        collect_c.finish()
        collect_d.finish()
        wait_all(got)
        pa, pb, pc_, pd = (piece(n, block_rows) for n in ("A", "B", "C", "D"))
        fc, fd = from_c[i], from_d[i]

        @pl.loop(0, 4)
        def _(j):
            add_blocks(a, (h, x, j, y, pa), from_a[i], j)
            add_blocks(a, (h, x, j, y, pb), from_b[i], j)

        @pl.loop(0, 2)
        def _(j):
            a[h, j, z, y, pc_] = low(
                a[h, j, z, y, pc_].astype(F32)
                + fc[0, j].astype(F32)
                + fc[1, j].astype(F32)
                + fc[2, j].astype(F32)
            )
            a[h, x, z, j, pd] = low(
                a[h, x, z, j, pd].astype(F32)
                + fd[0, j].astype(F32)
                + fd[1, j].astype(F32)
                + fd[2, j].astype(F32)
            )

        ab = piece("AB", block_rows)
        collect = Collect(sems, lambda o: a.at[h, x, o, y, ab], from_z[i], by_z[i])
        got = [
            sems.copy(a.at[h, 1 - x, z, y, pc_], end_c[i], px),
            sems.copy(a.at[h, x, z, 1 - y, pd], end_d[i], py),
        ]
        threes[i] = (collect, got)

    def step_three_forward(i):
        a, h = where(i)
        ab = piece("AB", block_rows)
        collect = threes[i][0]
        collect.part = lambda o: a.at[h, x, o, y, ab]
        collect.forward(lambda o: add_blocks(a, (h, x, o, y, ab), by_z[i], ...))

    def step_four(i):
        a, h = where(i)
        collect, got = threes.pop(i)
        collect.finish()
        wait_all(got)
        fz, o = from_z[i], outs[order[i // 2]]
        if o.shape[0] == block_rows:
            first, columns = 0, pl.ds(h * block_columns, block_columns)
        else:
            first, columns = h * block_rows, slice(None)

        def put(name, value):
            at = piece(name, block_rows)
            o[pl.ds(first + at.start, at.size), columns] = (
                a[h, x, z, y, at].astype(F32) + value
            )

        put("AB", fz[0].astype(F32) + fz[1].astype(F32) + fz[2].astype(F32))
        put("C", end_c[i][...].astype(F32))
        put("D", end_d[i][...].astype(F32))

    run_step = {
        "1": step_one,
        "2": step_two,
        "g": step_two_forward,
        "3": step_three,
        "f": step_three_forward,
        "4": step_four,
    }
    places = {"1": 0, "2": 1, "g": 2, "3": 3, "f": 4, "4": 5}
    steps = collections.deque(slots(halves, places, "12g3f4"))
    ready = [0]

    def advance(n):
        while n > 0 and steps and (steps[0][1] != "1" or steps[0][2] < ready[0]):
            unused, name, i = steps.popleft()
            run_step[name](i)
            n -= 1

    def done(m):
        ready[0] += 2
        advance(2)

    def put_square(m, at, value):
        for h in range(2):
            part = value[:, h * block_columns : (h + 1) * block_columns]
            total[m][h, at] = low(part).reshape(4, 2, block_rows, block_columns)

    def put_hidden(m, zz, value):
        for yy in range(2):
            for a in range(2):
                for h in range(2):
                    first = (2 * a + h) * block_rows
                    part = value[
                        first : first + block_rows,
                        yy * block_columns : (yy + 1) * block_columns,
                    ]
                    total[m][h, a, zz, yy] = low(part)

    def hidden_grad(m, left, right):
        for zz in range(4):
            put_hidden(m, zz, dot(left, right[:, zz * quarter : (zz + 1) * quarter]))

    def both(own, other):
        return jnp.concatenate([own, other], axis=0)

    def send_off(src, dst):
        return sems.copy(src, dst, pc, later=False)

    def pick(first, second):
        return jnp.where(first_live, first, second)

    def back_through(act, blocks):
        out = None
        for i, (a, b) in enumerate(blocks):
            term = dot_nt(act[a, b], square_block(wr, a, b))
            out = term if out is None else out + term
        return out

    every = ((0, 0), (0, 1), (1, 0), (1, 1))

    def self_part(mh, gps, gyt, mnt, sbt, l1t, du, r, cot_v, aa, ac, sqkv, sp, grad_aa, out_grad):
        loads = {
            name: local_copy(src, dst)
            for name, src, dst in (
                ("gyt", kept["gyt"], gyt),
                ("mh", kept["mh"], mh),
                ("wt", full[5], wt),
                ("cot", cot, cot_v),
                ("gps", kept["gps"], gps),
                ("wr", full[4], wr),
                ("aa", kept["aa"], aa),
                ("mnt", kept["mnt"], mnt),
                ("sqkv", kept["sqkv"], sqkv),
                ("sp", kept["sp"], sp),
                ("ac", kept["ac"], ac),
                ("sbt", kept["sbt"], sbt),
                ("l1t", kept["l1t"], l1t),
            )
        }
        clear()
        greet(place, sub_peers + dp_peers)
        loads["gyt"].wait()
        loads["mh"].wait()
        hidden_grad(5, gyt[...].reshape(width // 2, 2 * two), mh)
        done(5)

        for name in ("wt", "cot", "gps"):
            loads[name].wait()
        for at, value in (
            (pl.ds(0, rows), pick(cot_v[0], cot_v[1])),
            (pl.ds(rows, rows), pick(cot_v[1], cot_v[0])),
        ):
            grad_aa[at] = value
        gy = low(grad_aa[...])
        for s in range(4):
            at = pl.ds(s * quarter, quarter)
            du[s // 2, s % 2] = low(dot(gy, hidden_block(wt, s)) * gps[:, at].astype(F32))
        sent = send_off(du.at[:, 1 - c], du_sib)
        advance(2)
        for name in ("wr", "aa", "mnt"):
            loads[name].wait()
        grad, gain_row = norm_back(aa[...], gain[4:5], back_through(du, every))
        grad_aa[...] += grad
        gain_acc[0, 4:5] = gain_row
        advance(2)
        next_wr = local_copy(full[3], wr)
        next_wt = local_copy(full[2], wt)
        sent.wait_recv()
        for a in range(2):
            put_square(4, a, dot(mnt[...], both(du[a, c], du_sib[a])))
        done(4)

        r[1, 1] = low(grad_aa[...])
        for made in (next_wr, loads["sqkv"], loads["sp"], loads["ac"], loads["sbt"], loads["l1t"]):
            made.wait()
        out_grad[...] = low(dot_nt(r[1, 1], square_block(wr, 1, 1)))

        advance(2)
        for part in range(2):

            @pl.loop(part * pairs, (part + 1) * pairs)
            def _(i):
                at, row_at = lanes(i % pairs, 128), lanes(i // pairs, rows)
                r[0, 0, row_at, at], r[0, 1, row_at, at], r[1, 0, row_at, at] = attention_back(
                    stack_heads(sqkv[0, row_at, at]),
                    sqkv[1, row_at, at],
                    sqkv[2, row_at, at],
                    stack_heads(out_grad[row_at, at]),
                    sp[i],
                    None,
                )

            advance(2)

        sent_r = send_off(r.at[:, 1 - c], r_sib)
        grad, gain_row = norm_back(ac[...], gain[3:4], back_through(r, every[:3]))
        grad_ac[...] = grad_aa[...] + grad
        gain_acc[0, 3:4] = gain_row
        advance(2)
        sent_r.wait_recv()
        put_square(3, 0, dot(sbt[...], both(r[0, c], r_sib[0])))
        put_square(3, 1, dot(l1t[...], both(r[1, c], r_sib[1])))
        done(3)
        sent.wait_send()
        sent_r.wait_send()
        next_wt.wait()

    def cross_part(
        ch, gpc, ge, cnt, du, mid, lst, rs, xbt, kv, cp, cq, co, dco, xl, dxs, lat_v, grad_mid
    ):
        loads = {
            name: local_copy(src, dst)
            for name, src, dst in (
                ("ch", kept["ch"], ch),
                ("gpc", kept["gpc"], gpc),
                ("wr", full[1], wr),
                ("mid", kept["mid"], mid),
                ("cnt", kept["cnt"], cnt),
                ("cq", kept["cq"], cq),
                ("co", kept["co"], co),
                ("kv", kept["kv"], kv),
                ("cp", kept["cp"], cp),
                ("lst", kept["lst"], lst),
                ("xbt", kept["xbt"], xbt),
                ("lat", lat, lat_v),
            )
        }
        for i in range(2):
            lat_grad_dead = grad_ac[rows:]
            lat_grad[i] = lat_grad_dead
        low_grad = low(grad_ac[:rows])
        ge[...] = low_grad.T.reshape(2, 2, width // 4, rows)
        sent = [send_off(ge.at[:, 1 - c], ge_sib)]
        loads["gpc"].wait()
        for s in range(4):
            at = pl.ds(s * quarter, quarter)
            du[s // 2, s % 2] = low(dot(low_grad, hidden_block(wt, s)) * gpc[:, at].astype(F32))
        sent.append(send_off(du.at[:, 1 - c], dcu_sib))
        advance(2)
        loads["ch"].wait()
        sent[0].wait_recv()
        left = jnp.concatenate(
            [ge[:, c].reshape(width // 2, rows), ge_sib[...].reshape(width // 2, rows)], axis=1
        )
        hidden_grad(2, left, ch)
        done(2)

        for name in ("wr", "mid", "cnt"):
            loads[name].wait()
        grad, gain_row = norm_back(mid[...], gain[2:3], back_through(du, every))
        grad_mid[...] = grad_ac[:rows] + grad
        gain_acc[0, 2:3] = gain_row
        advance(2)
        next_wr = local_copy(full[0], wr)
        sent[1].wait_recv()
        for a in range(2):
            put_square(1, a, dot(cnt[...], both(du[a, c], dcu_sib[a])))
        done(1)

        rs[1] = low(grad_mid[...])
        next_wr.wait()
        dco[...] = low(dot_nt(rs[1], square_block(wr, 1, 1)))
        for name in ("cq", "co", "kv", "cp"):
            loads[name].wait()

        advance(2)
        for part in range(3):

            @pl.loop(part * pairs // 3, (part + 1) * pairs // 3)
            def _(p):
                at = lanes(p, 128)
                out_grad = stack_heads(dco[:, at])
                attended = co[:, at]
                delta = jnp.sum(
                    out_grad.astype(F32) * both(attended, attended), axis=-1, keepdims=True
                )
                rs[0, :, at], kv[0, :, at], kv[1, :, at] = attention_back(
                    stack_heads(cq[:, at]), kv[0, :, at], kv[1, :, at], out_grad, cp[p], delta
                )

            advance(2)

        sent.append(send_off(rs.at[1 - c], rs_sib))
        sent.append(send_off(kv.at[c], dkv_sib))
        advance(2)
        for name in ("lst", "xbt", "lat"):
            loads[name].wait()
        sent[2].wait_recv()
        sent[3].wait_recv()
        put_square(0, c, dot(lst[...], both(rs[c], rs_sib[...])))
        put_square(
            0, 1 - c, dot(xbt[:, :tokens], kv[1 - c]) + dot(xbt[:, tokens:], dkv_sib[...])
        )
        done(0)

        grad, gain_row = norm_back(
            pick(lat_v[0], lat_v[1]), gain[0:1], dot_nt(rs[0], square_block(wr, 0, 0))
        )
        gain_acc[0, 0:1] = gain_row
        live_grad = grad_mid[...] + grad
        lat_grad[0] = pick(live_grad, lat_grad[0])
        lat_grad[1] = pick(lat_grad[1], live_grad)
        advance(2)
        out = []
        parts = tokens // 128

        def fetch(i):
            return local_copy(kept["xl"].at[pl.ds(i * 128, 128)], xl.at[i % 2])

        fetched = fetch(0)
        for i in range(parts):
            at = pl.ds(i * 128, 128)
            fetched.wait()
            if i + 1 < parts:
                fetched = fetch(i + 1)
            if i >= 2:
                out[i - 2].wait()
            term = dot_nt(kv[0, at], square_block(wr, 0, 1))
            term += dot_nt(kv[1, at], square_block(wr, 1, 0))
            grad, gain_row = norm_back(xl[i % 2].astype(F32), gain[1:2], term)
            dxs[i % 2] = grad
            gain_acc[0, 1:2] += gain_row
            out.append(local_copy(dxs.at[i % 2], dx.at[at]))
            advance(2)
        for made in out[-2:]:
            made.wait()
        gain_one = [sems.copy(gain_acc.at[0], spot(gain_sub, k), sub_peers[k]) for k in range(3)]
        advance(3)
        wait_all(gain_one)
        gain_acc[1] = gain_acc[0] + gain_sub[0] + gain_sub[1] + gain_sub[2]
        gain_two = [sems.copy(gain_acc.at[1], spot(gain_dp, k), dp_peers[k]) for k in range(7)]
        for made in sent:
            made.wait_send()
        return gain_two

    def vmem(*shape, dtype=BF16):
        return pltpu.VMEM(shape, dtype)

    holder = {}

    pl.run_scoped(
        self_part,
        vmem(2 * two, hidden),
        vmem(two, hidden),
        vmem(2, width // 4, 2 * two),
        vmem(width, 2 * two),
        vmem(width, 2 * two),
        vmem(width, 2 * two),
        vmem(2, 2, two, quarter),
        vmem(2, 2, two, width),
        vmem(2, rows, width, dtype=F32),
        vmem(two, width, dtype=F32),
        vmem(two, width, dtype=F32),
        vmem(3, two, width),
        vmem(2 * pairs, two, rows),
        vmem(two, width, dtype=F32),
        vmem(two, width),
    )

    def run_cross(*bufs):
        holder["gain"] = cross_part(*bufs)

    pl.run_scoped(
        run_cross,
        vmem(two, hidden),
        vmem(rows, hidden),
        vmem(2, 2, width // 4, rows),
        vmem(width, two),
        vmem(2, 2, rows, quarter),
        vmem(rows, width, dtype=F32),
        vmem(width, two),
        vmem(2, rows, width),
        vmem(width, 2 * tokens),
        vmem(2, tokens, width),
        vmem(pairs, two, tokens),
        vmem(rows, width),
        vmem(rows, width, dtype=F32),
        vmem(rows, width),
        vmem(2, 128, width),
        vmem(2, 128, width, dtype=F32),
        vmem(2, rows, width, dtype=F32),
        vmem(rows, width, dtype=F32),
    )
    advance(len(steps))
    wait_all(holder["gain"])
    gain_out[...] = gain_acc[1] + jnp.sum(gain_dp[...], axis=0)
    sems.drain()


def backward_all(shard, full, norm_gain, latents, cotangent, flags, kept):
    count = len(full)
    rows, width = latents.shape[1:]
    tokens, hidden = kept["xl"].shape[0], kept["mh"].shape[1]
    dims = (rows, tokens, width, hidden)
    two = 2 * rows
    copies = 10 + 6 + 2 * count * (2 + 10 + 6)
    ring, halves = 3, 2 * count
    block_rows, block_columns = full[0].shape[5:]

    def room(number, lead, sixths):
        return [pltpu.VMEM(lead + (block_rows * sixths // 6, block_columns), BF16)] * number

    scratch = [pltpu.VMEM((2,) + full[0].shape[2:], BF16)] * count
    scratch += room(ring, (2, 4), 3) + room(ring, (4, 2), 3)
    scratch += room(halves, (4,), 1) + room(halves, (4,), 1)
    scratch += room(halves, (3, 2), 2) + room(halves, (3, 2), 2) + room(halves, (3,), 2)
    scratch += room(halves, (), 2) + room(halves, (), 2)
    scratch += room(halves, (2,), 2) + room(halves, (2,), 2) + room(halves, (), 2)
    scratch += [
        pltpu.VMEM(full[0].shape, BF16),
        pltpu.VMEM(full[2].shape, BF16),
        pltpu.VMEM((two, width), F32),
        pltpu.VMEM((2, two, hidden // 4), BF16),
        pltpu.VMEM((2, two, width), BF16),
        pltpu.VMEM((2, width // 4, rows), BF16),
        pltpu.VMEM((2, rows, hidden // 4), BF16),
        pltpu.VMEM((rows, width), BF16),
        pltpu.VMEM((tokens, width), BF16),
        pltpu.VMEM((2, 8, width), F32),
        pltpu.VMEM((3, 8, width), F32),
        pltpu.VMEM((7, 8, width), F32),
        pltpu.SemaphoreType.DMA((copies,)),
        pltpu.SemaphoreType.DMA((copies,)),
        pltpu.SemaphoreType.DMA((48,)),
        pltpu.SemaphoreType.REGULAR((halves - ring,)),
    ]
    shapes = [jax.ShapeDtypeStruct(d, F32) for d in shard]
    shapes += [
        jax.ShapeDtypeStruct((8, width), F32),
        jax.ShapeDtypeStruct(latents.shape, F32),
        jax.ShapeDtypeStruct((tokens, width), F32),
    ]
    outs = pl.pallas_call(
        functools.partial(backward_kernel, tuple(kept), dims),
        out_shape=shapes,
        in_specs=[ANY] * count + [VMEM, ANY, ANY, SMEM] + [ANY] * len(kept),
        out_specs=[VMEM] * (count + 2) + [ANY],
        scratch_shapes=scratch,
        compiler_params=pltpu.CompilerParams(
            collective_id=1, has_side_effects=True, vmem_limit_bytes=60 << 20
        ),
        name="backward_and_scatter",
    )(*full, norm_gain, latents, cotangent, flags, *kept.values())
    return outs[:count], *outs[count:]


def finish_kernel(gain_share, gain_rows, count, *refs):
    flags, result, lat_grad, tok_grad, gain_total = refs[:5]
    shards_in = refs[5 : 5 + count]
    out_result, out_lat, out_tok, out_gain = refs[5 + count : 9 + count]
    shards_out = refs[9 + count : 9 + 2 * count]
    gain_in, zeros, sems = refs[9 + 2 * count :]
    tokens = tok_grad.shape[0]
    live = jnp.where(flags[0] == 0, 0, 1)
    gain_copy = pltpu.make_async_copy(gain_total, gain_in, sems.at[0])
    copies = [
        (tok_grad, out_tok.at[live]),
        (result, out_result),
        (lat_grad, out_lat),
        *zip(shards_in, shards_out),
    ]
    gain_copy.start()
    started = [
        pltpu.make_async_copy(src, dst, sems.at[i + 1]) for i, (src, dst) in enumerate(copies)
    ]
    for made in started:
        made.start()
    zeros[...] = jnp.zeros_like(zeros)
    size = zeros.shape[0]
    for n in range(tokens // size):
        made = pltpu.make_async_copy(
            zeros, out_tok.at[1 - live, pl.ds(n * size, size)], sems.at[len(copies) + 1 + n]
        )
        made.start()
        started.append(made)
    gain_copy.wait()
    dp = lax.axis_index("dp")
    for i in range(8):

        @pl.when(dp == i)
        def _():
            out_gain[...] = gain_in[:gain_rows, i * gain_share : (i + 1) * gain_share]

    for made in started:
        made.wait()


def finish_all(gain_shape, flags, result, lat_grad, tok_grad, gain_total, shards_in):
    count, pieces = len(shards_in), 4
    tokens, width = tok_grad.shape
    arrays = [result, lat_grad, tok_grad, gain_total, *shards_in]
    shapes = [
        jax.ShapeDtypeStruct(result.shape, F32),
        jax.ShapeDtypeStruct(lat_grad.shape, F32),
        jax.ShapeDtypeStruct((2, tokens, width), F32),
        jax.ShapeDtypeStruct(gain_shape, F32),
    ]
    shapes += [jax.ShapeDtypeStruct(a.shape, F32) for a in shards_in]
    return pl.pallas_call(
        functools.partial(finish_kernel, gain_shape[1], gain_shape[0], count),
        out_shape=shapes,
        in_specs=[SMEM] + [ANY] * len(arrays),
        out_specs=[ANY] * 3 + [VMEM] + [ANY] * count,
        scratch_shapes=[
            pltpu.VMEM(gain_total.shape, F32),
            pltpu.VMEM((tokens // pieces, width), F32),
            pltpu.SemaphoreType.DMA((4 + count + pieces,)),
        ],
        compiler_params=pltpu.CompilerParams(vmem_limit_bytes=8 << 20),
        name="write_outputs",
    )(flags, *arrays)


def layer_norm(values, gain_row):
    centred = values - jnp.mean(values, axis=-1, keepdims=True)
    inverse = lax.rsqrt(jnp.mean(centred * centred, axis=-1, keepdims=True) + EPSILON)
    return centred * inverse * gain_row


def norm_backward(values, gain_row, gradient):
    unused, pull_back = jax.vjp(layer_norm, values, gain_row)
    return pull_back(gradient)


def gelu_tanh(values):
    return jax.nn.gelu(values, approximate=True)


def mm(left_side, weight):
    return jnp.dot(left_side, weight, preferred_element_type=F32)


def mm_nt(left_side, weight):
    return lax.dot_general(left_side, weight, (((1,), (1,)), ((), ())), preferred_element_type=F32)


def mm_tn(left_side, gradient):
    return lax.dot_general(
        left_side, gradient, (((0,), (0,)), ((), ())), preferred_element_type=F32
    )


def low(values):
    return values.astype(BF16)


def heads_of(values):
    return values.reshape(values.shape[:-1] + (HEADS, values.shape[-1] // HEADS))


def mlp_forward(residual, gain_row, up, down_t):
    normed = low(layer_norm(residual, gain_row))
    pre_act = mm(normed, up)
    hidden = low(gelu_tanh(pre_act))
    return normed, pre_act, hidden, mm_nt(hidden, down_t)


def mlp_backward(residual, gain_row, normed, pre_act, hidden, up, down_t, grad_out):
    grad_low = low(grad_out)
    grad_down_t = mm_tn(grad_low, hidden)
    grad_hidden = mm(grad_low, down_t)
    unused, gelu_back = jax.vjp(gelu_tanh, pre_act)
    grad_pre = low(gelu_back(grad_hidden)[0])
    grad_up = mm_tn(normed, grad_pre)
    grad_resid, grad_gain = norm_backward(residual, gain_row, mm_nt(grad_pre, up))
    return grad_resid, grad_gain, grad_up, grad_down_t


def live_layer(live_lat, dead_lat, tokens, count, live_cot, dead_cot, weights, norm_gain):
    c_attn, c_up, c_down_t, s_attn, s_up, s_down_t = weights
    rows, width = live_lat.shape
    scale = (width // HEADS) ** (-0.5)
    lat_low = low(layer_norm(live_lat, norm_gain[0]))
    queries = low(mm(lat_low, c_attn[:, :width]))
    token_values = tokens.astype(F32)
    tok_low = low(layer_norm(token_values, norm_gain[1]))
    kv_weight = c_attn[:, width : 3 * width]
    key_value = low(mm(tok_low, kv_weight))
    keys, values = heads_of(key_value[:, :width]), heads_of(key_value[:, width:])
    scores = (
        jnp.einsum("qhd,khd->hqk", heads_of(queries), keys, preferred_element_type=F32) * scale
    )
    valid = (jnp.arange(tokens.shape[0]) < count)[None, None, :]
    probs = jax.nn.softmax(jnp.where(valid, scores, MASKED), axis=-1)
    probs_low = low(probs)
    attended = jnp.einsum("hqk,khd->qhd", probs_low, values, preferred_element_type=F32)
    attended = attended.reshape(rows, width)
    cross_low = low(attended)
    middle = live_lat + mm(cross_low, c_attn[:, 3 * width :])
    c_norm, c_pre, c_hidden, c_mlp = mlp_forward(middle, norm_gain[2], c_up, c_down_t)
    after_cross = jnp.concatenate([middle + c_mlp, dead_lat], axis=0)

    self_low = low(layer_norm(after_cross, norm_gain[3]))
    qkv = low(mm(self_low, s_attn[:, : 3 * width])).reshape(2, rows, 3 * width)
    s_q = heads_of(qkv[..., :width])
    s_k = heads_of(qkv[..., width : 2 * width])
    s_v = heads_of(qkv[..., 2 * width :])
    s_scores = jnp.einsum("iqhd,ikhd->ihqk", s_q, s_k, preferred_element_type=F32) * scale
    s_probs = jax.nn.softmax(s_scores, axis=-1)
    s_probs_low = low(s_probs)
    s_out = jnp.einsum("ihqk,ikhd->iqhd", s_probs_low, s_v, preferred_element_type=F32)
    s_out_low = low(s_out.reshape(2 * rows, width))
    after_attn = after_cross + mm(s_out_low, s_attn[:, 3 * width :])
    m_norm, m_pre, m_hidden, m_mlp = mlp_forward(after_attn, norm_gain[4], s_up, s_down_t)
    result = after_attn + m_mlp

    cotangent = jnp.concatenate([live_cot, dead_cot], axis=0)
    grad_in, gain_four, d_s_up, d_s_down_t = mlp_backward(
        after_attn, norm_gain[4], m_norm, m_pre, m_hidden, s_up, s_down_t, cotangent
    )
    grad_attn = cotangent + grad_in
    grad_y = low(grad_attn)
    d_s_o = mm_tn(s_out_low, grad_y)
    grad_out = heads_of(low(mm_nt(grad_y, s_attn[:, 3 * width :])).reshape(2, rows, width))
    grad_probs = jnp.einsum("iqhd,ikhd->ihqk", grad_out, s_v, preferred_element_type=F32)
    delta = jnp.sum(grad_probs * s_probs, axis=-1, keepdims=True)
    grad_scores = low(s_probs * (grad_probs - delta))
    g_q = jnp.einsum("ihqk,ikhd->iqhd", grad_scores, s_k, preferred_element_type=F32) * scale
    g_k = jnp.einsum("ihqk,iqhd->ikhd", grad_scores, s_q, preferred_element_type=F32) * scale
    g_v = jnp.einsum("ihqk,iqhd->ikhd", s_probs_low, grad_out, preferred_element_type=F32)
    grad_qkv = low(
        jnp.concatenate([g.reshape(2 * rows, width) for g in (g_q, g_k, g_v)], axis=-1)
    )
    d_s_qkv = mm_tn(self_low, grad_qkv)
    grad_in, gain_three = norm_backward(
        after_cross, norm_gain[3], mm_nt(grad_qkv, s_attn[:, : 3 * width])
    )
    grad_cross = grad_attn + grad_in
    live_grad, dead_grad = grad_cross[:rows], grad_cross[rows:]
    grad_in, gain_two, d_c_up, d_c_down_t = mlp_backward(
        middle, norm_gain[2], c_norm, c_pre, c_hidden, c_up, c_down_t, live_grad
    )
    grad_middle = live_grad + grad_in
    grad_cross_y = low(grad_middle)
    d_c_o = mm_tn(cross_low, grad_cross_y)
    grad_cross_out = low(mm_nt(grad_cross_y, c_attn[:, 3 * width :]))
    out_heads = heads_of(grad_cross_out)
    grad_weights = jnp.einsum("qhd,khd->hqk", out_heads, values, preferred_element_type=F32)
    row_delta = jnp.transpose(jnp.sum(heads_of(grad_cross_out.astype(F32) * attended), axis=-1))
    grad_scores = low(probs * (grad_weights - row_delta[..., None]))
    grad_query = low(
        (
            jnp.einsum("hqk,khd->qhd", grad_scores, keys, preferred_element_type=F32) * scale
        ).reshape(rows, width)
    )
    grad_keys = (
        jnp.einsum("hqk,qhd->khd", grad_scores, heads_of(queries), preferred_element_type=F32)
        * scale
    )
    grad_values = jnp.einsum("hqk,qhd->khd", probs_low, out_heads, preferred_element_type=F32)
    grad_kv = low(
        jnp.concatenate(
            [grad_keys.reshape(-1, width), grad_values.reshape(-1, width)], axis=-1
        )
    )
    d_c_kv = mm_tn(tok_low, grad_kv)
    grad_tokens, gain_one = norm_backward(token_values, norm_gain[1], mm_nt(grad_kv, kv_weight))
    d_c_q = mm_tn(lat_low, grad_query)
    grad_in, gain_zero = norm_backward(
        live_lat, norm_gain[0], mm_nt(grad_query, c_attn[:, :width])
    )
    live_lat_grad = grad_middle + grad_in
    d_c_attn = low(jnp.concatenate([d_c_q, d_c_kv, d_c_o], axis=1))
    d_s_attn = low(jnp.concatenate([d_s_qkv, d_s_o], axis=1))
    gain_grad = jnp.stack([gain_zero, gain_one, gain_two, gain_three, gain_four])
    grads = (d_c_attn, low(d_c_up), low(d_c_down_t), d_s_attn, low(d_s_up), low(d_s_down_t))
    return result, live_lat_grad, dead_grad, grad_tokens, grads, gain_grad


def column_blocks(blocks):
    sub, dp, rows, columns = blocks.shape
    return blocks.transpose(1, 2, 0, 3).reshape(dp * rows, sub * columns)


def row_blocks(blocks):
    sub, dp, rows, columns = blocks.shape
    return blocks.transpose(0, 2, 1, 3).reshape(sub * rows, dp * columns)


def shards(*arrays, dp_size, sub_size):
    latents, inputs, counts, flags = arrays[:4]
    cross_attn, cross_up, cross_down, self_attn, self_up, self_down, gains, cotangent = arrays[4:]
    width = latents.shape[-1]
    own = (
        cross_attn,
        cross_up,
        jnp.transpose(cross_down),
        self_attn,
        self_up,
        jnp.transpose(self_down),
    )
    live = jnp.where(flags[0] == 0, 0, 1)
    here = (jnp.arange(inputs.shape[0]) == live)[:, None, None]
    if dp_size == 8 and sub_size == 4:
        full, norm_gain, result, kept = forward_all(
            own, gains, latents, inputs, cotangent, counts, flags
        )
        owned, gain_total, grad_latents, grad_tokens = backward_all(
            [w.shape for w in own], full, norm_gain, latents, cotangent, flags, kept
        )
        result, grad_latents, grad_inputs, gain_owned, *owned = finish_all(
            gains.shape, flags, result, grad_latents, grad_tokens, gain_total, owned
        )
        owned = [jnp.transpose(g) if i in (2, 5) else g for i, g in enumerate(owned)]
        return (result, grad_latents, grad_inputs, *owned, gain_owned)

    blocks = [lax.all_gather(lax.all_gather(w, "dp", axis=0), "sub", axis=0) for w in own]
    norm_gain = lax.all_gather(gains, "dp", axis=1, tiled=True)
    transposed = (False, False, True, False, False, True)
    weights = [
        row_blocks(b) if flip else column_blocks(b) for b, flip in zip(blocks, transposed)
    ]

    def item(array, index):
        return lax.dynamic_index_in_dim(array, index, 0, keepdims=False)

    result, live_grad, dead_grad, grad_tokens, grads, gain_grad = live_layer(
        item(latents, live),
        item(latents, 1 - live),
        item(inputs, live),
        item(counts, live),
        item(cotangent, live),
        item(cotangent, 1 - live),
        weights,
        norm_gain.astype(F32),
    )

    def both(live_part, dead_part):
        first = jnp.where(live == 0, live_part, dead_part)
        second = jnp.where(live == 0, dead_part, live_part)
        return jnp.stack([first, second])

    rows = latents.shape[1]
    result = both(result[:rows], result[rows:])
    grad_latents = both(live_grad, dead_grad)
    grad_inputs = jnp.where(here, grad_tokens[None], 0.0)

    def blocks_of(grad, shape, flip):
        r, c = shape
        if flip:
            return grad.reshape(sub_size, r, dp_size, c).transpose(0, 2, 1, 3)
        return grad.reshape(dp_size, r, sub_size, c).transpose(2, 0, 1, 3)

    grads = [blocks_of(g, w.shape, flip) for g, w, flip in zip(grads, own, transposed)]
    owned = [lax.psum_scatter(g, "sub", scatter_dimension=0) for g in grads]
    owned = [lax.psum_scatter(g.astype(F32), "dp", scatter_dimension=0) for g in owned]
    gain_owned = lax.psum(gain_grad, "sub")
    gain_owned = lax.psum_scatter(gain_owned, "dp", scatter_dimension=1, tiled=True)
    owned = [jnp.transpose(g) if flip else g for g, flip in zip(owned, transposed)]
    return (result, grad_latents, grad_inputs, *owned, gain_owned)


def solution(mesh):
    item = P(("dp", "sub"), None, None)
    weight = P("dp", "sub")
    gain = P(None, "dp")
    placed = (item, item, P(("dp", "sub")), P()) + (weight,) * 6 + (gain, item)
    return jax.shard_map(
        functools.partial(shards, dp_size=mesh.shape["dp"], sub_size=mesh.shape["sub"]),
        mesh=mesh,
        in_specs=placed,
        out_specs=(item, item, item) + (weight,) * 6 + (gain,),
        check_vma=False,
    )
```

```python
import collections
import functools

import jax
import jax.numpy as jnp
from jax import lax
from jax.experimental import pallas as pl
from jax.experimental.pallas import tpu as pltpu
from jax.sharding import PartitionSpec as P

HEADS = 12
EPSILON = 1e-05
MASKED = -1e30
MESH_ID = pl.DeviceIdType.MESH
F32 = jnp.float32
BF16 = jnp.bfloat16
ANY = pl.BlockSpec(memory_space=pl.ANY)
VMEM = pl.BlockSpec(memory_space=pltpu.VMEM)
SMEM = pl.BlockSpec(memory_space=pltpu.SMEM)


PIECES = {
    "C": (0, 2),
    "A": (2, 1),
    "B": (3, 1),
    "D": (4, 2),
    "CA": (0, 3),
    "AB": (2, 2),
    "BD": (3, 3),
}


def piece(name, rows):
    first, size = PIECES[name]
    return pl.ds(first * (rows // 6), size * (rows // 6))


class Place:
    def __init__(self):
        dp, sub = lax.axis_index("dp"), lax.axis_index("sub")
        self.z, self.y, self.x, self.c = dp // 2, dp % 2, sub // 2, sub % 2

    def dev(self, z=None, y=None, x=None, c=None):
        z = self.z if z is None else z
        y = self.y if y is None else y
        x = self.x if x is None else x
        c = self.c if c is None else c
        return (z * 2 + y, x * 2 + c)

    def zk(self, k):
        return (self.z + k) % 4


def now(ref):
    return ref() if callable(ref) else ref


def spot(ref, index):
    return lambda: ref.at[index]


def only_if(condition, action):
    if condition is None:
        action()
    else:
        pl.when(condition())(action)


class Flight:
    def __init__(self, sems, ref, send_index, recv_index):
        self.sems, self.ref, self.send_index, self.recv_index = sems, ref, send_index, recv_index

    def made(self):
        place = self.sems.place
        return pltpu.make_async_remote_copy(
            src_ref=now(self.ref),
            dst_ref=now(self.ref),
            send_sem=self.sems.send.at[self.send_index],
            recv_sem=self.sems.recv.at[self.recv_index],
            device_id=place.dev(c=1 - place.c),
            device_id_type=MESH_ID,
        )

    def wait_send(self):
        self.made().wait_send()

    def wait_recv(self):
        self.made().wait_recv()


class Sems:
    def __init__(self, place, send, recv):
        self.place, self.send, self.recv, self.count, self.sent = place, send, recv, 0, []

    def reserve(self, n):
        self.count += n
        return self.count - n

    def start(self, src, dst, device, send_index, recv_index, condition=None, later=True):
        def action():
            pltpu.make_async_remote_copy(
                src_ref=now(src),
                dst_ref=now(dst),
                send_sem=self.send.at[send_index],
                recv_sem=self.recv.at[recv_index],
                device_id=device,
                device_id_type=MESH_ID,
            ).start()

        only_if(condition, action)
        flight = Flight(self, dst, send_index, recv_index)
        if later:
            self.sent.append((condition, flight))
        return flight

    def copy(self, src, dst, device, later=True):
        index = self.reserve(1)
        return self.start(src, dst, device, index, index, later=later)

    def drain(self):
        for condition, flight in self.sent:
            only_if(condition, flight.wait_send)


def greet(place, devices):
    barrier = pltpu.get_barrier_semaphore()
    for device in devices:
        pl.semaphore_signal(barrier, inc=1, device_id=device, device_id_type=MESH_ID)
    pl.semaphore_wait(barrier, len(devices))


def wait_all(copies):
    for made in copies:
        made.wait_recv()


class Spread:
    def __init__(self, sems, src, where):
        self.sems, self.where, place = sems, where, sems.place
        self.base = sems.reserve(4)
        z = place.z
        for k, condition in ((1, lambda: z != 3), (2, None), (3, lambda: z != 0)):
            at = self.base + k - 1
            sems.start(src, where(z), place.dev(z=place.zk(k)), at, at, condition)

    def arrived(self, k):
        origin = self.sems.place.zk(4 - k)
        Flight(self.sems, self.where(origin), self.base + 3, self.base + k - 1).wait_recv()

    def forward(self):
        self.arrived(2)
        place = self.sems.place
        block = self.where(place.zk(2))
        for z, target, k in ((2, 3, 3), (1, 0, 1)):
            self.sems.start(
                block,
                block,
                place.dev(z=target),
                self.base + 3,
                self.base + k - 1,
                functools.partial(lambda z: place.z == z, z),
            )

    def finish(self):
        self.arrived(1)
        self.arrived(3)


class Collect:
    def __init__(self, sems, part, into, through):
        self.sems, self.part, self.into, self.through = sems, part, into, through
        place = sems.place
        self.base = sems.reserve(4)
        z = place.z
        for k, condition in (
            (1, lambda: z != 3),
            (2, lambda: (z == 0) | (z == 3)),
            (3, lambda: z != 0),
        ):
            self.send(k, condition)
        for k, end, middle in ((1, 3, 2), (3, 0, 1)):
            at = self.base + 3
            sems.start(part(place.zk(k)), through, place.dev(z=middle), at, at, functools.partial(lambda end: z == end, end))

    def send(self, k, condition):
        place, at = self.sems.place, self.base + k - 1
        self.sems.start(
            self.part(place.zk(k)),
            spot(self.into, k - 1),
            place.dev(z=place.zk(k)),
            at,
            at,
            condition,
        )

    def forward(self, add):
        place = self.sems.place

        def middle():
            return (place.z == 1) | (place.z == 2)

        @pl.when(middle())
        def _():
            Flight(self.sems, self.through, self.base + 3, self.base + 3).wait_recv()
            add(place.zk(2))

        self.send(2, middle)

    def finish(self):
        z = self.sems.place.z
        for k, condition in ((1, lambda: z != 0), (2, None), (3, lambda: z != 3)):
            flight = Flight(self.sems, spot(self.into, k - 1), self.base + 3, self.base + k - 1)
            only_if(condition, flight.wait_recv)


def slots(count, places, order):
    steps = []
    for slot in range(min(places.values()), count + max(places.values())):
        for name in order:
            i = slot - places[name]
            if 0 <= i < count:
                steps.append((slot, name, i))
    return steps


def dot(a, b):
    return jnp.dot(a, b, preferred_element_type=F32)


def dot_nt(a, b):
    return lax.dot_general(a, b, (((1,), (1,)), ((), ())), preferred_element_type=F32)


def low(values):
    return values.astype(BF16)


def normed(values):
    centred = values - jnp.mean(values, axis=-1, keepdims=True)
    inverse = lax.rsqrt(jnp.mean(centred * centred, axis=-1, keepdims=True) + EPSILON)
    return centred * inverse, inverse


def gelu_both(u):
    k, a = 0.7978845608028654, 0.044715
    square = u * u
    t = jnp.tanh(k * u * (1.0 + a * square))
    half = 0.5 * (1.0 + t)
    slope = half + (0.5 * k) * u * (1.0 - t * t) * (1.0 + (3.0 * a) * square)
    return u * half, slope


def square_block(ref, x, c):
    halves = []
    for h in range(2):
        block = ref[h, x, c]
        halves.append(block.reshape(-1, block.shape[3]))
    return jnp.concatenate(halves, axis=1)


def hidden_block(ref, z):
    parts = []
    for y in range(2):
        rows = [ref[h, x, c, z, y] for x in range(2) for c in range(2) for h in range(2)]
        parts.append(jnp.concatenate(rows, axis=0))
    return jnp.concatenate(parts, axis=1)


def left_half(shape):
    return lax.broadcasted_iota(jnp.int32, shape, 1) < 64


def stack_heads(values):
    left = left_half(values.shape)
    zero = jnp.zeros_like(values)
    return jnp.concatenate([jnp.where(left, values, zero), jnp.where(left, zero, values)], axis=0)


def join_heads(values):
    rows = values.shape[0] // 2
    top, bottom = values[:rows], values[rows:]
    return jnp.where(left_half(top.shape), top, bottom)


def lanes(index, size):
    return pl.ds(pl.multiple_of(index * size, size), size)


def kept_shapes(rows, tokens, width, hidden):
    two = 2 * rows
    return {
        "cq": ((rows, width), BF16),
        "kv": ((2, tokens, width), BF16),
        "cp": ((width // 128, two, tokens), BF16),
        "co": ((rows, width), F32),
        "mid": ((rows, width), F32),
        "gpc": ((rows, hidden), BF16),
        "ac": ((two, width), F32),
        "sqkv": ((3, two, width), BF16),
        "sp": ((2 * (width // 128), two, rows), BF16),
        "aa": ((two, width), F32),
        "gps": ((two, hidden), BF16),
        "xl": ((tokens, width), BF16),
    }


def paired_shapes(rows, tokens, width, hidden):
    two = 2 * rows
    return {
        "gyt": ((2, width // 4, 2 * two), BF16),
        "mh": ((2 * two, hidden), BF16),
        "mnt": ((width, 2 * two), BF16),
        "sbt": ((width, 2 * two), BF16),
        "l1t": ((width, 2 * two), BF16),
        "ch": ((two, hidden), BF16),
        "cnt": ((width, two), BF16),
        "lst": ((width, two), BF16),
        "xbt": ((width, 2 * tokens), BF16),
    }


def forward_kernel(names, dims, *refs):
    rows, tokens, width, hidden = dims
    two = 2 * rows
    count = 6
    refs = list(refs)

    def take(n):
        out = refs[:n]
        del refs[:n]
        return out

    own = take(count)
    gain, lat, tok, cot, live_counts, flags = take(6)
    full = take(count)
    gain_out, result = take(2)
    kept = dict(zip(names, take(len(names))))
    gain_all, lat_v, cot_v, tok_v, z2, xb, xbt, gyt, lst, wr0, wr1, wt = take(12)
    cq, kv, cp, co, mid, ch, gpc, ac, sqkv, sp, so, aa, mh, gps, xl, lt, cnt, mnt = take(18)
    gain_own, gain_one, zb_v, nb = take(4)
    send, recv, local = take(3)
    wr = (wr0, wr1)
    place = Place()
    x, y, z, c = place.x, place.y, place.z, place.c
    sems = Sems(place, send, recv)
    local_count = [0]
    local_open = []

    def local_copy(src, dst):
        made = pltpu.make_async_copy(src, dst, local.at[local_count[0]])
        local_count[0] += 1
        made.start()
        return made

    in_gain = local_copy(gain, gain_own)
    in_lat, in_tok, in_cot = local_copy(lat, lat_v), local_copy(tok, tok_v), local_copy(cot, cot_v)
    px, py, pc = place.dev(x=1 - x), place.dev(y=1 - y), place.dev(c=1 - c)
    me_dp = z * 2 + y
    dp_peers = [((me_dp + k) % 8, x * 2 + c) for k in range(1, 8)]
    greet(place, dp_peers + [px, pc])

    halves = 2 * count
    blocks = [full[i // 2].at[i % 2] for i in range(halves)]
    ones, twos, threes, across, placed = {}, {}, {}, {i: [] for i in range(halves)}, {}
    block_rows = full[0].shape[5]

    def shard(i):
        w, h = own[i // 2], i % 2
        if w.shape[0] == block_rows:
            return w, slice(None), pl.ds(h * (w.shape[1] // 2), w.shape[1] // 2), 0
        return w, slice(None), pl.ds(0, w.shape[1]), h * block_rows

    def own_piece(i, name):
        w, unused, columns, first = shard(i)
        at = piece(name, block_rows)
        return w.at[pl.ds(first + at.start, at.size), columns]

    def step_one(i):
        g = blocks[i]
        w, unused, columns, first = shard(i)
        placed[i] = local_copy(w.at[pl.ds(first, block_rows), columns], g.at[x, c, z, y])
        ab, pc_, pd = (piece(n, block_rows) for n in ("AB", "C", "D"))
        spread = Spread(sems, own_piece(i, "AB"), lambda o: g.at[x, c, o, y, ab])
        ones[i] = (
            spread,
            [
                sems.copy(own_piece(i, "C"), g.at[x, c, z, y, pc_], px),
                sems.copy(own_piece(i, "D"), g.at[x, c, z, y, pd], py),
            ],
        )

    def step_one_forward(i):
        ones[i][0].forward()

    def step_two(i):
        g = blocks[i]
        spread, got = ones.pop(i)
        placed.pop(i).wait()
        wait_all(got)
        pa, pb, pc_, pd = (piece(n, block_rows) for n in ("A", "B", "C", "D"))
        spread_c = Spread(sems, g.at[:, c, z, y, pc_], lambda o: g.at[:, c, o, y, pc_])
        spread_d = Spread(sems, g.at[x, c, z, :, pd], lambda o: g.at[x, c, o, :, pd])
        spread.finish()
        got = [
            sems.copy(g.at[x, c, :, y, pa], g.at[x, c, :, y, pa], px),
            sems.copy(g.at[x, c, :, y, pb], g.at[x, c, :, y, pb], py),
        ]
        twos[i] = ((spread_c, spread_d), got)

    def step_two_forward(i):
        for spread in twos[i][0]:
            spread.forward()

    def step_three(i):
        g = blocks[i]
        spreads, got = twos.pop(i)
        for spread in spreads:
            spread.finish()
        wait_all(got)
        ca, bd = piece("CA", block_rows), piece("BD", block_rows)
        threes[i] = [
            sems.copy(g.at[:, c, :, y, ca], g.at[:, c, :, y, ca], py),
            sems.copy(g.at[x, c, :, :, bd], g.at[x, c, :, :, bd], px),
        ]
        across[i] += [
            sems.copy(g.at[:, c, :, y, ca], g.at[:, c, :, y, ca], pc),
            sems.copy(g.at[x, c, :, :, bd], g.at[x, c, :, :, bd], pc),
        ]

    def step_four(i):
        wait_all(threes.pop(i))
        g = blocks[i]
        ca, bd = piece("CA", block_rows), piece("BD", block_rows)
        across[i] += [
            sems.copy(g.at[:, c, :, 1 - y, ca], g.at[:, c, :, 1 - y, ca], pc),
            sems.copy(g.at[1 - x, c, :, :, bd], g.at[1 - x, c, :, :, bd], pc),
        ]

    loading = {}

    def load(m, dst):
        def begin():
            for h in range(2):
                wait_all(across.pop(2 * m + h))
            loading[m] = local_copy(full[m], dst)

        return begin

    def keep(name, src):
        local_open.append(local_copy(src, kept[name]))

    def pair(name, mine, theirs, axis_size, axis):
        here, there = pl.ds(0, axis_size), pl.ds(axis_size, axis_size)
        dst = kept[name]

        def part(where):
            return dst.at[where] if axis == 0 else dst.at[:, where] if axis == 1 else dst.at[:, :, where]

        local_open.append(local_copy(mine, part(here)))
        across_pairs.append(sems.copy(theirs, part(there), pc))

    across_pairs = []
    gain_copies = []

    def pick(flag_first, first, second):
        return jnp.where(flag_first, first, second)

    first_live = flags[0] == 0
    live_count = jnp.where(first_live, live_counts[0], live_counts[1])

    def send_gains():
        in_gain.wait()
        gain_one[...] = jnp.zeros_like(gain_one)
        gain_one[: gain.shape[0], : gain.shape[1]] = gain_own[...]
        gain_all[me_dp] = gain_one[...]
        for device in dp_peers:
            gain_copies.append(sems.copy(gain_one, gain_all.at[me_dp], device))

    def start():
        wait_all(gain_copies)
        row = lax.broadcasted_iota(jnp.int32, (128, width), 0)
        column = lax.broadcasted_iota(jnp.int32, (128, width), 1)
        total = jnp.zeros((16, width), F32)
        share = width // 8
        for i in range(8):
            spread = low(jnp.where((column == row + share * i) & (row < share), 1.0, 0.0))
            total += dot(gain_all[i], spread)
        gain_out[...] = total
        in_lat.wait()
        in_cot.wait()
        z2[:rows] = pick(first_live, lat_v[0], lat_v[1])
        z2[rows:] = pick(first_live, lat_v[1], lat_v[0])
        zb = low(normed(z2[:rows])[0] * gain_out[0:1])
        zb_v[...] = zb
        lst[0] = zb.T
        gy_first = low(pick(first_live, cot_v[0], cot_v[1]))
        gy_last = low(pick(first_live, cot_v[1], cot_v[0]))
        gyt[:, :, :, :rows] = gy_first.T.reshape(2, 2, width // 4, rows)
        gyt[:, :, :, rows:] = gy_last.T.reshape(2, 2, width // 4, rows)
        pair("gyt", gyt.at[:, c], gyt.at[:, 1 - c], two, 2)

    def tokens_part(first, last):
        def run():
            if first == 0:
                in_tok.wait()

            @pl.loop(first, last)
            def _(i):
                at = lanes(i, 128)
                here = pick(first_live, tok_v[0, at], tok_v[1, at])
                xl[at] = here
                value = low(normed(here.astype(F32))[0] * gain_out[1:2])
                xb[at] = value
                xbt[:, at] = value.T

            if last == tokens // 128:
                keep("xl", xl)
                pair("xbt", xbt, xbt, tokens, 1)

        return run

    def cross_queries():
        loading[0].wait()
        cq[...] = low(dot(zb_v[...], square_block(wr[0], 0, 0)))
        keep("cq", cq)

    def keys_values(first, last):
        def run():
            for i in range(first, last):
                at = pl.ds(i * 256, 256)
                here = xb[at]
                kv[0, at] = low(dot(here, square_block(wr[0], 0, 1)))
                kv[1, at] = low(dot(here, square_block(wr[0], 1, 0)))
            if last == tokens // 256:
                keep("kv", kv)

        return run

    def cross_attention(first, last):
        def run():
            @pl.loop(first, last)
            def _(p):
                at = lanes(p, 128)
                q = stack_heads(cq[:, at] * jnp.asarray(0.125, BF16))
                s = dot_nt(q, kv[0, :, at])
                s = jnp.where(lax.broadcasted_iota(jnp.int32, s.shape, 1) < live_count, s, MASKED)
                e = jnp.exp(s - jnp.max(s, axis=-1, keepdims=True))
                prob = low(e * (1.0 / jnp.sum(e, axis=-1, keepdims=True)))
                cp[p] = prob
                co[:, at] = join_heads(dot(prob, kv[1, :, at]))

            if last == width // 128:
                keep("cp", cp)
                keep("co", co)

        return run

    def cross_out():
        cob = low(co[...])
        lst[1] = cob.T
        pair("lst", lst.at[c], lst.at[1 - c], rows, 1)
        mid[...] = z2[:rows] + dot(cob, square_block(wr[0], 1, 1))
        keep("mid", mid)
        cnb = low(normed(mid[...])[0] * gain_out[2:3])
        nb[:rows] = cnb
        cnt[...] = cnb.T
        pair("cnt", cnt, cnt, rows, 1)

    def up(m, w, left, out, slope, first, last, after):
        def run():
            if first == 0:
                loading[m].wait()

            @pl.loop(first, last)
            def _(s):
                at = lanes(s, hidden // 4)
                value, grad = gelu_both(dot(nb[:left], square_block(w, s // 2, s % 2)))
                out[:, at] = low(value)
                slope[:, at] = low(grad)

            if last == 4:
                after()

        return run

    def down(m, act):
        loading[m].wait()
        total = jnp.zeros((act.shape[0], width), F32)
        for s in range(4):
            at = pl.ds(s * (hidden // 4), hidden // 4)
            total += dot_nt(act[:, at], hidden_block(wt, s))
        return total

    def cross_up_done():
        pair("ch", ch, ch, rows, 0)
        keep("gpc", gpc)

    def self_up_done():
        pair("mh", mh, mh, two, 0)
        keep("gps", gps)

    def cross_down():
        ac[:rows] = mid[...] + down(2, ch)
        ac[rows:] = z2[rows:]
        keep("ac", ac)
        sb = low(normed(ac[...])[0] * gain_out[3:4])
        nb[...] = sb
        lt[0] = sb.T
        pair("sbt", lt.at[0], lt.at[0], two, 1)

    def self_project():
        loading[3].wait()
        sb = nb[...]
        for i, (a, b) in enumerate(((0, 0), (0, 1), (1, 0))):
            sqkv[i] = low(dot(sb, square_block(wr[0], a, b)))
        keep("sqkv", sqkv)

    def self_attention(first, last):
        pairs = width // 128

        def run():
            @pl.loop(first, last, unroll=3)
            def _(i):
                at, row_at = lanes(i % pairs, 128), lanes(i // pairs, rows)
                q = stack_heads(sqkv[0, row_at, at] * jnp.asarray(0.125, BF16))
                s = dot_nt(q, sqkv[1, row_at, at])
                e = jnp.exp(s - jnp.max(s, axis=-1, keepdims=True))
                prob = low(e * (1.0 / jnp.sum(e, axis=-1, keepdims=True)))
                sp[i] = prob
                so[row_at, at] = low(join_heads(dot(prob, sqkv[2, row_at, at])))

            if last == 2 * pairs:
                keep("sp", sp)

        return run

    def self_out():
        lt[1] = so[...].T
        pair("l1t", lt.at[c], lt.at[1 - c], two, 1)
        aa[...] = ac[...] + dot(so[...], square_block(wr[0], 1, 1))
        keep("aa", aa)
        mnb = low(normed(aa[...])[0] * gain_out[4:5])
        nb[...] = mnb
        mnt[...] = mnb.T
        pair("mnt", mnt, mnt, two, 1)

    def self_down():
        total = aa[...] + down(5, mh)
        result[0] = pick(first_live, total[:rows], total[rows:])
        result[1] = pick(first_live, total[rows:], total[:rows])

    pairs = width // 128
    work = collections.deque([(-2, send_gains), (1, start)])
    for n in range(4):
        work.append((1, tokens_part(n * tokens // 512, (n + 1) * tokens // 512)))
    for slot, part in (
        (4, load(0, wr[0])),
        (4, cross_queries),
        (4, keys_values(0, 1)),
        (4, keys_values(1, 2)),
        (4, keys_values(2, 3)),
        (4, keys_values(3, tokens // 256)),
        (4, cross_attention(0, 2)),
        (4, cross_attention(2, 4)),
        (4, cross_attention(4, pairs)),
        (4, cross_out),
        (6, load(1, wr[1])),
        (6, up(1, wr[1], rows, ch, gpc, 0, 2, cross_up_done)),
        (6, up(1, wr[1], rows, ch, gpc, 2, 4, cross_up_done)),
        (8, load(2, wt)),
        (8, cross_down),
        (10, load(3, wr[0])),
        (10, self_project),
        (10, self_attention(0, pairs)),
        (10, self_attention(pairs, 2 * pairs)),
        (10, self_out),
        (12, load(4, wr[1])),
        (12, up(4, wr[1], two, mh, gps, 0, 2, self_up_done)),
        (12, up(4, wr[1], two, mh, gps, 2, 4, self_up_done)),
        (14, load(5, wt)),
        (14, self_down),
    ):
        work.append((slot, part))
    steps = {
        "1": step_one,
        "f": step_one_forward,
        "2": step_two,
        "g": step_two_forward,
        "3": step_three,
        "4": step_four,
    }
    places = {"1": -2, "f": -1, "2": 0, "g": 0, "3": 1, "4": 2}
    for slot, name, i in slots(halves, places, "231fg4"):
        steps[name](i)
        if work and work[0][0] <= slot:
            work.popleft()[1]()
    while work:
        work.popleft()[1]()
    wait_all(across_pairs)
    for made in local_open:
        made.wait()
    sems.drain()


def half_shape(shard):
    return shard.shape[0], shard.shape[1] // 2


def forward_all(own, gain, latents, inputs, cotangent, counts, flags):
    count = len(own)
    rows, width = latents.shape[1:]
    tokens = inputs.shape[1]
    hidden = own[1].shape[1] * 4
    dims = (rows, tokens, width, hidden)
    two = 2 * rows
    kept = {**kept_shapes(*dims), **paired_shapes(*dims)}
    names = tuple(kept)
    copies = 7 + 2 * count * (6 + 10 + 4 + 2) + len(paired_shapes(*dims))
    block = (2, 2, 2, 4, 2) + half_shape(own[0])
    shapes = [jax.ShapeDtypeStruct(block, BF16) for w in own]
    shapes += [
        jax.ShapeDtypeStruct((16, width), F32),
        jax.ShapeDtypeStruct(latents.shape, F32),
    ]
    shapes += [jax.ShapeDtypeStruct(s, t) for s, t in kept.values()]
    pairs = width // 128
    scratch = [
        ((8, 16, 128), BF16),
        (latents.shape, F32),
        (latents.shape, F32),
        (inputs.shape, BF16),
        ((two, width), F32),
        ((tokens, width), BF16),
        ((width, tokens), BF16),
        ((2, 2, width // 4, two), BF16),
        ((2, width, rows), BF16),
        (block, BF16),
        (block, BF16),
        (block, BF16),
        ((rows, width), BF16),
        ((2, tokens, width), BF16),
        ((pairs, two, tokens), BF16),
        ((rows, width), F32),
        ((rows, width), F32),
        ((rows, hidden), BF16),
        ((rows, hidden), BF16),
        ((two, width), F32),
        ((3, two, width), BF16),
        ((2 * pairs, two, rows), BF16),
        ((two, width), BF16),
        ((two, width), F32),
        ((two, hidden), BF16),
        ((two, hidden), BF16),
        ((tokens, width), BF16),
        ((2, width, two), BF16),
        ((width, rows), BF16),
        ((width, two), BF16),
        (gain.shape, BF16),
        ((16, 128), BF16),
        ((rows, width), BF16),
        ((two, width), BF16),
    ]
    outs = pl.pallas_call(
        functools.partial(forward_kernel, names, dims),
        out_shape=shapes,
        in_specs=[ANY] * (count + 4) + [SMEM, SMEM],
        out_specs=[ANY] * count + [VMEM, VMEM] + [ANY] * len(names),
        scratch_shapes=[pltpu.VMEM(s, t) for s, t in scratch]
        + [
            pltpu.SemaphoreType.DMA((copies,)),
            pltpu.SemaphoreType.DMA((copies,)),
            pltpu.SemaphoreType.DMA((5 + 3 * count + len(names),)),
        ],
        compiler_params=pltpu.CompilerParams(
            collective_id=0, has_side_effects=True, vmem_limit_bytes=60 << 20
        ),
        name="gather_and_forward",
    )(*own, gain, latents, inputs, cotangent, counts, flags)
    full, (norm_gain, result) = outs[:count], outs[count : count + 2]
    return full, norm_gain, result, dict(zip(names, outs[count + 2 :]))


def norm_back(values, gain_row, gradient):
    unit, inverse = normed(values)
    scaled = gradient * gain_row
    grad = inverse * (
        scaled
        - jnp.mean(scaled, axis=-1, keepdims=True)
        - unit * jnp.mean(scaled * unit, axis=-1, keepdims=True)
    )
    return grad, jnp.sum(gradient * unit, axis=0, keepdims=True)


def attention_back(q, k, v, out_grad, prob, delta):
    prob_grad = dot_nt(out_grad, v)
    weight = prob.astype(F32)
    if delta is None:
        delta = jnp.sum(weight * prob_grad, axis=-1, keepdims=True)
    score_grad = low(weight * (prob_grad - delta))
    q_grad = join_heads(dot(score_grad, k)) * 0.125
    k_grad = low(dot(q.T, score_grad) * 0.125).T
    v_grad = low(dot(out_grad.T, prob)).T
    return low(q_grad), k_grad, v_grad


def add_blocks(total, where, part, there):
    total[where] = (total[where].astype(F32) + part[there].astype(F32)).astype(BF16)


def backward_kernel(names, dims, *refs):
    rows, tokens, width, hidden = dims
    two, quarter, pairs = 2 * rows, hidden // 4, width // 128
    count = 6
    halves, ring = 2 * count, 3
    order = (5, 4, 3, 2, 1, 0)
    refs = list(refs)

    def take(n):
        out = refs[:n]
        del refs[:n]
        return out

    full = take(count)
    gain, lat, cot, flags = take(4)
    kept = dict(zip(names, take(len(names))))
    outs = take(count)
    gain_out, lat_grad, dx = take(3)
    total = take(count)
    from_y, from_x = take(ring), take(ring)
    from_a, from_b, from_c, from_d, from_z, end_c, end_d = (take(halves) for _ in range(7))
    by_c, by_d, by_z = (take(halves) for _ in range(3))
    wr, wt, grad_ac, du_sib, r_sib, ge_sib, dcu_sib, rs_sib, dkv_sib = take(9)
    gain_acc, gain_sub, gain_dp, send, recv, local, free = take(7)
    place = Place()
    x, y, z, c = place.x, place.y, place.z, place.c
    sems = Sems(place, send, recv)
    local_count = [0]

    def local_copy(src, dst):
        made = pltpu.make_async_copy(src, dst, local.at[local_count[0]])
        local_count[0] += 1
        made.start()
        return made

    me_dp, me_sub = z * 2 + y, x * 2 + c
    sub_peers = [(me_dp, (me_sub + k) % 4) for k in (1, 2, 3)]
    dp_peers = [((me_dp + k) % 8, me_sub) for k in range(1, 8)]
    px, py, pc = place.dev(x=1 - x), place.dev(y=1 - y), place.dev(c=1 - c)
    first_live = flags[0] == 0
    gain_acc[...] = jnp.zeros_like(gain_acc)

    ones, twos, threes = {}, {}, {}
    block_rows, block_columns = total[0].shape[4:]

    def where(i):
        return total[order[i // 2]], i % 2

    def clear():
        for into in (*from_c, *from_d, *from_z):

            @pl.when(z == 0)
            def _():
                into[0] = jnp.zeros(into.shape[1:], BF16)

            @pl.when(z == 3)
            def _():
                into[2] = jnp.zeros(into.shape[1:], BF16)

    def step_one(i):
        a, h = where(i)
        if i >= ring:
            pl.semaphore_wait(free.at[i - ring], 2)
        ones[i] = [
            sems.copy(a.at[h, :, :, 1 - y, piece("CA", block_rows)], from_y[i % ring], py),
            sems.copy(a.at[h, 1 - x, :, :, piece("BD", block_rows)], from_x[i % ring], px),
        ]

    def step_two(i):
        a, h = where(i)
        wait_all(ones.pop(i))
        ca, bd = piece("CA", block_rows), piece("BD", block_rows)
        pa, pb, pc_, pd = (piece(n, block_rows) for n in ("A", "B", "C", "D"))
        fy, fx = from_y[i % ring], from_x[i % ring]

        @pl.loop(0, 8)
        def _(j):
            add_blocks(a, (h, j // 4, j % 4, y, ca), fy, (j // 4, j % 4))
            add_blocks(a, (h, x, j // 2, j % 2, bd), fx, (j // 2, j % 2))

        if i + ring < halves:
            for device in (px, py):
                pl.semaphore_signal(free.at[i], inc=1, device_id=device, device_id_type=MESH_ID)
        collect_c = Collect(sems, lambda o: a.at[h, :, o, y, pc_], from_c[i], by_c[i])
        collect_d = Collect(sems, lambda o: a.at[h, x, o, :, pd], from_d[i], by_d[i])
        got = [
            sems.copy(a.at[h, 1 - x, :, y, pa], from_a[i], px),
            sems.copy(a.at[h, x, :, 1 - y, pb], from_b[i], py),
        ]
        twos[i] = (collect_c, collect_d, got)

    def step_two_forward(i):
        a, h = where(i)
        pc_, pd = piece("C", block_rows), piece("D", block_rows)

        def add_c(o):
            for j in range(2):
                add_blocks(a, (h, j, o, y, pc_), by_c[i], j)

        def add_d(o):
            for j in range(2):
                add_blocks(a, (h, x, o, j, pd), by_d[i], j)

        twos[i][0].part = lambda o: a.at[h, :, o, y, pc_]
        twos[i][1].part = lambda o: a.at[h, x, o, :, pd]
        twos[i][0].forward(add_c)
        twos[i][1].forward(add_d)

    def step_three(i):
        a, h = where(i)
        collect_c, collect_d, got = twos.pop(i)
        collect_c.finish()
        collect_d.finish()
        wait_all(got)
        pa, pb, pc_, pd = (piece(n, block_rows) for n in ("A", "B", "C", "D"))
        fc, fd = from_c[i], from_d[i]

        @pl.loop(0, 4)
        def _(j):
            add_blocks(a, (h, x, j, y, pa), from_a[i], j)
            add_blocks(a, (h, x, j, y, pb), from_b[i], j)

        @pl.loop(0, 2)
        def _(j):
            a[h, j, z, y, pc_] = low(
                a[h, j, z, y, pc_].astype(F32)
                + fc[0, j].astype(F32)
                + fc[1, j].astype(F32)
                + fc[2, j].astype(F32)
            )
            a[h, x, z, j, pd] = low(
                a[h, x, z, j, pd].astype(F32)
                + fd[0, j].astype(F32)
                + fd[1, j].astype(F32)
                + fd[2, j].astype(F32)
            )

        ab = piece("AB", block_rows)
        collect = Collect(sems, lambda o: a.at[h, x, o, y, ab], from_z[i], by_z[i])
        got = [
            sems.copy(a.at[h, 1 - x, z, y, pc_], end_c[i], px),
            sems.copy(a.at[h, x, z, 1 - y, pd], end_d[i], py),
        ]
        threes[i] = (collect, got)

    def step_three_forward(i):
        a, h = where(i)
        ab = piece("AB", block_rows)
        collect = threes[i][0]
        collect.part = lambda o: a.at[h, x, o, y, ab]
        collect.forward(lambda o: add_blocks(a, (h, x, o, y, ab), by_z[i], ...))

    def step_four(i):
        a, h = where(i)
        collect, got = threes.pop(i)
        collect.finish()
        wait_all(got)
        fz, o = from_z[i], outs[order[i // 2]]
        if o.shape[0] == block_rows:
            first, columns = 0, pl.ds(h * block_columns, block_columns)
        else:
            first, columns = h * block_rows, slice(None)

        def put(name, value):
            at = piece(name, block_rows)
            o[pl.ds(first + at.start, at.size), columns] = (
                a[h, x, z, y, at].astype(F32) + value
            )

        put("AB", fz[0].astype(F32) + fz[1].astype(F32) + fz[2].astype(F32))
        put("C", end_c[i][...].astype(F32))
        put("D", end_d[i][...].astype(F32))

    run_step = {
        "1": step_one,
        "2": step_two,
        "g": step_two_forward,
        "3": step_three,
        "f": step_three_forward,
        "4": step_four,
    }
    places = {"1": 0, "2": 1, "g": 2, "3": 3, "f": 4, "4": 5}
    steps = collections.deque(slots(halves, places, "12g3f4"))
    ready = [0]

    def advance(n):
        while n > 0 and steps and (steps[0][1] != "1" or steps[0][2] < ready[0]):
            unused, name, i = steps.popleft()
            run_step[name](i)
            n -= 1

    def done(m):
        ready[0] += 2
        advance(2)

    def put_square(m, at, value):
        for h in range(2):
            part = value[:, h * block_columns : (h + 1) * block_columns]
            total[m][h, at] = low(part).reshape(4, 2, block_rows, block_columns)

    def put_hidden(m, zz, value):
        for yy in range(2):
            for a in range(2):
                for h in range(2):
                    first = (2 * a + h) * block_rows
                    part = value[
                        first : first + block_rows,
                        yy * block_columns : (yy + 1) * block_columns,
                    ]
                    total[m][h, a, zz, yy] = low(part)

    def hidden_grad(m, left, right):
        for zz in range(4):
            put_hidden(m, zz, dot(left, right[:, zz * quarter : (zz + 1) * quarter]))

    def both(own, other):
        return jnp.concatenate([own, other], axis=0)

    def send_off(src, dst):
        return sems.copy(src, dst, pc, later=False)

    def pick(first, second):
        return jnp.where(first_live, first, second)

    def back_through(act, blocks):
        out = None
        for i, (a, b) in enumerate(blocks):
            term = dot_nt(act[a, b], square_block(wr, a, b))
            out = term if out is None else out + term
        return out

    every = ((0, 0), (0, 1), (1, 0), (1, 1))

    def self_part(mh, gps, gyt, mnt, sbt, l1t, du, r, cot_v, aa, ac, sqkv, sp, grad_aa, out_grad):
        loads = {
            name: local_copy(src, dst)
            for name, src, dst in (
                ("gyt", kept["gyt"], gyt),
                ("mh", kept["mh"], mh),
                ("wt", full[5], wt),
                ("cot", cot, cot_v),
                ("gps", kept["gps"], gps),
                ("wr", full[4], wr),
                ("aa", kept["aa"], aa),
                ("mnt", kept["mnt"], mnt),
                ("sqkv", kept["sqkv"], sqkv),
                ("sp", kept["sp"], sp),
                ("ac", kept["ac"], ac),
                ("sbt", kept["sbt"], sbt),
                ("l1t", kept["l1t"], l1t),
            )
        }
        clear()
        greet(place, sub_peers + dp_peers)
        loads["gyt"].wait()
        loads["mh"].wait()
        for h in range(2):
            left = gyt[:, h * block_rows : (h + 1) * block_rows]
            left = left.reshape(2 * block_rows, 2 * two)
            for zz in range(4):
                value = dot(left, mh[:, zz * quarter : (zz + 1) * quarter])
                for yy in range(2):
                    part = value[:, yy * block_columns : (yy + 1) * block_columns]
                    total[5][h, :, zz, yy] = low(part).reshape(2, block_rows, block_columns)
            ready[0] += 1
            advance(1)

        for name in ("wt", "cot", "gps"):
            loads[name].wait()
        for at, value in (
            (pl.ds(0, rows), pick(cot_v[0], cot_v[1])),
            (pl.ds(rows, rows), pick(cot_v[1], cot_v[0])),
        ):
            grad_aa[at] = value
        gy = low(grad_aa[...])
        for s in range(4):
            at = pl.ds(s * quarter, quarter)
            du[s // 2, s % 2] = low(dot(gy, hidden_block(wt, s)) * gps[:, at].astype(F32))
        sent = send_off(du.at[:, 1 - c], du_sib)
        advance(2)
        for name in ("wr", "aa", "mnt"):
            loads[name].wait()
        grad, gain_row = norm_back(aa[...], gain[4:5], back_through(du, every))
        grad_aa[...] += grad
        gain_acc[0, 4:5] = gain_row
        advance(2)
        next_wr = local_copy(full[3], wr)
        next_wt = local_copy(full[2], wt)
        sent.wait_recv()
        for a in range(2):
            put_square(4, a, dot(mnt[...], both(du[a, c], du_sib[a])))
        done(4)

        r[1, 1] = low(grad_aa[...])
        for made in (next_wr, loads["sqkv"], loads["sp"], loads["ac"], loads["sbt"], loads["l1t"]):
            made.wait()
        out_grad[...] = low(dot_nt(r[1, 1], square_block(wr, 1, 1)))

        advance(2)
        for part in range(2):

            @pl.loop(part * pairs, (part + 1) * pairs, unroll=3)
            def _(i):
                at, row_at = lanes(i % pairs, 128), lanes(i // pairs, rows)
                r[0, 0, row_at, at], r[0, 1, row_at, at], r[1, 0, row_at, at] = attention_back(
                    stack_heads(sqkv[0, row_at, at]),
                    sqkv[1, row_at, at],
                    sqkv[2, row_at, at],
                    stack_heads(out_grad[row_at, at]),
                    sp[i],
                    None,
                )

            advance(2)

        sent_r = send_off(r.at[:, 1 - c], r_sib)
        grad, gain_row = norm_back(ac[...], gain[3:4], back_through(r, every[:3]))
        grad_ac[...] = grad_aa[...] + grad
        gain_acc[0, 3:4] = gain_row
        advance(2)
        sent_r.wait_recv()
        put_square(3, 0, dot(sbt[...], both(r[0, c], r_sib[0])))
        put_square(3, 1, dot(l1t[...], both(r[1, c], r_sib[1])))
        done(3)
        sent.wait_send()
        sent_r.wait_send()
        next_wt.wait()

    def cross_part(
        ch, gpc, ge, cnt, du, mid, lst, rs, xbt, kv, cp, cq, co, dco, xl, dxs, lat_v, grad_mid
    ):
        loads = {
            name: local_copy(src, dst)
            for name, src, dst in (
                ("ch", kept["ch"], ch),
                ("gpc", kept["gpc"], gpc),
                ("wr", full[1], wr),
                ("mid", kept["mid"], mid),
                ("cnt", kept["cnt"], cnt),
                ("cq", kept["cq"], cq),
                ("co", kept["co"], co),
                ("kv", kept["kv"], kv),
                ("cp", kept["cp"], cp),
                ("lst", kept["lst"], lst),
                ("xbt", kept["xbt"], xbt),
                ("lat", lat, lat_v),
            )
        }
        for i in range(2):
            lat_grad_dead = grad_ac[rows:]
            lat_grad[i] = lat_grad_dead
        low_grad = low(grad_ac[:rows])
        ge[...] = low_grad.T.reshape(2, 2, width // 4, rows)
        sent = [send_off(ge.at[:, 1 - c], ge_sib)]
        loads["gpc"].wait()
        for s in range(4):
            at = pl.ds(s * quarter, quarter)
            du[s // 2, s % 2] = low(dot(low_grad, hidden_block(wt, s)) * gpc[:, at].astype(F32))
        sent.append(send_off(du.at[:, 1 - c], dcu_sib))
        advance(2)
        loads["ch"].wait()
        sent[0].wait_recv()
        left = jnp.concatenate(
            [ge[:, c].reshape(width // 2, rows), ge_sib[...].reshape(width // 2, rows)], axis=1
        )
        hidden_grad(2, left, ch)
        done(2)

        for name in ("wr", "mid", "cnt"):
            loads[name].wait()
        grad, gain_row = norm_back(mid[...], gain[2:3], back_through(du, every))
        grad_mid[...] = grad_ac[:rows] + grad
        gain_acc[0, 2:3] = gain_row
        advance(2)
        next_wr = local_copy(full[0], wr)
        sent[1].wait_recv()
        for a in range(2):
            put_square(1, a, dot(cnt[...], both(du[a, c], dcu_sib[a])))
        done(1)

        rs[1] = low(grad_mid[...])
        next_wr.wait()
        dco[...] = low(dot_nt(rs[1], square_block(wr, 1, 1)))
        for name in ("cq", "co", "kv", "cp"):
            loads[name].wait()

        advance(2)
        for part in range(3):

            @pl.loop(part * pairs // 3, (part + 1) * pairs // 3, unroll=2)
            def _(p):
                at = lanes(p, 128)
                out_grad = stack_heads(dco[:, at])
                attended = co[:, at]
                delta = jnp.sum(
                    out_grad.astype(F32) * both(attended, attended), axis=-1, keepdims=True
                )
                rs[0, :, at], kv[0, :, at], kv[1, :, at] = attention_back(
                    stack_heads(cq[:, at]), kv[0, :, at], kv[1, :, at], out_grad, cp[p], delta
                )

            advance(2)

        sent.append(send_off(rs.at[1 - c], rs_sib))
        sent.append(send_off(kv.at[c], dkv_sib))
        advance(2)
        for name in ("lst", "xbt", "lat"):
            loads[name].wait()
        sent[2].wait_recv()
        sent[3].wait_recv()
        put_square(0, c, dot(lst[...], both(rs[c], rs_sib[...])))
        put_square(
            0, 1 - c, dot(xbt[:, :tokens], kv[1 - c]) + dot(xbt[:, tokens:], dkv_sib[...])
        )
        done(0)

        grad, gain_row = norm_back(
            pick(lat_v[0], lat_v[1]), gain[0:1], dot_nt(rs[0], square_block(wr, 0, 0))
        )
        gain_acc[0, 0:1] = gain_row
        live_grad = grad_mid[...] + grad
        lat_grad[0] = pick(live_grad, lat_grad[0])
        lat_grad[1] = pick(lat_grad[1], live_grad)
        advance(2)
        out = []
        parts = tokens // 128

        def fetch(i):
            return local_copy(kept["xl"].at[pl.ds(i * 128, 128)], xl.at[i % 2])

        fetched = fetch(0)
        for i in range(parts):
            at = pl.ds(i * 128, 128)
            fetched.wait()
            if i + 1 < parts:
                fetched = fetch(i + 1)
            if i >= 2:
                out[i - 2].wait()
            term = dot_nt(kv[0, at], square_block(wr, 0, 1))
            term += dot_nt(kv[1, at], square_block(wr, 1, 0))
            grad, gain_row = norm_back(xl[i % 2].astype(F32), gain[1:2], term)
            dxs[i % 2] = grad
            gain_acc[0, 1:2] += gain_row
            out.append(local_copy(dxs.at[i % 2], dx.at[at]))
            advance(2)
        for made in out[-2:]:
            made.wait()
        gain_one = [sems.copy(gain_acc.at[0], spot(gain_sub, k), sub_peers[k]) for k in range(3)]
        advance(3)
        wait_all(gain_one)
        gain_acc[1] = gain_acc[0] + gain_sub[0] + gain_sub[1] + gain_sub[2]
        gain_two = [sems.copy(gain_acc.at[1], spot(gain_dp, k), dp_peers[k]) for k in range(7)]
        for made in sent:
            made.wait_send()
        return gain_two

    def vmem(*shape, dtype=BF16):
        return pltpu.VMEM(shape, dtype)

    holder = {}

    pl.run_scoped(
        self_part,
        vmem(2 * two, hidden),
        vmem(two, hidden),
        vmem(2, width // 4, 2 * two),
        vmem(width, 2 * two),
        vmem(width, 2 * two),
        vmem(width, 2 * two),
        vmem(2, 2, two, quarter),
        vmem(2, 2, two, width),
        vmem(2, rows, width, dtype=F32),
        vmem(two, width, dtype=F32),
        vmem(two, width, dtype=F32),
        vmem(3, two, width),
        vmem(2 * pairs, two, rows),
        vmem(two, width, dtype=F32),
        vmem(two, width),
    )

    def run_cross(*bufs):
        holder["gain"] = cross_part(*bufs)

    pl.run_scoped(
        run_cross,
        vmem(two, hidden),
        vmem(rows, hidden),
        vmem(2, 2, width // 4, rows),
        vmem(width, two),
        vmem(2, 2, rows, quarter),
        vmem(rows, width, dtype=F32),
        vmem(width, two),
        vmem(2, rows, width),
        vmem(width, 2 * tokens),
        vmem(2, tokens, width),
        vmem(pairs, two, tokens),
        vmem(rows, width),
        vmem(rows, width, dtype=F32),
        vmem(rows, width),
        vmem(2, 128, width),
        vmem(2, 128, width, dtype=F32),
        vmem(2, rows, width, dtype=F32),
        vmem(rows, width, dtype=F32),
    )
    advance(len(steps))
    wait_all(holder["gain"])
    gain_out[...] = gain_acc[1] + jnp.sum(gain_dp[...], axis=0)
    sems.drain()


def backward_all(shard, full, norm_gain, latents, cotangent, flags, kept):
    count = len(full)
    rows, width = latents.shape[1:]
    tokens, hidden = kept["xl"].shape[0], kept["mh"].shape[1]
    dims = (rows, tokens, width, hidden)
    two = 2 * rows
    copies = 10 + 6 + 2 * count * (2 + 10 + 6)
    ring, halves = 3, 2 * count
    block_rows, block_columns = full[0].shape[5:]

    def room(number, lead, sixths):
        return [pltpu.VMEM(lead + (block_rows * sixths // 6, block_columns), BF16)] * number

    scratch = [pltpu.VMEM((2,) + full[0].shape[2:], BF16)] * count
    scratch += room(ring, (2, 4), 3) + room(ring, (4, 2), 3)
    scratch += room(halves, (4,), 1) + room(halves, (4,), 1)
    scratch += room(halves, (3, 2), 2) + room(halves, (3, 2), 2) + room(halves, (3,), 2)
    scratch += room(halves, (), 2) + room(halves, (), 2)
    scratch += room(halves, (2,), 2) + room(halves, (2,), 2) + room(halves, (), 2)
    scratch += [
        pltpu.VMEM(full[0].shape, BF16),
        pltpu.VMEM(full[2].shape, BF16),
        pltpu.VMEM((two, width), F32),
        pltpu.VMEM((2, two, hidden // 4), BF16),
        pltpu.VMEM((2, two, width), BF16),
        pltpu.VMEM((2, width // 4, rows), BF16),
        pltpu.VMEM((2, rows, hidden // 4), BF16),
        pltpu.VMEM((rows, width), BF16),
        pltpu.VMEM((tokens, width), BF16),
        pltpu.VMEM((2, 8, width), F32),
        pltpu.VMEM((3, 8, width), F32),
        pltpu.VMEM((7, 8, width), F32),
        pltpu.SemaphoreType.DMA((copies,)),
        pltpu.SemaphoreType.DMA((copies,)),
        pltpu.SemaphoreType.DMA((48,)),
        pltpu.SemaphoreType.REGULAR((halves - ring,)),
    ]
    shapes = [jax.ShapeDtypeStruct(d, F32) for d in shard]
    shapes += [
        jax.ShapeDtypeStruct((8, width), F32),
        jax.ShapeDtypeStruct(latents.shape, F32),
        jax.ShapeDtypeStruct((tokens, width), F32),
    ]
    outs = pl.pallas_call(
        functools.partial(backward_kernel, tuple(kept), dims),
        out_shape=shapes,
        in_specs=[ANY] * count + [VMEM, ANY, ANY, SMEM] + [ANY] * len(kept),
        out_specs=[VMEM] * (count + 2) + [ANY],
        scratch_shapes=scratch,
        compiler_params=pltpu.CompilerParams(
            collective_id=1, has_side_effects=True, vmem_limit_bytes=60 << 20
        ),
        name="backward_and_scatter",
    )(*full, norm_gain, latents, cotangent, flags, *kept.values())
    return outs[:count], *outs[count:]


def finish_kernel(gain_share, gain_rows, count, *refs):
    flags, result, lat_grad, tok_grad, gain_total = refs[:5]
    shards_in = refs[5 : 5 + count]
    out_result, out_lat, out_tok, out_gain = refs[5 + count : 9 + count]
    shards_out = refs[9 + count : 9 + 2 * count]
    gain_in, zeros, sems_in, sems_out = refs[9 + 2 * count : 13 + 2 * count]
    held = refs[13 + 2 * count :]
    tokens, pieces = tok_grad.shape[0], held[-1].shape[0]
    size = tokens // pieces
    live = jnp.where(flags[0] == 0, 0, 1)
    moves = []
    for n in range(pieces):
        at = pl.ds(n * size, size)
        moves.append((tok_grad.at[at], held[-1].at[n], out_tok.at[live, at]))
    moves += zip((result, lat_grad, *shards_in), held, (out_result, out_lat, *shards_out))
    gain_copy = pltpu.make_async_copy(gain_total, gain_in, sems_in.at[len(moves)])
    reads = [
        pltpu.make_async_copy(src, room, sems_in.at[i]) for i, (src, room, dst) in enumerate(moves)
    ]
    for made in reads:
        made.start()
    gain_copy.start()
    zeros[...] = jnp.zeros_like(zeros)
    started = []
    for n in range(pieces):
        started.append(
            pltpu.make_async_copy(
                zeros, out_tok.at[1 - live, pl.ds(n * size, size)], sems_out.at[len(moves) + n]
            )
        )
        started[-1].start()
    for i, (src, room, dst) in enumerate(moves):
        reads[i].wait()
        started.append(pltpu.make_async_copy(room, dst, sems_out.at[i]))
        started[-1].start()
    gain_copy.wait()
    dp = lax.axis_index("dp")
    for i in range(8):

        @pl.when(dp == i)
        def _():
            out_gain[...] = gain_in[:gain_rows, i * gain_share : (i + 1) * gain_share]

    for made in started:
        made.wait()


def finish_all(gain_shape, flags, result, lat_grad, tok_grad, gain_total, shards_in):
    count, pieces = len(shards_in), 4
    tokens, width = tok_grad.shape
    arrays = [result, lat_grad, tok_grad, gain_total, *shards_in]
    shapes = [
        jax.ShapeDtypeStruct(result.shape, F32),
        jax.ShapeDtypeStruct(lat_grad.shape, F32),
        jax.ShapeDtypeStruct((2, tokens, width), F32),
        jax.ShapeDtypeStruct(gain_shape, F32),
    ]
    shapes += [jax.ShapeDtypeStruct(a.shape, F32) for a in shards_in]
    return pl.pallas_call(
        functools.partial(finish_kernel, gain_shape[1], gain_shape[0], count),
        out_shape=shapes,
        in_specs=[SMEM] + [ANY] * len(arrays),
        out_specs=[ANY] * 3 + [VMEM] + [ANY] * count,
        scratch_shapes=[
            pltpu.VMEM(gain_total.shape, F32),
            pltpu.VMEM((tokens // pieces, width), F32),
            pltpu.SemaphoreType.DMA((3 + count + pieces,)),
            pltpu.SemaphoreType.DMA((2 + count + 2 * pieces,)),
            *(pltpu.VMEM(a.shape, F32) for a in (result, lat_grad, *shards_in)),
            pltpu.VMEM((pieces, tokens // pieces, width), F32),
        ],
        compiler_params=pltpu.CompilerParams(vmem_limit_bytes=60 << 20),
        name="write_outputs",
    )(flags, *arrays)


def layer_norm(values, gain_row):
    centred = values - jnp.mean(values, axis=-1, keepdims=True)
    inverse = lax.rsqrt(jnp.mean(centred * centred, axis=-1, keepdims=True) + EPSILON)
    return centred * inverse * gain_row


def norm_backward(values, gain_row, gradient):
    unused, pull_back = jax.vjp(layer_norm, values, gain_row)
    return pull_back(gradient)


def gelu_tanh(values):
    return jax.nn.gelu(values, approximate=True)


def mm(left_side, weight):
    return jnp.dot(left_side, weight, preferred_element_type=F32)


def mm_nt(left_side, weight):
    return lax.dot_general(left_side, weight, (((1,), (1,)), ((), ())), preferred_element_type=F32)


def mm_tn(left_side, gradient):
    return lax.dot_general(
        left_side, gradient, (((0,), (0,)), ((), ())), preferred_element_type=F32
    )


def low(values):
    return values.astype(BF16)


def heads_of(values):
    return values.reshape(values.shape[:-1] + (HEADS, values.shape[-1] // HEADS))


def mlp_forward(residual, gain_row, up, down_t):
    normed = low(layer_norm(residual, gain_row))
    pre_act = mm(normed, up)
    hidden = low(gelu_tanh(pre_act))
    return normed, pre_act, hidden, mm_nt(hidden, down_t)


def mlp_backward(residual, gain_row, normed, pre_act, hidden, up, down_t, grad_out):
    grad_low = low(grad_out)
    grad_down_t = mm_tn(grad_low, hidden)
    grad_hidden = mm(grad_low, down_t)
    unused, gelu_back = jax.vjp(gelu_tanh, pre_act)
    grad_pre = low(gelu_back(grad_hidden)[0])
    grad_up = mm_tn(normed, grad_pre)
    grad_resid, grad_gain = norm_backward(residual, gain_row, mm_nt(grad_pre, up))
    return grad_resid, grad_gain, grad_up, grad_down_t


def live_layer(live_lat, dead_lat, tokens, count, live_cot, dead_cot, weights, norm_gain):
    c_attn, c_up, c_down_t, s_attn, s_up, s_down_t = weights
    rows, width = live_lat.shape
    scale = (width // HEADS) ** (-0.5)
    lat_low = low(layer_norm(live_lat, norm_gain[0]))
    queries = low(mm(lat_low, c_attn[:, :width]))
    token_values = tokens.astype(F32)
    tok_low = low(layer_norm(token_values, norm_gain[1]))
    kv_weight = c_attn[:, width : 3 * width]
    key_value = low(mm(tok_low, kv_weight))
    keys, values = heads_of(key_value[:, :width]), heads_of(key_value[:, width:])
    scores = (
        jnp.einsum("qhd,khd->hqk", heads_of(queries), keys, preferred_element_type=F32) * scale
    )
    valid = (jnp.arange(tokens.shape[0]) < count)[None, None, :]
    probs = jax.nn.softmax(jnp.where(valid, scores, MASKED), axis=-1)
    probs_low = low(probs)
    attended = jnp.einsum("hqk,khd->qhd", probs_low, values, preferred_element_type=F32)
    attended = attended.reshape(rows, width)
    cross_low = low(attended)
    middle = live_lat + mm(cross_low, c_attn[:, 3 * width :])
    c_norm, c_pre, c_hidden, c_mlp = mlp_forward(middle, norm_gain[2], c_up, c_down_t)
    after_cross = jnp.concatenate([middle + c_mlp, dead_lat], axis=0)

    self_low = low(layer_norm(after_cross, norm_gain[3]))
    qkv = low(mm(self_low, s_attn[:, : 3 * width])).reshape(2, rows, 3 * width)
    s_q = heads_of(qkv[..., :width])
    s_k = heads_of(qkv[..., width : 2 * width])
    s_v = heads_of(qkv[..., 2 * width :])
    s_scores = jnp.einsum("iqhd,ikhd->ihqk", s_q, s_k, preferred_element_type=F32) * scale
    s_probs = jax.nn.softmax(s_scores, axis=-1)
    s_probs_low = low(s_probs)
    s_out = jnp.einsum("ihqk,ikhd->iqhd", s_probs_low, s_v, preferred_element_type=F32)
    s_out_low = low(s_out.reshape(2 * rows, width))
    after_attn = after_cross + mm(s_out_low, s_attn[:, 3 * width :])
    m_norm, m_pre, m_hidden, m_mlp = mlp_forward(after_attn, norm_gain[4], s_up, s_down_t)
    result = after_attn + m_mlp

    cotangent = jnp.concatenate([live_cot, dead_cot], axis=0)
    grad_in, gain_four, d_s_up, d_s_down_t = mlp_backward(
        after_attn, norm_gain[4], m_norm, m_pre, m_hidden, s_up, s_down_t, cotangent
    )
    grad_attn = cotangent + grad_in
    grad_y = low(grad_attn)
    d_s_o = mm_tn(s_out_low, grad_y)
    grad_out = heads_of(low(mm_nt(grad_y, s_attn[:, 3 * width :])).reshape(2, rows, width))
    grad_probs = jnp.einsum("iqhd,ikhd->ihqk", grad_out, s_v, preferred_element_type=F32)
    delta = jnp.sum(grad_probs * s_probs, axis=-1, keepdims=True)
    grad_scores = low(s_probs * (grad_probs - delta))
    g_q = jnp.einsum("ihqk,ikhd->iqhd", grad_scores, s_k, preferred_element_type=F32) * scale
    g_k = jnp.einsum("ihqk,iqhd->ikhd", grad_scores, s_q, preferred_element_type=F32) * scale
    g_v = jnp.einsum("ihqk,iqhd->ikhd", s_probs_low, grad_out, preferred_element_type=F32)
    grad_qkv = low(
        jnp.concatenate([g.reshape(2 * rows, width) for g in (g_q, g_k, g_v)], axis=-1)
    )
    d_s_qkv = mm_tn(self_low, grad_qkv)
    grad_in, gain_three = norm_backward(
        after_cross, norm_gain[3], mm_nt(grad_qkv, s_attn[:, : 3 * width])
    )
    grad_cross = grad_attn + grad_in
    live_grad, dead_grad = grad_cross[:rows], grad_cross[rows:]
    grad_in, gain_two, d_c_up, d_c_down_t = mlp_backward(
        middle, norm_gain[2], c_norm, c_pre, c_hidden, c_up, c_down_t, live_grad
    )
    grad_middle = live_grad + grad_in
    grad_cross_y = low(grad_middle)
    d_c_o = mm_tn(cross_low, grad_cross_y)
    grad_cross_out = low(mm_nt(grad_cross_y, c_attn[:, 3 * width :]))
    out_heads = heads_of(grad_cross_out)
    grad_weights = jnp.einsum("qhd,khd->hqk", out_heads, values, preferred_element_type=F32)
    row_delta = jnp.transpose(jnp.sum(heads_of(grad_cross_out.astype(F32) * attended), axis=-1))
    grad_scores = low(probs * (grad_weights - row_delta[..., None]))
    grad_query = low(
        (
            jnp.einsum("hqk,khd->qhd", grad_scores, keys, preferred_element_type=F32) * scale
        ).reshape(rows, width)
    )
    grad_keys = (
        jnp.einsum("hqk,qhd->khd", grad_scores, heads_of(queries), preferred_element_type=F32)
        * scale
    )
    grad_values = jnp.einsum("hqk,qhd->khd", probs_low, out_heads, preferred_element_type=F32)
    grad_kv = low(
        jnp.concatenate(
            [grad_keys.reshape(-1, width), grad_values.reshape(-1, width)], axis=-1
        )
    )
    d_c_kv = mm_tn(tok_low, grad_kv)
    grad_tokens, gain_one = norm_backward(token_values, norm_gain[1], mm_nt(grad_kv, kv_weight))
    d_c_q = mm_tn(lat_low, grad_query)
    grad_in, gain_zero = norm_backward(
        live_lat, norm_gain[0], mm_nt(grad_query, c_attn[:, :width])
    )
    live_lat_grad = grad_middle + grad_in
    d_c_attn = low(jnp.concatenate([d_c_q, d_c_kv, d_c_o], axis=1))
    d_s_attn = low(jnp.concatenate([d_s_qkv, d_s_o], axis=1))
    gain_grad = jnp.stack([gain_zero, gain_one, gain_two, gain_three, gain_four])
    grads = (d_c_attn, low(d_c_up), low(d_c_down_t), d_s_attn, low(d_s_up), low(d_s_down_t))
    return result, live_lat_grad, dead_grad, grad_tokens, grads, gain_grad


def column_blocks(blocks):
    sub, dp, rows, columns = blocks.shape
    return blocks.transpose(1, 2, 0, 3).reshape(dp * rows, sub * columns)


def row_blocks(blocks):
    sub, dp, rows, columns = blocks.shape
    return blocks.transpose(0, 2, 1, 3).reshape(sub * rows, dp * columns)


def shards(*arrays, dp_size, sub_size):
    latents, inputs, counts, flags = arrays[:4]
    cross_attn, cross_up, cross_down, self_attn, self_up, self_down, gains, cotangent = arrays[4:]
    width = latents.shape[-1]
    own = (
        cross_attn,
        cross_up,
        jnp.transpose(cross_down),
        self_attn,
        self_up,
        jnp.transpose(self_down),
    )
    live = jnp.where(flags[0] == 0, 0, 1)
    here = (jnp.arange(inputs.shape[0]) == live)[:, None, None]
    if dp_size == 8 and sub_size == 4:
        full, norm_gain, result, kept = forward_all(
            own, gains, latents, inputs, cotangent, counts, flags
        )
        owned, gain_total, grad_latents, grad_tokens = backward_all(
            [w.shape for w in own], full, norm_gain, latents, cotangent, flags, kept
        )
        result, grad_latents, grad_inputs, gain_owned, *owned = finish_all(
            gains.shape, flags, result, grad_latents, grad_tokens, gain_total, owned
        )
        owned = [jnp.transpose(g) if i in (2, 5) else g for i, g in enumerate(owned)]
        return (result, grad_latents, grad_inputs, *owned, gain_owned)

    blocks = [lax.all_gather(lax.all_gather(w, "dp", axis=0), "sub", axis=0) for w in own]
    norm_gain = lax.all_gather(gains, "dp", axis=1, tiled=True)
    transposed = (False, False, True, False, False, True)
    weights = [
        row_blocks(b) if flip else column_blocks(b) for b, flip in zip(blocks, transposed)
    ]

    def item(array, index):
        return lax.dynamic_index_in_dim(array, index, 0, keepdims=False)

    result, live_grad, dead_grad, grad_tokens, grads, gain_grad = live_layer(
        item(latents, live),
        item(latents, 1 - live),
        item(inputs, live),
        item(counts, live),
        item(cotangent, live),
        item(cotangent, 1 - live),
        weights,
        norm_gain.astype(F32),
    )

    def both(live_part, dead_part):
        first = jnp.where(live == 0, live_part, dead_part)
        second = jnp.where(live == 0, dead_part, live_part)
        return jnp.stack([first, second])

    rows = latents.shape[1]
    result = both(result[:rows], result[rows:])
    grad_latents = both(live_grad, dead_grad)
    grad_inputs = jnp.where(here, grad_tokens[None], 0.0)

    def blocks_of(grad, shape, flip):
        r, c = shape
        if flip:
            return grad.reshape(sub_size, r, dp_size, c).transpose(0, 2, 1, 3)
        return grad.reshape(dp_size, r, sub_size, c).transpose(2, 0, 1, 3)

    grads = [blocks_of(g, w.shape, flip) for g, w, flip in zip(grads, own, transposed)]
    owned = [lax.psum_scatter(g, "sub", scatter_dimension=0) for g in grads]
    owned = [lax.psum_scatter(g.astype(F32), "dp", scatter_dimension=0) for g in owned]
    gain_owned = lax.psum(gain_grad, "sub")
    gain_owned = lax.psum_scatter(gain_owned, "dp", scatter_dimension=1, tiled=True)
    owned = [jnp.transpose(g) if flip else g for g, flip in zip(owned, transposed)]
    return (result, grad_latents, grad_inputs, *owned, gain_owned)


def solution(mesh):
    item = P(("dp", "sub"), None, None)
    weight = P("dp", "sub")
    gain = P(None, "dp")
    placed = (item, item, P(("dp", "sub")), P()) + (weight,) * 6 + (gain, item)
    return jax.shard_map(
        functools.partial(shards, dp_size=mesh.shape["dp"], sub_size=mesh.shape["sub"]),
        mesh=mesh,
        in_specs=placed,
        out_specs=(item, item, item) + (weight,) * 6 + (gain,),
        check_vma=False,
    )
```

```python
import collections
import functools

import jax
import jax.numpy as jnp
from jax import lax
from jax.experimental import pallas as pl
from jax.experimental.pallas import tpu as pltpu
from jax.sharding import PartitionSpec as P

HEADS = 12
EPSILON = 1e-05
MASKED = -1e30
MESH_ID = pl.DeviceIdType.MESH
F32 = jnp.float32
BF16 = jnp.bfloat16
ANY = pl.BlockSpec(memory_space=pl.ANY)
VMEM = pl.BlockSpec(memory_space=pltpu.VMEM)
SMEM = pl.BlockSpec(memory_space=pltpu.SMEM)


PIECES = {
    "C": (0, 2),
    "A": (2, 1),
    "B": (3, 1),
    "D": (4, 2),
    "CA": (0, 3),
    "AB": (2, 2),
    "BD": (3, 3),
}


def piece(name, rows):
    first, size = PIECES[name]
    return pl.ds(first * (rows // 6), size * (rows // 6))


class Place:
    def __init__(self):
        dp, sub = lax.axis_index("dp"), lax.axis_index("sub")
        self.z, self.y, self.x, self.c = dp // 2, dp % 2, sub // 2, sub % 2

    def dev(self, z=None, y=None, x=None, c=None):
        z = self.z if z is None else z
        y = self.y if y is None else y
        x = self.x if x is None else x
        c = self.c if c is None else c
        return (z * 2 + y, x * 2 + c)

    def zk(self, k):
        return (self.z + k) % 4


def now(ref):
    return ref() if callable(ref) else ref


def spot(ref, index):
    return lambda: ref.at[index]


def only_if(condition, action):
    if condition is None:
        action()
    else:
        pl.when(condition())(action)


class Flight:
    def __init__(self, sems, ref, send_index, recv_index):
        self.sems, self.ref, self.send_index, self.recv_index = sems, ref, send_index, recv_index

    def made(self):
        place = self.sems.place
        return pltpu.make_async_remote_copy(
            src_ref=now(self.ref),
            dst_ref=now(self.ref),
            send_sem=self.sems.send.at[self.send_index],
            recv_sem=self.sems.recv.at[self.recv_index],
            device_id=place.dev(c=1 - place.c),
            device_id_type=MESH_ID,
        )

    def wait_send(self):
        self.made().wait_send()

    def wait_recv(self):
        self.made().wait_recv()


class Sems:
    def __init__(self, place, send, recv):
        self.place, self.send, self.recv, self.count, self.sent = place, send, recv, 0, []

    def reserve(self, n):
        self.count += n
        return self.count - n

    def start(self, src, dst, device, send_index, recv_index, condition=None, later=True):
        def action():
            pltpu.make_async_remote_copy(
                src_ref=now(src),
                dst_ref=now(dst),
                send_sem=self.send.at[send_index],
                recv_sem=self.recv.at[recv_index],
                device_id=device,
                device_id_type=MESH_ID,
            ).start()

        only_if(condition, action)
        flight = Flight(self, dst, send_index, recv_index)
        if later:
            self.sent.append((condition, flight))
        return flight

    def copy(self, src, dst, device, later=True):
        index = self.reserve(1)
        return self.start(src, dst, device, index, index, later=later)

    def drain(self):
        for condition, flight in self.sent:
            only_if(condition, flight.wait_send)


def greet(place, devices):
    barrier = pltpu.get_barrier_semaphore()
    for device in devices:
        pl.semaphore_signal(barrier, inc=1, device_id=device, device_id_type=MESH_ID)
    pl.semaphore_wait(barrier, len(devices))


def wait_all(copies):
    for made in copies:
        made.wait_recv()


class Spread:
    def __init__(self, sems, src, where):
        self.sems, self.where, place = sems, where, sems.place
        self.base = sems.reserve(4)
        z = place.z
        for k, condition in ((1, lambda: z != 3), (2, None), (3, lambda: z != 0)):
            at = self.base + k - 1
            sems.start(src, where(z), place.dev(z=place.zk(k)), at, at, condition)

    def arrived(self, k):
        origin = self.sems.place.zk(4 - k)
        Flight(self.sems, self.where(origin), self.base + 3, self.base + k - 1).wait_recv()

    def forward(self):
        self.arrived(2)
        place = self.sems.place
        block = self.where(place.zk(2))
        for z, target, k in ((2, 3, 3), (1, 0, 1)):
            self.sems.start(
                block,
                block,
                place.dev(z=target),
                self.base + 3,
                self.base + k - 1,
                functools.partial(lambda z: place.z == z, z),
            )

    def finish(self):
        self.arrived(1)
        self.arrived(3)


class Collect:
    def __init__(self, sems, part, into, through):
        self.sems, self.part, self.into, self.through = sems, part, into, through
        place = sems.place
        self.base = sems.reserve(4)
        z = place.z
        for k, condition in (
            (1, lambda: z != 3),
            (2, lambda: (z == 0) | (z == 3)),
            (3, lambda: z != 0),
        ):
            self.send(k, condition)
        for k, end, middle in ((1, 3, 2), (3, 0, 1)):
            at = self.base + 3
            sems.start(part(place.zk(k)), through, place.dev(z=middle), at, at, functools.partial(lambda end: z == end, end))

    def send(self, k, condition):
        place, at = self.sems.place, self.base + k - 1
        self.sems.start(
            self.part(place.zk(k)),
            spot(self.into, k - 1),
            place.dev(z=place.zk(k)),
            at,
            at,
            condition,
        )

    def forward(self, add):
        place = self.sems.place

        def middle():
            return (place.z == 1) | (place.z == 2)

        @pl.when(middle())
        def _():
            Flight(self.sems, self.through, self.base + 3, self.base + 3).wait_recv()
            add(place.zk(2))

        self.send(2, middle)

    def finish(self):
        z = self.sems.place.z
        for k, condition in ((1, lambda: z != 0), (2, None), (3, lambda: z != 3)):
            flight = Flight(self.sems, spot(self.into, k - 1), self.base + 3, self.base + k - 1)
            only_if(condition, flight.wait_recv)


def slots(count, places, order):
    steps = []
    for slot in range(min(places.values()), count + max(places.values())):
        for name in order:
            i = slot - places[name]
            if 0 <= i < count:
                steps.append((slot, name, i))
    return steps


def dot(a, b):
    return jnp.dot(a, b, preferred_element_type=F32)


def dot_nt(a, b):
    return lax.dot_general(a, b, (((1,), (1,)), ((), ())), preferred_element_type=F32)


def low(values):
    return values.astype(BF16)


def normed(values):
    centred = values - jnp.mean(values, axis=-1, keepdims=True)
    inverse = lax.rsqrt(jnp.mean(centred * centred, axis=-1, keepdims=True) + EPSILON)
    return centred * inverse, inverse


def gelu_both(u):
    k, a = 0.7978845608028654, 0.044715
    square = u * u
    t = jnp.tanh(k * u * (1.0 + a * square))
    half = 0.5 * (1.0 + t)
    slope = half + (0.5 * k) * u * (1.0 - t * t) * (1.0 + (3.0 * a) * square)
    return u * half, slope


def square_block(ref, x, c):
    halves = []
    for h in range(2):
        block = ref[h, x, c]
        halves.append(block.reshape(-1, block.shape[3]))
    return jnp.concatenate(halves, axis=1)


def hidden_block(ref, z):
    parts = []
    for y in range(2):
        rows = [ref[h, x, c, z, y] for x in range(2) for c in range(2) for h in range(2)]
        parts.append(jnp.concatenate(rows, axis=0))
    return jnp.concatenate(parts, axis=1)


def left_half(shape):
    return lax.broadcasted_iota(jnp.int32, shape, 1) < 64


def stack_heads(values):
    left = left_half(values.shape)
    zero = jnp.zeros_like(values)
    return jnp.concatenate([jnp.where(left, values, zero), jnp.where(left, zero, values)], axis=0)


def join_heads(values):
    rows = values.shape[0] // 2
    top, bottom = values[:rows], values[rows:]
    return jnp.where(left_half(top.shape), top, bottom)


def lanes(index, size):
    return pl.ds(pl.multiple_of(index * size, size), size)


def kept_shapes(rows, tokens, width, hidden):
    two = 2 * rows
    return {
        "cq": ((rows, width), BF16),
        "kv": ((2, tokens, width), BF16),
        "cp": ((width // 128, two, tokens), BF16),
        "co": ((rows, width), F32),
        "mid": ((rows, width), F32),
        "gpc": ((rows, hidden), BF16),
        "ac": ((two, width), F32),
        "sqkv": ((3, two, width), BF16),
        "sp": ((2 * (width // 128), two, rows), BF16),
        "aa": ((two, width), F32),
        "gps": ((two, hidden), BF16),
        "xl": ((tokens, width), BF16),
    }


def paired_shapes(rows, tokens, width, hidden):
    two = 2 * rows
    return {
        "gyt": ((2, width // 4, 2 * two), BF16),
        "mh": ((2 * two, hidden), BF16),
        "mnt": ((width, 2 * two), BF16),
        "sbt": ((width, 2 * two), BF16),
        "l1t": ((width, 2 * two), BF16),
        "ch": ((two, hidden), BF16),
        "cnt": ((width, two), BF16),
        "lst": ((width, two), BF16),
        "xbt": ((width, 2 * tokens), BF16),
    }


def forward_kernel(names, dims, *refs):
    rows, tokens, width, hidden = dims
    two = 2 * rows
    count = 6
    refs = list(refs)

    def take(n):
        out = refs[:n]
        del refs[:n]
        return out

    own = take(count)
    gain, lat, tok, cot, live_counts, flags = take(6)
    full = take(count)
    gain_out, result = take(2)
    kept = dict(zip(names, take(len(names))))
    gain_all, lat_v, cot_v, tok_v, z2, xb, xbt, gyt, lst, wr0, wr1, wt = take(12)
    cq, kv, cp, co, mid, ch, gpc, ac, sqkv, sp, so, aa, mh, gps, xl, lt, cnt, mnt = take(18)
    gain_own, gain_one, zb_v, nb = take(4)
    send, recv, local = take(3)
    wr = (wr0, wr1)
    place = Place()
    x, y, z, c = place.x, place.y, place.z, place.c
    sems = Sems(place, send, recv)
    local_count = [0]
    local_open = []

    def local_copy(src, dst):
        made = pltpu.make_async_copy(src, dst, local.at[local_count[0]])
        local_count[0] += 1
        made.start()
        return made

    in_gain = local_copy(gain, gain_own)
    in_lat, in_tok, in_cot = local_copy(lat, lat_v), local_copy(tok, tok_v), local_copy(cot, cot_v)
    px, py, pc = place.dev(x=1 - x), place.dev(y=1 - y), place.dev(c=1 - c)
    me_dp = z * 2 + y
    dp_peers = [((me_dp + k) % 8, x * 2 + c) for k in range(1, 8)]
    greet(place, dp_peers + [px, pc])

    halves = 2 * count
    blocks = [full[i // 2].at[i % 2] for i in range(halves)]
    ones, twos, threes, across, placed = {}, {}, {}, {i: [] for i in range(halves)}, {}
    block_rows = full[0].shape[5]

    def shard(i):
        w, h = own[i // 2], i % 2
        if w.shape[0] == block_rows:
            return w, slice(None), pl.ds(h * (w.shape[1] // 2), w.shape[1] // 2), 0
        return w, slice(None), pl.ds(0, w.shape[1]), h * block_rows

    def own_piece(i, name):
        w, unused, columns, first = shard(i)
        at = piece(name, block_rows)
        return w.at[pl.ds(first + at.start, at.size), columns]

    def step_one(i):
        g = blocks[i]
        w, unused, columns, first = shard(i)
        placed[i] = local_copy(w.at[pl.ds(first, block_rows), columns], g.at[x, c, z, y])
        ab, pc_, pd = (piece(n, block_rows) for n in ("AB", "C", "D"))
        spread = Spread(sems, own_piece(i, "AB"), lambda o: g.at[x, c, o, y, ab])
        ones[i] = (
            spread,
            [
                sems.copy(own_piece(i, "C"), g.at[x, c, z, y, pc_], px),
                sems.copy(own_piece(i, "D"), g.at[x, c, z, y, pd], py),
            ],
        )

    def step_one_forward(i):
        ones[i][0].forward()

    def step_two(i):
        g = blocks[i]
        spread, got = ones.pop(i)
        placed.pop(i).wait()
        wait_all(got)
        pa, pb, pc_, pd = (piece(n, block_rows) for n in ("A", "B", "C", "D"))
        spread_c = Spread(sems, g.at[:, c, z, y, pc_], lambda o: g.at[:, c, o, y, pc_])
        spread_d = Spread(sems, g.at[x, c, z, :, pd], lambda o: g.at[x, c, o, :, pd])
        spread.finish()
        got = [
            sems.copy(g.at[x, c, :, y, pa], g.at[x, c, :, y, pa], px),
            sems.copy(g.at[x, c, :, y, pb], g.at[x, c, :, y, pb], py),
        ]
        twos[i] = ((spread_c, spread_d), got)

    def step_two_forward(i):
        for spread in twos[i][0]:
            spread.forward()

    def step_three(i):
        g = blocks[i]
        spreads, got = twos.pop(i)
        for spread in spreads:
            spread.finish()
        wait_all(got)
        ca, bd = piece("CA", block_rows), piece("BD", block_rows)
        threes[i] = [
            sems.copy(g.at[:, c, :, y, ca], g.at[:, c, :, y, ca], py),
            sems.copy(g.at[x, c, :, :, bd], g.at[x, c, :, :, bd], px),
        ]
        across[i] += [
            sems.copy(g.at[:, c, :, y, ca], g.at[:, c, :, y, ca], pc),
            sems.copy(g.at[x, c, :, :, bd], g.at[x, c, :, :, bd], pc),
        ]

    def step_four(i):
        wait_all(threes.pop(i))
        g = blocks[i]
        ca, bd = piece("CA", block_rows), piece("BD", block_rows)
        across[i] += [
            sems.copy(g.at[:, c, :, 1 - y, ca], g.at[:, c, :, 1 - y, ca], pc),
            sems.copy(g.at[1 - x, c, :, :, bd], g.at[1 - x, c, :, :, bd], pc),
        ]

    loading = {}

    def load(m, dst):
        def begin():
            for h in range(2):
                wait_all(across.pop(2 * m + h))
            loading[m] = local_copy(full[m], dst)

        return begin

    def keep(name, src):
        local_open.append(local_copy(src, kept[name]))

    def pair(name, mine, theirs, axis_size, axis):
        here, there = pl.ds(0, axis_size), pl.ds(axis_size, axis_size)
        dst = kept[name]

        def part(where):
            return dst.at[where] if axis == 0 else dst.at[:, where] if axis == 1 else dst.at[:, :, where]

        local_open.append(local_copy(mine, part(here)))
        across_pairs.append(sems.copy(theirs, part(there), pc))

    across_pairs = []
    gain_copies = []

    def pick(flag_first, first, second):
        return jnp.where(flag_first, first, second)

    first_live = flags[0] == 0
    live_count = jnp.where(first_live, live_counts[0], live_counts[1])

    def send_gains():
        in_gain.wait()
        gain_one[...] = jnp.zeros_like(gain_one)
        gain_one[: gain.shape[0], : gain.shape[1]] = gain_own[...]
        gain_all[me_dp] = gain_one[...]
        for device in dp_peers:
            gain_copies.append(sems.copy(gain_one, gain_all.at[me_dp], device))

    def start():
        wait_all(gain_copies)
        row = lax.broadcasted_iota(jnp.int32, (128, width), 0)
        column = lax.broadcasted_iota(jnp.int32, (128, width), 1)
        share = width // 8
        gain_out[...] = jnp.zeros_like(gain_out)

        @pl.loop(0, 8)
        def _(i):
            spread = low(jnp.where((column == row + share * i) & (row < share), 1.0, 0.0))
            gain_out[...] += dot(gain_all[i], spread)

        in_lat.wait()
        in_cot.wait()
        z2[:rows] = pick(first_live, lat_v[0], lat_v[1])
        z2[rows:] = pick(first_live, lat_v[1], lat_v[0])
        zb = low(normed(z2[:rows])[0] * gain_out[0:1])
        zb_v[...] = zb
        lst[0] = zb.T
        gy_first = low(pick(first_live, cot_v[0], cot_v[1]))
        gy_last = low(pick(first_live, cot_v[1], cot_v[0]))
        gyt[:, :, :, :rows] = gy_first.T.reshape(2, 2, width // 4, rows)
        gyt[:, :, :, rows:] = gy_last.T.reshape(2, 2, width // 4, rows)
        pair("gyt", gyt.at[:, c], gyt.at[:, 1 - c], two, 2)

    def tokens_part(first, last):
        def run():
            if first == 0:
                in_tok.wait()

            @pl.loop(first, last)
            def _(i):
                at = lanes(i, 128)
                here = pick(first_live, tok_v[0, at], tok_v[1, at])
                xl[at] = here
                value = low(normed(here.astype(F32))[0] * gain_out[1:2])
                xb[at] = value
                xbt[:, at] = value.T

            if last == tokens // 128:
                keep("xl", xl)
                pair("xbt", xbt, xbt, tokens, 1)

        return run

    def cross_queries():
        loading[0].wait()
        cq[...] = low(dot(zb_v[...], square_block(wr[0], 0, 0)))
        keep("cq", cq)

    def keys_values(first, last):
        def run():
            for i in range(first, last):
                at = pl.ds(i * 256, 256)

                @pl.loop(0, 2)
                def _(j):
                    kv[j, at] = low(dot(xb[at], square_block(wr[0], j, 1 - j)))

            if last == tokens // 256:
                keep("kv", kv)

        return run

    def cross_attention(first, last):
        def run():
            @pl.loop(first, last)
            def _(p):
                at = lanes(p, 128)
                q = stack_heads(cq[:, at] * jnp.asarray(0.125, BF16))
                s = dot_nt(q, kv[0, :, at])
                s = jnp.where(lax.broadcasted_iota(jnp.int32, s.shape, 1) < live_count, s, MASKED)
                e = jnp.exp(s - jnp.max(s, axis=-1, keepdims=True))
                prob = low(e * (1.0 / jnp.sum(e, axis=-1, keepdims=True)))
                cp[p] = prob
                co[:, at] = join_heads(dot(prob, kv[1, :, at]))

            if last == width // 128:
                keep("cp", cp)
                keep("co", co)

        return run

    def cross_out():
        cob = low(co[...])
        lst[1] = cob.T
        pair("lst", lst.at[c], lst.at[1 - c], rows, 1)
        mid[...] = z2[:rows] + dot(cob, square_block(wr[0], 1, 1))
        keep("mid", mid)
        cnb = low(normed(mid[...])[0] * gain_out[2:3])
        nb[:rows] = cnb
        cnt[...] = cnb.T
        pair("cnt", cnt, cnt, rows, 1)

    def up(m, w, left, out, slope, first, last, after):
        def run():
            if first == 0:
                loading[m].wait()

            @pl.loop(first, last)
            def _(s):
                at = lanes(s, hidden // 4)
                value, grad = gelu_both(dot(nb[:left], square_block(w, s // 2, s % 2)))
                out[:, at] = low(value)
                slope[:, at] = low(grad)

            if last == 4:
                after()

        return run

    def down(m, act, into):
        loading[m].wait()

        @pl.loop(0, 4)
        def _(s):
            into[...] += dot_nt(act[:, lanes(s, hidden // 4)], hidden_block(wt, s))

    def cross_up_done():
        pair("ch", ch, ch, rows, 0)
        keep("gpc", gpc)

    def self_up_done():
        pair("mh", mh, mh, two, 0)
        keep("gps", gps)

    def cross_down():
        ac[:rows] = mid[...]
        ac[rows:] = z2[rows:]
        down(2, ch, ac.at[pl.ds(0, rows)])
        keep("ac", ac)
        sb = low(normed(ac[...])[0] * gain_out[3:4])
        nb[...] = sb
        lt[0] = sb.T
        pair("sbt", lt.at[0], lt.at[0], two, 1)

    def self_project():
        loading[3].wait()
        @pl.loop(0, 3)
        def _(i):
            sqkv[i] = low(dot(nb[...], square_block(wr[0], i // 2, i % 2)))

        keep("sqkv", sqkv)

    def self_attention(first, last):
        pairs = width // 128

        def run():
            @pl.loop(first, last, unroll=3)
            def _(i):
                at, row_at = lanes(i % pairs, 128), lanes(i // pairs, rows)
                q = stack_heads(sqkv[0, row_at, at] * jnp.asarray(0.125, BF16))
                s = dot_nt(q, sqkv[1, row_at, at])
                e = jnp.exp(s - jnp.max(s, axis=-1, keepdims=True))
                prob = low(e * (1.0 / jnp.sum(e, axis=-1, keepdims=True)))
                sp[i] = prob
                so[row_at, at] = low(join_heads(dot(prob, sqkv[2, row_at, at])))

            if last == 2 * pairs:
                keep("sp", sp)

        return run

    def self_out():
        lt[1] = so[...].T
        pair("l1t", lt.at[c], lt.at[1 - c], two, 1)
        aa[...] = ac[...] + dot(so[...], square_block(wr[0], 1, 1))
        keep("aa", aa)
        mnb = low(normed(aa[...])[0] * gain_out[4:5])
        nb[...] = mnb
        mnt[...] = mnb.T
        pair("mnt", mnt, mnt, two, 1)

    def self_down():
        z2[...] = aa[...]
        down(5, mh, z2)
        total = z2[...]
        result[0] = pick(first_live, total[:rows], total[rows:])
        result[1] = pick(first_live, total[rows:], total[:rows])

    pairs = width // 128
    work = collections.deque([(-2, send_gains), (1, start)])
    for n in range(4):
        work.append((1, tokens_part(n * tokens // 512, (n + 1) * tokens // 512)))
    for slot, part in (
        (4, load(0, wr[0])),
        (4, cross_queries),
        (4, keys_values(0, 1)),
        (4, keys_values(1, 2)),
        (4, keys_values(2, 3)),
        (4, keys_values(3, tokens // 256)),
        (4, cross_attention(0, 2)),
        (4, cross_attention(2, 4)),
        (4, cross_attention(4, pairs)),
        (4, cross_out),
        (6, load(1, wr[1])),
        (6, up(1, wr[1], rows, ch, gpc, 0, 2, cross_up_done)),
        (6, up(1, wr[1], rows, ch, gpc, 2, 4, cross_up_done)),
        (8, load(2, wt)),
        (8, cross_down),
        (10, load(3, wr[0])),
        (10, self_project),
        (10, self_attention(0, pairs)),
        (10, self_attention(pairs, 2 * pairs)),
        (10, self_out),
        (12, load(4, wr[1])),
        (12, up(4, wr[1], two, mh, gps, 0, 2, self_up_done)),
        (12, up(4, wr[1], two, mh, gps, 2, 4, self_up_done)),
        (14, load(5, wt)),
        (14, self_down),
    ):
        work.append((slot, part))
    steps = {
        "1": step_one,
        "f": step_one_forward,
        "2": step_two,
        "g": step_two_forward,
        "3": step_three,
        "4": step_four,
    }
    places = {"1": -2, "f": -1, "2": 0, "g": 0, "3": 1, "4": 2}
    for slot, name, i in slots(halves, places, "231fg4"):
        steps[name](i)
        if work and work[0][0] <= slot:
            work.popleft()[1]()
    while work:
        work.popleft()[1]()
    wait_all(across_pairs)
    for made in local_open:
        made.wait()
    sems.drain()


def half_shape(shard):
    return shard.shape[0], shard.shape[1] // 2


def forward_all(own, gain, latents, inputs, cotangent, counts, flags):
    count = len(own)
    rows, width = latents.shape[1:]
    tokens = inputs.shape[1]
    hidden = own[1].shape[1] * 4
    dims = (rows, tokens, width, hidden)
    two = 2 * rows
    kept = {**kept_shapes(*dims), **paired_shapes(*dims)}
    names = tuple(kept)
    copies = 7 + 2 * count * (6 + 10 + 4 + 2) + len(paired_shapes(*dims))
    block = (2, 2, 2, 4, 2) + half_shape(own[0])
    shapes = [jax.ShapeDtypeStruct(block, BF16) for w in own]
    shapes += [
        jax.ShapeDtypeStruct((16, width), F32),
        jax.ShapeDtypeStruct(latents.shape, F32),
    ]
    shapes += [jax.ShapeDtypeStruct(s, t) for s, t in kept.values()]
    pairs = width // 128
    scratch = [
        ((8, 16, 128), BF16),
        (latents.shape, F32),
        (latents.shape, F32),
        (inputs.shape, BF16),
        ((two, width), F32),
        ((tokens, width), BF16),
        ((width, tokens), BF16),
        ((2, 2, width // 4, two), BF16),
        ((2, width, rows), BF16),
        (block, BF16),
        (block, BF16),
        (block, BF16),
        ((rows, width), BF16),
        ((2, tokens, width), BF16),
        ((pairs, two, tokens), BF16),
        ((rows, width), F32),
        ((rows, width), F32),
        ((rows, hidden), BF16),
        ((rows, hidden), BF16),
        ((two, width), F32),
        ((3, two, width), BF16),
        ((2 * pairs, two, rows), BF16),
        ((two, width), BF16),
        ((two, width), F32),
        ((two, hidden), BF16),
        ((two, hidden), BF16),
        ((tokens, width), BF16),
        ((2, width, two), BF16),
        ((width, rows), BF16),
        ((width, two), BF16),
        (gain.shape, BF16),
        ((16, 128), BF16),
        ((rows, width), BF16),
        ((two, width), BF16),
    ]
    outs = pl.pallas_call(
        functools.partial(forward_kernel, names, dims),
        out_shape=shapes,
        in_specs=[ANY] * (count + 4) + [SMEM, SMEM],
        out_specs=[ANY] * count + [VMEM, VMEM] + [ANY] * len(names),
        scratch_shapes=[pltpu.VMEM(s, t) for s, t in scratch]
        + [
            pltpu.SemaphoreType.DMA((copies,)),
            pltpu.SemaphoreType.DMA((copies,)),
            pltpu.SemaphoreType.DMA((5 + 3 * count + len(names),)),
        ],
        compiler_params=pltpu.CompilerParams(
            collective_id=0, has_side_effects=True, vmem_limit_bytes=60 << 20
        ),
        name="gather_and_forward",
    )(*own, gain, latents, inputs, cotangent, counts, flags)
    full, (norm_gain, result) = outs[:count], outs[count : count + 2]
    return full, norm_gain, result, dict(zip(names, outs[count + 2 :]))


def norm_back(values, gain_row, gradient):
    unit, inverse = normed(values)
    scaled = gradient * gain_row
    grad = inverse * (
        scaled
        - jnp.mean(scaled, axis=-1, keepdims=True)
        - unit * jnp.mean(scaled * unit, axis=-1, keepdims=True)
    )
    return grad, jnp.sum(gradient * unit, axis=0, keepdims=True)


def attention_back(q, k, v, out_grad, prob, delta):
    prob_grad = dot_nt(out_grad, v)
    weight = prob.astype(F32)
    if delta is None:
        delta = jnp.sum(weight * prob_grad, axis=-1, keepdims=True)
    score_grad = low(weight * (prob_grad - delta))
    q_grad = join_heads(dot(score_grad, k)) * 0.125
    k_grad = low(dot(q.T, score_grad) * 0.125).T
    v_grad = low(dot(out_grad.T, prob)).T
    return low(q_grad), k_grad, v_grad


def add_blocks(total, where, part, there):
    total[where] = (total[where].astype(F32) + part[there].astype(F32)).astype(BF16)


def backward_kernel(names, dims, *refs):
    rows, tokens, width, hidden = dims
    two, quarter, pairs = 2 * rows, hidden // 4, width // 128
    count = 6
    halves, ring = 2 * count, 3
    order = (5, 4, 3, 2, 1, 0)
    refs = list(refs)

    def take(n):
        out = refs[:n]
        del refs[:n]
        return out

    full = take(count)
    gain, lat, cot, flags = take(4)
    kept = dict(zip(names, take(len(names))))
    outs = take(count)
    gain_out, lat_grad, dx = take(3)
    total = take(count)
    from_y, from_x = take(ring), take(ring)
    from_a, from_b, from_c, from_d, from_z, end_c, end_d = (take(halves) for _ in range(7))
    by_c, by_d, by_z = (take(halves) for _ in range(3))
    wr, wt, grad_ac, du_sib, r_sib, ge_sib, dcu_sib, rs_sib, dkv_sib = take(9)
    gain_acc, gain_sub, gain_dp, send, recv, local, free = take(7)
    place = Place()
    x, y, z, c = place.x, place.y, place.z, place.c
    sems = Sems(place, send, recv)
    local_count = [0]

    def local_copy(src, dst):
        made = pltpu.make_async_copy(src, dst, local.at[local_count[0]])
        local_count[0] += 1
        made.start()
        return made

    me_dp, me_sub = z * 2 + y, x * 2 + c
    sub_peers = [(me_dp, (me_sub + k) % 4) for k in (1, 2, 3)]
    dp_peers = [((me_dp + k) % 8, me_sub) for k in range(1, 8)]
    px, py, pc = place.dev(x=1 - x), place.dev(y=1 - y), place.dev(c=1 - c)
    first_live = flags[0] == 0
    gain_acc[...] = jnp.zeros_like(gain_acc)

    ones, twos, threes = {}, {}, {}
    block_rows, block_columns = total[0].shape[4:]

    def where(i):
        return total[order[i // 2]], i % 2

    def clear():
        for into in (*from_c, *from_d, *from_z):

            @pl.when(z == 0)
            def _():
                into[0] = jnp.zeros(into.shape[1:], BF16)

            @pl.when(z == 3)
            def _():
                into[2] = jnp.zeros(into.shape[1:], BF16)

    def step_one(i):
        a, h = where(i)
        if i >= ring:
            pl.semaphore_wait(free.at[i - ring], 2)
        ones[i] = [
            sems.copy(a.at[h, :, :, 1 - y, piece("CA", block_rows)], from_y[i % ring], py),
            sems.copy(a.at[h, 1 - x, :, :, piece("BD", block_rows)], from_x[i % ring], px),
        ]

    def step_two(i):
        a, h = where(i)
        wait_all(ones.pop(i))
        ca, bd = piece("CA", block_rows), piece("BD", block_rows)
        pa, pb, pc_, pd = (piece(n, block_rows) for n in ("A", "B", "C", "D"))
        fy, fx = from_y[i % ring], from_x[i % ring]

        @pl.loop(0, 8)
        def _(j):
            add_blocks(a, (h, j // 4, j % 4, y, ca), fy, (j // 4, j % 4))
            add_blocks(a, (h, x, j // 2, j % 2, bd), fx, (j // 2, j % 2))

        if i + ring < halves:
            for device in (px, py):
                pl.semaphore_signal(free.at[i], inc=1, device_id=device, device_id_type=MESH_ID)
        collect_c = Collect(sems, lambda o: a.at[h, :, o, y, pc_], from_c[i], by_c[i])
        collect_d = Collect(sems, lambda o: a.at[h, x, o, :, pd], from_d[i], by_d[i])
        got = [
            sems.copy(a.at[h, 1 - x, :, y, pa], from_a[i], px),
            sems.copy(a.at[h, x, :, 1 - y, pb], from_b[i], py),
        ]
        twos[i] = (collect_c, collect_d, got)

    def step_two_forward(i):
        a, h = where(i)
        pc_, pd = piece("C", block_rows), piece("D", block_rows)

        def add_c(o):
            for j in range(2):
                add_blocks(a, (h, j, o, y, pc_), by_c[i], j)

        def add_d(o):
            for j in range(2):
                add_blocks(a, (h, x, o, j, pd), by_d[i], j)

        twos[i][0].part = lambda o: a.at[h, :, o, y, pc_]
        twos[i][1].part = lambda o: a.at[h, x, o, :, pd]
        twos[i][0].forward(add_c)
        twos[i][1].forward(add_d)

    def step_three(i):
        a, h = where(i)
        collect_c, collect_d, got = twos.pop(i)
        collect_c.finish()
        collect_d.finish()
        wait_all(got)
        pa, pb, pc_, pd = (piece(n, block_rows) for n in ("A", "B", "C", "D"))
        fc, fd = from_c[i], from_d[i]

        @pl.loop(0, 4)
        def _(j):
            add_blocks(a, (h, x, j, y, pa), from_a[i], j)
            add_blocks(a, (h, x, j, y, pb), from_b[i], j)

        @pl.loop(0, 2)
        def _(j):
            a[h, j, z, y, pc_] = low(
                a[h, j, z, y, pc_].astype(F32)
                + fc[0, j].astype(F32)
                + fc[1, j].astype(F32)
                + fc[2, j].astype(F32)
            )
            a[h, x, z, j, pd] = low(
                a[h, x, z, j, pd].astype(F32)
                + fd[0, j].astype(F32)
                + fd[1, j].astype(F32)
                + fd[2, j].astype(F32)
            )

        ab = piece("AB", block_rows)
        collect = Collect(sems, lambda o: a.at[h, x, o, y, ab], from_z[i], by_z[i])
        got = [
            sems.copy(a.at[h, 1 - x, z, y, pc_], end_c[i], px),
            sems.copy(a.at[h, x, z, 1 - y, pd], end_d[i], py),
        ]
        threes[i] = (collect, got)

    def step_three_forward(i):
        a, h = where(i)
        ab = piece("AB", block_rows)
        collect = threes[i][0]
        collect.part = lambda o: a.at[h, x, o, y, ab]
        collect.forward(lambda o: add_blocks(a, (h, x, o, y, ab), by_z[i], ...))

    def step_four(i):
        a, h = where(i)
        collect, got = threes.pop(i)
        collect.finish()
        wait_all(got)
        fz, o = from_z[i], outs[order[i // 2]]
        if o.shape[0] == block_rows:
            first, columns = 0, pl.ds(h * block_columns, block_columns)
        else:
            first, columns = h * block_rows, slice(None)

        def put(name, value):
            at = piece(name, block_rows)
            o[pl.ds(first + at.start, at.size), columns] = (
                a[h, x, z, y, at].astype(F32) + value
            )

        put("AB", fz[0].astype(F32) + fz[1].astype(F32) + fz[2].astype(F32))
        put("C", end_c[i][...].astype(F32))
        put("D", end_d[i][...].astype(F32))

    run_step = {
        "1": step_one,
        "2": step_two,
        "g": step_two_forward,
        "3": step_three,
        "f": step_three_forward,
        "4": step_four,
    }
    places = {"1": 0, "2": 1, "g": 2, "3": 3, "f": 4, "4": 5}
    steps = collections.deque(slots(halves, places, "12g3f4"))
    ready = [0]

    def advance(n):
        while n > 0 and steps and (steps[0][1] != "1" or steps[0][2] < ready[0]):
            unused, name, i = steps.popleft()
            run_step[name](i)
            n -= 1

    def done(m):
        ready[0] += 2
        advance(2)

    def square_grad(m, at, products):
        size = 4 * block_rows

        @pl.loop(0, 2)
        def _(n):
            rows_at = pl.ds(pl.multiple_of(n * size, size), size)
            value = None
            for left, right in products:
                term = dot(left[rows_at], right())
                value = term if value is None else value + term
            for h in range(2):
                part = low(value[:, h * block_columns : (h + 1) * block_columns])
                total[m][h, at, pl.ds(n * 2, 2)] = part.reshape(2, 2, block_rows, block_columns)

    def put_hidden(m, h, zz, value):
        for yy in range(2):
            part = value[:, yy * block_columns : (yy + 1) * block_columns]
            total[m][h, :, zz, yy] = low(part).reshape(2, block_rows, block_columns)

    def hidden_grad(m, h, left, right):
        @pl.loop(0, 4)
        def _(zz):
            put_hidden(m, h, zz, dot(left, right[:, lanes(zz, quarter)]))

    def both(own, other):
        return jnp.concatenate([own, other], axis=0)

    def send_off(src, dst):
        return sems.copy(src, dst, pc, later=False)

    def pick(first, second):
        return jnp.where(first_live, first, second)

    def back_through(into, act, blocks):
        into[...] = jnp.zeros_like(into)

        @pl.loop(0, blocks)
        def _(s):
            into[...] += dot_nt(act[s // 2, s % 2], square_block(wr, s // 2, s % 2))

    def self_part(mh, gps, gyt, mnt, sbt, l1t, du, r, cot_v, aa, ac, sqkv, sp, grad_aa, out_grad):
        loads = {
            name: local_copy(src, dst)
            for name, src, dst in (
                ("gyt", kept["gyt"], gyt),
                ("mh", kept["mh"], mh),
                ("wt", full[5], wt),
                ("cot", cot, cot_v),
                ("gps", kept["gps"], gps),
                ("wr", full[4], wr),
                ("aa", kept["aa"], aa),
                ("mnt", kept["mnt"], mnt),
                ("sqkv", kept["sqkv"], sqkv),
                ("sp", kept["sp"], sp),
                ("ac", kept["ac"], ac),
                ("sbt", kept["sbt"], sbt),
                ("l1t", kept["l1t"], l1t),
            )
        }
        clear()
        greet(place, sub_peers + dp_peers)
        loads["gyt"].wait()
        loads["mh"].wait()
        for h in range(2):
            left = gyt[:, h * block_rows : (h + 1) * block_rows]
            left = left.reshape(2 * block_rows, 2 * two)
            hidden_grad(5, h, left, mh)
            ready[0] += 1
            advance(1)

        for name in ("wt", "cot", "gps"):
            loads[name].wait()
        for at, value in (
            (pl.ds(0, rows), pick(cot_v[0], cot_v[1])),
            (pl.ds(rows, rows), pick(cot_v[1], cot_v[0])),
        ):
            grad_aa[at] = value
        out_grad[...] = low(grad_aa[...])

        @pl.loop(0, 4)
        def _(s):
            grad = dot(out_grad[...], hidden_block(wt, s))
            du[s // 2, s % 2] = low(grad * gps[:, lanes(s, quarter)].astype(F32))

        sent = send_off(du.at[:, 1 - c], du_sib)
        advance(2)
        for name in ("wr", "aa", "mnt"):
            loads[name].wait()
        back_through(grad_ac, du, 4)
        grad, gain_row = norm_back(aa[...], gain[4:5], grad_ac[...])
        grad_aa[...] += grad
        gain_acc[0, 4:5] = gain_row
        advance(2)
        next_wr = local_copy(full[3], wr)
        next_wt = local_copy(full[2], wt)
        sent.wait_recv()

        @pl.loop(0, 2)
        def _(a):
            square_grad(4, a, [(mnt, lambda: both(du[a, c], du_sib[a]))])

        done(4)

        r[1, 1] = low(grad_aa[...])
        for made in (next_wr, loads["sqkv"], loads["sp"], loads["ac"], loads["sbt"], loads["l1t"]):
            made.wait()
        out_grad[...] = low(dot_nt(r[1, 1], square_block(wr, 1, 1)))

        advance(2)
        for part in range(2):

            @pl.loop(part * pairs, (part + 1) * pairs, unroll=3)
            def _(i):
                at, row_at = lanes(i % pairs, 128), lanes(i // pairs, rows)
                r[0, 0, row_at, at], r[0, 1, row_at, at], r[1, 0, row_at, at] = attention_back(
                    stack_heads(sqkv[0, row_at, at]),
                    sqkv[1, row_at, at],
                    sqkv[2, row_at, at],
                    stack_heads(out_grad[row_at, at]),
                    sp[i],
                    None,
                )

            advance(2)

        sent_r = send_off(r.at[:, 1 - c], r_sib)
        back_through(grad_ac, r, 3)
        grad, gain_row = norm_back(ac[...], gain[3:4], grad_ac[...])
        grad_ac[...] = grad_aa[...] + grad
        gain_acc[0, 3:4] = gain_row
        advance(2)
        sent_r.wait_recv()
        square_grad(3, 0, [(sbt, lambda: both(r[0, c], r_sib[0]))])
        square_grad(3, 1, [(l1t, lambda: both(r[1, c], r_sib[1]))])
        done(3)
        sent.wait_send()
        sent_r.wait_send()
        next_wt.wait()

    def cross_part(
        ch, gpc, ge, cnt, du, mid, lst, rs, xbt, kv, cp, cq, co, dco, xl, dxs, lat_v, grad_mid
    ):
        loads = {
            name: local_copy(src, dst)
            for name, src, dst in (
                ("ch", kept["ch"], ch),
                ("gpc", kept["gpc"], gpc),
                ("wr", full[1], wr),
                ("mid", kept["mid"], mid),
                ("cnt", kept["cnt"], cnt),
                ("cq", kept["cq"], cq),
                ("co", kept["co"], co),
                ("kv", kept["kv"], kv),
                ("cp", kept["cp"], cp),
                ("lst", kept["lst"], lst),
                ("xbt", kept["xbt"], xbt),
                ("lat", lat, lat_v),
            )
        }
        for i in range(2):
            lat_grad_dead = grad_ac[rows:]
            lat_grad[i] = lat_grad_dead
        low_grad = low(grad_ac[:rows])
        ge[...] = low_grad.T.reshape(2, 2, width // 4, rows)
        sent = [send_off(ge.at[:, 1 - c], ge_sib)]
        loads["gpc"].wait()
        dco[...] = low_grad

        @pl.loop(0, 4)
        def _(s):
            grad = dot(dco[...], hidden_block(wt, s))
            du[s // 2, s % 2] = low(grad * gpc[:, lanes(s, quarter)].astype(F32))

        sent.append(send_off(du.at[:, 1 - c], dcu_sib))
        advance(2)
        loads["ch"].wait()
        sent[0].wait_recv()
        for h in range(2):
            at = pl.ds(h * block_rows, block_rows)
            left = [g.reshape(2 * block_rows, rows) for g in (ge[:, c, at], ge_sib[:, at])]
            hidden_grad(2, h, jnp.concatenate(left, axis=1), ch)
        done(2)

        for name in ("wr", "mid", "cnt"):
            loads[name].wait()
        back_through(grad_mid, du, 4)
        grad, gain_row = norm_back(mid[...], gain[2:3], grad_mid[...])
        grad_mid[...] = grad_ac[:rows] + grad
        gain_acc[0, 2:3] = gain_row
        advance(2)
        next_wr = local_copy(full[0], wr)
        sent[1].wait_recv()

        @pl.loop(0, 2)
        def _(a):
            square_grad(1, a, [(cnt, lambda: both(du[a, c], dcu_sib[a]))])

        done(1)

        rs[1] = low(grad_mid[...])
        next_wr.wait()
        dco[...] = low(dot_nt(rs[1], square_block(wr, 1, 1)))
        for name in ("cq", "co", "kv", "cp"):
            loads[name].wait()

        advance(2)
        for part in range(3):

            @pl.loop(part * pairs // 3, (part + 1) * pairs // 3, unroll=2)
            def _(p):
                at = lanes(p, 128)
                out_grad = stack_heads(dco[:, at])
                attended = co[:, at]
                delta = jnp.sum(
                    out_grad.astype(F32) * both(attended, attended), axis=-1, keepdims=True
                )
                rs[0, :, at], kv[0, :, at], kv[1, :, at] = attention_back(
                    stack_heads(cq[:, at]), kv[0, :, at], kv[1, :, at], out_grad, cp[p], delta
                )

            advance(2)

        sent.append(send_off(rs.at[1 - c], rs_sib))
        sent.append(send_off(kv.at[c], dkv_sib))
        advance(2)
        for name in ("lst", "xbt", "lat"):
            loads[name].wait()
        sent[2].wait_recv()
        sent[3].wait_recv()
        square_grad(0, c, [(lst, lambda: both(rs[c], rs_sib[...]))])
        own_tokens, their_tokens = (xbt.at[:, pl.ds(n * tokens, tokens)] for n in range(2))
        square_grad(
            0,
            1 - c,
            [(own_tokens, lambda: kv[1 - c]), (their_tokens, lambda: dkv_sib[...])],
        )
        done(0)

        grad, gain_row = norm_back(
            pick(lat_v[0], lat_v[1]), gain[0:1], dot_nt(rs[0], square_block(wr, 0, 0))
        )
        gain_acc[0, 0:1] = gain_row
        live_grad = grad_mid[...] + grad
        lat_grad[0] = pick(live_grad, lat_grad[0])
        lat_grad[1] = pick(lat_grad[1], live_grad)
        advance(2)
        out = []
        parts = tokens // 256

        def fetch(n):
            return [
                local_copy(kept["xl"].at[pl.ds(n * 256 + i * 128, 128)], xl.at[i]) for i in range(2)
            ]

        fetched = fetch(0)
        for n in range(parts):
            for made in fetched + out:
                made.wait()

            @pl.loop(0, 2)
            def _(i):
                at = pl.ds(pl.multiple_of(n * 256 + i * 128, 128), 128)
                term = dot_nt(kv[0, at], square_block(wr, 0, 1))
                term += dot_nt(kv[1, at], square_block(wr, 1, 0))
                grad, gain_row = norm_back(xl[i].astype(F32), gain[1:2], term)
                dxs[i] = grad
                gain_acc[0, 1:2] += gain_row

            if n + 1 < parts:
                fetched = fetch(n + 1)
            out = [
                local_copy(dxs.at[i], dx.at[pl.ds(n * 256 + i * 128, 128)]) for i in range(2)
            ]
            advance(3)
        for made in out:
            made.wait()
        gain_one = [sems.copy(gain_acc.at[0], spot(gain_sub, k), sub_peers[k]) for k in range(3)]
        advance(3)
        wait_all(gain_one)
        gain_acc[1] = gain_acc[0] + gain_sub[0] + gain_sub[1] + gain_sub[2]
        gain_two = [sems.copy(gain_acc.at[1], spot(gain_dp, k), dp_peers[k]) for k in range(7)]
        for made in sent:
            made.wait_send()
        return gain_two

    def vmem(*shape, dtype=BF16):
        return pltpu.VMEM(shape, dtype)

    holder = {}

    pl.run_scoped(
        self_part,
        vmem(2 * two, hidden),
        vmem(two, hidden),
        vmem(2, width // 4, 2 * two),
        vmem(width, 2 * two),
        vmem(width, 2 * two),
        vmem(width, 2 * two),
        vmem(2, 2, two, quarter),
        vmem(2, 2, two, width),
        vmem(2, rows, width, dtype=F32),
        vmem(two, width, dtype=F32),
        vmem(two, width, dtype=F32),
        vmem(3, two, width),
        vmem(2 * pairs, two, rows),
        vmem(two, width, dtype=F32),
        vmem(two, width),
    )

    def run_cross(*bufs):
        holder["gain"] = cross_part(*bufs)

    pl.run_scoped(
        run_cross,
        vmem(two, hidden),
        vmem(rows, hidden),
        vmem(2, 2, width // 4, rows),
        vmem(width, two),
        vmem(2, 2, rows, quarter),
        vmem(rows, width, dtype=F32),
        vmem(width, two),
        vmem(2, rows, width),
        vmem(width, 2 * tokens),
        vmem(2, tokens, width),
        vmem(pairs, two, tokens),
        vmem(rows, width),
        vmem(rows, width, dtype=F32),
        vmem(rows, width),
        vmem(2, 128, width),
        vmem(2, 128, width, dtype=F32),
        vmem(2, rows, width, dtype=F32),
        vmem(rows, width, dtype=F32),
    )
    advance(len(steps))
    wait_all(holder["gain"])
    gain_out[...] = gain_acc[1] + jnp.sum(gain_dp[...], axis=0)
    sems.drain()


def backward_all(shard, full, norm_gain, latents, cotangent, flags, kept):
    count = len(full)
    rows, width = latents.shape[1:]
    tokens, hidden = kept["xl"].shape[0], kept["mh"].shape[1]
    dims = (rows, tokens, width, hidden)
    two = 2 * rows
    copies = 10 + 6 + 2 * count * (2 + 10 + 6)
    ring, halves = 3, 2 * count
    block_rows, block_columns = full[0].shape[5:]

    def room(number, lead, sixths):
        return [pltpu.VMEM(lead + (block_rows * sixths // 6, block_columns), BF16)] * number

    scratch = [pltpu.VMEM((2,) + full[0].shape[2:], BF16)] * count
    scratch += room(ring, (2, 4), 3) + room(ring, (4, 2), 3)
    scratch += room(halves, (4,), 1) + room(halves, (4,), 1)
    scratch += room(halves, (3, 2), 2) + room(halves, (3, 2), 2) + room(halves, (3,), 2)
    scratch += room(halves, (), 2) + room(halves, (), 2)
    scratch += room(halves, (2,), 2) + room(halves, (2,), 2) + room(halves, (), 2)
    scratch += [
        pltpu.VMEM(full[0].shape, BF16),
        pltpu.VMEM(full[2].shape, BF16),
        pltpu.VMEM((two, width), F32),
        pltpu.VMEM((2, two, hidden // 4), BF16),
        pltpu.VMEM((2, two, width), BF16),
        pltpu.VMEM((2, width // 4, rows), BF16),
        pltpu.VMEM((2, rows, hidden // 4), BF16),
        pltpu.VMEM((rows, width), BF16),
        pltpu.VMEM((tokens, width), BF16),
        pltpu.VMEM((2, 8, width), F32),
        pltpu.VMEM((3, 8, width), F32),
        pltpu.VMEM((7, 8, width), F32),
        pltpu.SemaphoreType.DMA((copies,)),
        pltpu.SemaphoreType.DMA((copies,)),
        pltpu.SemaphoreType.DMA((48,)),
        pltpu.SemaphoreType.REGULAR((halves - ring,)),
    ]
    shapes = [jax.ShapeDtypeStruct(d, F32) for d in shard]
    shapes += [
        jax.ShapeDtypeStruct((8, width), F32),
        jax.ShapeDtypeStruct(latents.shape, F32),
        jax.ShapeDtypeStruct((tokens, width), F32),
    ]
    outs = pl.pallas_call(
        functools.partial(backward_kernel, tuple(kept), dims),
        out_shape=shapes,
        in_specs=[ANY] * count + [VMEM, ANY, ANY, SMEM] + [ANY] * len(kept),
        out_specs=[VMEM] * (count + 2) + [ANY],
        scratch_shapes=scratch,
        compiler_params=pltpu.CompilerParams(
            collective_id=1, has_side_effects=True, vmem_limit_bytes=60 << 20
        ),
        name="backward_and_scatter",
    )(*full, norm_gain, latents, cotangent, flags, *kept.values())
    return outs[:count], *outs[count:]


def finish_kernel(gain_share, gain_rows, count, *refs):
    flags, result, lat_grad, tok_grad, gain_total = refs[:5]
    shards_in = refs[5 : 5 + count]
    out_result, out_lat, out_tok, out_gain = refs[5 + count : 9 + count]
    shards_out = refs[9 + count : 9 + 2 * count]
    gain_in, zeros, sems_in, sems_out = refs[9 + 2 * count : 13 + 2 * count]
    held = refs[13 + 2 * count :]
    tokens, pieces = tok_grad.shape[0], held[-1].shape[0]
    size = tokens // pieces
    live = jnp.where(flags[0] == 0, 0, 1)
    moves = []
    for n in range(pieces):
        at = pl.ds(n * size, size)
        moves.append((tok_grad.at[at], held[-1].at[n], out_tok.at[live, at]))
    moves += zip((result, lat_grad, *shards_in), held, (out_result, out_lat, *shards_out))
    gain_copy = pltpu.make_async_copy(gain_total, gain_in, sems_in.at[len(moves)])
    reads = [
        pltpu.make_async_copy(src, room, sems_in.at[i]) for i, (src, room, dst) in enumerate(moves)
    ]
    for made in reads:
        made.start()
    gain_copy.start()
    zeros[...] = jnp.zeros_like(zeros)
    started = []
    for n in range(pieces):
        started.append(
            pltpu.make_async_copy(
                zeros, out_tok.at[1 - live, pl.ds(n * size, size)], sems_out.at[len(moves) + n]
            )
        )
        started[-1].start()
    for i, (src, room, dst) in enumerate(moves):
        reads[i].wait()
        started.append(pltpu.make_async_copy(room, dst, sems_out.at[i]))
        started[-1].start()
    gain_copy.wait()
    dp = lax.axis_index("dp")
    for i in range(8):

        @pl.when(dp == i)
        def _():
            out_gain[...] = gain_in[:gain_rows, i * gain_share : (i + 1) * gain_share]

    for made in started:
        made.wait()


def finish_all(gain_shape, flags, result, lat_grad, tok_grad, gain_total, shards_in):
    count, pieces = len(shards_in), 4
    tokens, width = tok_grad.shape
    arrays = [result, lat_grad, tok_grad, gain_total, *shards_in]
    shapes = [
        jax.ShapeDtypeStruct(result.shape, F32),
        jax.ShapeDtypeStruct(lat_grad.shape, F32),
        jax.ShapeDtypeStruct((2, tokens, width), F32),
        jax.ShapeDtypeStruct(gain_shape, F32),
    ]
    shapes += [jax.ShapeDtypeStruct(a.shape, F32) for a in shards_in]
    return pl.pallas_call(
        functools.partial(finish_kernel, gain_shape[1], gain_shape[0], count),
        out_shape=shapes,
        in_specs=[SMEM] + [ANY] * len(arrays),
        out_specs=[ANY] * 3 + [VMEM] + [ANY] * count,
        scratch_shapes=[
            pltpu.VMEM(gain_total.shape, F32),
            pltpu.VMEM((tokens // pieces, width), F32),
            pltpu.SemaphoreType.DMA((3 + count + pieces,)),
            pltpu.SemaphoreType.DMA((2 + count + 2 * pieces,)),
            *(pltpu.VMEM(a.shape, F32) for a in (result, lat_grad, *shards_in)),
            pltpu.VMEM((pieces, tokens // pieces, width), F32),
        ],
        compiler_params=pltpu.CompilerParams(vmem_limit_bytes=60 << 20),
        name="write_outputs",
    )(flags, *arrays)


def layer_norm(values, gain_row):
    centred = values - jnp.mean(values, axis=-1, keepdims=True)
    inverse = lax.rsqrt(jnp.mean(centred * centred, axis=-1, keepdims=True) + EPSILON)
    return centred * inverse * gain_row


def norm_backward(values, gain_row, gradient):
    unused, pull_back = jax.vjp(layer_norm, values, gain_row)
    return pull_back(gradient)


def gelu_tanh(values):
    return jax.nn.gelu(values, approximate=True)


def mm(left_side, weight):
    return jnp.dot(left_side, weight, preferred_element_type=F32)


def mm_nt(left_side, weight):
    return lax.dot_general(left_side, weight, (((1,), (1,)), ((), ())), preferred_element_type=F32)


def mm_tn(left_side, gradient):
    return lax.dot_general(
        left_side, gradient, (((0,), (0,)), ((), ())), preferred_element_type=F32
    )


def low(values):
    return values.astype(BF16)


def heads_of(values):
    return values.reshape(values.shape[:-1] + (HEADS, values.shape[-1] // HEADS))


def mlp_forward(residual, gain_row, up, down_t):
    normed = low(layer_norm(residual, gain_row))
    pre_act = mm(normed, up)
    hidden = low(gelu_tanh(pre_act))
    return normed, pre_act, hidden, mm_nt(hidden, down_t)


def mlp_backward(residual, gain_row, normed, pre_act, hidden, up, down_t, grad_out):
    grad_low = low(grad_out)
    grad_down_t = mm_tn(grad_low, hidden)
    grad_hidden = mm(grad_low, down_t)
    unused, gelu_back = jax.vjp(gelu_tanh, pre_act)
    grad_pre = low(gelu_back(grad_hidden)[0])
    grad_up = mm_tn(normed, grad_pre)
    grad_resid, grad_gain = norm_backward(residual, gain_row, mm_nt(grad_pre, up))
    return grad_resid, grad_gain, grad_up, grad_down_t


def live_layer(live_lat, dead_lat, tokens, count, live_cot, dead_cot, weights, norm_gain):
    c_attn, c_up, c_down_t, s_attn, s_up, s_down_t = weights
    rows, width = live_lat.shape
    scale = (width // HEADS) ** (-0.5)
    lat_low = low(layer_norm(live_lat, norm_gain[0]))
    queries = low(mm(lat_low, c_attn[:, :width]))
    token_values = tokens.astype(F32)
    tok_low = low(layer_norm(token_values, norm_gain[1]))
    kv_weight = c_attn[:, width : 3 * width]
    key_value = low(mm(tok_low, kv_weight))
    keys, values = heads_of(key_value[:, :width]), heads_of(key_value[:, width:])
    scores = (
        jnp.einsum("qhd,khd->hqk", heads_of(queries), keys, preferred_element_type=F32) * scale
    )
    valid = (jnp.arange(tokens.shape[0]) < count)[None, None, :]
    probs = jax.nn.softmax(jnp.where(valid, scores, MASKED), axis=-1)
    probs_low = low(probs)
    attended = jnp.einsum("hqk,khd->qhd", probs_low, values, preferred_element_type=F32)
    attended = attended.reshape(rows, width)
    cross_low = low(attended)
    middle = live_lat + mm(cross_low, c_attn[:, 3 * width :])
    c_norm, c_pre, c_hidden, c_mlp = mlp_forward(middle, norm_gain[2], c_up, c_down_t)
    after_cross = jnp.concatenate([middle + c_mlp, dead_lat], axis=0)

    self_low = low(layer_norm(after_cross, norm_gain[3]))
    qkv = low(mm(self_low, s_attn[:, : 3 * width])).reshape(2, rows, 3 * width)
    s_q = heads_of(qkv[..., :width])
    s_k = heads_of(qkv[..., width : 2 * width])
    s_v = heads_of(qkv[..., 2 * width :])
    s_scores = jnp.einsum("iqhd,ikhd->ihqk", s_q, s_k, preferred_element_type=F32) * scale
    s_probs = jax.nn.softmax(s_scores, axis=-1)
    s_probs_low = low(s_probs)
    s_out = jnp.einsum("ihqk,ikhd->iqhd", s_probs_low, s_v, preferred_element_type=F32)
    s_out_low = low(s_out.reshape(2 * rows, width))
    after_attn = after_cross + mm(s_out_low, s_attn[:, 3 * width :])
    m_norm, m_pre, m_hidden, m_mlp = mlp_forward(after_attn, norm_gain[4], s_up, s_down_t)
    result = after_attn + m_mlp

    cotangent = jnp.concatenate([live_cot, dead_cot], axis=0)
    grad_in, gain_four, d_s_up, d_s_down_t = mlp_backward(
        after_attn, norm_gain[4], m_norm, m_pre, m_hidden, s_up, s_down_t, cotangent
    )
    grad_attn = cotangent + grad_in
    grad_y = low(grad_attn)
    d_s_o = mm_tn(s_out_low, grad_y)
    grad_out = heads_of(low(mm_nt(grad_y, s_attn[:, 3 * width :])).reshape(2, rows, width))
    grad_probs = jnp.einsum("iqhd,ikhd->ihqk", grad_out, s_v, preferred_element_type=F32)
    delta = jnp.sum(grad_probs * s_probs, axis=-1, keepdims=True)
    grad_scores = low(s_probs * (grad_probs - delta))
    g_q = jnp.einsum("ihqk,ikhd->iqhd", grad_scores, s_k, preferred_element_type=F32) * scale
    g_k = jnp.einsum("ihqk,iqhd->ikhd", grad_scores, s_q, preferred_element_type=F32) * scale
    g_v = jnp.einsum("ihqk,iqhd->ikhd", s_probs_low, grad_out, preferred_element_type=F32)
    grad_qkv = low(
        jnp.concatenate([g.reshape(2 * rows, width) for g in (g_q, g_k, g_v)], axis=-1)
    )
    d_s_qkv = mm_tn(self_low, grad_qkv)
    grad_in, gain_three = norm_backward(
        after_cross, norm_gain[3], mm_nt(grad_qkv, s_attn[:, : 3 * width])
    )
    grad_cross = grad_attn + grad_in
    live_grad, dead_grad = grad_cross[:rows], grad_cross[rows:]
    grad_in, gain_two, d_c_up, d_c_down_t = mlp_backward(
        middle, norm_gain[2], c_norm, c_pre, c_hidden, c_up, c_down_t, live_grad
    )
    grad_middle = live_grad + grad_in
    grad_cross_y = low(grad_middle)
    d_c_o = mm_tn(cross_low, grad_cross_y)
    grad_cross_out = low(mm_nt(grad_cross_y, c_attn[:, 3 * width :]))
    out_heads = heads_of(grad_cross_out)
    grad_weights = jnp.einsum("qhd,khd->hqk", out_heads, values, preferred_element_type=F32)
    row_delta = jnp.transpose(jnp.sum(heads_of(grad_cross_out.astype(F32) * attended), axis=-1))
    grad_scores = low(probs * (grad_weights - row_delta[..., None]))
    grad_query = low(
        (
            jnp.einsum("hqk,khd->qhd", grad_scores, keys, preferred_element_type=F32) * scale
        ).reshape(rows, width)
    )
    grad_keys = (
        jnp.einsum("hqk,qhd->khd", grad_scores, heads_of(queries), preferred_element_type=F32)
        * scale
    )
    grad_values = jnp.einsum("hqk,qhd->khd", probs_low, out_heads, preferred_element_type=F32)
    grad_kv = low(
        jnp.concatenate(
            [grad_keys.reshape(-1, width), grad_values.reshape(-1, width)], axis=-1
        )
    )
    d_c_kv = mm_tn(tok_low, grad_kv)
    grad_tokens, gain_one = norm_backward(token_values, norm_gain[1], mm_nt(grad_kv, kv_weight))
    d_c_q = mm_tn(lat_low, grad_query)
    grad_in, gain_zero = norm_backward(
        live_lat, norm_gain[0], mm_nt(grad_query, c_attn[:, :width])
    )
    live_lat_grad = grad_middle + grad_in
    d_c_attn = low(jnp.concatenate([d_c_q, d_c_kv, d_c_o], axis=1))
    d_s_attn = low(jnp.concatenate([d_s_qkv, d_s_o], axis=1))
    gain_grad = jnp.stack([gain_zero, gain_one, gain_two, gain_three, gain_four])
    grads = (d_c_attn, low(d_c_up), low(d_c_down_t), d_s_attn, low(d_s_up), low(d_s_down_t))
    return result, live_lat_grad, dead_grad, grad_tokens, grads, gain_grad


def column_blocks(blocks):
    sub, dp, rows, columns = blocks.shape
    return blocks.transpose(1, 2, 0, 3).reshape(dp * rows, sub * columns)


def row_blocks(blocks):
    sub, dp, rows, columns = blocks.shape
    return blocks.transpose(0, 2, 1, 3).reshape(sub * rows, dp * columns)


def shards(*arrays, dp_size, sub_size):
    latents, inputs, counts, flags = arrays[:4]
    cross_attn, cross_up, cross_down, self_attn, self_up, self_down, gains, cotangent = arrays[4:]
    width = latents.shape[-1]
    own = (
        cross_attn,
        cross_up,
        jnp.transpose(cross_down),
        self_attn,
        self_up,
        jnp.transpose(self_down),
    )
    live = jnp.where(flags[0] == 0, 0, 1)
    here = (jnp.arange(inputs.shape[0]) == live)[:, None, None]
    if dp_size == 8 and sub_size == 4:
        full, norm_gain, result, kept = forward_all(
            own, gains, latents, inputs, cotangent, counts, flags
        )
        owned, gain_total, grad_latents, grad_tokens = backward_all(
            [w.shape for w in own], full, norm_gain, latents, cotangent, flags, kept
        )
        result, grad_latents, grad_inputs, gain_owned, *owned = finish_all(
            gains.shape, flags, result, grad_latents, grad_tokens, gain_total, owned
        )
        owned = [jnp.transpose(g) if i in (2, 5) else g for i, g in enumerate(owned)]
        return (result, grad_latents, grad_inputs, *owned, gain_owned)

    blocks = [lax.all_gather(lax.all_gather(w, "dp", axis=0), "sub", axis=0) for w in own]
    norm_gain = lax.all_gather(gains, "dp", axis=1, tiled=True)
    transposed = (False, False, True, False, False, True)
    weights = [
        row_blocks(b) if flip else column_blocks(b) for b, flip in zip(blocks, transposed)
    ]

    def item(array, index):
        return lax.dynamic_index_in_dim(array, index, 0, keepdims=False)

    result, live_grad, dead_grad, grad_tokens, grads, gain_grad = live_layer(
        item(latents, live),
        item(latents, 1 - live),
        item(inputs, live),
        item(counts, live),
        item(cotangent, live),
        item(cotangent, 1 - live),
        weights,
        norm_gain.astype(F32),
    )

    def both(live_part, dead_part):
        first = jnp.where(live == 0, live_part, dead_part)
        second = jnp.where(live == 0, dead_part, live_part)
        return jnp.stack([first, second])

    rows = latents.shape[1]
    result = both(result[:rows], result[rows:])
    grad_latents = both(live_grad, dead_grad)
    grad_inputs = jnp.where(here, grad_tokens[None], 0.0)

    def blocks_of(grad, shape, flip):
        r, c = shape
        if flip:
            return grad.reshape(sub_size, r, dp_size, c).transpose(0, 2, 1, 3)
        return grad.reshape(dp_size, r, sub_size, c).transpose(2, 0, 1, 3)

    grads = [blocks_of(g, w.shape, flip) for g, w, flip in zip(grads, own, transposed)]
    owned = [lax.psum_scatter(g, "sub", scatter_dimension=0) for g in grads]
    owned = [lax.psum_scatter(g.astype(F32), "dp", scatter_dimension=0) for g in owned]
    gain_owned = lax.psum(gain_grad, "sub")
    gain_owned = lax.psum_scatter(gain_owned, "dp", scatter_dimension=1, tiled=True)
    owned = [jnp.transpose(g) if flip else g for g, flip in zip(owned, transposed)]
    return (result, grad_latents, grad_inputs, *owned, gain_owned)


def solution(mesh):
    item = P(("dp", "sub"), None, None)
    weight = P("dp", "sub")
    gain = P(None, "dp")
    placed = (item, item, P(("dp", "sub")), P()) + (weight,) * 6 + (gain, item)
    return jax.shard_map(
        functools.partial(shards, dp_size=mesh.shape["dp"], sub_size=mesh.shape["sub"]),
        mesh=mesh,
        in_specs=placed,
        out_specs=(item, item, item) + (weight,) * 6 + (gain,),
        check_vma=False,
    )
```

```python
import collections
import functools

import jax
import jax.numpy as jnp
from jax import lax
from jax.experimental import pallas as pl
from jax.experimental.pallas import tpu as pltpu
from jax.sharding import PartitionSpec as P

HEADS = 12
EPSILON = 1e-05
MASKED = -1e30
MESH_ID = pl.DeviceIdType.MESH
F32 = jnp.float32
BF16 = jnp.bfloat16
ANY = pl.BlockSpec(memory_space=pl.ANY)
VMEM = pl.BlockSpec(memory_space=pltpu.VMEM)
SMEM = pl.BlockSpec(memory_space=pltpu.SMEM)


PIECES = {
    "C": (0, 2),
    "A": (2, 1),
    "B": (3, 1),
    "D": (4, 2),
    "CA": (0, 3),
    "AB": (2, 2),
    "BD": (3, 3),
}


def piece(name, rows):
    first, size = PIECES[name]
    return pl.ds(first * (rows // 6), size * (rows // 6))


class Place:
    def __init__(self):
        dp, sub = lax.axis_index("dp"), lax.axis_index("sub")
        self.z, self.y, self.x, self.c = dp // 2, dp % 2, sub // 2, sub % 2

    def dev(self, z=None, y=None, x=None, c=None):
        z = self.z if z is None else z
        y = self.y if y is None else y
        x = self.x if x is None else x
        c = self.c if c is None else c
        return (z * 2 + y, x * 2 + c)

    def zk(self, k):
        return (self.z + k) % 4


def now(ref):
    return ref() if callable(ref) else ref


def spot(ref, index):
    return lambda: ref.at[index]


def only_if(condition, action):
    if condition is None:
        action()
    else:
        pl.when(condition())(action)


class Flight:
    def __init__(self, sems, ref, send_index, recv_index):
        self.sems, self.ref, self.send_index, self.recv_index = sems, ref, send_index, recv_index

    def made(self):
        place = self.sems.place
        return pltpu.make_async_remote_copy(
            src_ref=now(self.ref),
            dst_ref=now(self.ref),
            send_sem=self.sems.send.at[self.send_index],
            recv_sem=self.sems.recv.at[self.recv_index],
            device_id=place.dev(c=1 - place.c),
            device_id_type=MESH_ID,
        )

    def wait_send(self):
        self.made().wait_send()

    def wait_recv(self):
        self.made().wait_recv()


class Sems:
    def __init__(self, place, send, recv):
        self.place, self.send, self.recv, self.count, self.sent = place, send, recv, 0, []

    def reserve(self, n):
        self.count += n
        return self.count - n

    def start(self, src, dst, device, send_index, recv_index, condition=None, later=True):
        def action():
            pltpu.make_async_remote_copy(
                src_ref=now(src),
                dst_ref=now(dst),
                send_sem=self.send.at[send_index],
                recv_sem=self.recv.at[recv_index],
                device_id=device,
                device_id_type=MESH_ID,
            ).start()

        only_if(condition, action)
        flight = Flight(self, dst, send_index, recv_index)
        if later:
            self.sent.append((condition, flight))
        return flight

    def copy(self, src, dst, device, later=True):
        index = self.reserve(1)
        return self.start(src, dst, device, index, index, later=later)

    def drain(self):
        for condition, flight in self.sent:
            only_if(condition, flight.wait_send)


def greet(place, devices):
    barrier = pltpu.get_barrier_semaphore()
    for device in devices:
        pl.semaphore_signal(barrier, inc=1, device_id=device, device_id_type=MESH_ID)
    pl.semaphore_wait(barrier, len(devices))


def wait_all(copies):
    for made in copies:
        made.wait_recv()


class Spread:
    def __init__(self, sems, src, where):
        self.sems, self.where, place = sems, where, sems.place
        self.base = sems.reserve(4)
        z = place.z
        for k, condition in ((1, lambda: z != 3), (2, None), (3, lambda: z != 0)):
            at = self.base + k - 1
            sems.start(src, where(z), place.dev(z=place.zk(k)), at, at, condition)

    def arrived(self, k):
        origin = self.sems.place.zk(4 - k)
        Flight(self.sems, self.where(origin), self.base + 3, self.base + k - 1).wait_recv()

    def forward(self):
        self.arrived(2)
        place = self.sems.place
        block = self.where(place.zk(2))
        for z, target, k in ((2, 3, 3), (1, 0, 1)):
            self.sems.start(
                block,
                block,
                place.dev(z=target),
                self.base + 3,
                self.base + k - 1,
                functools.partial(lambda z: place.z == z, z),
            )

    def finish(self):
        self.arrived(1)
        self.arrived(3)


class Collect:
    def __init__(self, sems, part, into, through):
        self.sems, self.part, self.into, self.through = sems, part, into, through
        place = sems.place
        self.base = sems.reserve(4)
        z = place.z
        for k, condition in (
            (1, lambda: z != 3),
            (2, lambda: (z == 0) | (z == 3)),
            (3, lambda: z != 0),
        ):
            self.send(k, condition)
        for k, end, middle in ((1, 3, 2), (3, 0, 1)):
            at = self.base + 3
            sems.start(part(place.zk(k)), through, place.dev(z=middle), at, at, functools.partial(lambda end: z == end, end))

    def send(self, k, condition):
        place, at = self.sems.place, self.base + k - 1
        self.sems.start(
            self.part(place.zk(k)),
            spot(self.into, k - 1),
            place.dev(z=place.zk(k)),
            at,
            at,
            condition,
        )

    def forward(self, add):
        place = self.sems.place

        def middle():
            return (place.z == 1) | (place.z == 2)

        @pl.when(middle())
        def _():
            Flight(self.sems, self.through, self.base + 3, self.base + 3).wait_recv()
            add(place.zk(2))

        self.send(2, middle)

    def finish(self):
        z = self.sems.place.z
        for k, condition in ((1, lambda: z != 0), (2, None), (3, lambda: z != 3)):
            flight = Flight(self.sems, spot(self.into, k - 1), self.base + 3, self.base + k - 1)
            only_if(condition, flight.wait_recv)


def slots(count, places, order):
    steps = []
    for slot in range(min(places.values()), count + max(places.values())):
        for name in order:
            i = slot - places[name]
            if 0 <= i < count:
                steps.append((slot, name, i))
    return steps


def dot(a, b):
    return jnp.dot(a, b, preferred_element_type=F32)


def dot_nt(a, b):
    return lax.dot_general(a, b, (((1,), (1,)), ((), ())), preferred_element_type=F32)


def low(values):
    return values.astype(BF16)


def normed(values):
    centred = values - jnp.mean(values, axis=-1, keepdims=True)
    inverse = lax.rsqrt(jnp.mean(centred * centred, axis=-1, keepdims=True) + EPSILON)
    return centred * inverse, inverse


def gelu_both(u):
    k, a = 0.7978845608028654, 0.044715
    square = u * u
    t = jnp.tanh(k * u * (1.0 + a * square))
    half = 0.5 * (1.0 + t)
    slope = half + (0.5 * k) * u * (1.0 - t * t) * (1.0 + (3.0 * a) * square)
    return u * half, slope


def square_block(ref, x, c):
    halves = []
    for h in range(2):
        block = ref[h, x, c]
        halves.append(block.reshape(-1, block.shape[3]))
    return jnp.concatenate(halves, axis=1)


def hidden_block(ref, z):
    parts = []
    for y in range(2):
        rows = [ref[h, x, c, z, y] for x in range(2) for c in range(2) for h in range(2)]
        parts.append(jnp.concatenate(rows, axis=0))
    return jnp.concatenate(parts, axis=1)


def left_half(shape):
    return lax.broadcasted_iota(jnp.int32, shape, 1) < 64


def stack_heads(values):
    left = left_half(values.shape)
    zero = jnp.zeros_like(values)
    return jnp.concatenate([jnp.where(left, values, zero), jnp.where(left, zero, values)], axis=0)


def join_heads(values):
    rows = values.shape[0] // 2
    top, bottom = values[:rows], values[rows:]
    return jnp.where(left_half(top.shape), top, bottom)


def lanes(index, size):
    return pl.ds(pl.multiple_of(index * size, size), size)


def kept_shapes(rows, tokens, width, hidden):
    two = 2 * rows
    return {
        "cq": ((rows, width), BF16),
        "kv": ((2, tokens, width), BF16),
        "cp": ((width // 128, two, tokens), BF16),
        "co": ((rows, width), F32),
        "mid": ((rows, width), F32),
        "gpc": ((rows, hidden), BF16),
        "ac": ((two, width), F32),
        "sqkv": ((3, two, width), BF16),
        "sp": ((2 * (width // 128), two, rows), BF16),
        "aa": ((two, width), F32),
        "gps": ((two, hidden), BF16),
        "xl": ((tokens, width), BF16),
    }


def paired_shapes(rows, tokens, width, hidden):
    two = 2 * rows
    return {
        "gyt": ((2, width // 4, 2 * two), BF16),
        "mh": ((2 * two, hidden), BF16),
        "mnt": ((width, 2 * two), BF16),
        "sbt": ((width, 2 * two), BF16),
        "l1t": ((width, 2 * two), BF16),
        "ch": ((two, hidden), BF16),
        "cnt": ((width, two), BF16),
        "lst": ((width, two), BF16),
        "xbt": ((width, 2 * tokens), BF16),
    }


def forward_kernel(names, dims, *refs):
    rows, tokens, width, hidden = dims
    two = 2 * rows
    count = 6
    refs = list(refs)

    def take(n):
        out = refs[:n]
        del refs[:n]
        return out

    own = take(count)
    gain, lat, tok, cot, live_counts, flags = take(6)
    full = take(count)
    gain_out, result = take(2)
    kept = dict(zip(names, take(len(names))))
    gain_all, lat_v, cot_v, tok_v, z2, xb, xbt, gyt, lst, wr0, wr1, wt = take(12)
    cq, kv, cp, co, mid, ch, gpc, ac, sqkv, sp, so, aa, mh, gps, xl, lt, cnt, mnt = take(18)
    gain_own, gain_one, zb_v, nb = take(4)
    send, recv, local = take(3)
    wr = (wr0, wr1)
    place = Place()
    x, y, z, c = place.x, place.y, place.z, place.c
    sems = Sems(place, send, recv)
    local_count = [0]
    local_open = []

    def local_copy(src, dst):
        made = pltpu.make_async_copy(src, dst, local.at[local_count[0]])
        local_count[0] += 1
        made.start()
        return made

    in_gain = local_copy(gain, gain_own)
    in_lat, in_tok, in_cot = local_copy(lat, lat_v), local_copy(tok, tok_v), local_copy(cot, cot_v)
    px, py, pc = place.dev(x=1 - x), place.dev(y=1 - y), place.dev(c=1 - c)
    me_dp = z * 2 + y
    dp_peers = [((me_dp + k) % 8, x * 2 + c) for k in range(1, 8)]
    greet(place, dp_peers + [px, pc])

    halves = 2 * count
    blocks = [full[i // 2].at[i % 2] for i in range(halves)]
    ones, twos, threes, across, placed = {}, {}, {}, {i: [] for i in range(halves)}, {}
    block_rows = full[0].shape[5]

    def shard(i):
        w, h = own[i // 2], i % 2
        if w.shape[0] == block_rows:
            return w, slice(None), pl.ds(h * (w.shape[1] // 2), w.shape[1] // 2), 0
        return w, slice(None), pl.ds(0, w.shape[1]), h * block_rows

    def own_piece(i, name):
        w, unused, columns, first = shard(i)
        at = piece(name, block_rows)
        return w.at[pl.ds(first + at.start, at.size), columns]

    def step_one(i):
        g = blocks[i]
        w, unused, columns, first = shard(i)
        placed[i] = local_copy(w.at[pl.ds(first, block_rows), columns], g.at[x, c, z, y])
        ab, pc_, pd = (piece(n, block_rows) for n in ("AB", "C", "D"))
        spread = Spread(sems, own_piece(i, "AB"), lambda o: g.at[x, c, o, y, ab])
        ones[i] = (
            spread,
            [
                sems.copy(own_piece(i, "C"), g.at[x, c, z, y, pc_], px),
                sems.copy(own_piece(i, "D"), g.at[x, c, z, y, pd], py),
            ],
        )

    def step_one_forward(i):
        ones[i][0].forward()

    def step_two(i):
        g = blocks[i]
        spread, got = ones.pop(i)
        placed.pop(i).wait()
        wait_all(got)
        pa, pb, pc_, pd = (piece(n, block_rows) for n in ("A", "B", "C", "D"))
        spread_c = Spread(sems, g.at[:, c, z, y, pc_], lambda o: g.at[:, c, o, y, pc_])
        spread_d = Spread(sems, g.at[x, c, z, :, pd], lambda o: g.at[x, c, o, :, pd])
        spread.finish()
        got = [
            sems.copy(g.at[x, c, :, y, pa], g.at[x, c, :, y, pa], px),
            sems.copy(g.at[x, c, :, y, pb], g.at[x, c, :, y, pb], py),
        ]
        twos[i] = ((spread_c, spread_d), got)

    def step_two_forward(i):
        for spread in twos[i][0]:
            spread.forward()

    def step_three(i):
        g = blocks[i]
        spreads, got = twos.pop(i)
        for spread in spreads:
            spread.finish()
        wait_all(got)
        ca, bd = piece("CA", block_rows), piece("BD", block_rows)
        threes[i] = [
            sems.copy(g.at[:, c, :, y, ca], g.at[:, c, :, y, ca], py),
            sems.copy(g.at[x, c, :, :, bd], g.at[x, c, :, :, bd], px),
        ]
        across[i] += [
            sems.copy(g.at[:, c, :, y, ca], g.at[:, c, :, y, ca], pc),
            sems.copy(g.at[x, c, :, :, bd], g.at[x, c, :, :, bd], pc),
        ]

    def step_four(i):
        wait_all(threes.pop(i))
        g = blocks[i]
        ca, bd = piece("CA", block_rows), piece("BD", block_rows)
        across[i] += [
            sems.copy(g.at[:, c, :, 1 - y, ca], g.at[:, c, :, 1 - y, ca], pc),
            sems.copy(g.at[1 - x, c, :, :, bd], g.at[1 - x, c, :, :, bd], pc),
        ]

    loading = {}

    def load(m, dst):
        def begin():
            for h in range(2):
                wait_all(across.pop(2 * m + h))
            loading[m] = local_copy(full[m], dst)

        return begin

    def keep(name, src):
        local_open.append(local_copy(src, kept[name]))

    def pair(name, mine, theirs, axis_size, axis):
        here, there = pl.ds(0, axis_size), pl.ds(axis_size, axis_size)
        dst = kept[name]

        def part(where):
            return dst.at[where] if axis == 0 else dst.at[:, where] if axis == 1 else dst.at[:, :, where]

        local_open.append(local_copy(mine, part(here)))
        across_pairs.append(sems.copy(theirs, part(there), pc))

    across_pairs = []
    gain_copies = []

    def pick(flag_first, first, second):
        return jnp.where(flag_first, first, second)

    first_live = flags[0] == 0
    live_count = jnp.where(first_live, live_counts[0], live_counts[1])

    def send_gains():
        in_gain.wait()
        gain_one[...] = jnp.zeros_like(gain_one)
        gain_one[: gain.shape[0], : gain.shape[1]] = gain_own[...]
        gain_all[me_dp] = gain_one[...]
        for device in dp_peers:
            gain_copies.append(sems.copy(gain_one, gain_all.at[me_dp], device))

    def start():
        wait_all(gain_copies)
        row = lax.broadcasted_iota(jnp.int32, (128, width), 0)
        column = lax.broadcasted_iota(jnp.int32, (128, width), 1)
        share = width // 8
        gain_out[...] = jnp.zeros_like(gain_out)

        @pl.loop(0, 8)
        def _(i):
            spread = low(jnp.where((column == row + share * i) & (row < share), 1.0, 0.0))
            gain_out[...] += dot(gain_all[i], spread)

        in_lat.wait()
        in_cot.wait()
        z2[:rows] = pick(first_live, lat_v[0], lat_v[1])
        z2[rows:] = pick(first_live, lat_v[1], lat_v[0])
        zb = low(normed(z2[:rows])[0] * gain_out[0:1])
        zb_v[...] = zb
        lst[0] = zb.T
        gy_first = low(pick(first_live, cot_v[0], cot_v[1]))
        gy_last = low(pick(first_live, cot_v[1], cot_v[0]))
        gyt[:, :, :, :rows] = gy_first.T.reshape(2, 2, width // 4, rows)
        gyt[:, :, :, rows:] = gy_last.T.reshape(2, 2, width // 4, rows)
        pair("gyt", gyt.at[:, c], gyt.at[:, 1 - c], two, 2)

    def tokens_part(first, last):
        def run():
            if first == 0:
                in_tok.wait()

            @pl.loop(first, last)
            def _(i):
                at = lanes(i, 128)
                here = pick(first_live, tok_v[0, at], tok_v[1, at])
                xl[at] = here
                value = low(normed(here.astype(F32))[0] * gain_out[1:2])
                xb[at] = value
                xbt[:, at] = value.T

            if last == tokens // 128:
                keep("xl", xl)
                pair("xbt", xbt, xbt, tokens, 1)

        return run

    def cross_queries():
        loading[0].wait()
        cq[...] = low(dot(zb_v[...], square_block(wr[0], 0, 0)))
        keep("cq", cq)

    def keys_values(first, last):
        def run():
            for i in range(first, last):
                at = pl.ds(i * 256, 256)

                @pl.loop(0, 2)
                def _(j):
                    kv[j, at] = low(dot(xb[at], square_block(wr[0], j, 1 - j)))

            if last == tokens // 256:
                keep("kv", kv)

        return run

    def cross_attention(first, last):
        def run():
            @pl.loop(first, last)
            def _(p):
                at = lanes(p, 128)
                q = stack_heads(cq[:, at] * jnp.asarray(0.125, BF16))
                s = dot_nt(q, kv[0, :, at])
                s = jnp.where(lax.broadcasted_iota(jnp.int32, s.shape, 1) < live_count, s, MASKED)
                e = jnp.exp(s - jnp.max(s, axis=-1, keepdims=True))
                prob = low(e * (1.0 / jnp.sum(e, axis=-1, keepdims=True)))
                cp[p] = prob
                co[:, at] = join_heads(dot(prob, kv[1, :, at]))

            if last == width // 128:
                keep("cp", cp)
                keep("co", co)

        return run

    def cross_out():
        cob = low(co[...])
        lst[1] = cob.T
        pair("lst", lst.at[c], lst.at[1 - c], rows, 1)
        mid[...] = z2[:rows] + dot(cob, square_block(wr[0], 1, 1))
        keep("mid", mid)
        cnb = low(normed(mid[...])[0] * gain_out[2:3])
        nb[:rows] = cnb
        cnt[...] = cnb.T
        pair("cnt", cnt, cnt, rows, 1)

    def up(m, w, left, out, slope, first, last, after):
        def run():
            if first == 0:
                loading[m].wait()

            @pl.loop(first, last)
            def _(s):
                at = lanes(s, hidden // 4)
                value, grad = gelu_both(dot(nb[:left], square_block(w, s // 2, s % 2)))
                out[:, at] = low(value)
                slope[:, at] = low(grad)

            if last == 4:
                after()

        return run

    def down(m, act, into):
        loading[m].wait()

        @pl.loop(0, 4)
        def _(s):
            into[...] += dot_nt(act[:, lanes(s, hidden // 4)], hidden_block(wt, s))

    def cross_up_done():
        pair("ch", ch, ch, rows, 0)
        keep("gpc", gpc)

    def self_up_done():
        pair("mh", mh, mh, two, 0)
        keep("gps", gps)

    def cross_down():
        ac[:rows] = mid[...]
        ac[rows:] = z2[rows:]
        down(2, ch, ac.at[pl.ds(0, rows)])
        keep("ac", ac)
        sb = low(normed(ac[...])[0] * gain_out[3:4])
        nb[...] = sb
        lt[0] = sb.T
        pair("sbt", lt.at[0], lt.at[0], two, 1)

    def self_project():
        loading[3].wait()
        @pl.loop(0, 3)
        def _(i):
            sqkv[i] = low(dot(nb[...], square_block(wr[0], i // 2, i % 2)))

        keep("sqkv", sqkv)

    def self_attention(first, last):
        pairs = width // 128

        def run():
            @pl.loop(first, last, unroll=3)
            def _(i):
                at, row_at = lanes(i % pairs, 128), lanes(i // pairs, rows)
                q = stack_heads(sqkv[0, row_at, at] * jnp.asarray(0.125, BF16))
                s = dot_nt(q, sqkv[1, row_at, at])
                e = jnp.exp(s - jnp.max(s, axis=-1, keepdims=True))
                prob = low(e * (1.0 / jnp.sum(e, axis=-1, keepdims=True)))
                sp[i] = prob
                so[row_at, at] = low(join_heads(dot(prob, sqkv[2, row_at, at])))

            if last == 2 * pairs:
                keep("sp", sp)

        return run

    def self_out():
        lt[1] = so[...].T
        pair("l1t", lt.at[c], lt.at[1 - c], two, 1)
        aa[...] = ac[...] + dot(so[...], square_block(wr[0], 1, 1))
        keep("aa", aa)
        mnb = low(normed(aa[...])[0] * gain_out[4:5])
        nb[...] = mnb
        mnt[...] = mnb.T
        pair("mnt", mnt, mnt, two, 1)

    def self_down():
        z2[...] = aa[...]
        down(5, mh, z2)
        total = z2[...]
        result[0] = pick(first_live, total[:rows], total[rows:])
        result[1] = pick(first_live, total[rows:], total[:rows])

    pairs = width // 128
    work = collections.deque([(-2, send_gains), (1, start)])
    for n in range(4):
        work.append((1, tokens_part(n * tokens // 512, (n + 1) * tokens // 512)))
    for slot, part in (
        (4, load(0, wr[0])),
        (4, cross_queries),
        (4, keys_values(0, 1)),
        (4, keys_values(1, 2)),
        (4, keys_values(2, 3)),
        (4, keys_values(3, tokens // 256)),
        (4, cross_attention(0, 2)),
        (4, cross_attention(2, 4)),
        (4, cross_attention(4, pairs)),
        (4, cross_out),
        (6, load(1, wr[1])),
        (6, up(1, wr[1], rows, ch, gpc, 0, 2, cross_up_done)),
        (6, up(1, wr[1], rows, ch, gpc, 2, 4, cross_up_done)),
        (8, load(2, wt)),
        (8, cross_down),
        (10, load(3, wr[0])),
        (10, self_project),
        (10, self_attention(0, pairs)),
        (10, self_attention(pairs, 2 * pairs)),
        (10, self_out),
        (12, load(4, wr[1])),
        (12, up(4, wr[1], two, mh, gps, 0, 2, self_up_done)),
        (12, up(4, wr[1], two, mh, gps, 2, 4, self_up_done)),
        (14, load(5, wt)),
        (14, self_down),
    ):
        work.append((slot, part))
    steps = {
        "1": step_one,
        "f": step_one_forward,
        "2": step_two,
        "g": step_two_forward,
        "3": step_three,
        "4": step_four,
    }
    places = {"1": -2, "f": -1, "2": 0, "g": 0, "3": 1, "4": 2}
    for slot, name, i in slots(halves, places, "2314fg"):
        steps[name](i)
        if work and work[0][0] <= slot:
            work.popleft()[1]()
    while work:
        work.popleft()[1]()
    wait_all(across_pairs)
    for made in local_open:
        made.wait()
    sems.drain()


def half_shape(shard):
    return shard.shape[0], shard.shape[1] // 2


def forward_all(own, gain, latents, inputs, cotangent, counts, flags):
    count = len(own)
    rows, width = latents.shape[1:]
    tokens = inputs.shape[1]
    hidden = own[1].shape[1] * 4
    dims = (rows, tokens, width, hidden)
    two = 2 * rows
    kept = {**kept_shapes(*dims), **paired_shapes(*dims)}
    names = tuple(kept)
    copies = 7 + 2 * count * (6 + 10 + 4 + 2) + len(paired_shapes(*dims))
    block = (2, 2, 2, 4, 2) + half_shape(own[0])
    shapes = [jax.ShapeDtypeStruct(block, BF16) for w in own]
    shapes += [
        jax.ShapeDtypeStruct((16, width), F32),
        jax.ShapeDtypeStruct(latents.shape, F32),
    ]
    shapes += [jax.ShapeDtypeStruct(s, t) for s, t in kept.values()]
    pairs = width // 128
    scratch = [
        ((8, 16, 128), BF16),
        (latents.shape, F32),
        (latents.shape, F32),
        (inputs.shape, BF16),
        ((two, width), F32),
        ((tokens, width), BF16),
        ((width, tokens), BF16),
        ((2, 2, width // 4, two), BF16),
        ((2, width, rows), BF16),
        (block, BF16),
        (block, BF16),
        (block, BF16),
        ((rows, width), BF16),
        ((2, tokens, width), BF16),
        ((pairs, two, tokens), BF16),
        ((rows, width), F32),
        ((rows, width), F32),
        ((rows, hidden), BF16),
        ((rows, hidden), BF16),
        ((two, width), F32),
        ((3, two, width), BF16),
        ((2 * pairs, two, rows), BF16),
        ((two, width), BF16),
        ((two, width), F32),
        ((two, hidden), BF16),
        ((two, hidden), BF16),
        ((tokens, width), BF16),
        ((2, width, two), BF16),
        ((width, rows), BF16),
        ((width, two), BF16),
        (gain.shape, BF16),
        ((16, 128), BF16),
        ((rows, width), BF16),
        ((two, width), BF16),
    ]
    outs = pl.pallas_call(
        functools.partial(forward_kernel, names, dims),
        out_shape=shapes,
        in_specs=[ANY] * (count + 4) + [SMEM, SMEM],
        out_specs=[ANY] * count + [VMEM, VMEM] + [ANY] * len(names),
        scratch_shapes=[pltpu.VMEM(s, t) for s, t in scratch]
        + [
            pltpu.SemaphoreType.DMA((copies,)),
            pltpu.SemaphoreType.DMA((copies,)),
            pltpu.SemaphoreType.DMA((5 + 3 * count + len(names),)),
        ],
        compiler_params=pltpu.CompilerParams(
            collective_id=0, has_side_effects=True, vmem_limit_bytes=60 << 20
        ),
        name="gather_and_forward",
    )(*own, gain, latents, inputs, cotangent, counts, flags)
    full, (norm_gain, result) = outs[:count], outs[count : count + 2]
    return full, norm_gain, result, dict(zip(names, outs[count + 2 :]))


def norm_back(values, gain_row, gradient):
    unit, inverse = normed(values)
    scaled = gradient * gain_row
    grad = inverse * (
        scaled
        - jnp.mean(scaled, axis=-1, keepdims=True)
        - unit * jnp.mean(scaled * unit, axis=-1, keepdims=True)
    )
    return grad, jnp.sum(gradient * unit, axis=0, keepdims=True)


def attention_back(q, k, v, out_grad, prob, delta):
    prob_grad = dot_nt(out_grad, v)
    weight = prob.astype(F32)
    if delta is None:
        delta = jnp.sum(weight * prob_grad, axis=-1, keepdims=True)
    score_grad = low(weight * (prob_grad - delta))
    q_grad = join_heads(dot(score_grad, k)) * 0.125
    k_grad = low(dot(q.T, score_grad) * 0.125).T
    v_grad = low(dot(out_grad.T, prob)).T
    return low(q_grad), k_grad, v_grad


def add_blocks(total, where, part, there):
    total[where] = (total[where].astype(F32) + part[there].astype(F32)).astype(BF16)


def backward_kernel(names, dims, *refs):
    rows, tokens, width, hidden = dims
    two, quarter, pairs = 2 * rows, hidden // 4, width // 128
    count = 6
    halves, ring = 2 * count, 3
    order = (5, 4, 3, 2, 1, 0)
    refs = list(refs)

    def take(n):
        out = refs[:n]
        del refs[:n]
        return out

    full = take(count)
    gain, lat, cot, flags = take(4)
    kept = dict(zip(names, take(len(names))))
    outs = take(count)
    gain_out, lat_grad, dx = take(3)
    total = take(count)
    from_y, from_x = take(ring), take(ring)
    from_a, from_b, from_c, from_d, from_z, end_c, end_d = (take(halves) for _ in range(7))
    by_c, by_d, by_z = (take(halves) for _ in range(3))
    wr, wt, grad_ac, du_sib, r_sib, ge_sib, dcu_sib, rs_sib, dkv_sib = take(9)
    gain_acc, gain_sub, gain_dp, send, recv, local, free = take(7)
    place = Place()
    x, y, z, c = place.x, place.y, place.z, place.c
    sems = Sems(place, send, recv)
    local_count = [0]

    def local_copy(src, dst):
        made = pltpu.make_async_copy(src, dst, local.at[local_count[0]])
        local_count[0] += 1
        made.start()
        return made

    me_dp, me_sub = z * 2 + y, x * 2 + c
    sub_peers = [(me_dp, (me_sub + k) % 4) for k in (1, 2, 3)]
    dp_peers = [((me_dp + k) % 8, me_sub) for k in range(1, 8)]
    px, py, pc = place.dev(x=1 - x), place.dev(y=1 - y), place.dev(c=1 - c)
    first_live = flags[0] == 0
    gain_acc[...] = jnp.zeros_like(gain_acc)

    ones, twos, threes = {}, {}, {}
    block_rows, block_columns = total[0].shape[4:]

    def where(i):
        return total[order[i // 2]], i % 2

    def clear():
        for into in (*from_c, *from_d, *from_z):

            @pl.when(z == 0)
            def _():
                into[0] = jnp.zeros(into.shape[1:], BF16)

            @pl.when(z == 3)
            def _():
                into[2] = jnp.zeros(into.shape[1:], BF16)

    def step_one(i):
        a, h = where(i)
        if i >= ring:
            pl.semaphore_wait(free.at[i - ring], 2)
        ones[i] = [
            sems.copy(a.at[h, :, :, 1 - y, piece("CA", block_rows)], from_y[i % ring], py),
            sems.copy(a.at[h, 1 - x, :, :, piece("BD", block_rows)], from_x[i % ring], px),
        ]

    def step_two(i):
        a, h = where(i)
        wait_all(ones.pop(i))
        ca, bd = piece("CA", block_rows), piece("BD", block_rows)
        pa, pb, pc_, pd = (piece(n, block_rows) for n in ("A", "B", "C", "D"))
        fy, fx = from_y[i % ring], from_x[i % ring]

        @pl.loop(0, 8)
        def _(j):
            add_blocks(a, (h, j // 4, j % 4, y, ca), fy, (j // 4, j % 4))
            add_blocks(a, (h, x, j // 2, j % 2, bd), fx, (j // 2, j % 2))

        if i + ring < halves:
            for device in (px, py):
                pl.semaphore_signal(free.at[i], inc=1, device_id=device, device_id_type=MESH_ID)
        collect_c = Collect(sems, lambda o: a.at[h, :, o, y, pc_], from_c[i], by_c[i])
        collect_d = Collect(sems, lambda o: a.at[h, x, o, :, pd], from_d[i], by_d[i])
        got = [
            sems.copy(a.at[h, 1 - x, :, y, pa], from_a[i], px),
            sems.copy(a.at[h, x, :, 1 - y, pb], from_b[i], py),
        ]
        twos[i] = (collect_c, collect_d, got)

    def step_two_forward(i):
        a, h = where(i)
        pc_, pd = piece("C", block_rows), piece("D", block_rows)

        def add_c(o):
            for j in range(2):
                add_blocks(a, (h, j, o, y, pc_), by_c[i], j)

        def add_d(o):
            for j in range(2):
                add_blocks(a, (h, x, o, j, pd), by_d[i], j)

        twos[i][0].part = lambda o: a.at[h, :, o, y, pc_]
        twos[i][1].part = lambda o: a.at[h, x, o, :, pd]
        twos[i][0].forward(add_c)
        twos[i][1].forward(add_d)

    def step_three(i):
        a, h = where(i)
        collect_c, collect_d, got = twos.pop(i)
        collect_c.finish()
        collect_d.finish()
        wait_all(got)
        pa, pb, pc_, pd = (piece(n, block_rows) for n in ("A", "B", "C", "D"))
        fc, fd = from_c[i], from_d[i]

        @pl.loop(0, 4)
        def _(j):
            add_blocks(a, (h, x, j, y, pa), from_a[i], j)
            add_blocks(a, (h, x, j, y, pb), from_b[i], j)

        @pl.loop(0, 2)
        def _(j):
            a[h, j, z, y, pc_] = low(
                a[h, j, z, y, pc_].astype(F32)
                + fc[0, j].astype(F32)
                + fc[1, j].astype(F32)
                + fc[2, j].astype(F32)
            )
            a[h, x, z, j, pd] = low(
                a[h, x, z, j, pd].astype(F32)
                + fd[0, j].astype(F32)
                + fd[1, j].astype(F32)
                + fd[2, j].astype(F32)
            )

        ab = piece("AB", block_rows)
        collect = Collect(sems, lambda o: a.at[h, x, o, y, ab], from_z[i], by_z[i])
        got = [
            sems.copy(a.at[h, 1 - x, z, y, pc_], end_c[i], px),
            sems.copy(a.at[h, x, z, 1 - y, pd], end_d[i], py),
        ]
        threes[i] = (collect, got)

    def step_three_forward(i):
        a, h = where(i)
        ab = piece("AB", block_rows)
        collect = threes[i][0]
        collect.part = lambda o: a.at[h, x, o, y, ab]
        collect.forward(lambda o: add_blocks(a, (h, x, o, y, ab), by_z[i], ...))

    def step_four(i):
        a, h = where(i)
        collect, got = threes.pop(i)
        collect.finish()
        wait_all(got)
        fz, o = from_z[i], outs[order[i // 2]]
        if o.shape[0] == block_rows:
            first, columns = 0, pl.ds(h * block_columns, block_columns)
        else:
            first, columns = h * block_rows, slice(None)

        def put(name, value):
            at = piece(name, block_rows)
            o[pl.ds(first + at.start, at.size), columns] = (
                a[h, x, z, y, at].astype(F32) + value
            )

        put("AB", fz[0].astype(F32) + fz[1].astype(F32) + fz[2].astype(F32))
        put("C", end_c[i][...].astype(F32))
        put("D", end_d[i][...].astype(F32))

    run_step = {
        "1": step_one,
        "2": step_two,
        "g": step_two_forward,
        "3": step_three,
        "f": step_three_forward,
        "4": step_four,
    }
    places = {"1": 0, "2": 1, "g": 2, "3": 3, "f": 4, "4": 5}
    steps = collections.deque(slots(halves, places, "12g3f4"))
    ready = [0]

    def advance(n):
        while n > 0 and steps and (steps[0][1] != "1" or steps[0][2] < ready[0]):
            unused, name, i = steps.popleft()
            run_step[name](i)
            n -= 1

    def done(m):
        ready[0] += 2
        advance(2)

    def square_grad(m, at, products):
        size = 4 * block_rows

        @pl.loop(0, 2)
        def _(n):
            rows_at = pl.ds(pl.multiple_of(n * size, size), size)
            value = None
            for left, right in products:
                term = dot(left[rows_at], right())
                value = term if value is None else value + term
            for h in range(2):
                part = low(value[:, h * block_columns : (h + 1) * block_columns])
                total[m][h, at, pl.ds(n * 2, 2)] = part.reshape(2, 2, block_rows, block_columns)

    def put_hidden(m, h, zz, value):
        for yy in range(2):
            part = value[:, yy * block_columns : (yy + 1) * block_columns]
            total[m][h, :, zz, yy] = low(part).reshape(2, block_rows, block_columns)

    def hidden_grad(m, h, left, right):
        @pl.loop(0, 4)
        def _(zz):
            put_hidden(m, h, zz, dot(left, right[:, lanes(zz, quarter)]))

    def both(own, other):
        return jnp.concatenate([own, other], axis=0)

    def send_off(src, dst):
        return sems.copy(src, dst, pc, later=False)

    def pick(first, second):
        return jnp.where(first_live, first, second)

    def back_through(into, act, blocks):
        into[...] = jnp.zeros_like(into)

        @pl.loop(0, blocks)
        def _(s):
            into[...] += dot_nt(act[s // 2, s % 2], square_block(wr, s // 2, s % 2))

    def self_part(mh, gps, gyt, mnt, sbt, l1t, du, r, cot_v, aa, ac, sqkv, sp, grad_aa, out_grad):
        loads = {
            name: local_copy(src, dst)
            for name, src, dst in (
                ("gyt", kept["gyt"], gyt),
                ("mh", kept["mh"], mh),
                ("wt", full[5], wt),
                ("cot", cot, cot_v),
                ("gps", kept["gps"], gps),
                ("wr", full[4], wr),
                ("aa", kept["aa"], aa),
                ("mnt", kept["mnt"], mnt),
                ("sqkv", kept["sqkv"], sqkv),
                ("sp", kept["sp"], sp),
                ("ac", kept["ac"], ac),
                ("sbt", kept["sbt"], sbt),
                ("l1t", kept["l1t"], l1t),
            )
        }
        clear()
        greet(place, sub_peers + dp_peers)
        loads["gyt"].wait()
        loads["mh"].wait()
        for h in range(2):
            left = gyt[:, h * block_rows : (h + 1) * block_rows]
            left = left.reshape(2 * block_rows, 2 * two)
            hidden_grad(5, h, left, mh)
            ready[0] += 1
            advance(1)

        for name in ("wt", "cot", "gps"):
            loads[name].wait()
        for at, value in (
            (pl.ds(0, rows), pick(cot_v[0], cot_v[1])),
            (pl.ds(rows, rows), pick(cot_v[1], cot_v[0])),
        ):
            grad_aa[at] = value
        out_grad[...] = low(grad_aa[...])

        @pl.loop(0, 4)
        def _(s):
            grad = dot(out_grad[...], hidden_block(wt, s))
            du[s // 2, s % 2] = low(grad * gps[:, lanes(s, quarter)].astype(F32))

        sent = send_off(du.at[:, 1 - c], du_sib)
        advance(2)
        for name in ("wr", "aa", "mnt"):
            loads[name].wait()
        back_through(grad_ac, du, 4)
        grad, gain_row = norm_back(aa[...], gain[4:5], grad_ac[...])
        grad_aa[...] += grad
        gain_acc[0, 4:5] = gain_row
        advance(2)
        next_wr = local_copy(full[3], wr)
        next_wt = local_copy(full[2], wt)
        sent.wait_recv()

        @pl.loop(0, 2)
        def _(a):
            square_grad(4, a, [(mnt, lambda: both(du[a, c], du_sib[a]))])

        done(4)

        r[1, 1] = low(grad_aa[...])
        for made in (next_wr, loads["sqkv"], loads["sp"], loads["ac"], loads["sbt"], loads["l1t"]):
            made.wait()
        out_grad[...] = low(dot_nt(r[1, 1], square_block(wr, 1, 1)))

        advance(2)
        for part in range(2):

            @pl.loop(part * pairs, (part + 1) * pairs, unroll=3)
            def _(i):
                at, row_at = lanes(i % pairs, 128), lanes(i // pairs, rows)
                r[0, 0, row_at, at], r[0, 1, row_at, at], r[1, 0, row_at, at] = attention_back(
                    stack_heads(sqkv[0, row_at, at]),
                    sqkv[1, row_at, at],
                    sqkv[2, row_at, at],
                    stack_heads(out_grad[row_at, at]),
                    sp[i],
                    None,
                )

            advance(2)

        sent_r = send_off(r.at[:, 1 - c], r_sib)
        back_through(grad_ac, r, 3)
        grad, gain_row = norm_back(ac[...], gain[3:4], grad_ac[...])
        grad_ac[...] = grad_aa[...] + grad
        gain_acc[0, 3:4] = gain_row
        advance(2)
        sent_r.wait_recv()
        square_grad(3, 0, [(sbt, lambda: both(r[0, c], r_sib[0]))])
        square_grad(3, 1, [(l1t, lambda: both(r[1, c], r_sib[1]))])
        done(3)
        sent.wait_send()
        sent_r.wait_send()
        next_wt.wait()

    def cross_part(
        ch, gpc, ge, cnt, du, mid, lst, rs, xbt, kv, cp, cq, co, dco, xl, dxs, lat_v, grad_mid
    ):
        loads = {
            name: local_copy(src, dst)
            for name, src, dst in (
                ("ch", kept["ch"], ch),
                ("gpc", kept["gpc"], gpc),
                ("wr", full[1], wr),
                ("mid", kept["mid"], mid),
                ("cnt", kept["cnt"], cnt),
                ("cq", kept["cq"], cq),
                ("co", kept["co"], co),
                ("kv", kept["kv"], kv),
                ("cp", kept["cp"], cp),
                ("lst", kept["lst"], lst),
                ("xbt", kept["xbt"], xbt),
                ("lat", lat, lat_v),
            )
        }
        for i in range(2):
            lat_grad_dead = grad_ac[rows:]
            lat_grad[i] = lat_grad_dead
        low_grad = low(grad_ac[:rows])
        ge[...] = low_grad.T.reshape(2, 2, width // 4, rows)
        sent = [send_off(ge.at[:, 1 - c], ge_sib)]
        loads["gpc"].wait()
        dco[...] = low_grad

        @pl.loop(0, 4)
        def _(s):
            grad = dot(dco[...], hidden_block(wt, s))
            du[s // 2, s % 2] = low(grad * gpc[:, lanes(s, quarter)].astype(F32))

        sent.append(send_off(du.at[:, 1 - c], dcu_sib))
        advance(2)
        loads["ch"].wait()
        sent[0].wait_recv()
        for h in range(2):
            at = pl.ds(h * block_rows, block_rows)
            left = [g.reshape(2 * block_rows, rows) for g in (ge[:, c, at], ge_sib[:, at])]
            hidden_grad(2, h, jnp.concatenate(left, axis=1), ch)
        done(2)

        for name in ("wr", "mid", "cnt"):
            loads[name].wait()
        back_through(grad_mid, du, 4)
        grad, gain_row = norm_back(mid[...], gain[2:3], grad_mid[...])
        grad_mid[...] = grad_ac[:rows] + grad
        gain_acc[0, 2:3] = gain_row
        advance(2)
        next_wr = local_copy(full[0], wr)
        sent[1].wait_recv()

        @pl.loop(0, 2)
        def _(a):
            square_grad(1, a, [(cnt, lambda: both(du[a, c], dcu_sib[a]))])

        done(1)

        rs[1] = low(grad_mid[...])
        next_wr.wait()
        dco[...] = low(dot_nt(rs[1], square_block(wr, 1, 1)))
        for name in ("cq", "co", "kv", "cp"):
            loads[name].wait()

        advance(2)
        for part in range(3):

            @pl.loop(part * pairs // 3, (part + 1) * pairs // 3, unroll=2)
            def _(p):
                at = lanes(p, 128)
                out_grad = stack_heads(dco[:, at])
                attended = co[:, at]
                delta = jnp.sum(
                    out_grad.astype(F32) * both(attended, attended), axis=-1, keepdims=True
                )
                rs[0, :, at], kv[0, :, at], kv[1, :, at] = attention_back(
                    stack_heads(cq[:, at]), kv[0, :, at], kv[1, :, at], out_grad, cp[p], delta
                )

            advance(2)

        sent.append(send_off(rs.at[1 - c], rs_sib))
        sent.append(send_off(kv.at[c], dkv_sib))
        advance(2)
        for name in ("lst", "xbt", "lat"):
            loads[name].wait()
        sent[2].wait_recv()
        sent[3].wait_recv()
        square_grad(0, c, [(lst, lambda: both(rs[c], rs_sib[...]))])
        own_tokens, their_tokens = (xbt.at[:, pl.ds(n * tokens, tokens)] for n in range(2))
        square_grad(
            0,
            1 - c,
            [(own_tokens, lambda: kv[1 - c]), (their_tokens, lambda: dkv_sib[...])],
        )
        done(0)

        grad, gain_row = norm_back(
            pick(lat_v[0], lat_v[1]), gain[0:1], dot_nt(rs[0], square_block(wr, 0, 0))
        )
        gain_acc[0, 0:1] = gain_row
        live_grad = grad_mid[...] + grad
        lat_grad[0] = pick(live_grad, lat_grad[0])
        lat_grad[1] = pick(lat_grad[1], live_grad)
        advance(2)
        out = []
        parts = tokens // 256

        def fetch(n):
            return [
                local_copy(kept["xl"].at[pl.ds(n * 256 + i * 128, 128)], xl.at[i]) for i in range(2)
            ]

        fetched = fetch(0)
        for n in range(parts):
            for made in fetched + out:
                made.wait()

            @pl.loop(0, 2)
            def _(i):
                at = pl.ds(pl.multiple_of(n * 256 + i * 128, 128), 128)
                term = dot_nt(kv[0, at], square_block(wr, 0, 1))
                term += dot_nt(kv[1, at], square_block(wr, 1, 0))
                grad, gain_row = norm_back(xl[i].astype(F32), gain[1:2], term)
                dxs[i] = grad
                gain_acc[0, 1:2] += gain_row

            if n + 1 < parts:
                fetched = fetch(n + 1)
            out = [
                local_copy(dxs.at[i], dx.at[pl.ds(n * 256 + i * 128, 128)]) for i in range(2)
            ]
            advance(3)
        for made in out:
            made.wait()
        gain_one = [sems.copy(gain_acc.at[0], spot(gain_sub, k), sub_peers[k]) for k in range(3)]
        advance(3)
        wait_all(gain_one)
        gain_acc[1] = gain_acc[0] + gain_sub[0] + gain_sub[1] + gain_sub[2]
        gain_two = [sems.copy(gain_acc.at[1], spot(gain_dp, k), dp_peers[k]) for k in range(7)]
        for made in sent:
            made.wait_send()
        return gain_two

    def vmem(*shape, dtype=BF16):
        return pltpu.VMEM(shape, dtype)

    holder = {}

    pl.run_scoped(
        self_part,
        vmem(2 * two, hidden),
        vmem(two, hidden),
        vmem(2, width // 4, 2 * two),
        vmem(width, 2 * two),
        vmem(width, 2 * two),
        vmem(width, 2 * two),
        vmem(2, 2, two, quarter),
        vmem(2, 2, two, width),
        vmem(2, rows, width, dtype=F32),
        vmem(two, width, dtype=F32),
        vmem(two, width, dtype=F32),
        vmem(3, two, width),
        vmem(2 * pairs, two, rows),
        vmem(two, width, dtype=F32),
        vmem(two, width),
    )

    def run_cross(*bufs):
        holder["gain"] = cross_part(*bufs)

    pl.run_scoped(
        run_cross,
        vmem(two, hidden),
        vmem(rows, hidden),
        vmem(2, 2, width // 4, rows),
        vmem(width, two),
        vmem(2, 2, rows, quarter),
        vmem(rows, width, dtype=F32),
        vmem(width, two),
        vmem(2, rows, width),
        vmem(width, 2 * tokens),
        vmem(2, tokens, width),
        vmem(pairs, two, tokens),
        vmem(rows, width),
        vmem(rows, width, dtype=F32),
        vmem(rows, width),
        vmem(2, 128, width),
        vmem(2, 128, width, dtype=F32),
        vmem(2, rows, width, dtype=F32),
        vmem(rows, width, dtype=F32),
    )
    advance(len(steps))
    wait_all(holder["gain"])
    gain_out[...] = gain_acc[1] + jnp.sum(gain_dp[...], axis=0)
    sems.drain()


def backward_all(shard, full, norm_gain, latents, cotangent, flags, kept):
    count = len(full)
    rows, width = latents.shape[1:]
    tokens, hidden = kept["xl"].shape[0], kept["mh"].shape[1]
    dims = (rows, tokens, width, hidden)
    two = 2 * rows
    copies = 10 + 6 + 2 * count * (2 + 10 + 6)
    ring, halves = 3, 2 * count
    block_rows, block_columns = full[0].shape[5:]

    def room(number, lead, sixths):
        return [pltpu.VMEM(lead + (block_rows * sixths // 6, block_columns), BF16)] * number

    scratch = [pltpu.VMEM((2,) + full[0].shape[2:], BF16)] * count
    scratch += room(ring, (2, 4), 3) + room(ring, (4, 2), 3)
    scratch += room(halves, (4,), 1) + room(halves, (4,), 1)
    scratch += room(halves, (3, 2), 2) + room(halves, (3, 2), 2) + room(halves, (3,), 2)
    scratch += room(halves, (), 2) + room(halves, (), 2)
    scratch += room(halves, (2,), 2) + room(halves, (2,), 2) + room(halves, (), 2)
    scratch += [
        pltpu.VMEM(full[0].shape, BF16),
        pltpu.VMEM(full[2].shape, BF16),
        pltpu.VMEM((two, width), F32),
        pltpu.VMEM((2, two, hidden // 4), BF16),
        pltpu.VMEM((2, two, width), BF16),
        pltpu.VMEM((2, width // 4, rows), BF16),
        pltpu.VMEM((2, rows, hidden // 4), BF16),
        pltpu.VMEM((rows, width), BF16),
        pltpu.VMEM((tokens, width), BF16),
        pltpu.VMEM((2, 8, width), F32),
        pltpu.VMEM((3, 8, width), F32),
        pltpu.VMEM((7, 8, width), F32),
        pltpu.SemaphoreType.DMA((copies,)),
        pltpu.SemaphoreType.DMA((copies,)),
        pltpu.SemaphoreType.DMA((48,)),
        pltpu.SemaphoreType.REGULAR((halves - ring,)),
    ]
    shapes = [jax.ShapeDtypeStruct(d, F32) for d in shard]
    shapes += [
        jax.ShapeDtypeStruct((8, width), F32),
        jax.ShapeDtypeStruct(latents.shape, F32),
        jax.ShapeDtypeStruct((tokens, width), F32),
    ]
    outs = pl.pallas_call(
        functools.partial(backward_kernel, tuple(kept), dims),
        out_shape=shapes,
        in_specs=[ANY] * count + [VMEM, ANY, ANY, SMEM] + [ANY] * len(kept),
        out_specs=[VMEM] * (count + 2) + [ANY],
        scratch_shapes=scratch,
        compiler_params=pltpu.CompilerParams(
            collective_id=1, has_side_effects=True, vmem_limit_bytes=60 << 20
        ),
        name="backward_and_scatter",
    )(*full, norm_gain, latents, cotangent, flags, *kept.values())
    return outs[:count], *outs[count:]


def finish_kernel(gain_share, gain_rows, count, *refs):
    flags, result, lat_grad, tok_grad, gain_total = refs[:5]
    shards_in = refs[5 : 5 + count]
    out_result, out_lat, out_tok, out_gain = refs[5 + count : 9 + count]
    shards_out = refs[9 + count : 9 + 2 * count]
    gain_in, zeros, sems_in, sems_out = refs[9 + 2 * count : 13 + 2 * count]
    held = refs[13 + 2 * count :]
    tokens, pieces = tok_grad.shape[0], held[-1].shape[0]
    size = tokens // pieces
    live = jnp.where(flags[0] == 0, 0, 1)
    moves = []
    for n in range(pieces):
        at = pl.ds(n * size, size)
        moves.append((tok_grad.at[at], held[-1].at[n], out_tok.at[live, at]))
    moves += zip((result, lat_grad, *shards_in), held, (out_result, out_lat, *shards_out))
    gain_copy = pltpu.make_async_copy(gain_total, gain_in, sems_in.at[len(moves)])
    reads = [
        pltpu.make_async_copy(src, room, sems_in.at[i]) for i, (src, room, dst) in enumerate(moves)
    ]
    for made in reads:
        made.start()
    gain_copy.start()
    zeros[...] = jnp.zeros_like(zeros)
    started = []
    for n in range(pieces):
        started.append(
            pltpu.make_async_copy(
                zeros, out_tok.at[1 - live, pl.ds(n * size, size)], sems_out.at[len(moves) + n]
            )
        )
        started[-1].start()
    for i, (src, room, dst) in enumerate(moves):
        reads[i].wait()
        started.append(pltpu.make_async_copy(room, dst, sems_out.at[i]))
        started[-1].start()
    gain_copy.wait()
    dp = lax.axis_index("dp")
    for i in range(8):

        @pl.when(dp == i)
        def _():
            out_gain[...] = gain_in[:gain_rows, i * gain_share : (i + 1) * gain_share]

    for made in started:
        made.wait()


def finish_all(gain_shape, flags, result, lat_grad, tok_grad, gain_total, shards_in):
    count, pieces = len(shards_in), 4
    tokens, width = tok_grad.shape
    arrays = [result, lat_grad, tok_grad, gain_total, *shards_in]
    shapes = [
        jax.ShapeDtypeStruct(result.shape, F32),
        jax.ShapeDtypeStruct(lat_grad.shape, F32),
        jax.ShapeDtypeStruct((2, tokens, width), F32),
        jax.ShapeDtypeStruct(gain_shape, F32),
    ]
    shapes += [jax.ShapeDtypeStruct(a.shape, F32) for a in shards_in]
    return pl.pallas_call(
        functools.partial(finish_kernel, gain_shape[1], gain_shape[0], count),
        out_shape=shapes,
        in_specs=[SMEM] + [ANY] * len(arrays),
        out_specs=[ANY] * 3 + [VMEM] + [ANY] * count,
        scratch_shapes=[
            pltpu.VMEM(gain_total.shape, F32),
            pltpu.VMEM((tokens // pieces, width), F32),
            pltpu.SemaphoreType.DMA((3 + count + pieces,)),
            pltpu.SemaphoreType.DMA((2 + count + 2 * pieces,)),
            *(pltpu.VMEM(a.shape, F32) for a in (result, lat_grad, *shards_in)),
            pltpu.VMEM((pieces, tokens // pieces, width), F32),
        ],
        compiler_params=pltpu.CompilerParams(vmem_limit_bytes=60 << 20),
        name="write_outputs",
    )(flags, *arrays)


def layer_norm(values, gain_row):
    centred = values - jnp.mean(values, axis=-1, keepdims=True)
    inverse = lax.rsqrt(jnp.mean(centred * centred, axis=-1, keepdims=True) + EPSILON)
    return centred * inverse * gain_row


def norm_backward(values, gain_row, gradient):
    unused, pull_back = jax.vjp(layer_norm, values, gain_row)
    return pull_back(gradient)


def gelu_tanh(values):
    return jax.nn.gelu(values, approximate=True)


def mm(left_side, weight):
    return jnp.dot(left_side, weight, preferred_element_type=F32)


def mm_nt(left_side, weight):
    return lax.dot_general(left_side, weight, (((1,), (1,)), ((), ())), preferred_element_type=F32)


def mm_tn(left_side, gradient):
    return lax.dot_general(
        left_side, gradient, (((0,), (0,)), ((), ())), preferred_element_type=F32
    )


def low(values):
    return values.astype(BF16)


def heads_of(values):
    return values.reshape(values.shape[:-1] + (HEADS, values.shape[-1] // HEADS))


def mlp_forward(residual, gain_row, up, down_t):
    normed = low(layer_norm(residual, gain_row))
    pre_act = mm(normed, up)
    hidden = low(gelu_tanh(pre_act))
    return normed, pre_act, hidden, mm_nt(hidden, down_t)


def mlp_backward(residual, gain_row, normed, pre_act, hidden, up, down_t, grad_out):
    grad_low = low(grad_out)
    grad_down_t = mm_tn(grad_low, hidden)
    grad_hidden = mm(grad_low, down_t)
    unused, gelu_back = jax.vjp(gelu_tanh, pre_act)
    grad_pre = low(gelu_back(grad_hidden)[0])
    grad_up = mm_tn(normed, grad_pre)
    grad_resid, grad_gain = norm_backward(residual, gain_row, mm_nt(grad_pre, up))
    return grad_resid, grad_gain, grad_up, grad_down_t


def live_layer(live_lat, dead_lat, tokens, count, live_cot, dead_cot, weights, norm_gain):
    c_attn, c_up, c_down_t, s_attn, s_up, s_down_t = weights
    rows, width = live_lat.shape
    scale = (width // HEADS) ** (-0.5)
    lat_low = low(layer_norm(live_lat, norm_gain[0]))
    queries = low(mm(lat_low, c_attn[:, :width]))
    token_values = tokens.astype(F32)
    tok_low = low(layer_norm(token_values, norm_gain[1]))
    kv_weight = c_attn[:, width : 3 * width]
    key_value = low(mm(tok_low, kv_weight))
    keys, values = heads_of(key_value[:, :width]), heads_of(key_value[:, width:])
    scores = (
        jnp.einsum("qhd,khd->hqk", heads_of(queries), keys, preferred_element_type=F32) * scale
    )
    valid = (jnp.arange(tokens.shape[0]) < count)[None, None, :]
    probs = jax.nn.softmax(jnp.where(valid, scores, MASKED), axis=-1)
    probs_low = low(probs)
    attended = jnp.einsum("hqk,khd->qhd", probs_low, values, preferred_element_type=F32)
    attended = attended.reshape(rows, width)
    cross_low = low(attended)
    middle = live_lat + mm(cross_low, c_attn[:, 3 * width :])
    c_norm, c_pre, c_hidden, c_mlp = mlp_forward(middle, norm_gain[2], c_up, c_down_t)
    after_cross = jnp.concatenate([middle + c_mlp, dead_lat], axis=0)

    self_low = low(layer_norm(after_cross, norm_gain[3]))
    qkv = low(mm(self_low, s_attn[:, : 3 * width])).reshape(2, rows, 3 * width)
    s_q = heads_of(qkv[..., :width])
    s_k = heads_of(qkv[..., width : 2 * width])
    s_v = heads_of(qkv[..., 2 * width :])
    s_scores = jnp.einsum("iqhd,ikhd->ihqk", s_q, s_k, preferred_element_type=F32) * scale
    s_probs = jax.nn.softmax(s_scores, axis=-1)
    s_probs_low = low(s_probs)
    s_out = jnp.einsum("ihqk,ikhd->iqhd", s_probs_low, s_v, preferred_element_type=F32)
    s_out_low = low(s_out.reshape(2 * rows, width))
    after_attn = after_cross + mm(s_out_low, s_attn[:, 3 * width :])
    m_norm, m_pre, m_hidden, m_mlp = mlp_forward(after_attn, norm_gain[4], s_up, s_down_t)
    result = after_attn + m_mlp

    cotangent = jnp.concatenate([live_cot, dead_cot], axis=0)
    grad_in, gain_four, d_s_up, d_s_down_t = mlp_backward(
        after_attn, norm_gain[4], m_norm, m_pre, m_hidden, s_up, s_down_t, cotangent
    )
    grad_attn = cotangent + grad_in
    grad_y = low(grad_attn)
    d_s_o = mm_tn(s_out_low, grad_y)
    grad_out = heads_of(low(mm_nt(grad_y, s_attn[:, 3 * width :])).reshape(2, rows, width))
    grad_probs = jnp.einsum("iqhd,ikhd->ihqk", grad_out, s_v, preferred_element_type=F32)
    delta = jnp.sum(grad_probs * s_probs, axis=-1, keepdims=True)
    grad_scores = low(s_probs * (grad_probs - delta))
    g_q = jnp.einsum("ihqk,ikhd->iqhd", grad_scores, s_k, preferred_element_type=F32) * scale
    g_k = jnp.einsum("ihqk,iqhd->ikhd", grad_scores, s_q, preferred_element_type=F32) * scale
    g_v = jnp.einsum("ihqk,iqhd->ikhd", s_probs_low, grad_out, preferred_element_type=F32)
    grad_qkv = low(
        jnp.concatenate([g.reshape(2 * rows, width) for g in (g_q, g_k, g_v)], axis=-1)
    )
    d_s_qkv = mm_tn(self_low, grad_qkv)
    grad_in, gain_three = norm_backward(
        after_cross, norm_gain[3], mm_nt(grad_qkv, s_attn[:, : 3 * width])
    )
    grad_cross = grad_attn + grad_in
    live_grad, dead_grad = grad_cross[:rows], grad_cross[rows:]
    grad_in, gain_two, d_c_up, d_c_down_t = mlp_backward(
        middle, norm_gain[2], c_norm, c_pre, c_hidden, c_up, c_down_t, live_grad
    )
    grad_middle = live_grad + grad_in
    grad_cross_y = low(grad_middle)
    d_c_o = mm_tn(cross_low, grad_cross_y)
    grad_cross_out = low(mm_nt(grad_cross_y, c_attn[:, 3 * width :]))
    out_heads = heads_of(grad_cross_out)
    grad_weights = jnp.einsum("qhd,khd->hqk", out_heads, values, preferred_element_type=F32)
    row_delta = jnp.transpose(jnp.sum(heads_of(grad_cross_out.astype(F32) * attended), axis=-1))
    grad_scores = low(probs * (grad_weights - row_delta[..., None]))
    grad_query = low(
        (
            jnp.einsum("hqk,khd->qhd", grad_scores, keys, preferred_element_type=F32) * scale
        ).reshape(rows, width)
    )
    grad_keys = (
        jnp.einsum("hqk,qhd->khd", grad_scores, heads_of(queries), preferred_element_type=F32)
        * scale
    )
    grad_values = jnp.einsum("hqk,qhd->khd", probs_low, out_heads, preferred_element_type=F32)
    grad_kv = low(
        jnp.concatenate(
            [grad_keys.reshape(-1, width), grad_values.reshape(-1, width)], axis=-1
        )
    )
    d_c_kv = mm_tn(tok_low, grad_kv)
    grad_tokens, gain_one = norm_backward(token_values, norm_gain[1], mm_nt(grad_kv, kv_weight))
    d_c_q = mm_tn(lat_low, grad_query)
    grad_in, gain_zero = norm_backward(
        live_lat, norm_gain[0], mm_nt(grad_query, c_attn[:, :width])
    )
    live_lat_grad = grad_middle + grad_in
    d_c_attn = low(jnp.concatenate([d_c_q, d_c_kv, d_c_o], axis=1))
    d_s_attn = low(jnp.concatenate([d_s_qkv, d_s_o], axis=1))
    gain_grad = jnp.stack([gain_zero, gain_one, gain_two, gain_three, gain_four])
    grads = (d_c_attn, low(d_c_up), low(d_c_down_t), d_s_attn, low(d_s_up), low(d_s_down_t))
    return result, live_lat_grad, dead_grad, grad_tokens, grads, gain_grad


def column_blocks(blocks):
    sub, dp, rows, columns = blocks.shape
    return blocks.transpose(1, 2, 0, 3).reshape(dp * rows, sub * columns)


def row_blocks(blocks):
    sub, dp, rows, columns = blocks.shape
    return blocks.transpose(0, 2, 1, 3).reshape(sub * rows, dp * columns)


def shards(*arrays, dp_size, sub_size):
    latents, inputs, counts, flags = arrays[:4]
    cross_attn, cross_up, cross_down, self_attn, self_up, self_down, gains, cotangent = arrays[4:]
    width = latents.shape[-1]
    own = (
        cross_attn,
        cross_up,
        jnp.transpose(cross_down),
        self_attn,
        self_up,
        jnp.transpose(self_down),
    )
    live = jnp.where(flags[0] == 0, 0, 1)
    here = (jnp.arange(inputs.shape[0]) == live)[:, None, None]
    if dp_size == 8 and sub_size == 4:
        full, norm_gain, result, kept = forward_all(
            own, gains, latents, inputs, cotangent, counts, flags
        )
        owned, gain_total, grad_latents, grad_tokens = backward_all(
            [w.shape for w in own], full, norm_gain, latents, cotangent, flags, kept
        )
        result, grad_latents, grad_inputs, gain_owned, *owned = finish_all(
            gains.shape, flags, result, grad_latents, grad_tokens, gain_total, owned
        )
        owned = [jnp.transpose(g) if i in (2, 5) else g for i, g in enumerate(owned)]
        return (result, grad_latents, grad_inputs, *owned, gain_owned)

    blocks = [lax.all_gather(lax.all_gather(w, "dp", axis=0), "sub", axis=0) for w in own]
    norm_gain = lax.all_gather(gains, "dp", axis=1, tiled=True)
    transposed = (False, False, True, False, False, True)
    weights = [
        row_blocks(b) if flip else column_blocks(b) for b, flip in zip(blocks, transposed)
    ]

    def item(array, index):
        return lax.dynamic_index_in_dim(array, index, 0, keepdims=False)

    result, live_grad, dead_grad, grad_tokens, grads, gain_grad = live_layer(
        item(latents, live),
        item(latents, 1 - live),
        item(inputs, live),
        item(counts, live),
        item(cotangent, live),
        item(cotangent, 1 - live),
        weights,
        norm_gain.astype(F32),
    )

    def both(live_part, dead_part):
        first = jnp.where(live == 0, live_part, dead_part)
        second = jnp.where(live == 0, dead_part, live_part)
        return jnp.stack([first, second])

    rows = latents.shape[1]
    result = both(result[:rows], result[rows:])
    grad_latents = both(live_grad, dead_grad)
    grad_inputs = jnp.where(here, grad_tokens[None], 0.0)

    def blocks_of(grad, shape, flip):
        r, c = shape
        if flip:
            return grad.reshape(sub_size, r, dp_size, c).transpose(0, 2, 1, 3)
        return grad.reshape(dp_size, r, sub_size, c).transpose(2, 0, 1, 3)

    grads = [blocks_of(g, w.shape, flip) for g, w, flip in zip(grads, own, transposed)]
    owned = [lax.psum_scatter(g, "sub", scatter_dimension=0) for g in grads]
    owned = [lax.psum_scatter(g.astype(F32), "dp", scatter_dimension=0) for g in owned]
    gain_owned = lax.psum(gain_grad, "sub")
    gain_owned = lax.psum_scatter(gain_owned, "dp", scatter_dimension=1, tiled=True)
    owned = [jnp.transpose(g) if flip else g for g, flip in zip(owned, transposed)]
    return (result, grad_latents, grad_inputs, *owned, gain_owned)


def solution(mesh):
    item = P(("dp", "sub"), None, None)
    weight = P("dp", "sub")
    gain = P(None, "dp")
    placed = (item, item, P(("dp", "sub")), P()) + (weight,) * 6 + (gain, item)
    return jax.shard_map(
        functools.partial(shards, dp_size=mesh.shape["dp"], sub_size=mesh.shape["sub"]),
        mesh=mesh,
        in_specs=placed,
        out_specs=(item, item, item) + (weight,) * 6 + (gain,),
        check_vma=False,
    )
```

```python
import collections
import functools

import jax
import jax.numpy as jnp
from jax import lax
from jax.experimental import pallas as pl
from jax.experimental.pallas import tpu as pltpu
from jax.sharding import PartitionSpec as P

HEADS = 12
EPSILON = 1e-05
MASKED = -1e30
MESH_ID = pl.DeviceIdType.MESH
F32 = jnp.float32
BF16 = jnp.bfloat16
ANY = pl.BlockSpec(memory_space=pl.ANY)
VMEM = pl.BlockSpec(memory_space=pltpu.VMEM)
SMEM = pl.BlockSpec(memory_space=pltpu.SMEM)


PIECES = {
    "C": (0, 2),
    "A": (2, 1),
    "B": (3, 1),
    "D": (4, 2),
    "CA": (0, 3),
    "AB": (2, 2),
    "BD": (3, 3),
}


def piece(name, rows):
    first, size = PIECES[name]
    return pl.ds(first * (rows // 6), size * (rows // 6))


class Place:
    def __init__(self):
        dp, sub = lax.axis_index("dp"), lax.axis_index("sub")
        self.z, self.y, self.x, self.c = dp // 2, dp % 2, sub // 2, sub % 2

    def dev(self, z=None, y=None, x=None, c=None):
        z = self.z if z is None else z
        y = self.y if y is None else y
        x = self.x if x is None else x
        c = self.c if c is None else c
        return (z * 2 + y, x * 2 + c)

    def zk(self, k):
        return (self.z + k) % 4


def now(ref):
    return ref() if callable(ref) else ref


def spot(ref, index):
    return lambda: ref.at[index]


def only_if(condition, action):
    if condition is None:
        action()
    else:
        pl.when(condition())(action)


class Flight:
    def __init__(self, sems, ref, send_index, recv_index):
        self.sems, self.ref, self.send_index, self.recv_index = sems, ref, send_index, recv_index

    def made(self):
        place = self.sems.place
        return pltpu.make_async_remote_copy(
            src_ref=now(self.ref),
            dst_ref=now(self.ref),
            send_sem=self.sems.send.at[self.send_index],
            recv_sem=self.sems.recv.at[self.recv_index],
            device_id=place.dev(c=1 - place.c),
            device_id_type=MESH_ID,
        )

    def wait_send(self):
        self.made().wait_send()

    def wait_recv(self):
        self.made().wait_recv()


class Sems:
    def __init__(self, place, send, recv):
        self.place, self.send, self.recv, self.count, self.sent = place, send, recv, 0, []

    def reserve(self, n):
        self.count += n
        return self.count - n

    def start(self, src, dst, device, send_index, recv_index, condition=None, later=True):
        def action():
            pltpu.make_async_remote_copy(
                src_ref=now(src),
                dst_ref=now(dst),
                send_sem=self.send.at[send_index],
                recv_sem=self.recv.at[recv_index],
                device_id=device,
                device_id_type=MESH_ID,
            ).start()

        only_if(condition, action)
        flight = Flight(self, dst, send_index, recv_index)
        if later:
            self.sent.append((condition, flight))
        return flight

    def copy(self, src, dst, device, later=True):
        index = self.reserve(1)
        return self.start(src, dst, device, index, index, later=later)

    def drain(self):
        for condition, flight in self.sent:
            only_if(condition, flight.wait_send)


def greet(place, devices):
    barrier = pltpu.get_barrier_semaphore()
    for device in devices:
        pl.semaphore_signal(barrier, inc=1, device_id=device, device_id_type=MESH_ID)
    pl.semaphore_wait(barrier, len(devices))


def wait_all(copies):
    for made in copies:
        made.wait_recv()


class Spread:
    def __init__(self, sems, src, where):
        self.sems, self.where, place = sems, where, sems.place
        self.base = sems.reserve(4)
        z = place.z
        for k, condition in ((1, lambda: z != 3), (2, None), (3, lambda: z != 0)):
            at = self.base + k - 1
            sems.start(src, where(z), place.dev(z=place.zk(k)), at, at, condition)

    def arrived(self, k):
        origin = self.sems.place.zk(4 - k)
        Flight(self.sems, self.where(origin), self.base + 3, self.base + k - 1).wait_recv()

    def forward(self):
        self.arrived(2)
        place = self.sems.place
        block = self.where(place.zk(2))
        for z, target, k in ((2, 3, 3), (1, 0, 1)):
            self.sems.start(
                block,
                block,
                place.dev(z=target),
                self.base + 3,
                self.base + k - 1,
                functools.partial(lambda z: place.z == z, z),
            )

    def finish(self):
        self.arrived(1)
        self.arrived(3)


class Collect:
    def __init__(self, sems, part, into, through):
        self.sems, self.part, self.into, self.through = sems, part, into, through
        place = sems.place
        self.base = sems.reserve(4)
        z = place.z
        for k, condition in (
            (1, lambda: z != 3),
            (2, lambda: (z == 0) | (z == 3)),
            (3, lambda: z != 0),
        ):
            self.send(k, condition)
        for k, end, middle in ((1, 3, 2), (3, 0, 1)):
            at = self.base + 3
            sems.start(part(place.zk(k)), through, place.dev(z=middle), at, at, functools.partial(lambda end: z == end, end))

    def send(self, k, condition):
        place, at = self.sems.place, self.base + k - 1
        self.sems.start(
            self.part(place.zk(k)),
            spot(self.into, k - 1),
            place.dev(z=place.zk(k)),
            at,
            at,
            condition,
        )

    def forward(self, add):
        place = self.sems.place

        def middle():
            return (place.z == 1) | (place.z == 2)

        @pl.when(middle())
        def _():
            Flight(self.sems, self.through, self.base + 3, self.base + 3).wait_recv()
            add(place.zk(2))

        self.send(2, middle)

    def finish(self):
        z = self.sems.place.z
        for k, condition in ((1, lambda: z != 0), (2, None), (3, lambda: z != 3)):
            flight = Flight(self.sems, spot(self.into, k - 1), self.base + 3, self.base + k - 1)
            only_if(condition, flight.wait_recv)


def slots(count, places, order):
    steps = []
    for slot in range(min(places.values()), count + max(places.values())):
        for name in order:
            i = slot - places[name]
            if 0 <= i < count:
                steps.append((slot, name, i))
    return steps


def dot(a, b):
    return jnp.dot(a, b, preferred_element_type=F32)


def dot_nt(a, b):
    return lax.dot_general(a, b, (((1,), (1,)), ((), ())), preferred_element_type=F32)


def low(values):
    return values.astype(BF16)


def normed(values):
    centred = values - jnp.mean(values, axis=-1, keepdims=True)
    inverse = lax.rsqrt(jnp.mean(centred * centred, axis=-1, keepdims=True) + EPSILON)
    return centred * inverse, inverse


def gelu_both(u):
    k, a = 0.7978845608028654, 0.044715
    square = u * u
    t = jnp.tanh(k * u * (1.0 + a * square))
    half = 0.5 * (1.0 + t)
    slope = half + (0.5 * k) * u * (1.0 - t * t) * (1.0 + (3.0 * a) * square)
    return u * half, slope


def square_block(ref, x, c):
    halves = []
    for h in range(2):
        block = ref[h, x, c]
        halves.append(block.reshape(-1, block.shape[3]))
    return jnp.concatenate(halves, axis=1)


def hidden_block(ref, z):
    parts = []
    for y in range(2):
        rows = [ref[h, x, c, z, y] for x in range(2) for c in range(2) for h in range(2)]
        parts.append(jnp.concatenate(rows, axis=0))
    return jnp.concatenate(parts, axis=1)


def left_half(shape):
    return lax.broadcasted_iota(jnp.int32, shape, 1) < 64


def stack_heads(values):
    left = left_half(values.shape)
    zero = jnp.zeros_like(values)
    return jnp.concatenate([jnp.where(left, values, zero), jnp.where(left, zero, values)], axis=0)


def join_heads(values):
    rows = values.shape[0] // 2
    top, bottom = values[:rows], values[rows:]
    return jnp.where(left_half(top.shape), top, bottom)


def lanes(index, size):
    return pl.ds(pl.multiple_of(index * size, size), size)


def kept_shapes(rows, tokens, width, hidden):
    two = 2 * rows
    return {
        "cq": ((rows, width), BF16),
        "kv": ((2, tokens, width), BF16),
        "cp": ((width // 128, two, tokens), BF16),
        "co": ((rows, width), F32),
        "mid": ((rows, width), F32),
        "gpc": ((rows, hidden), BF16),
        "ac": ((two, width), F32),
        "sqkv": ((3, two, width), BF16),
        "sp": ((2 * (width // 128), two, rows), BF16),
        "aa": ((two, width), F32),
        "gps": ((two, hidden), BF16),
        "xl": ((tokens, width), BF16),
    }


def paired_shapes(rows, tokens, width, hidden):
    two = 2 * rows
    return {
        "gyt": ((2, width // 4, 2 * two), BF16),
        "mh": ((2 * two, hidden), BF16),
        "mnt": ((width, 2 * two), BF16),
        "sbt": ((width, 2 * two), BF16),
        "l1t": ((width, 2 * two), BF16),
        "ch": ((two, hidden), BF16),
        "cnt": ((width, two), BF16),
        "lst": ((width, two), BF16),
        "xbt": ((width, 2 * tokens), BF16),
    }


def forward_kernel(names, dims, *refs):
    rows, tokens, width, hidden = dims
    two = 2 * rows
    count = 6
    refs = list(refs)

    def take(n):
        out = refs[:n]
        del refs[:n]
        return out

    own = take(count)
    gain, lat, tok, cot, live_counts, flags = take(6)
    full = take(count)
    gain_out, result = take(2)
    kept = dict(zip(names, take(len(names))))
    gain_all, lat_v, cot_v, tok_v, z2, xb, xbt, gyt, lst, wr0, wr1, wt = take(12)
    cq, kv, cp, co, mid, ch, gpc, ac, sqkv, sp, so, aa, mh, gps, xl, lt, cnt, mnt = take(18)
    gain_own, gain_one, zb_v, nb = take(4)
    send, recv, local = take(3)
    wr = (wr0, wr1)
    place = Place()
    x, y, z, c = place.x, place.y, place.z, place.c
    sems = Sems(place, send, recv)
    local_count = [0]
    local_open = []

    def local_copy(src, dst):
        made = pltpu.make_async_copy(src, dst, local.at[local_count[0]])
        local_count[0] += 1
        made.start()
        return made

    in_gain = local_copy(gain, gain_own)
    in_lat, in_tok, in_cot = local_copy(lat, lat_v), local_copy(tok, tok_v), local_copy(cot, cot_v)
    px, py, pc = place.dev(x=1 - x), place.dev(y=1 - y), place.dev(c=1 - c)
    me_dp = z * 2 + y
    dp_peers = [((me_dp + k) % 8, x * 2 + c) for k in range(1, 8)]
    greet(place, dp_peers + [px, pc])

    halves = 2 * count
    blocks = [full[i // 2].at[i % 2] for i in range(halves)]
    ones, twos, threes, across, placed = {}, {}, {}, {i: [] for i in range(halves)}, {}
    block_rows = full[0].shape[5]

    def shard(i):
        w, h = own[i // 2], i % 2
        if w.shape[0] == block_rows:
            return w, slice(None), pl.ds(h * (w.shape[1] // 2), w.shape[1] // 2), 0
        return w, slice(None), pl.ds(0, w.shape[1]), h * block_rows

    def own_piece(i, name):
        w, unused, columns, first = shard(i)
        at = piece(name, block_rows)
        return w.at[pl.ds(first + at.start, at.size), columns]

    def step_one(i):
        g = blocks[i]
        w, unused, columns, first = shard(i)
        placed[i] = local_copy(w.at[pl.ds(first, block_rows), columns], g.at[x, c, z, y])
        ab, pc_, pd = (piece(n, block_rows) for n in ("AB", "C", "D"))
        spread = Spread(sems, own_piece(i, "AB"), lambda o: g.at[x, c, o, y, ab])
        ones[i] = (
            spread,
            [
                sems.copy(own_piece(i, "C"), g.at[x, c, z, y, pc_], px),
                sems.copy(own_piece(i, "D"), g.at[x, c, z, y, pd], py),
            ],
        )

    def step_one_forward(i):
        ones[i][0].forward()

    def step_two(i):
        g = blocks[i]
        spread, got = ones.pop(i)
        placed.pop(i).wait()
        wait_all(got)
        pa, pb, pc_, pd = (piece(n, block_rows) for n in ("A", "B", "C", "D"))
        spread_c = Spread(sems, g.at[:, c, z, y, pc_], lambda o: g.at[:, c, o, y, pc_])
        spread_d = Spread(sems, g.at[x, c, z, :, pd], lambda o: g.at[x, c, o, :, pd])
        spread.finish()
        got = [
            sems.copy(g.at[x, c, :, y, pa], g.at[x, c, :, y, pa], px),
            sems.copy(g.at[x, c, :, y, pb], g.at[x, c, :, y, pb], py),
        ]
        twos[i] = ((spread_c, spread_d), got)

    def step_two_forward(i):
        for spread in twos[i][0]:
            spread.forward()

    def step_three(i):
        g = blocks[i]
        spreads, got = twos.pop(i)
        for spread in spreads:
            spread.finish()
        wait_all(got)
        ca, bd = piece("CA", block_rows), piece("BD", block_rows)
        threes[i] = [
            sems.copy(g.at[:, c, :, y, ca], g.at[:, c, :, y, ca], py),
            sems.copy(g.at[x, c, :, :, bd], g.at[x, c, :, :, bd], px),
        ]
        across[i] += [
            sems.copy(g.at[:, c, :, y, ca], g.at[:, c, :, y, ca], pc),
            sems.copy(g.at[x, c, :, :, bd], g.at[x, c, :, :, bd], pc),
        ]

    def step_four(i):
        wait_all(threes.pop(i))
        g = blocks[i]
        ca, bd = piece("CA", block_rows), piece("BD", block_rows)
        across[i] += [
            sems.copy(g.at[:, c, :, 1 - y, ca], g.at[:, c, :, 1 - y, ca], pc),
            sems.copy(g.at[1 - x, c, :, :, bd], g.at[1 - x, c, :, :, bd], pc),
        ]

    loading = {}

    def load(m, dst):
        def begin():
            for h in range(2):
                wait_all(across.pop(2 * m + h))
            loading[m] = local_copy(full[m], dst)

        return begin

    def keep(name, src):
        local_open.append(local_copy(src, kept[name]))

    def pair(name, mine, theirs, axis_size, axis):
        here, there = pl.ds(0, axis_size), pl.ds(axis_size, axis_size)
        dst = kept[name]

        def part(where):
            return dst.at[where] if axis == 0 else dst.at[:, where] if axis == 1 else dst.at[:, :, where]

        local_open.append(local_copy(mine, part(here)))
        across_pairs.append(sems.copy(theirs, part(there), pc))

    across_pairs = []
    gain_copies = []

    def pick(flag_first, first, second):
        return jnp.where(flag_first, first, second)

    first_live = flags[0] == 0
    live_count = jnp.where(first_live, live_counts[0], live_counts[1])

    def send_gains():
        in_gain.wait()
        gain_one[...] = jnp.zeros_like(gain_one)
        gain_one[: gain.shape[0], : gain.shape[1]] = gain_own[...]
        gain_all[me_dp] = gain_one[...]
        for device in dp_peers:
            gain_copies.append(sems.copy(gain_one, gain_all.at[me_dp], device))

    def start():
        wait_all(gain_copies)
        row = lax.broadcasted_iota(jnp.int32, (128, width), 0)
        column = lax.broadcasted_iota(jnp.int32, (128, width), 1)
        share = width // 8
        gain_out[...] = jnp.zeros_like(gain_out)

        @pl.loop(0, 8)
        def _(i):
            spread = low(jnp.where((column == row + share * i) & (row < share), 1.0, 0.0))
            gain_out[...] += dot(gain_all[i], spread)

        in_lat.wait()
        in_cot.wait()
        z2[:rows] = pick(first_live, lat_v[0], lat_v[1])
        z2[rows:] = pick(first_live, lat_v[1], lat_v[0])
        zb = low(normed(z2[:rows])[0] * gain_out[0:1])
        zb_v[...] = zb
        lst[0] = zb.T
        gy_first = low(pick(first_live, cot_v[0], cot_v[1]))
        gy_last = low(pick(first_live, cot_v[1], cot_v[0]))
        gyt[:, :, :, :rows] = gy_first.T.reshape(2, 2, width // 4, rows)
        gyt[:, :, :, rows:] = gy_last.T.reshape(2, 2, width // 4, rows)
        pair("gyt", gyt.at[:, c], gyt.at[:, 1 - c], two, 2)

    def tokens_part(first, last):
        def run():
            if first == 0:
                in_tok.wait()

            @pl.loop(first, last)
            def _(i):
                at = lanes(i, 128)
                here = pick(first_live, tok_v[0, at], tok_v[1, at])
                xl[at] = here
                value = low(normed(here.astype(F32))[0] * gain_out[1:2])
                xb[at] = value
                xbt[:, at] = value.T

            if last == tokens // 128:
                keep("xl", xl)
                pair("xbt", xbt, xbt, tokens, 1)

        return run

    def cross_queries():
        loading[0].wait()
        cq[...] = low(dot(zb_v[...], square_block(wr[0], 0, 0)))
        keep("cq", cq)

    def keys_values(first, last):
        def run():
            for i in range(first, last):
                at = pl.ds(i * 256, 256)

                @pl.loop(0, 2)
                def _(j):
                    kv[j, at] = low(dot(xb[at], square_block(wr[0], j, 1 - j)))

            if last == tokens // 256:
                keep("kv", kv)

        return run

    def cross_attention(first, last):
        def run():
            @pl.loop(first, last)
            def _(p):
                at = lanes(p, 128)
                q = stack_heads(cq[:, at] * jnp.asarray(0.125, BF16))
                s = dot_nt(q, kv[0, :, at])
                s = jnp.where(lax.broadcasted_iota(jnp.int32, s.shape, 1) < live_count, s, MASKED)
                e = jnp.exp(s - jnp.max(s, axis=-1, keepdims=True))
                prob = low(e * (1.0 / jnp.sum(e, axis=-1, keepdims=True)))
                cp[p] = prob
                co[:, at] = join_heads(dot(prob, kv[1, :, at]))

            if last == width // 128:
                keep("cp", cp)
                keep("co", co)

        return run

    def cross_out():
        cob = low(co[...])
        lst[1] = cob.T
        pair("lst", lst.at[c], lst.at[1 - c], rows, 1)
        mid[...] = z2[:rows] + dot(cob, square_block(wr[0], 1, 1))
        keep("mid", mid)
        cnb = low(normed(mid[...])[0] * gain_out[2:3])
        nb[:rows] = cnb
        cnt[...] = cnb.T
        pair("cnt", cnt, cnt, rows, 1)

    def up(m, w, left, out, slope, first, last, after):
        def run():
            if first == 0:
                loading[m].wait()

            @pl.loop(first, last)
            def _(s):
                at = lanes(s, hidden // 4)
                value, grad = gelu_both(dot(nb[:left], square_block(w, s // 2, s % 2)))
                out[:, at] = low(value)
                slope[:, at] = low(grad)

            if last == 4:
                after()

        return run

    def down(m, act, into):
        loading[m].wait()

        @pl.loop(0, 4)
        def _(s):
            into[...] += dot_nt(act[:, lanes(s, hidden // 4)], hidden_block(wt, s))

    def cross_up_done():
        pair("ch", ch, ch, rows, 0)
        keep("gpc", gpc)

    def self_up_done():
        pair("mh", mh, mh, two, 0)
        keep("gps", gps)

    def cross_down():
        ac[:rows] = mid[...]
        ac[rows:] = z2[rows:]
        down(2, ch, ac.at[pl.ds(0, rows)])
        keep("ac", ac)
        sb = low(normed(ac[...])[0] * gain_out[3:4])
        nb[...] = sb
        lt[0] = sb.T
        pair("sbt", lt.at[0], lt.at[0], two, 1)

    def self_project():
        loading[3].wait()
        @pl.loop(0, 3)
        def _(i):
            sqkv[i] = low(dot(nb[...], square_block(wr[0], i // 2, i % 2)))

        keep("sqkv", sqkv)

    def self_attention(first, last):
        pairs = width // 128

        def run():
            @pl.loop(first, last, unroll=3)
            def _(i):
                at, row_at = lanes(i % pairs, 128), lanes(i // pairs, rows)
                q = stack_heads(sqkv[0, row_at, at] * jnp.asarray(0.125, BF16))
                s = dot_nt(q, sqkv[1, row_at, at])
                e = jnp.exp(s - jnp.max(s, axis=-1, keepdims=True))
                prob = low(e * (1.0 / jnp.sum(e, axis=-1, keepdims=True)))
                sp[i] = prob
                so[row_at, at] = low(join_heads(dot(prob, sqkv[2, row_at, at])))

            if last == 2 * pairs:
                keep("sp", sp)

        return run

    def self_out():
        lt[1] = so[...].T
        pair("l1t", lt.at[c], lt.at[1 - c], two, 1)
        aa[...] = ac[...] + dot(so[...], square_block(wr[0], 1, 1))
        keep("aa", aa)
        mnb = low(normed(aa[...])[0] * gain_out[4:5])
        nb[...] = mnb
        mnt[...] = mnb.T
        pair("mnt", mnt, mnt, two, 1)

    def self_down():
        z2[...] = aa[...]
        down(5, mh, z2)
        total = z2[...]
        result[0] = pick(first_live, total[:rows], total[rows:])
        result[1] = pick(first_live, total[rows:], total[:rows])

    pairs = width // 128
    work = collections.deque([(-2, send_gains), (1, start)])
    for n in range(4):
        work.append((1, tokens_part(n * tokens // 512, (n + 1) * tokens // 512)))
    for slot, part in (
        (4, load(0, wr[0])),
        (4, cross_queries),
        (4, keys_values(0, 1)),
        (4, keys_values(1, 2)),
        (4, keys_values(2, 3)),
        (4, keys_values(3, tokens // 256)),
        (4, cross_attention(0, 2)),
        (4, cross_attention(2, 4)),
        (4, cross_attention(4, pairs)),
        (4, cross_out),
        (6, load(1, wr[1])),
        (6, up(1, wr[1], rows, ch, gpc, 0, 2, cross_up_done)),
        (6, up(1, wr[1], rows, ch, gpc, 2, 4, cross_up_done)),
        (8, load(2, wt)),
        (8, cross_down),
        (10, load(3, wr[0])),
        (10, self_project),
        (10, self_attention(0, pairs)),
        (10, self_attention(pairs, 2 * pairs)),
        (10, self_out),
        (12, load(4, wr[1])),
        (12, up(4, wr[1], two, mh, gps, 0, 2, self_up_done)),
        (12, up(4, wr[1], two, mh, gps, 2, 4, self_up_done)),
        (14, load(5, wt)),
        (14, self_down),
    ):
        work.append((slot, part))
    steps = {
        "1": step_one,
        "f": step_one_forward,
        "2": step_two,
        "g": step_two_forward,
        "3": step_three,
        "4": step_four,
    }
    places = {"1": -2, "f": -1, "2": 0, "g": 0, "3": 1, "4": 2}
    for slot, name, i in slots(halves, places, "2314fg"):
        steps[name](i)
        if work and work[0][0] <= slot and name in "234f":
            work.popleft()[1]()
    while work:
        work.popleft()[1]()
    wait_all(across_pairs)
    for made in local_open:
        made.wait()
    sems.drain()


def half_shape(shard):
    return shard.shape[0], shard.shape[1] // 2


def forward_all(own, gain, latents, inputs, cotangent, counts, flags):
    count = len(own)
    rows, width = latents.shape[1:]
    tokens = inputs.shape[1]
    hidden = own[1].shape[1] * 4
    dims = (rows, tokens, width, hidden)
    two = 2 * rows
    kept = {**kept_shapes(*dims), **paired_shapes(*dims)}
    names = tuple(kept)
    copies = 7 + 2 * count * (6 + 10 + 4 + 2) + len(paired_shapes(*dims))
    block = (2, 2, 2, 4, 2) + half_shape(own[0])
    shapes = [jax.ShapeDtypeStruct(block, BF16) for w in own]
    shapes += [
        jax.ShapeDtypeStruct((16, width), F32),
        jax.ShapeDtypeStruct(latents.shape, F32),
    ]
    shapes += [jax.ShapeDtypeStruct(s, t) for s, t in kept.values()]
    pairs = width // 128
    scratch = [
        ((8, 16, 128), BF16),
        (latents.shape, F32),
        (latents.shape, F32),
        (inputs.shape, BF16),
        ((two, width), F32),
        ((tokens, width), BF16),
        ((width, tokens), BF16),
        ((2, 2, width // 4, two), BF16),
        ((2, width, rows), BF16),
        (block, BF16),
        (block, BF16),
        (block, BF16),
        ((rows, width), BF16),
        ((2, tokens, width), BF16),
        ((pairs, two, tokens), BF16),
        ((rows, width), F32),
        ((rows, width), F32),
        ((rows, hidden), BF16),
        ((rows, hidden), BF16),
        ((two, width), F32),
        ((3, two, width), BF16),
        ((2 * pairs, two, rows), BF16),
        ((two, width), BF16),
        ((two, width), F32),
        ((two, hidden), BF16),
        ((two, hidden), BF16),
        ((tokens, width), BF16),
        ((2, width, two), BF16),
        ((width, rows), BF16),
        ((width, two), BF16),
        (gain.shape, BF16),
        ((16, 128), BF16),
        ((rows, width), BF16),
        ((two, width), BF16),
    ]
    outs = pl.pallas_call(
        functools.partial(forward_kernel, names, dims),
        out_shape=shapes,
        in_specs=[ANY] * (count + 4) + [SMEM, SMEM],
        out_specs=[ANY] * count + [VMEM, VMEM] + [ANY] * len(names),
        scratch_shapes=[pltpu.VMEM(s, t) for s, t in scratch]
        + [
            pltpu.SemaphoreType.DMA((copies,)),
            pltpu.SemaphoreType.DMA((copies,)),
            pltpu.SemaphoreType.DMA((5 + 3 * count + len(names),)),
        ],
        compiler_params=pltpu.CompilerParams(
            collective_id=0, has_side_effects=True, vmem_limit_bytes=60 << 20
        ),
        name="gather_and_forward",
    )(*own, gain, latents, inputs, cotangent, counts, flags)
    full, (norm_gain, result) = outs[:count], outs[count : count + 2]
    return full, norm_gain, result, dict(zip(names, outs[count + 2 :]))


def norm_back(values, gain_row, gradient):
    unit, inverse = normed(values)
    scaled = gradient * gain_row
    grad = inverse * (
        scaled
        - jnp.mean(scaled, axis=-1, keepdims=True)
        - unit * jnp.mean(scaled * unit, axis=-1, keepdims=True)
    )
    return grad, jnp.sum(gradient * unit, axis=0, keepdims=True)


def attention_back(q, k, v, out_grad, prob, delta):
    prob_grad = dot_nt(out_grad, v)
    weight = prob.astype(F32)
    if delta is None:
        delta = jnp.sum(weight * prob_grad, axis=-1, keepdims=True)
    score_grad = low(weight * (prob_grad - delta))
    q_grad = join_heads(dot(score_grad, k)) * 0.125
    k_grad = low(dot(q.T, score_grad) * 0.125).T
    v_grad = low(dot(out_grad.T, prob)).T
    return low(q_grad), k_grad, v_grad


def add_blocks(total, where, part, there):
    total[where] = (total[where].astype(F32) + part[there].astype(F32)).astype(BF16)


def backward_kernel(names, dims, *refs):
    rows, tokens, width, hidden = dims
    two, quarter, pairs = 2 * rows, hidden // 4, width // 128
    count = 6
    halves, ring = 2 * count, 3
    order = (5, 4, 3, 2, 1, 0)
    refs = list(refs)

    def take(n):
        out = refs[:n]
        del refs[:n]
        return out

    full = take(count)
    gain, lat, cot, flags = take(4)
    kept = dict(zip(names, take(len(names))))
    outs = take(count)
    gain_out, lat_grad, dx = take(3)
    total = take(count)
    from_y, from_x = take(ring), take(ring)
    from_a, from_b, from_c, from_d, from_z, end_c, end_d = (take(halves) for _ in range(7))
    by_c, by_d, by_z = (take(halves) for _ in range(3))
    wr, wt, grad_ac, du_sib, r_sib, ge_sib, dcu_sib, rs_sib, dkv_sib = take(9)
    gain_acc, gain_sub, gain_dp, send, recv, local, free = take(7)
    place = Place()
    x, y, z, c = place.x, place.y, place.z, place.c
    sems = Sems(place, send, recv)
    local_count = [0]

    def local_copy(src, dst):
        made = pltpu.make_async_copy(src, dst, local.at[local_count[0]])
        local_count[0] += 1
        made.start()
        return made

    me_dp, me_sub = z * 2 + y, x * 2 + c
    sub_peers = [(me_dp, (me_sub + k) % 4) for k in (1, 2, 3)]
    dp_peers = [((me_dp + k) % 8, me_sub) for k in range(1, 8)]
    px, py, pc = place.dev(x=1 - x), place.dev(y=1 - y), place.dev(c=1 - c)
    first_live = flags[0] == 0
    gain_acc[...] = jnp.zeros_like(gain_acc)

    ones, twos, threes = {}, {}, {}
    block_rows, block_columns = total[0].shape[4:]

    def where(i):
        return total[order[i // 2]], i % 2

    def clear():
        for into in (*from_c, *from_d, *from_z):

            @pl.when(z == 0)
            def _():
                into[0] = jnp.zeros(into.shape[1:], BF16)

            @pl.when(z == 3)
            def _():
                into[2] = jnp.zeros(into.shape[1:], BF16)

    def step_one(i):
        a, h = where(i)
        if i >= ring:
            pl.semaphore_wait(free.at[i - ring], 2)
        ones[i] = [
            sems.copy(a.at[h, :, :, 1 - y, piece("CA", block_rows)], from_y[i % ring], py),
            sems.copy(a.at[h, 1 - x, :, :, piece("BD", block_rows)], from_x[i % ring], px),
        ]

    def step_two(i):
        a, h = where(i)
        wait_all(ones.pop(i))
        ca, bd = piece("CA", block_rows), piece("BD", block_rows)
        pa, pb, pc_, pd = (piece(n, block_rows) for n in ("A", "B", "C", "D"))
        fy, fx = from_y[i % ring], from_x[i % ring]

        @pl.loop(0, 8)
        def _(j):
            add_blocks(a, (h, j // 4, j % 4, y, ca), fy, (j // 4, j % 4))
            add_blocks(a, (h, x, j // 2, j % 2, bd), fx, (j // 2, j % 2))

        if i + ring < halves:
            for device in (px, py):
                pl.semaphore_signal(free.at[i], inc=1, device_id=device, device_id_type=MESH_ID)
        collect_c = Collect(sems, lambda o: a.at[h, :, o, y, pc_], from_c[i], by_c[i])
        collect_d = Collect(sems, lambda o: a.at[h, x, o, :, pd], from_d[i], by_d[i])
        got = [
            sems.copy(a.at[h, 1 - x, :, y, pa], from_a[i], px),
            sems.copy(a.at[h, x, :, 1 - y, pb], from_b[i], py),
        ]
        twos[i] = (collect_c, collect_d, got)

    def step_two_forward(i):
        a, h = where(i)
        pc_, pd = piece("C", block_rows), piece("D", block_rows)

        def add_c(o):
            for j in range(2):
                add_blocks(a, (h, j, o, y, pc_), by_c[i], j)

        def add_d(o):
            for j in range(2):
                add_blocks(a, (h, x, o, j, pd), by_d[i], j)

        twos[i][0].part = lambda o: a.at[h, :, o, y, pc_]
        twos[i][1].part = lambda o: a.at[h, x, o, :, pd]
        twos[i][0].forward(add_c)
        twos[i][1].forward(add_d)

    def step_three(i):
        a, h = where(i)
        collect_c, collect_d, got = twos.pop(i)
        collect_c.finish()
        collect_d.finish()
        wait_all(got)
        pa, pb, pc_, pd = (piece(n, block_rows) for n in ("A", "B", "C", "D"))
        fc, fd = from_c[i], from_d[i]

        @pl.loop(0, 4)
        def _(j):
            add_blocks(a, (h, x, j, y, pa), from_a[i], j)
            add_blocks(a, (h, x, j, y, pb), from_b[i], j)

        @pl.loop(0, 2)
        def _(j):
            a[h, j, z, y, pc_] = low(
                a[h, j, z, y, pc_].astype(F32)
                + fc[0, j].astype(F32)
                + fc[1, j].astype(F32)
                + fc[2, j].astype(F32)
            )
            a[h, x, z, j, pd] = low(
                a[h, x, z, j, pd].astype(F32)
                + fd[0, j].astype(F32)
                + fd[1, j].astype(F32)
                + fd[2, j].astype(F32)
            )

        ab = piece("AB", block_rows)
        collect = Collect(sems, lambda o: a.at[h, x, o, y, ab], from_z[i], by_z[i])
        got = [
            sems.copy(a.at[h, 1 - x, z, y, pc_], end_c[i], px),
            sems.copy(a.at[h, x, z, 1 - y, pd], end_d[i], py),
        ]
        threes[i] = (collect, got)

    def step_three_forward(i):
        a, h = where(i)
        ab = piece("AB", block_rows)
        collect = threes[i][0]
        collect.part = lambda o: a.at[h, x, o, y, ab]
        collect.forward(lambda o: add_blocks(a, (h, x, o, y, ab), by_z[i], ...))

    def step_four(i):
        a, h = where(i)
        collect, got = threes.pop(i)
        collect.finish()
        wait_all(got)
        fz, o = from_z[i], outs[order[i // 2]]
        if o.shape[0] == block_rows:
            first, columns = 0, pl.ds(h * block_columns, block_columns)
        else:
            first, columns = h * block_rows, slice(None)

        def put(name, value):
            at = piece(name, block_rows)
            o[pl.ds(first + at.start, at.size), columns] = (
                a[h, x, z, y, at].astype(F32) + value
            )

        put("AB", fz[0].astype(F32) + fz[1].astype(F32) + fz[2].astype(F32))
        put("C", end_c[i][...].astype(F32))
        put("D", end_d[i][...].astype(F32))

    run_step = {
        "1": step_one,
        "2": step_two,
        "g": step_two_forward,
        "3": step_three,
        "f": step_three_forward,
        "4": step_four,
    }
    places = {"1": 0, "2": 1, "g": 2, "3": 3, "f": 4, "4": 5}
    steps = collections.deque(slots(halves, places, "12g3f4"))
    ready = [0]

    def advance(n):
        while n > 0 and steps and (steps[0][1] != "1" or steps[0][2] < ready[0]):
            unused, name, i = steps.popleft()
            run_step[name](i)
            n -= 1

    def done(m):
        ready[0] += 2
        advance(2)

    def square_grad(m, at, products):
        size = 4 * block_rows

        @pl.loop(0, 2)
        def _(n):
            rows_at = pl.ds(pl.multiple_of(n * size, size), size)
            value = None
            for left, right in products:
                term = dot(left[rows_at], right())
                value = term if value is None else value + term
            for h in range(2):
                part = low(value[:, h * block_columns : (h + 1) * block_columns])
                total[m][h, at, pl.ds(n * 2, 2)] = part.reshape(2, 2, block_rows, block_columns)

    def put_hidden(m, h, zz, value):
        for yy in range(2):
            part = value[:, yy * block_columns : (yy + 1) * block_columns]
            total[m][h, :, zz, yy] = low(part).reshape(2, block_rows, block_columns)

    def hidden_grad(m, h, left, right):
        @pl.loop(0, 4)
        def _(zz):
            put_hidden(m, h, zz, dot(left, right[:, lanes(zz, quarter)]))

    def both(own, other):
        return jnp.concatenate([own, other], axis=0)

    def send_off(src, dst):
        return sems.copy(src, dst, pc, later=False)

    def pick(first, second):
        return jnp.where(first_live, first, second)

    def back_through(into, act, blocks):
        into[...] = jnp.zeros_like(into)

        @pl.loop(0, blocks)
        def _(s):
            into[...] += dot_nt(act[s // 2, s % 2], square_block(wr, s // 2, s % 2))

    def self_part(mh, gps, gyt, mnt, sbt, l1t, du, r, cot_v, aa, ac, sqkv, sp, grad_aa, out_grad):
        loads = {
            name: local_copy(src, dst)
            for name, src, dst in (
                ("gyt", kept["gyt"], gyt),
                ("mh", kept["mh"], mh),
                ("wt", full[5], wt),
                ("cot", cot, cot_v),
                ("gps", kept["gps"], gps),
                ("wr", full[4], wr),
                ("aa", kept["aa"], aa),
                ("mnt", kept["mnt"], mnt),
                ("sqkv", kept["sqkv"], sqkv),
                ("sp", kept["sp"], sp),
                ("ac", kept["ac"], ac),
                ("sbt", kept["sbt"], sbt),
                ("l1t", kept["l1t"], l1t),
            )
        }
        clear()
        greet(place, sub_peers + dp_peers)
        loads["gyt"].wait()
        loads["mh"].wait()
        for h in range(2):
            left = gyt[:, h * block_rows : (h + 1) * block_rows]
            left = left.reshape(2 * block_rows, 2 * two)
            hidden_grad(5, h, left, mh)
            ready[0] += 1
            advance(1)

        for name in ("wt", "cot", "gps"):
            loads[name].wait()
        for at, value in (
            (pl.ds(0, rows), pick(cot_v[0], cot_v[1])),
            (pl.ds(rows, rows), pick(cot_v[1], cot_v[0])),
        ):
            grad_aa[at] = value
        out_grad[...] = low(grad_aa[...])

        @pl.loop(0, 4)
        def _(s):
            grad = dot(out_grad[...], hidden_block(wt, s))
            du[s // 2, s % 2] = low(grad * gps[:, lanes(s, quarter)].astype(F32))

        sent = send_off(du.at[:, 1 - c], du_sib)
        advance(2)
        for name in ("wr", "aa", "mnt"):
            loads[name].wait()
        back_through(grad_ac, du, 4)
        grad, gain_row = norm_back(aa[...], gain[4:5], grad_ac[...])
        grad_aa[...] += grad
        gain_acc[0, 4:5] = gain_row
        advance(2)
        next_wr = local_copy(full[3], wr)
        next_wt = local_copy(full[2], wt)
        sent.wait_recv()

        @pl.loop(0, 2)
        def _(a):
            square_grad(4, a, [(mnt, lambda: both(du[a, c], du_sib[a]))])

        done(4)

        r[1, 1] = low(grad_aa[...])
        for made in (next_wr, loads["sqkv"], loads["sp"], loads["ac"], loads["sbt"], loads["l1t"]):
            made.wait()
        out_grad[...] = low(dot_nt(r[1, 1], square_block(wr, 1, 1)))

        advance(2)
        for part in range(2):

            @pl.loop(part * pairs, (part + 1) * pairs, unroll=3)
            def _(i):
                at, row_at = lanes(i % pairs, 128), lanes(i // pairs, rows)
                r[0, 0, row_at, at], r[0, 1, row_at, at], r[1, 0, row_at, at] = attention_back(
                    stack_heads(sqkv[0, row_at, at]),
                    sqkv[1, row_at, at],
                    sqkv[2, row_at, at],
                    stack_heads(out_grad[row_at, at]),
                    sp[i],
                    None,
                )

            advance(2)

        sent_r = send_off(r.at[:, 1 - c], r_sib)
        back_through(grad_ac, r, 3)
        grad, gain_row = norm_back(ac[...], gain[3:4], grad_ac[...])
        grad_ac[...] = grad_aa[...] + grad
        gain_acc[0, 3:4] = gain_row
        advance(2)
        sent_r.wait_recv()
        square_grad(3, 0, [(sbt, lambda: both(r[0, c], r_sib[0]))])
        square_grad(3, 1, [(l1t, lambda: both(r[1, c], r_sib[1]))])
        done(3)
        sent.wait_send()
        sent_r.wait_send()
        next_wt.wait()

    def cross_part(
        ch, gpc, ge, cnt, du, mid, lst, rs, xbt, kv, cp, cq, co, dco, xl, dxs, lat_v, grad_mid
    ):
        loads = {
            name: local_copy(src, dst)
            for name, src, dst in (
                ("ch", kept["ch"], ch),
                ("gpc", kept["gpc"], gpc),
                ("wr", full[1], wr),
                ("mid", kept["mid"], mid),
                ("cnt", kept["cnt"], cnt),
                ("cq", kept["cq"], cq),
                ("co", kept["co"], co),
                ("kv", kept["kv"], kv),
                ("cp", kept["cp"], cp),
                ("lst", kept["lst"], lst),
                ("xbt", kept["xbt"], xbt),
                ("lat", lat, lat_v),
            )
        }
        for i in range(2):
            lat_grad_dead = grad_ac[rows:]
            lat_grad[i] = lat_grad_dead
        low_grad = low(grad_ac[:rows])
        ge[...] = low_grad.T.reshape(2, 2, width // 4, rows)
        sent = [send_off(ge.at[:, 1 - c], ge_sib)]
        loads["gpc"].wait()
        dco[...] = low_grad

        @pl.loop(0, 4)
        def _(s):
            grad = dot(dco[...], hidden_block(wt, s))
            du[s // 2, s % 2] = low(grad * gpc[:, lanes(s, quarter)].astype(F32))

        sent.append(send_off(du.at[:, 1 - c], dcu_sib))
        advance(2)
        loads["ch"].wait()
        sent[0].wait_recv()
        for h in range(2):
            at = pl.ds(h * block_rows, block_rows)
            left = [g.reshape(2 * block_rows, rows) for g in (ge[:, c, at], ge_sib[:, at])]
            hidden_grad(2, h, jnp.concatenate(left, axis=1), ch)
        done(2)

        for name in ("wr", "mid", "cnt"):
            loads[name].wait()
        back_through(grad_mid, du, 4)
        grad, gain_row = norm_back(mid[...], gain[2:3], grad_mid[...])
        grad_mid[...] = grad_ac[:rows] + grad
        gain_acc[0, 2:3] = gain_row
        advance(2)
        next_wr = local_copy(full[0], wr)
        sent[1].wait_recv()

        @pl.loop(0, 2)
        def _(a):
            square_grad(1, a, [(cnt, lambda: both(du[a, c], dcu_sib[a]))])

        done(1)

        rs[1] = low(grad_mid[...])
        next_wr.wait()
        dco[...] = low(dot_nt(rs[1], square_block(wr, 1, 1)))
        for name in ("cq", "co", "kv", "cp"):
            loads[name].wait()

        advance(2)
        for part in range(3):

            @pl.loop(part * pairs // 3, (part + 1) * pairs // 3, unroll=2)
            def _(p):
                at = lanes(p, 128)
                out_grad = stack_heads(dco[:, at])
                attended = co[:, at]
                delta = jnp.sum(
                    out_grad.astype(F32) * both(attended, attended), axis=-1, keepdims=True
                )
                rs[0, :, at], kv[0, :, at], kv[1, :, at] = attention_back(
                    stack_heads(cq[:, at]), kv[0, :, at], kv[1, :, at], out_grad, cp[p], delta
                )

            advance(2)

        sent.append(send_off(rs.at[1 - c], rs_sib))
        sent.append(send_off(kv.at[c], dkv_sib))
        advance(2)
        for name in ("lst", "xbt", "lat"):
            loads[name].wait()
        sent[2].wait_recv()
        sent[3].wait_recv()
        square_grad(0, c, [(lst, lambda: both(rs[c], rs_sib[...]))])
        own_tokens, their_tokens = (xbt.at[:, pl.ds(n * tokens, tokens)] for n in range(2))
        square_grad(
            0,
            1 - c,
            [(own_tokens, lambda: kv[1 - c]), (their_tokens, lambda: dkv_sib[...])],
        )
        done(0)

        grad, gain_row = norm_back(
            pick(lat_v[0], lat_v[1]), gain[0:1], dot_nt(rs[0], square_block(wr, 0, 0))
        )
        gain_acc[0, 0:1] = gain_row
        live_grad = grad_mid[...] + grad
        lat_grad[0] = pick(live_grad, lat_grad[0])
        lat_grad[1] = pick(lat_grad[1], live_grad)
        advance(2)
        out = []
        parts = tokens // 256

        def fetch(n):
            return [
                local_copy(kept["xl"].at[pl.ds(n * 256 + i * 128, 128)], xl.at[i]) for i in range(2)
            ]

        fetched = fetch(0)
        for n in range(parts):
            for made in fetched + out:
                made.wait()

            @pl.loop(0, 2)
            def _(i):
                at = pl.ds(pl.multiple_of(n * 256 + i * 128, 128), 128)
                term = dot_nt(kv[0, at], square_block(wr, 0, 1))
                term += dot_nt(kv[1, at], square_block(wr, 1, 0))
                grad, gain_row = norm_back(xl[i].astype(F32), gain[1:2], term)
                dxs[i] = grad
                gain_acc[0, 1:2] += gain_row

            if n + 1 < parts:
                fetched = fetch(n + 1)
            out = [
                local_copy(dxs.at[i], dx.at[pl.ds(n * 256 + i * 128, 128)]) for i in range(2)
            ]
            advance(3)
        for made in out:
            made.wait()
        gain_one = [sems.copy(gain_acc.at[0], spot(gain_sub, k), sub_peers[k]) for k in range(3)]
        advance(3)
        wait_all(gain_one)
        gain_acc[1] = gain_acc[0] + gain_sub[0] + gain_sub[1] + gain_sub[2]
        gain_two = [sems.copy(gain_acc.at[1], spot(gain_dp, k), dp_peers[k]) for k in range(7)]
        for made in sent:
            made.wait_send()
        return gain_two

    def vmem(*shape, dtype=BF16):
        return pltpu.VMEM(shape, dtype)

    holder = {}

    pl.run_scoped(
        self_part,
        vmem(2 * two, hidden),
        vmem(two, hidden),
        vmem(2, width // 4, 2 * two),
        vmem(width, 2 * two),
        vmem(width, 2 * two),
        vmem(width, 2 * two),
        vmem(2, 2, two, quarter),
        vmem(2, 2, two, width),
        vmem(2, rows, width, dtype=F32),
        vmem(two, width, dtype=F32),
        vmem(two, width, dtype=F32),
        vmem(3, two, width),
        vmem(2 * pairs, two, rows),
        vmem(two, width, dtype=F32),
        vmem(two, width),
    )

    def run_cross(*bufs):
        holder["gain"] = cross_part(*bufs)

    pl.run_scoped(
        run_cross,
        vmem(two, hidden),
        vmem(rows, hidden),
        vmem(2, 2, width // 4, rows),
        vmem(width, two),
        vmem(2, 2, rows, quarter),
        vmem(rows, width, dtype=F32),
        vmem(width, two),
        vmem(2, rows, width),
        vmem(width, 2 * tokens),
        vmem(2, tokens, width),
        vmem(pairs, two, tokens),
        vmem(rows, width),
        vmem(rows, width, dtype=F32),
        vmem(rows, width),
        vmem(2, 128, width),
        vmem(2, 128, width, dtype=F32),
        vmem(2, rows, width, dtype=F32),
        vmem(rows, width, dtype=F32),
    )
    advance(len(steps))
    wait_all(holder["gain"])
    gain_out[...] = gain_acc[1] + jnp.sum(gain_dp[...], axis=0)
    sems.drain()


def backward_all(shard, full, norm_gain, latents, cotangent, flags, kept):
    count = len(full)
    rows, width = latents.shape[1:]
    tokens, hidden = kept["xl"].shape[0], kept["mh"].shape[1]
    dims = (rows, tokens, width, hidden)
    two = 2 * rows
    copies = 10 + 6 + 2 * count * (2 + 10 + 6)
    ring, halves = 3, 2 * count
    block_rows, block_columns = full[0].shape[5:]

    def room(number, lead, sixths):
        return [pltpu.VMEM(lead + (block_rows * sixths // 6, block_columns), BF16)] * number

    scratch = [pltpu.VMEM((2,) + full[0].shape[2:], BF16)] * count
    scratch += room(ring, (2, 4), 3) + room(ring, (4, 2), 3)
    scratch += room(halves, (4,), 1) + room(halves, (4,), 1)
    scratch += room(halves, (3, 2), 2) + room(halves, (3, 2), 2) + room(halves, (3,), 2)
    scratch += room(halves, (), 2) + room(halves, (), 2)
    scratch += room(halves, (2,), 2) + room(halves, (2,), 2) + room(halves, (), 2)
    scratch += [
        pltpu.VMEM(full[0].shape, BF16),
        pltpu.VMEM(full[2].shape, BF16),
        pltpu.VMEM((two, width), F32),
        pltpu.VMEM((2, two, hidden // 4), BF16),
        pltpu.VMEM((2, two, width), BF16),
        pltpu.VMEM((2, width // 4, rows), BF16),
        pltpu.VMEM((2, rows, hidden // 4), BF16),
        pltpu.VMEM((rows, width), BF16),
        pltpu.VMEM((tokens, width), BF16),
        pltpu.VMEM((2, 8, width), F32),
        pltpu.VMEM((3, 8, width), F32),
        pltpu.VMEM((7, 8, width), F32),
        pltpu.SemaphoreType.DMA((copies,)),
        pltpu.SemaphoreType.DMA((copies,)),
        pltpu.SemaphoreType.DMA((48,)),
        pltpu.SemaphoreType.REGULAR((halves - ring,)),
    ]
    shapes = [jax.ShapeDtypeStruct(d, F32) for d in shard]
    shapes += [
        jax.ShapeDtypeStruct((8, width), F32),
        jax.ShapeDtypeStruct(latents.shape, F32),
        jax.ShapeDtypeStruct((tokens, width), F32),
    ]
    outs = pl.pallas_call(
        functools.partial(backward_kernel, tuple(kept), dims),
        out_shape=shapes,
        in_specs=[ANY] * count + [VMEM, ANY, ANY, SMEM] + [ANY] * len(kept),
        out_specs=[VMEM] * (count + 2) + [ANY],
        scratch_shapes=scratch,
        compiler_params=pltpu.CompilerParams(
            collective_id=1, has_side_effects=True, vmem_limit_bytes=60 << 20
        ),
        name="backward_and_scatter",
    )(*full, norm_gain, latents, cotangent, flags, *kept.values())
    return outs[:count], *outs[count:]


def finish_kernel(gain_share, gain_rows, count, *refs):
    flags, result, lat_grad, tok_grad, gain_total = refs[:5]
    shards_in = refs[5 : 5 + count]
    out_result, out_lat, out_tok, out_gain = refs[5 + count : 9 + count]
    shards_out = refs[9 + count : 9 + 2 * count]
    gain_in, zeros, sems_in, sems_out = refs[9 + 2 * count : 13 + 2 * count]
    held = refs[13 + 2 * count :]
    tokens, pieces = tok_grad.shape[0], held[-1].shape[0]
    size = tokens // pieces
    live = jnp.where(flags[0] == 0, 0, 1)
    moves = []
    for n in range(pieces):
        at = pl.ds(n * size, size)
        moves.append((tok_grad.at[at], held[-1].at[n], out_tok.at[live, at]))
    moves += zip((result, lat_grad, *shards_in), held, (out_result, out_lat, *shards_out))
    gain_copy = pltpu.make_async_copy(gain_total, gain_in, sems_in.at[len(moves)])
    reads = [
        pltpu.make_async_copy(src, room, sems_in.at[i]) for i, (src, room, dst) in enumerate(moves)
    ]
    for made in reads:
        made.start()
    gain_copy.start()
    zeros[...] = jnp.zeros_like(zeros)
    started = []
    for n in range(pieces):
        started.append(
            pltpu.make_async_copy(
                zeros, out_tok.at[1 - live, pl.ds(n * size, size)], sems_out.at[len(moves) + n]
            )
        )
        started[-1].start()
    for i, (src, room, dst) in enumerate(moves):
        reads[i].wait()
        started.append(pltpu.make_async_copy(room, dst, sems_out.at[i]))
        started[-1].start()
    gain_copy.wait()
    dp = lax.axis_index("dp")
    for i in range(8):

        @pl.when(dp == i)
        def _():
            out_gain[...] = gain_in[:gain_rows, i * gain_share : (i + 1) * gain_share]

    for made in started:
        made.wait()


def finish_all(gain_shape, flags, result, lat_grad, tok_grad, gain_total, shards_in):
    count, pieces = len(shards_in), 8
    tokens, width = tok_grad.shape
    arrays = [result, lat_grad, tok_grad, gain_total, *shards_in]
    shapes = [
        jax.ShapeDtypeStruct(result.shape, F32),
        jax.ShapeDtypeStruct(lat_grad.shape, F32),
        jax.ShapeDtypeStruct((2, tokens, width), F32),
        jax.ShapeDtypeStruct(gain_shape, F32),
    ]
    shapes += [jax.ShapeDtypeStruct(a.shape, F32) for a in shards_in]
    return pl.pallas_call(
        functools.partial(finish_kernel, gain_shape[1], gain_shape[0], count),
        out_shape=shapes,
        in_specs=[SMEM] + [ANY] * len(arrays),
        out_specs=[ANY] * 3 + [VMEM] + [ANY] * count,
        scratch_shapes=[
            pltpu.VMEM(gain_total.shape, F32),
            pltpu.VMEM((tokens // pieces, width), F32),
            pltpu.SemaphoreType.DMA((3 + count + pieces,)),
            pltpu.SemaphoreType.DMA((2 + count + 2 * pieces,)),
            *(pltpu.VMEM(a.shape, F32) for a in (result, lat_grad, *shards_in)),
            pltpu.VMEM((pieces, tokens // pieces, width), F32),
        ],
        compiler_params=pltpu.CompilerParams(vmem_limit_bytes=60 << 20),
        name="write_outputs",
    )(flags, *arrays)


def layer_norm(values, gain_row):
    centred = values - jnp.mean(values, axis=-1, keepdims=True)
    inverse = lax.rsqrt(jnp.mean(centred * centred, axis=-1, keepdims=True) + EPSILON)
    return centred * inverse * gain_row


def norm_backward(values, gain_row, gradient):
    unused, pull_back = jax.vjp(layer_norm, values, gain_row)
    return pull_back(gradient)


def gelu_tanh(values):
    return jax.nn.gelu(values, approximate=True)


def mm(left_side, weight):
    return jnp.dot(left_side, weight, preferred_element_type=F32)


def mm_nt(left_side, weight):
    return lax.dot_general(left_side, weight, (((1,), (1,)), ((), ())), preferred_element_type=F32)


def mm_tn(left_side, gradient):
    return lax.dot_general(
        left_side, gradient, (((0,), (0,)), ((), ())), preferred_element_type=F32
    )


def low(values):
    return values.astype(BF16)


def heads_of(values):
    return values.reshape(values.shape[:-1] + (HEADS, values.shape[-1] // HEADS))


def mlp_forward(residual, gain_row, up, down_t):
    normed = low(layer_norm(residual, gain_row))
    pre_act = mm(normed, up)
    hidden = low(gelu_tanh(pre_act))
    return normed, pre_act, hidden, mm_nt(hidden, down_t)


def mlp_backward(residual, gain_row, normed, pre_act, hidden, up, down_t, grad_out):
    grad_low = low(grad_out)
    grad_down_t = mm_tn(grad_low, hidden)
    grad_hidden = mm(grad_low, down_t)
    unused, gelu_back = jax.vjp(gelu_tanh, pre_act)
    grad_pre = low(gelu_back(grad_hidden)[0])
    grad_up = mm_tn(normed, grad_pre)
    grad_resid, grad_gain = norm_backward(residual, gain_row, mm_nt(grad_pre, up))
    return grad_resid, grad_gain, grad_up, grad_down_t


def live_layer(live_lat, dead_lat, tokens, count, live_cot, dead_cot, weights, norm_gain):
    c_attn, c_up, c_down_t, s_attn, s_up, s_down_t = weights
    rows, width = live_lat.shape
    scale = (width // HEADS) ** (-0.5)
    lat_low = low(layer_norm(live_lat, norm_gain[0]))
    queries = low(mm(lat_low, c_attn[:, :width]))
    token_values = tokens.astype(F32)
    tok_low = low(layer_norm(token_values, norm_gain[1]))
    kv_weight = c_attn[:, width : 3 * width]
    key_value = low(mm(tok_low, kv_weight))
    keys, values = heads_of(key_value[:, :width]), heads_of(key_value[:, width:])
    scores = (
        jnp.einsum("qhd,khd->hqk", heads_of(queries), keys, preferred_element_type=F32) * scale
    )
    valid = (jnp.arange(tokens.shape[0]) < count)[None, None, :]
    probs = jax.nn.softmax(jnp.where(valid, scores, MASKED), axis=-1)
    probs_low = low(probs)
    attended = jnp.einsum("hqk,khd->qhd", probs_low, values, preferred_element_type=F32)
    attended = attended.reshape(rows, width)
    cross_low = low(attended)
    middle = live_lat + mm(cross_low, c_attn[:, 3 * width :])
    c_norm, c_pre, c_hidden, c_mlp = mlp_forward(middle, norm_gain[2], c_up, c_down_t)
    after_cross = jnp.concatenate([middle + c_mlp, dead_lat], axis=0)

    self_low = low(layer_norm(after_cross, norm_gain[3]))
    qkv = low(mm(self_low, s_attn[:, : 3 * width])).reshape(2, rows, 3 * width)
    s_q = heads_of(qkv[..., :width])
    s_k = heads_of(qkv[..., width : 2 * width])
    s_v = heads_of(qkv[..., 2 * width :])
    s_scores = jnp.einsum("iqhd,ikhd->ihqk", s_q, s_k, preferred_element_type=F32) * scale
    s_probs = jax.nn.softmax(s_scores, axis=-1)
    s_probs_low = low(s_probs)
    s_out = jnp.einsum("ihqk,ikhd->iqhd", s_probs_low, s_v, preferred_element_type=F32)
    s_out_low = low(s_out.reshape(2 * rows, width))
    after_attn = after_cross + mm(s_out_low, s_attn[:, 3 * width :])
    m_norm, m_pre, m_hidden, m_mlp = mlp_forward(after_attn, norm_gain[4], s_up, s_down_t)
    result = after_attn + m_mlp

    cotangent = jnp.concatenate([live_cot, dead_cot], axis=0)
    grad_in, gain_four, d_s_up, d_s_down_t = mlp_backward(
        after_attn, norm_gain[4], m_norm, m_pre, m_hidden, s_up, s_down_t, cotangent
    )
    grad_attn = cotangent + grad_in
    grad_y = low(grad_attn)
    d_s_o = mm_tn(s_out_low, grad_y)
    grad_out = heads_of(low(mm_nt(grad_y, s_attn[:, 3 * width :])).reshape(2, rows, width))
    grad_probs = jnp.einsum("iqhd,ikhd->ihqk", grad_out, s_v, preferred_element_type=F32)
    delta = jnp.sum(grad_probs * s_probs, axis=-1, keepdims=True)
    grad_scores = low(s_probs * (grad_probs - delta))
    g_q = jnp.einsum("ihqk,ikhd->iqhd", grad_scores, s_k, preferred_element_type=F32) * scale
    g_k = jnp.einsum("ihqk,iqhd->ikhd", grad_scores, s_q, preferred_element_type=F32) * scale
    g_v = jnp.einsum("ihqk,iqhd->ikhd", s_probs_low, grad_out, preferred_element_type=F32)
    grad_qkv = low(
        jnp.concatenate([g.reshape(2 * rows, width) for g in (g_q, g_k, g_v)], axis=-1)
    )
    d_s_qkv = mm_tn(self_low, grad_qkv)
    grad_in, gain_three = norm_backward(
        after_cross, norm_gain[3], mm_nt(grad_qkv, s_attn[:, : 3 * width])
    )
    grad_cross = grad_attn + grad_in
    live_grad, dead_grad = grad_cross[:rows], grad_cross[rows:]
    grad_in, gain_two, d_c_up, d_c_down_t = mlp_backward(
        middle, norm_gain[2], c_norm, c_pre, c_hidden, c_up, c_down_t, live_grad
    )
    grad_middle = live_grad + grad_in
    grad_cross_y = low(grad_middle)
    d_c_o = mm_tn(cross_low, grad_cross_y)
    grad_cross_out = low(mm_nt(grad_cross_y, c_attn[:, 3 * width :]))
    out_heads = heads_of(grad_cross_out)
    grad_weights = jnp.einsum("qhd,khd->hqk", out_heads, values, preferred_element_type=F32)
    row_delta = jnp.transpose(jnp.sum(heads_of(grad_cross_out.astype(F32) * attended), axis=-1))
    grad_scores = low(probs * (grad_weights - row_delta[..., None]))
    grad_query = low(
        (
            jnp.einsum("hqk,khd->qhd", grad_scores, keys, preferred_element_type=F32) * scale
        ).reshape(rows, width)
    )
    grad_keys = (
        jnp.einsum("hqk,qhd->khd", grad_scores, heads_of(queries), preferred_element_type=F32)
        * scale
    )
    grad_values = jnp.einsum("hqk,qhd->khd", probs_low, out_heads, preferred_element_type=F32)
    grad_kv = low(
        jnp.concatenate(
            [grad_keys.reshape(-1, width), grad_values.reshape(-1, width)], axis=-1
        )
    )
    d_c_kv = mm_tn(tok_low, grad_kv)
    grad_tokens, gain_one = norm_backward(token_values, norm_gain[1], mm_nt(grad_kv, kv_weight))
    d_c_q = mm_tn(lat_low, grad_query)
    grad_in, gain_zero = norm_backward(
        live_lat, norm_gain[0], mm_nt(grad_query, c_attn[:, :width])
    )
    live_lat_grad = grad_middle + grad_in
    d_c_attn = low(jnp.concatenate([d_c_q, d_c_kv, d_c_o], axis=1))
    d_s_attn = low(jnp.concatenate([d_s_qkv, d_s_o], axis=1))
    gain_grad = jnp.stack([gain_zero, gain_one, gain_two, gain_three, gain_four])
    grads = (d_c_attn, low(d_c_up), low(d_c_down_t), d_s_attn, low(d_s_up), low(d_s_down_t))
    return result, live_lat_grad, dead_grad, grad_tokens, grads, gain_grad


def column_blocks(blocks):
    sub, dp, rows, columns = blocks.shape
    return blocks.transpose(1, 2, 0, 3).reshape(dp * rows, sub * columns)


def row_blocks(blocks):
    sub, dp, rows, columns = blocks.shape
    return blocks.transpose(0, 2, 1, 3).reshape(sub * rows, dp * columns)


def shards(*arrays, dp_size, sub_size):
    latents, inputs, counts, flags = arrays[:4]
    cross_attn, cross_up, cross_down, self_attn, self_up, self_down, gains, cotangent = arrays[4:]
    width = latents.shape[-1]
    own = (
        cross_attn,
        cross_up,
        jnp.transpose(cross_down),
        self_attn,
        self_up,
        jnp.transpose(self_down),
    )
    live = jnp.where(flags[0] == 0, 0, 1)
    here = (jnp.arange(inputs.shape[0]) == live)[:, None, None]
    if dp_size == 8 and sub_size == 4:
        full, norm_gain, result, kept = forward_all(
            own, gains, latents, inputs, cotangent, counts, flags
        )
        owned, gain_total, grad_latents, grad_tokens = backward_all(
            [w.shape for w in own], full, norm_gain, latents, cotangent, flags, kept
        )
        result, grad_latents, grad_inputs, gain_owned, *owned = finish_all(
            gains.shape, flags, result, grad_latents, grad_tokens, gain_total, owned
        )
        owned = [jnp.transpose(g) if i in (2, 5) else g for i, g in enumerate(owned)]
        return (result, grad_latents, grad_inputs, *owned, gain_owned)

    blocks = [lax.all_gather(lax.all_gather(w, "dp", axis=0), "sub", axis=0) for w in own]
    norm_gain = lax.all_gather(gains, "dp", axis=1, tiled=True)
    transposed = (False, False, True, False, False, True)
    weights = [
        row_blocks(b) if flip else column_blocks(b) for b, flip in zip(blocks, transposed)
    ]

    def item(array, index):
        return lax.dynamic_index_in_dim(array, index, 0, keepdims=False)

    result, live_grad, dead_grad, grad_tokens, grads, gain_grad = live_layer(
        item(latents, live),
        item(latents, 1 - live),
        item(inputs, live),
        item(counts, live),
        item(cotangent, live),
        item(cotangent, 1 - live),
        weights,
        norm_gain.astype(F32),
    )

    def both(live_part, dead_part):
        first = jnp.where(live == 0, live_part, dead_part)
        second = jnp.where(live == 0, dead_part, live_part)
        return jnp.stack([first, second])

    rows = latents.shape[1]
    result = both(result[:rows], result[rows:])
    grad_latents = both(live_grad, dead_grad)
    grad_inputs = jnp.where(here, grad_tokens[None], 0.0)

    def blocks_of(grad, shape, flip):
        r, c = shape
        if flip:
            return grad.reshape(sub_size, r, dp_size, c).transpose(0, 2, 1, 3)
        return grad.reshape(dp_size, r, sub_size, c).transpose(2, 0, 1, 3)

    grads = [blocks_of(g, w.shape, flip) for g, w, flip in zip(grads, own, transposed)]
    owned = [lax.psum_scatter(g, "sub", scatter_dimension=0) for g in grads]
    owned = [lax.psum_scatter(g.astype(F32), "dp", scatter_dimension=0) for g in owned]
    gain_owned = lax.psum(gain_grad, "sub")
    gain_owned = lax.psum_scatter(gain_owned, "dp", scatter_dimension=1, tiled=True)
    owned = [jnp.transpose(g) if flip else g for g, flip in zip(owned, transposed)]
    return (result, grad_latents, grad_inputs, *owned, gain_owned)


def solution(mesh):
    item = P(("dp", "sub"), None, None)
    weight = P("dp", "sub")
    gain = P(None, "dp")
    placed = (item, item, P(("dp", "sub")), P()) + (weight,) * 6 + (gain, item)
    return jax.shard_map(
        functools.partial(shards, dp_size=mesh.shape["dp"], sub_size=mesh.shape["sub"]),
        mesh=mesh,
        in_specs=placed,
        out_specs=(item, item, item) + (weight,) * 6 + (gain,),
        check_vma=False,
    )
```
